32 devices in a mesh: pts: 8 (over y, x, core), cells: 4 (over z).
Axes of the slice: x: 2, y: 2, z: 4, core: 2. Of those that a mesh axis runs over, the one named last changes fastest.
Arguments:
- codes: int32 [4096, 512], P(('pts', 'cells')), may hold values from -127 to 127
- exponents: int32 [4096], P(('pts', 'cells')), may hold values from 6 to 9
- centroids: bfloat16 [24576, 512], P('cells'), as said below
- counters: int32 [24576], P('cells'), may hold values from 0 to 4095
Outputs:
- cell_sums: float32 [4, 6144, 512], P('cells', 'pts')
- cell_mass: float32 [4, 6144], P('cells', 'pts')
The draws below stay inside these ranges and needn't reach their ends.
Inputs may be any that keep to these rules, and one draw needn't show every extreme that they name: `centroids`: centroids are real-valued with row scales that differ from row to row.
All inputs are finite; a program needn't handle non-finite values.
Results may differ from the reference program's by a relative error of at most 0.013.
Values may be sent and summed in bfloat16 or wider, within the bound.
No kernel may reach another device: no remote copies, remote signals or barrier semaphores. Data moves between devices by JAX's collectives and lax.ppermute only.
A program may use at most 64 MiB of HBM per device.

```python
import jax
import jax.numpy as jnp
from jax import lax

D = 512
K = 24576
PTS = 4096
C_DEV = 6144
N_CELLS = 4


def draw_centroids(key, part):
    first = jax.random.fold_in(key, 11)
    second = jax.random.fold_in(key, 12)
    row_scale = jnp.exp(jax.random.uniform(second, (K, 1), jnp.float32, -1.2, 1.2))
    base = jax.random.normal(first, (K, D), jnp.float32)
    return (base * row_scale).astype(jnp.bfloat16)


def set_ends(drawn, key, smallest, high):
    shape = drawn.shape
    index_at = [jax.random.randint(jax.random.fold_in(key, axis), (), 0, shape[axis]) for axis in range(len(shape))]
    drawn = drawn.at[tuple(index_at)].set(smallest)
    longest = shape.index(max(shape))
    index_at[longest] = (index_at[longest] + 1) % shape[longest]
    return drawn.at[tuple(index_at)].set(high)


def setup_inputs(seed: int = 0) -> dict:
    key_list = jax.random.split(jax.random.key(seed), 5)
    return {
        "codes": set_ends(jax.random.randint(key_list[0], (PTS, D), -127, 128), jax.random.fold_in(key_list[0], 1), -127, 127).astype(jnp.int32),
        "exponents": set_ends(jax.random.randint(key_list[1], (PTS,), 6, 10), jax.random.fold_in(key_list[1], 1), 6, 9).astype(jnp.int32),
        "centroids": draw_centroids(jax.random.fold_in(key_list[4], 71), 0),
        "counters": set_ends(jax.random.randint(key_list[3], (K,), 0, 4096), jax.random.fold_in(key_list[3], 1), 0, 4095).astype(jnp.int32),
    }


def reference(codes, exponents, centroids, counters):
    points = (codes.astype(jnp.float32) * jnp.exp2(-exponents.astype(jnp.float32))[:, None]).astype(jnp.bfloat16)
    inverse = lax.rsqrt(counters.astype(jnp.float32) + 1.0)
    beta = 4.0 / D ** 0.5
    block = 512 if PTS % 512 == 0 else PTS
    blocks = points.reshape(PTS // block, block, D)

    def step(carry, rows):
        sums, mass = carry
        logits = jnp.dot(rows, centroids.T, preferred_element_type=jnp.float32) * beta
        top = lax.optimization_barrier(jnp.max(logits, axis=1, keepdims=True))
        expo = jnp.exp(logits - top)
        total = lax.optimization_barrier(jnp.sum(expo, axis=1))
        novel = jnp.dot(expo, inverse, preferred_element_type=jnp.float32)
        weight = novel / total
        share = (expo * (weight / total)[:, None]).astype(jnp.bfloat16)
        mass = mass + lax.optimization_barrier(jnp.sum(share.astype(jnp.float32), axis=0))
        sums = sums + jnp.dot(share.T, rows, preferred_element_type=jnp.float32)
        return ((sums, mass), None)
    init = (jnp.zeros((K, D), jnp.float32), jnp.zeros((K,), jnp.float32))
    (sums, mass), unused = lax.scan(step, init, blocks)
    return (sums.reshape(N_CELLS, C_DEV, D), mass.reshape(N_CELLS, C_DEV))
```

```python
import math

import jax
import jax.numpy as jnp
from jax import lax
from jax.sharding import Mesh, PartitionSpec as P

GATHER_BYTES = 8 << 20


def to_points(codes, exponents):
    scaled = codes.astype(jnp.float32) * jnp.exp2(-exponents.astype(jnp.float32))[:, None]
    return scaled.astype(jnp.bfloat16)


def split_points(codes, exponents, centroids, counters):
    local_rows = to_points(codes, exponents)
    points = lax.all_gather(local_rows, "cells", axis=0, tiled=True)
    beta = 4.0 / math.sqrt(points.shape[1])
    logits = (
        lax.dot_general(
            points, centroids, (((1,), (1,)), ((), ())), preferred_element_type=jnp.float32
        )
        * beta
    )
    inverse = lax.rsqrt(counters.astype(jnp.float32) + 1.0)
    top = lax.pmax(jnp.max(logits, axis=1), "cells")
    expo = jnp.exp(logits - top[:, None])
    total, novel = lax.psum(
        (jnp.sum(expo, axis=1), jnp.dot(expo, inverse, preferred_element_type=jnp.float32)), "cells"
    )
    weight = novel / total
    share = (expo * (weight / total)[:, None]).astype(jnp.bfloat16)
    mass_local = jnp.sum(share.astype(jnp.float32), axis=0)
    sums_local = lax.dot_general(
        share, points, (((0,), (0,)), ((), ())), preferred_element_type=jnp.float32
    )
    pts = ("hi", "lo")
    sums = lax.psum_scatter(sums_local, pts, scatter_dimension=0, tiled=True)
    mass = lax.psum_scatter(mass_local, pts, scatter_dimension=0, tiled=True)
    return (sums[None], mass[None])


def split_cells(codes, exponents, centroids, counters):
    n_hi, n_lo = lax.axis_size("hi"), lax.axis_size("lo")
    hi, lo = lax.axis_index("hi"), lax.axis_index("lo")
    group = ("hi", "cells")
    local_rows = to_points(codes, exponents)
    points = lax.all_gather(local_rows, group, axis=0, tiled=True)
    beta = 4.0 / math.sqrt(points.shape[1])
    per_pair = centroids.shape[0] // n_hi
    mine = lax.dynamic_slice_in_dim(centroids, hi * per_pair, per_pair)
    inverse = lax.rsqrt(
        lax.dynamic_slice_in_dim(counters, hi * per_pair, per_pair).astype(jnp.float32) + 1.0
    )
    logits = (
        lax.dot_general(
            points, mine, (((1,), (1,)), ((), ())), preferred_element_type=jnp.float32
        )
        * beta
    )
    top = jnp.max(logits, axis=1)
    expo = jnp.exp(logits - top[:, None])
    stats = jnp.stack(
        [top, jnp.sum(expo, axis=1), jnp.dot(expo, inverse, preferred_element_type=jnp.float32)]
    )
    every = lax.all_gather(stats, group, axis=0)
    tops = every[:, 0]
    highest = jnp.max(tops, axis=0)
    scale = jnp.exp(tops - highest)
    total = jnp.sum(every[:, 1] * scale, axis=0)
    novel = jnp.sum(every[:, 2] * scale, axis=0)
    factor = jnp.exp(top - highest) * (novel / total / total)
    share = (expo * factor[:, None]).astype(jnp.bfloat16)
    per_device = per_pair // n_lo
    sums = mass = None
    for step in range(n_lo):
        away = (n_lo - 1 - step)
        block = lax.dynamic_slice_in_dim(share, (lo + away) % n_lo * per_device, per_device, axis=1)
        part = lax.dot_general(block, points, (((0,), (0,)), ((), ())), preferred_element_type=jnp.float32)
        part_mass = jnp.sum(block.astype(jnp.float32), axis=0)
        if away:
            hops = [(at, (at + away) % n_lo) for at in range(n_lo)]
            part, part_mass = (lax.ppermute(a, "lo", hops) for a in (part, part_mass))
        sums = part if sums is None else sums + part
        mass = part_mass if mass is None else mass + part_mass
    return (sums[None], mass[None])


def solution(mesh):
    pts, cells = (mesh.shape[name] for name in ("pts", "cells"))
    fine = Mesh(mesh.devices.reshape(pts // 2, 2, cells), ("hi", "lo", "cells"))
    in_specs = (P(("hi", "lo", "cells"), None), P(("hi", "lo", "cells")), P("cells", None), P("cells"))
    out_specs = (P("cells", ("hi", "lo"), None), P("cells", ("hi", "lo")))

    def run(codes, exponents, centroids, counters):
        small = codes.size * 2 <= GATHER_BYTES
        body = split_cells if small else split_points
        mapped = jax.shard_map(body, mesh=fine, in_specs=in_specs, out_specs=out_specs, check_vma=False)
        return mapped(codes, exponents, centroids, counters)

    return run
```

```python
import functools
import math

import jax
import jax.numpy as jnp
from jax import lax
from jax.experimental import pallas as pl
from jax.experimental.pallas import tpu as pltpu
from jax.sharding import Mesh, PartitionSpec as P

GATHER_BYTES = 8 << 20
VMEM_BYTES = 40 << 20


def to_points(codes, exponents):
    scaled = codes.astype(jnp.float32) * jnp.exp2(-exponents.astype(jnp.float32))[:, None]
    return scaled.astype(jnp.bfloat16)


def split_points(codes, exponents, centroids, counters):
    local_rows = to_points(codes, exponents)
    points = lax.all_gather(local_rows, "cells", axis=0, tiled=True)
    beta = 4.0 / math.sqrt(points.shape[1])
    logits = (
        lax.dot_general(
            points, centroids, (((1,), (1,)), ((), ())), preferred_element_type=jnp.float32
        )
        * beta
    )
    inverse = lax.rsqrt(counters.astype(jnp.float32) + 1.0)
    top = lax.pmax(jnp.max(logits, axis=1), "cells")
    expo = jnp.exp(logits - top[:, None])
    total, novel = lax.psum(
        (jnp.sum(expo, axis=1), jnp.dot(expo, inverse, preferred_element_type=jnp.float32)), "cells"
    )
    weight = novel / total
    share = (expo * (weight / total)[:, None]).astype(jnp.bfloat16)
    mass_local = jnp.sum(share.astype(jnp.float32), axis=0)
    sums_local = lax.dot_general(
        share, points, (((0,), (0,)), ((), ())), preferred_element_type=jnp.float32
    )
    sums = lax.psum_scatter(sums_local, "pts", scatter_dimension=0, tiled=True)
    mass = lax.psum_scatter(mass_local, "pts", scatter_dimension=0, tiled=True)
    return (sums[None], mass[None])


def swap(a, axis):
    return lax.ppermute(a, axis, [(0, 1), (1, 0)])


def rotate(a, axis, by):
    size = lax.axis_size(axis)
    return lax.ppermute(a, axis, [((at + by) % size, at) for at in range(size)])


def expo_kernel(rate, near, along_x, along_y, across, cells, inverse, expo, block_top, stats, points):
    step = pl.program_id(0)
    rows = near.shape[0]

    @pl.when(step == 0)
    def _():
        for at, piece in enumerate((near, along_x, along_y, across)):
            points[at * rows : (at + 1) * rows, :] = piece[...]

    logits = lax.dot_general(
        cells[...], points[...], (((1,), (1,)), ((), ())), preferred_element_type=jnp.float32
    )
    top = jnp.max(logits, axis=0, keepdims=True)
    value = jnp.exp2((logits - top) * rate)
    expo[...] = value.astype(jnp.bfloat16)
    total = jnp.sum(value, axis=0, keepdims=True)
    novel = jnp.sum(value * inverse[...], axis=0, keepdims=True)
    block_top[pl.ds(step, 1), :] = top

    @pl.when(step == 0)
    def _():
        stats[...] = jnp.concatenate([top, total, novel], axis=0)

    @pl.when(step > 0)
    def _():
        so_far = stats[...]
        highest = jnp.maximum(so_far[:1], top)
        old, new = jnp.exp2((so_far[:1] - highest) * rate), jnp.exp2((top - highest) * rate)
        stats[...] = jnp.concatenate(
            [highest, so_far[1:2] * old + total * new, so_far[2:] * old + novel * new], axis=0
        )


def expo_call(rate, block, pieces, cells, inverse):
    rows, width = pieces[0].shape
    count, n_points = cells.shape[0], rows * len(pieces)
    steps = count // block
    whole = lambda *shape: pl.BlockSpec(shape, lambda i: (0,) * len(shape))
    return pl.pallas_call(
        functools.partial(expo_kernel, rate),
        grid=(steps,),
        in_specs=[whole(rows, width)] * 4
        + [pl.BlockSpec((block, width), lambda i: (i, 0)), pl.BlockSpec((block, 1), lambda i: (i, 0))],
        out_specs=[
            pl.BlockSpec((block, n_points), lambda i: (i, 0)),
            whole(steps, n_points),
            whole(3, n_points),
            whole(n_points, width),
        ],
        out_shape=[
            jax.ShapeDtypeStruct((count, n_points), jnp.bfloat16),
            jax.ShapeDtypeStruct((steps, n_points), jnp.float32),
            jax.ShapeDtypeStruct((3, n_points), jnp.float32),
            jax.ShapeDtypeStruct((n_points, width), jnp.bfloat16),
        ],
        compiler_params=pltpu.CompilerParams(vmem_limit_bytes=VMEM_BYTES),
        cost_estimate=pl.CostEstimate(
            flops=2 * count * n_points * width,
            bytes_accessed=2 * (count * width + n_points * width + count * n_points),
            transcendentals=count * n_points,
        ),
    )(*pieces, cells, inverse)


def sums_kernel(n, *refs):
    expos, points, (factor, sums, mass) = refs[:n], refs[n : 2 * n], refs[2 * n :]
    total, weight = None, None
    for at in range(n):
        share = (expos[at][...].astype(jnp.float32) * factor[0, at : at + 1, :]).astype(jnp.bfloat16)
        part = jnp.dot(share, points[at][...], preferred_element_type=jnp.float32)
        wide = share.astype(jnp.float32)
        lanes = sum(wide[:, i : i + 128] for i in range(0, wide.shape[1], 128))
        total = part if total is None else total + part
        weight = lanes if weight is None else weight + lanes
    sums[...] = total.astype(sums.dtype)
    mass[0] = jnp.sum(weight.T, axis=0, keepdims=True)


def sums_call(block, first, count, expos, points, factor, dtype):
    n = len(expos)
    n_points, width = points[0].shape
    return pl.pallas_call(
        functools.partial(sums_kernel, n),
        grid=(count,),
        in_specs=[pl.BlockSpec((block, n_points), lambda i: (i + first, 0))] * n
        + [pl.BlockSpec((n_points, width), lambda i: (0, 0))] * n
        + [pl.BlockSpec((1, n, n_points), lambda i: (i + first, 0, 0))],
        out_specs=[
            pl.BlockSpec((block, width), lambda i: (i, 0)),
            pl.BlockSpec((1, 1, block), lambda i: (i, 0, 0)),
        ],
        out_shape=[
            jax.ShapeDtypeStruct((count * block, width), dtype),
            jax.ShapeDtypeStruct((count, 1, block), jnp.float32),
        ],
        compiler_params=pltpu.CompilerParams(vmem_limit_bytes=VMEM_BYTES),
        cost_estimate=pl.CostEstimate(
            flops=2 * count * block * n * n_points * width,
            bytes_accessed=2 * n * n_points * (count * block + width) + 4 * count * block * width,
            transcendentals=0,
        ),
    )(*expos, *points, factor)


def merge(rate, stats):
    highest = functools.reduce(jnp.maximum, [s[0] for s in stats])
    scales = [jnp.exp2((s[0] - highest) * rate) for s in stats]
    total = sum(s[1] * scale for s, scale in zip(stats, scales))
    novel = sum(s[2] * scale for s, scale in zip(stats, scales))
    return jnp.stack([highest, total, novel])


def split_cells(codes, exponents, centroids, counters):
    n = lax.axis_size("cells")
    chip = lax.axis_index("y") * lax.axis_size("x") + lax.axis_index("x")
    lo = lax.axis_index("lo")
    own = to_points(codes, exponents)
    rate = 4.0 / math.sqrt(own.shape[1]) * math.log2(math.e)

    per_device = centroids.shape[0] // (4 * 2)
    block = per_device // 2

    def halves(a):
        start = chip * 2 * per_device
        other = lax.dynamic_slice_in_dim(a, start + (1 - lo) * per_device, per_device)
        return jnp.concatenate([other, lax.dynamic_slice_in_dim(a, start + lo * per_device, per_device)])

    cells = halves(centroids)
    inverse = lax.rsqrt(halves(counters).astype(jnp.float32) + 1.0)[:, None]

    expos, tops, stats, points = [], [], [], []
    for shift in range(n):
        near = rotate(own, "cells", shift) if shift else own
        along_x, along_y = swap(near, "x"), swap(near, "y")
        across = swap(along_x, "y") if shift % 2 else swap(along_y, "x")
        expo, top, stat, chunk = expo_call(rate, block, (near, along_x, along_y, across), cells, inverse)
        from_x, from_y = swap(stat, "x"), swap(stat, "y")
        from_xy = lax.ppermute(stat, ("y", "x"), [(0, 3), (1, 2), (2, 1), (3, 0)])
        place = lambda a, order: a.reshape(3, 4, -1)[:, list(order)].reshape(a.shape)
        stat = merge(
            rate,
            [stat, place(from_x, (1, 0, 3, 2)), place(from_y, (2, 3, 0, 1)), place(from_xy, (3, 2, 1, 0))],
        )
        expos.append(expo), tops.append(top), stats.append(stat), points.append(chunk)

    mine = jnp.stack(stats)
    others = [rotate(mine, "cells", shift) for shift in range(1, n)]
    factors = []
    for shift in range(n):
        top, total, novel = merge(
            rate, [mine[shift]] + [a[(shift - by) % n] for by, a in zip(range(1, n), others)]
        )
        factors.append(jnp.exp2((tops[shift] - top) * rate) * (novel / total / total))
    factor = jnp.stack(factors, axis=1)

    there, mass_there = sums_call(block, 0, 2, expos, points, factor, jnp.bfloat16)
    there, mass_there = swap(there, "lo"), swap(mass_there, "lo")
    here, mass_here = sums_call(block, 2, 2, expos, points, factor, jnp.float32)
    return ((here + there.astype(jnp.float32))[None], (mass_here + mass_there).reshape(1, -1))


def solution(mesh):
    pts, cells = (mesh.shape[name] for name in ("pts", "cells"))
    square = pts == 8
    shape, names = ((2, 2, 2, cells), ("y", "x", "lo", "cells")) if square else ((pts, cells), ("pts", "cells"))
    fine = Mesh(mesh.devices.reshape(shape), names)
    spread = names[:-1]
    in_specs = (P(names, None), P(names), P("cells", None), P("cells"))
    out_specs = (P("cells", spread, None), P("cells", spread))

    def run(codes, exponents, centroids, counters):
        small = codes.size * 2 <= GATHER_BYTES
        body = split_cells if square and small else split_points
        mapped = jax.shard_map(body, mesh=fine, in_specs=in_specs, out_specs=out_specs, check_vma=False)
        return mapped(codes, exponents, centroids, counters)

    return run
```

```python
import functools
import math

import jax
import jax.numpy as jnp
from jax import lax
from jax.experimental import pallas as pl
from jax.experimental.pallas import tpu as pltpu
from jax.sharding import Mesh, PartitionSpec as P

GATHER_BYTES = 8 << 20
VMEM_BYTES = 16 << 20


def to_points(codes, exponents):
    scaled = codes.astype(jnp.float32) * jnp.exp2(-exponents.astype(jnp.float32))[:, None]
    return scaled.astype(jnp.bfloat16)


def split_points(codes, exponents, centroids, counters):
    local_rows = to_points(codes, exponents)
    points = lax.all_gather(local_rows, "cells", axis=0, tiled=True)
    beta = 4.0 / math.sqrt(points.shape[1])
    logits = (
        lax.dot_general(
            points, centroids, (((1,), (1,)), ((), ())), preferred_element_type=jnp.float32
        )
        * beta
    )
    inverse = lax.rsqrt(counters.astype(jnp.float32) + 1.0)
    top = lax.pmax(jnp.max(logits, axis=1), "cells")
    expo = jnp.exp(logits - top[:, None])
    total, novel = lax.psum(
        (jnp.sum(expo, axis=1), jnp.dot(expo, inverse, preferred_element_type=jnp.float32)), "cells"
    )
    weight = novel / total
    share = (expo * (weight / total)[:, None]).astype(jnp.bfloat16)
    mass_local = jnp.sum(share.astype(jnp.float32), axis=0)
    sums_local = lax.dot_general(
        share, points, (((0,), (0,)), ((), ())), preferred_element_type=jnp.float32
    )
    sums = lax.psum_scatter(sums_local, "pts", scatter_dimension=0, tiled=True)
    mass = lax.psum_scatter(mass_local, "pts", scatter_dimension=0, tiled=True)
    return (sums[None], mass[None])


def exchange(a, axes, partner):
    count = math.prod(lax.axis_size(axis) for axis in axes)
    return lax.ppermute(a, axes, [(partner(at), at) for at in range(count)])


def in_vmem(n):
    return [pl.BlockSpec(memory_space=pltpu.VMEM)] * n


def points_kernel(codes, exponents, points):
    rows, width = codes.shape
    scale = jnp.exp2(-exponents[...].astype(jnp.float32))
    scale = jnp.broadcast_to(scale, (128, rows)).T
    for at in range(0, width, 128):
        points[:, at : at + 128] = (codes[:, at : at + 128].astype(jnp.float32) * scale).astype(jnp.bfloat16)


def points_call(codes, exponents):
    return pl.pallas_call(
        points_kernel,
        in_specs=in_vmem(2),
        out_specs=in_vmem(1)[0],
        out_shape=jax.ShapeDtypeStruct(codes.shape, jnp.bfloat16),
        compiler_params=pltpu.CompilerParams(vmem_limit_bytes=VMEM_BYTES),
    )(codes, exponents[None])


def expo_kernel(rate, block, place, near, first, second, cells, inverse, expo, tops, stats, points):
    rows = near.shape[0]
    pieces = (near[...], first[...], second[:rows, :], second[rows:, :])
    for at, piece in enumerate(pieces):
        points[pl.ds(pl.multiple_of(place[at] * rows, rows), rows), :] = piece
    every = points[...]
    highest = total = novel = None
    for at in range(cells.shape[0] // block):
        here = slice(at * block, (at + 1) * block)
        logits = lax.dot_general(
            cells[here, :], every, (((1,), (1,)), ((), ())), preferred_element_type=jnp.float32
        )
        top = jnp.max(logits, axis=0, keepdims=True)
        value = jnp.exp2((logits - top) * rate)
        expo[here, :] = value.astype(jnp.bfloat16)
        tops[at : at + 1, :] = top
        part = jnp.sum(value, axis=0, keepdims=True)
        weighed = jnp.concatenate(
            [
                jnp.sum(value[:, i : i + 128] * inverse[here, :], axis=0, keepdims=True)
                for i in range(0, value.shape[1], 128)
            ],
            axis=1,
        )
        if at:
            higher = jnp.maximum(highest, top)
            old, new = jnp.exp2((highest - higher) * rate), jnp.exp2((top - higher) * rate)
            highest, total, novel = higher, total * old + part * new, novel * old + weighed * new
        else:
            highest, total, novel = top, part, weighed
    stats[...] = jnp.concatenate([highest, total, novel], axis=0)


def expo_call(rate, block, place, pieces, cells, inverse):
    count, width = cells.shape
    n_points = sum(piece.shape[0] for piece in pieces)
    return pl.pallas_call(
        functools.partial(expo_kernel, rate, block),
        in_specs=[pl.BlockSpec(memory_space=pltpu.SMEM)] + in_vmem(5),
        out_specs=in_vmem(4),
        out_shape=[
            jax.ShapeDtypeStruct((count, n_points), jnp.bfloat16),
            jax.ShapeDtypeStruct((count // block, n_points), jnp.float32),
            jax.ShapeDtypeStruct((3, n_points), jnp.float32),
            jax.ShapeDtypeStruct((n_points, width), jnp.bfloat16),
        ],
        compiler_params=pltpu.CompilerParams(vmem_limit_bytes=VMEM_BYTES),
        cost_estimate=pl.CostEstimate(
            flops=2 * count * n_points * width,
            bytes_accessed=2 * (count * width + n_points * width + count * n_points),
            transcendentals=count * n_points,
        ),
    )(place, *pieces, cells, inverse)


def weighed_sums(first, count, expos, points, factor):
    total = weight = None
    for at, (expo, chunk) in enumerate(zip(expos, points)):
        scale = factor[at, first // count : first // count + 1, :]
        share = (expo[first : first + count, :].astype(jnp.float32) * scale).astype(jnp.bfloat16)
        part = jnp.dot(share, chunk[...], preferred_element_type=jnp.float32)
        wide = share.astype(jnp.float32)
        lanes = sum(wide[:, i : i + 128] for i in range(0, wide.shape[1], 128))
        total = part if total is None else total + part
        weight = lanes if weight is None else weight + lanes
    return total, jnp.sum(weight.T, axis=0, keepdims=True)


def sums_kernel(n, block, first, *refs):
    expos, points, (factor, sums, mass) = refs[:n], refs[n : 2 * n], refs[2 * n :]
    for at in range(sums.shape[0] // block):
        here = slice(at * block, (at + 1) * block)
        total, weight = weighed_sums((first + at) * block, block, expos, points, factor)
        sums[here, :] = total.astype(sums.dtype)
        mass[:, here] = weight


def last_kernel(n, block, first, *refs):
    expos, points, (factor, early, early_mass, there, there_mass, sums, mass) = refs[:n], refs[n : 2 * n], refs[2 * n :]
    done = early.shape[0]
    sums[:done, :] = early[...] + there[:done, :].astype(jnp.float32)
    mass[:, :done] = early_mass[...] + there_mass[:, :done]
    for at in range(sums.shape[0] // block - done // block):
        here = slice(done + at * block, done + (at + 1) * block)
        total, weight = weighed_sums((first + at) * block, block, expos, points, factor)
        sums[here, :] = total + there[here, :].astype(jnp.float32)
        mass[:, here] = weight + there_mass[:, here]


def sums_call(kernel, block, first, count, expos, points, factor, *more, rows, dtype):
    n = len(expos)
    n_points, width = points[0].shape
    return pl.pallas_call(
        functools.partial(kernel, n, block, first),
        in_specs=in_vmem(2 * n + 1 + len(more)),
        out_specs=in_vmem(2),
        out_shape=[jax.ShapeDtypeStruct((rows, width), dtype), jax.ShapeDtypeStruct((1, rows), jnp.float32)],
        compiler_params=pltpu.CompilerParams(vmem_limit_bytes=VMEM_BYTES),
        cost_estimate=pl.CostEstimate(
            flops=2 * count * block * n * n_points * width,
            bytes_accessed=2 * n * n_points * (count * block + width) + 4 * rows * width,
            transcendentals=0,
        ),
    )(*expos, *points, factor, *more)


def merge(rate, mine, theirs):
    top = jnp.maximum(mine[0], theirs[0])
    old, new = jnp.exp2((mine[0] - top) * rate), jnp.exp2((theirs[0] - top) * rate)
    return jnp.stack([top, mine[1] * old + theirs[1] * new, mine[2] * old + theirs[2] * new])


def split_cells(codes, exponents, centroids, counters):
    chip = lax.axis_index("y") * 2 + lax.axis_index("x")
    lo = lax.axis_index("lo")
    own = points_call(codes, exponents)
    rate = 4.0 / math.sqrt(own.shape[1]) * math.log2(math.e)
    plane = ("y", "x", "lo")

    turn = lambda a: exchange(a, plane, lambda at: at ^ (4 if at % 2 else 2))
    turn_back = lambda a: exchange(a, plane, lambda at: at ^ (2 if at % 2 else 4))
    along_z = lambda a, by: exchange(a, ("cells",), lambda at: at ^ by)
    place = jnp.stack([chip, chip ^ (1 + lo), chip ^ (2 - lo), chip ^ 3]).astype(jnp.int32)

    per_device = centroids.shape[0] // 8
    block = per_device // 2

    def halves(a):
        start = chip * 2 * per_device
        other = lax.dynamic_slice_in_dim(a, start + (1 - lo) * per_device, per_device)
        return jnp.concatenate([other, lax.dynamic_slice_in_dim(a, start + lo * per_device, per_device)])

    cells = halves(centroids)
    inverse = lax.rsqrt(halves(counters).astype(jnp.float32) + 1.0)
    inverse = jnp.broadcast_to(inverse[:, None], (inverse.shape[0], 128))

    expos, tops, stats, points = [], [], [], []
    for step in range(4):
        near = along_z(own, step) if step else own
        first = turn(near)
        second = turn_back(jnp.concatenate([near, first]))
        expo, top, stat, chunk = expo_call(rate, block, place, (near, first, second), cells, inverse)
        expos.append(expo), tops.append(top), stats.append(stat), points.append(chunk)

    stat = jnp.stack(stats, axis=1)
    for axis in ("x", "y"):
        stat = merge(rate, stat, exchange(stat, (axis,), lambda at: at ^ 1))
    for by in (1, 2):
        theirs = along_z(stat, by)
        theirs = jnp.stack([theirs[:, step ^ by] for step in range(4)], axis=1)
        stat = merge(rate, stat, theirs)
    factor = jnp.exp2((jnp.stack(tops) - stat[0][:, None]) * rate) * (stat[2] / stat[1] / stat[1])[:, None]

    sums = functools.partial(sums_call, expos=expos, points=points, factor=factor)
    there, there_mass = sums(sums_kernel, block, 0, 2, rows=per_device, dtype=jnp.bfloat16)
    there, there_mass = (exchange(a, ("lo",), lambda at: at ^ 1) for a in (there, there_mass))
    early, early_mass = sums(sums_kernel, block, 2, 1, rows=block, dtype=jnp.float32)
    out, mass = sums_call(
        last_kernel, block, 3, 1, expos, points, factor, early, early_mass, there, there_mass,
        rows=per_device, dtype=jnp.float32,
    )
    return (out[None], mass)


def solution(mesh):
    pts, cells = (mesh.shape[name] for name in ("pts", "cells"))
    square = (pts, cells) == (8, 4)
    shape, names = ((2, 2, 2, cells), ("y", "x", "lo", "cells")) if square else ((pts, cells), ("pts", "cells"))
    fine = Mesh(mesh.devices.reshape(shape), names)
    spread = names[:-1]
    in_specs = (P(names, None), P(names), P("cells", None), P("cells"))
    out_specs = (P("cells", spread, None), P("cells", spread))

    def run(codes, exponents, centroids, counters):
        small = codes.size * 2 <= GATHER_BYTES
        body = split_cells if square and small else split_points
        mapped = jax.shard_map(body, mesh=fine, in_specs=in_specs, out_specs=out_specs, check_vma=False)
        return mapped(codes, exponents, centroids, counters)

    return run
```

```python
import functools
import math

import jax
import jax.numpy as jnp
from jax import lax
from jax.experimental import pallas as pl
from jax.experimental.pallas import tpu as pltpu
from jax.sharding import Mesh, PartitionSpec as P

GATHER_BYTES = 8 << 20
VMEM_BYTES = 16 << 20


def to_points(codes, exponents):
    scale = lax.shift_left(jnp.ones_like(exponents), 16 - exponents).astype(jnp.float32) * 2.0**-16
    return (codes.astype(jnp.float32) * scale[:, None]).astype(jnp.bfloat16)


def split_points(codes, exponents, centroids, counters):
    local_rows = to_points(codes, exponents)
    points = lax.all_gather(local_rows, "cells", axis=0, tiled=True)
    beta = 4.0 / math.sqrt(points.shape[1])
    logits = (
        lax.dot_general(
            points, centroids, (((1,), (1,)), ((), ())), preferred_element_type=jnp.float32
        )
        * beta
    )
    inverse = lax.rsqrt(counters.astype(jnp.float32) + 1.0)
    top = lax.pmax(jnp.max(logits, axis=1), "cells")
    expo = jnp.exp(logits - top[:, None])
    total, novel = lax.psum(
        (jnp.sum(expo, axis=1), jnp.dot(expo, inverse, preferred_element_type=jnp.float32)), "cells"
    )
    weight = novel / total
    share = (expo * (weight / total)[:, None]).astype(jnp.bfloat16)
    mass_local = jnp.sum(share.astype(jnp.float32), axis=0)
    sums_local = lax.dot_general(
        share, points, (((0,), (0,)), ((), ())), preferred_element_type=jnp.float32
    )
    sums = lax.psum_scatter(sums_local, "pts", scatter_dimension=0, tiled=True)
    mass = lax.psum_scatter(mass_local, "pts", scatter_dimension=0, tiled=True)
    return (sums[None], mass[None])


def exchange(a, axes, partner):
    count = math.prod(lax.axis_size(axis) for axis in axes)
    return lax.ppermute(a, axes, [(partner(at), at) for at in range(count)])


def in_vmem(n):
    return [pl.BlockSpec(memory_space=pltpu.VMEM)] * n


def join_kernel(above, below, *refs):
    out, rows = refs[-1], above.shape[0]
    out[:rows, :] = above[...]
    out[rows:, :] = below[...]


def join(above, below, *after):
    return pl.pallas_call(
        join_kernel,
        in_specs=in_vmem(2 + len(after)),
        out_specs=in_vmem(1)[0],
        out_shape=jax.ShapeDtypeStruct((above.shape[0] + below.shape[0], above.shape[1]), above.dtype),
        compiler_params=pltpu.CompilerParams(vmem_limit_bytes=VMEM_BYTES),
    )(above, below, *after)


def expo_kernel(rate, block, place, near, first, second, cells, inverse, expo, tops, stats, points):
    rows = near.shape[0]
    pieces = (near[...], first[...], second[:rows, :], second[rows:, :])
    for at, piece in enumerate(pieces):
        points[pl.ds(pl.multiple_of(place[at] * rows, rows), rows), :] = piece
    every = points[...]
    highest = total = novel = None
    for at in range(cells.shape[0] // block):
        here = slice(at * block, (at + 1) * block)
        logits = lax.dot_general(
            cells[here, :], every, (((1,), (1,)), ((), ())), preferred_element_type=jnp.float32
        )
        top = jnp.max(logits, axis=0, keepdims=True)
        value = jnp.exp2((logits - top) * rate)
        expo[here, :] = value.astype(jnp.bfloat16)
        tops[at : at + 1, :] = top
        part = jnp.sum(value, axis=0, keepdims=True)
        weighed = jnp.concatenate(
            [
                jnp.sum(value[:, i : i + 128] * inverse[here, :], axis=0, keepdims=True)
                for i in range(0, value.shape[1], 128)
            ],
            axis=1,
        )
        if at:
            higher = jnp.maximum(highest, top)
            old, new = jnp.exp2((highest - higher) * rate), jnp.exp2((top - higher) * rate)
            highest, total, novel = higher, total * old + part * new, novel * old + weighed * new
        else:
            highest, total, novel = top, part, weighed
    stats[...] = jnp.concatenate([highest, total, novel], axis=0)


def expo_call(rate, block, place, pieces, cells, inverse):
    count, width = cells.shape
    n_points = sum(piece.shape[0] for piece in pieces)
    return pl.pallas_call(
        functools.partial(expo_kernel, rate, block),
        in_specs=[pl.BlockSpec(memory_space=pltpu.SMEM)] + in_vmem(5),
        out_specs=in_vmem(4),
        out_shape=[
            jax.ShapeDtypeStruct((count, n_points), jnp.bfloat16),
            jax.ShapeDtypeStruct((count // block, n_points), jnp.float32),
            jax.ShapeDtypeStruct((3, n_points), jnp.float32),
            jax.ShapeDtypeStruct((n_points, width), jnp.bfloat16),
        ],
        compiler_params=pltpu.CompilerParams(vmem_limit_bytes=VMEM_BYTES),
        cost_estimate=pl.CostEstimate(
            flops=2 * count * n_points * width,
            bytes_accessed=2 * (count * width + n_points * width + count * n_points),
            transcendentals=count * n_points,
        ),
    )(place, *pieces, cells, inverse)


def weighed_sums(at, count, expos, points, factor):
    total = weight = None
    here = pl.ds(pl.multiple_of(at * count, count), count)
    for expo, chunk, scales in zip(expos, points, factor):
        share = (expo[here, :].astype(jnp.float32) * scales[pl.ds(at, 1), :]).astype(jnp.bfloat16)
        part = jnp.dot(share, chunk[...], preferred_element_type=jnp.float32)
        wide = share.astype(jnp.float32)
        lanes = sum(wide[:, i : i + 128] for i in range(0, wide.shape[1], 128))
        total = part if total is None else total + part
        weight = lanes if weight is None else weight + lanes
    return total, jnp.sum(weight.T, axis=0, keepdims=True)


def sums_kernel(n, block, skip, half, *refs):
    expos, points, factor, (sums, mass) = refs[:n], refs[n : 2 * n], refs[2 * n], refs[2 * n + 1 :]
    factor = [factor.at[at] for at in range(n)]
    for at in range(sums.shape[0] // block):
        here = slice(at * block, (at + 1) * block)
        total, weight = weighed_sums(half[0] * 2 + skip + at, block, expos, points, factor)
        sums[here, :] = total.astype(sums.dtype)
        mass[:, here] = weight


def last_kernel(n, block, skip, half, *refs):
    expos, points, factor = refs[:n], refs[n : 2 * n], refs[2 * n]
    early, early_mass, there, there_mass, sums, mass, out, left = refs[2 * n + 1 :]
    factor = [factor.at[at] for at in range(n)]
    copies = []

    def store(start, stop, value):
        out[start:stop, :] = value + there[start:stop, :].astype(jnp.float32)
        here = pl.ds(start, stop - start)
        copies.append(pltpu.make_async_copy(out.at[here, :], sums.at[here, :], left.at[len(copies)]))
        copies[-1].start()

    store(0, skip * block, early[...])
    mass[:, : skip * block] = early_mass[...] + there_mass[:, : skip * block]
    for at in range(skip, out.shape[0] // block):
        start, stop = at * block, (at + 1) * block
        total, weight = weighed_sums(half[0] * 2 + at, block, expos, points, factor)
        store(start, stop, total)
        mass[:, start:stop] = weight + there_mass[:, start:stop]
    for copy in copies:
        copy.wait()


def sums_call(kernel, block, skip, rows, dtype, half, expos, points, factor, *more, last=False):
    n = len(expos)
    n_points, width = points[0].shape
    work = rows // block - skip if last else rows // block
    return pl.pallas_call(
        functools.partial(kernel, n, block, skip),
        in_specs=[pl.BlockSpec(memory_space=pltpu.SMEM)] + in_vmem(2 * n + 1 + len(more)),
        out_specs=[pl.BlockSpec(memory_space=pltpu.HBM if last else pltpu.VMEM)] + in_vmem(1),
        out_shape=[jax.ShapeDtypeStruct((rows, width), dtype), jax.ShapeDtypeStruct((1, rows), jnp.float32)],
        scratch_shapes=[pltpu.VMEM((rows, width), dtype), pltpu.SemaphoreType.DMA((1 + work,))] if last else [],
        compiler_params=pltpu.CompilerParams(vmem_limit_bytes=VMEM_BYTES),
        cost_estimate=pl.CostEstimate(
            flops=2 * work * block * n * n_points * width,
            bytes_accessed=2 * n * n_points * (work * block + width) + 4 * rows * width,
            transcendentals=0,
        ),
    )(half, *expos, *points, factor, *more)


def merge(rate, stats):
    top = functools.reduce(jnp.maximum, [s[0] for s in stats])
    scales = [jnp.exp2((s[0] - top) * rate) for s in stats]
    total = sum(s[1] * scale for s, scale in zip(stats, scales))
    novel = sum(s[2] * scale for s, scale in zip(stats, scales))
    return jnp.stack([top, total, novel])


def split_cells(codes, exponents, centroids, counters):
    chip = lax.axis_index("y") * 2 + lax.axis_index("x")
    lo = lax.axis_index("lo")
    own = to_points(codes, exponents)
    rate = 4.0 / math.sqrt(own.shape[1]) * math.log2(math.e)
    plane = ("y", "x", "lo")

    turn = lambda a: exchange(a, plane, lambda at: at ^ (4 if at % 2 else 2))
    turn_back = lambda a: exchange(a, plane, lambda at: at ^ (2 if at % 2 else 4))
    along_z = lambda a, by: exchange(a, ("cells",), lambda at: at ^ by)
    place = jnp.stack([chip, chip ^ (1 + lo), chip ^ (2 - lo), chip ^ 3]).astype(jnp.int32)

    per_device = centroids.shape[0] // 8
    block = per_device // 2

    cells, counts = (lax.dynamic_slice_in_dim(a, chip * 2 * per_device, 2 * per_device) for a in (centroids, counters))
    inverse = lax.rsqrt(counts.astype(jnp.float32) + 1.0)
    inverse = jnp.broadcast_to(inverse[:, None], (inverse.shape[0], 128))

    nears = [own] + [along_z(own, by) for by in (1, 2, 3)]
    firsts = [turn(near) for near in nears]
    expos, tops, stats, points = [], [], [], []
    for step, (near, first) in enumerate(zip(nears, firsts)):
        second = turn_back(join(near, first, *stats[step - 2 : step - 1] if step > 1 else ()))
        expo, top, stat, chunk = expo_call(rate, block, place, (near, first, second), cells, inverse)
        expos.append(expo), tops.append(top), stats.append(stat), points.append(chunk)

    stat = jnp.stack(stats, axis=1)
    stat = merge(rate, [stat] + [exchange(stat, ("y", "x"), lambda at: at ^ by) for by in (1, 2, 3)])
    every = [stat]
    for by in (1, 2, 3):
        theirs = along_z(stat, by)
        every.append(jnp.stack([theirs[:, step ^ by] for step in range(4)], axis=1))
    stat = merge(rate, every)
    factor = jnp.exp2((jnp.stack(tops) - stat[0][:, None]) * rate) * (stat[2] / stat[1] / stat[1])[:, None]

    other, mine = ((a * jnp.ones((1,), jnp.int32)).astype(jnp.int32) for a in (1 - lo, lo))
    parts = (expos, points, factor)
    there, there_mass = sums_call(sums_kernel, block, 0, per_device, jnp.bfloat16, other, *parts)
    there, there_mass = (exchange(a, ("lo",), lambda at: at ^ 1) for a in (there, there_mass))
    early, early_mass = sums_call(sums_kernel, block, 0, block, jnp.float32, mine, *parts)
    out, mass = sums_call(
        last_kernel, block, 1, per_device, jnp.float32, mine, *parts, early, early_mass, there, there_mass, last=True
    )
    return (out[None], mass)


def solution(mesh):
    pts, cells = (mesh.shape[name] for name in ("pts", "cells"))
    square = (pts, cells) == (8, 4)
    shape, names = ((2, 2, 2, cells), ("y", "x", "lo", "cells")) if square else ((pts, cells), ("pts", "cells"))
    fine = Mesh(mesh.devices.reshape(shape), names)
    spread = names[:-1]
    in_specs = (P(names, None), P(names), P("cells", None), P("cells"))
    out_specs = (P("cells", spread, None), P("cells", spread))

    def run(codes, exponents, centroids, counters):
        small = codes.size * 2 <= GATHER_BYTES
        body = split_cells if square and small else split_points
        mapped = jax.shard_map(body, mesh=fine, in_specs=in_specs, out_specs=out_specs, check_vma=False)
        return mapped(codes, exponents, centroids, counters)

    return run
```

```python
import functools
import math

import jax
import jax.numpy as jnp
from jax import lax
from jax.experimental import pallas as pl
from jax.experimental.pallas import tpu as pltpu
from jax.sharding import Mesh, PartitionSpec as P

GATHER_BYTES = 8 << 20
VMEM_BYTES = 4 << 20
SUMS_VMEM_BYTES = 16 << 20


def to_points(codes, exponents):
    scale = lax.shift_left(jnp.ones_like(exponents), 16 - exponents).astype(jnp.float32) * 2.0**-16
    return (codes.astype(jnp.float32) * scale[:, None]).astype(jnp.bfloat16)


def split_points(codes, exponents, centroids, counters):
    local_rows = to_points(codes, exponents)
    points = lax.all_gather(local_rows, "cells", axis=0, tiled=True)
    beta = 4.0 / math.sqrt(points.shape[1])
    logits = (
        lax.dot_general(
            points, centroids, (((1,), (1,)), ((), ())), preferred_element_type=jnp.float32
        )
        * beta
    )
    inverse = lax.rsqrt(counters.astype(jnp.float32) + 1.0)
    top = lax.pmax(jnp.max(logits, axis=1), "cells")
    expo = jnp.exp(logits - top[:, None])
    total, novel = lax.psum(
        (jnp.sum(expo, axis=1), jnp.dot(expo, inverse, preferred_element_type=jnp.float32)), "cells"
    )
    weight = novel / total
    share = (expo * (weight / total)[:, None]).astype(jnp.bfloat16)
    mass_local = jnp.sum(share.astype(jnp.float32), axis=0)
    sums_local = lax.dot_general(
        share, points, (((0,), (0,)), ((), ())), preferred_element_type=jnp.float32
    )
    sums = lax.psum_scatter(sums_local, "pts", scatter_dimension=0, tiled=True)
    mass = lax.psum_scatter(mass_local, "pts", scatter_dimension=0, tiled=True)
    return (sums[None], mass[None])


def exchange(a, axes, partner):
    count = math.prod(lax.axis_size(axis) for axis in axes)
    return lax.ppermute(a, axes, [(partner(at), at) for at in range(count)])


def in_vmem(n):
    return [pl.BlockSpec(memory_space=pltpu.VMEM)] * n


def hold(a, after):
    def kernel(a, after, out):
        out[...] = a[...]

    return pl.pallas_call(
        kernel,
        in_specs=in_vmem(2),
        out_specs=in_vmem(1)[0],
        out_shape=jax.ShapeDtypeStruct(a.shape, a.dtype),
        compiler_params=pltpu.CompilerParams(vmem_limit_bytes=VMEM_BYTES),
    )(a, after)


def expo_kernel(rate, block, place, *refs):
    pieces, (cells, inverse, expo, tops, stats, points) = refs[:4], refs[4:]
    rows = pieces[0].shape[0]
    for at, piece in enumerate(pieces):
        points[pl.ds(pl.multiple_of(place[at] * rows, rows), rows), :] = piece[...]
    every = points[...]
    highest = total = novel = None
    for at in range(cells.shape[0] // block):
        here = slice(at * block, (at + 1) * block)
        logits = lax.dot_general(
            cells[here, :], every, (((1,), (1,)), ((), ())), preferred_element_type=jnp.float32
        )
        top = jnp.max(logits, axis=0, keepdims=True)
        value = jnp.exp2((logits - top) * rate)
        expo[here, :] = value.astype(jnp.bfloat16)
        tops[at : at + 1, :] = top
        part = jnp.sum(value, axis=0, keepdims=True)
        weighed = jnp.concatenate(
            [
                jnp.sum(value[:, i : i + 128] * inverse[here, :], axis=0, keepdims=True)
                for i in range(0, value.shape[1], 128)
            ],
            axis=1,
        )
        if at:
            higher = jnp.maximum(highest, top)
            old, new = jnp.exp2((highest - higher) * rate), jnp.exp2((top - higher) * rate)
            highest, total, novel = higher, total * old + part * new, novel * old + weighed * new
        else:
            highest, total, novel = top, part, weighed
    stats[...] = jnp.concatenate([highest, total, novel], axis=0)


def expo_call(rate, block, place, pieces, cells, inverse):
    count, width = cells.shape
    n_points = sum(piece.shape[0] for piece in pieces)
    return pl.pallas_call(
        functools.partial(expo_kernel, rate, block),
        in_specs=[pl.BlockSpec(memory_space=pltpu.SMEM)] + in_vmem(6),
        out_specs=in_vmem(4),
        out_shape=[
            jax.ShapeDtypeStruct((count, n_points), jnp.bfloat16),
            jax.ShapeDtypeStruct((count // block, n_points), jnp.float32),
            jax.ShapeDtypeStruct((3, n_points), jnp.float32),
            jax.ShapeDtypeStruct((n_points, width), jnp.bfloat16),
        ],
        compiler_params=pltpu.CompilerParams(vmem_limit_bytes=VMEM_BYTES),
        cost_estimate=pl.CostEstimate(
            flops=2 * count * n_points * width,
            bytes_accessed=2 * (count * width + n_points * width + count * n_points),
            transcendentals=count * n_points,
        ),
    )(place, *pieces, cells, inverse)


def weighed_sums(at, count, expos, points, factor):
    total = weight = None
    here = pl.ds(pl.multiple_of(at * count, count), count)
    for expo, chunk, scales in zip(expos, points, factor):
        share = (expo[here, :].astype(jnp.float32) * scales[pl.ds(at, 1), :]).astype(jnp.bfloat16)
        part = jnp.dot(share, chunk[...], preferred_element_type=jnp.float32)
        wide = share.astype(jnp.float32)
        lanes = sum(wide[:, i : i + 128] for i in range(0, wide.shape[1], 128))
        total = part if total is None else total + part
        weight = lanes if weight is None else weight + lanes
    return total, jnp.sum(weight.T, axis=0, keepdims=True)


def sums_kernel(n, block, half, *refs):
    expos, points, factor, (sums, mass) = refs[:n], refs[n : 2 * n], refs[2 * n], refs[2 * n + 1 :]
    factor = [factor.at[at] for at in range(n)]

    @pl.loop(0, sums.shape[0] // block)
    def _(at):
        here = pl.ds(pl.multiple_of(at * block, block), block)
        total, weight = weighed_sums(half[0] + at, block, expos, points, factor)
        sums[here, :] = total.astype(sums.dtype)
        mass[:, here] = weight


def last_kernel(n, block, half, *refs):
    expos, points, factor = refs[:n], refs[n : 2 * n], refs[2 * n]
    early, early_mass, there, there_mass, sums, mass, out, left = refs[2 * n + 1 :]
    factor = [factor.at[at] for at in range(n)]
    rows, skip = there.shape[0], early.shape[0]

    def copy(at):
        here = pl.ds(at * block, block)
        return pltpu.make_async_copy(out.at[at % 2], sums.at[here, :], left.at[at % 2])

    mass[:, :skip] = early_mass[...] + there_mass[:, :skip]
    for at in range(rows // block):
        here = slice(at * block, (at + 1) * block)
        if at >= 2:
            copy(at - 2).wait()
        if at * block < skip:
            total = early[here, :]
        else:
            total, weight = weighed_sums(half[0] + at, block, expos, points, factor)
            mass[:, here] = weight + there_mass[:, here]
        out[at % 2] = total + there[here, :].astype(jnp.float32)
        copy(at).start()
    for at in range(max(rows // block - 2, 0), rows // block):
        copy(at).wait()


def sums_call(kernel, block, rows, dtype, half, expos, points, factor, *more):
    n, last = len(expos), kernel is last_kernel
    n_points, width = points[0].shape
    work = rows - more[0].shape[0] if last else rows
    return pl.pallas_call(
        functools.partial(kernel, n, block),
        in_specs=[pl.BlockSpec(memory_space=pltpu.SMEM)] + in_vmem(2 * n + 1 + len(more)),
        out_specs=[pl.BlockSpec(memory_space=pltpu.HBM if last else pltpu.VMEM)] + in_vmem(1),
        out_shape=[jax.ShapeDtypeStruct((rows, width), dtype), jax.ShapeDtypeStruct((1, rows), jnp.float32)],
        scratch_shapes=[pltpu.VMEM((2, block, width), dtype), pltpu.SemaphoreType.DMA((2,))] if last else [],
        compiler_params=pltpu.CompilerParams(vmem_limit_bytes=SUMS_VMEM_BYTES),
        cost_estimate=pl.CostEstimate(
            flops=2 * work * n * n_points * width,
            bytes_accessed=2 * n * n_points * (work + width) + 4 * rows * width,
            transcendentals=0,
        ),
    )(half, *expos, *points, factor, *more)


def merge(rate, stats):
    top = jnp.max(stats[:, 0], axis=0)
    scale = jnp.exp2((stats[:, 0] - top) * rate)
    return jnp.stack([top, jnp.sum(stats[:, 1] * scale, axis=0), jnp.sum(stats[:, 2] * scale, axis=0)])


def everyone(a, axes):
    count = math.prod(lax.axis_size(axis) for axis in axes)
    return lax.all_to_all(jnp.broadcast_to(a, (count, *a.shape)), axes, 0, 0)


def shuffle(a, by):
    a = jnp.where(by & 1, jnp.stack([a[:, d ^ 1] for d in range(4)], axis=1), a)
    return jnp.where(by & 2, jnp.stack([a[:, d ^ 2] for d in range(4)], axis=1), a)


def split_cells(codes, exponents, centroids, counters):
    chip = lax.axis_index("y") * 2 + lax.axis_index("x")
    lo = lax.axis_index("lo")
    own = to_points(codes, exponents)
    rate = 4.0 / math.sqrt(own.shape[1]) * math.log2(math.e)
    plane = ("y", "x", "lo")

    turn = lambda a: exchange(a, plane, lambda at: at ^ (4 if at % 2 else 2))
    turn_back = lambda a: exchange(a, plane, lambda at: at ^ (2 if at % 2 else 4))
    along_z = lambda a, by: exchange(a, ("cells",), lambda at: at ^ by)
    place = jnp.stack([chip, chip ^ (1 + lo), chip ^ (2 - lo), chip ^ 3]).astype(jnp.int32)

    per_device = centroids.shape[0] // 8
    block = per_device // 3

    cells, counts = (lax.dynamic_slice_in_dim(a, chip * 2 * per_device, 2 * per_device) for a in (centroids, counters))
    inverse = lax.rsqrt(counts.astype(jnp.float32) + 1.0)
    inverse = jnp.broadcast_to(inverse[:, None], (inverse.shape[0], 128))

    nears = [own] + [along_z(own, by) for by in (1, 2, 3)]
    expos, tops, stats, points = [], [], [], []
    for step, near in enumerate(nears):
        first, second = turn(near), turn_back(near)
        across = turn_back(hold(first, stats[step // 2]) if step % 2 else first)
        expo, top, stat, chunk = expo_call(rate, block, place, (near, first, second, across), cells, inverse)
        expos.append(expo), tops.append(top), stats.append(stat), points.append(chunk)

    z = lax.axis_index("cells")
    stat = shuffle(jnp.stack(stats, axis=1), z)
    for axes in (("y", "x"), ("cells",)):
        stat = merge(rate, everyone(stat, axes))
    stat = shuffle(stat, z)
    factor = jnp.exp2((jnp.stack(tops) - stat[0][:, None]) * rate) * (stat[2] / stat[1] / stat[1])[:, None]

    other, mine = ((a * jnp.full((1,), per_device // block)).astype(jnp.int32) for a in (1 - lo, lo))
    parts = (expos, points, factor)
    there, there_mass = sums_call(sums_kernel, block, per_device, jnp.bfloat16, other, *parts)
    there, there_mass = (exchange(a, ("lo",), lambda at: at ^ 1) for a in (there, there_mass))
    early, early_mass = sums_call(sums_kernel, block, 2 * block, jnp.float32, mine, *parts)
    out, mass = sums_call(
        last_kernel, block, per_device, jnp.float32, mine, *parts, early, early_mass, there, there_mass
    )
    return (out[None], mass)


def solution(mesh):
    pts, cells = (mesh.shape[name] for name in ("pts", "cells"))
    square = (pts, cells) == (8, 4)
    shape, names = ((2, 2, 2, cells), ("y", "x", "lo", "cells")) if square else ((pts, cells), ("pts", "cells"))
    fine = Mesh(mesh.devices.reshape(shape), names)
    spread = names[:-1]
    in_specs = (P(names, None), P(names), P("cells", None), P("cells"))
    out_specs = (P("cells", spread, None), P("cells", spread))

    def run(codes, exponents, centroids, counters):
        small = codes.size * 2 <= GATHER_BYTES
        body = split_cells if square and small else split_points
        mapped = jax.shard_map(body, mesh=fine, in_specs=in_specs, out_specs=out_specs, check_vma=False)
        return mapped(codes, exponents, centroids, counters)

    return run
```

```python
import functools
import math

import jax
import jax.numpy as jnp
from jax import lax
from jax.experimental import pallas as pl
from jax.experimental.pallas import tpu as pltpu
from jax.sharding import Mesh, PartitionSpec as P

GATHER_BYTES = 8 << 20
VMEM_BYTES = 4 << 20
SUMS_VMEM_BYTES = 16 << 20


def to_points(codes, exponents):
    scale = lax.shift_left(jnp.ones_like(exponents), 16 - exponents).astype(jnp.float32) * 2.0**-16
    return (codes.astype(jnp.float32) * scale[:, None]).astype(jnp.bfloat16)


def split_points(codes, exponents, centroids, counters):
    local_rows = to_points(codes, exponents)
    points = lax.all_gather(local_rows, "cells", axis=0, tiled=True)
    beta = 4.0 / math.sqrt(points.shape[1])
    logits = (
        lax.dot_general(
            points, centroids, (((1,), (1,)), ((), ())), preferred_element_type=jnp.float32
        )
        * beta
    )
    inverse = lax.rsqrt(counters.astype(jnp.float32) + 1.0)
    top = lax.pmax(jnp.max(logits, axis=1), "cells")
    expo = jnp.exp(logits - top[:, None])
    total, novel = lax.psum(
        (jnp.sum(expo, axis=1), jnp.dot(expo, inverse, preferred_element_type=jnp.float32)), "cells"
    )
    weight = novel / total
    share = (expo * (weight / total)[:, None]).astype(jnp.bfloat16)
    mass_local = jnp.sum(share.astype(jnp.float32), axis=0)
    sums_local = lax.dot_general(
        share, points, (((0,), (0,)), ((), ())), preferred_element_type=jnp.float32
    )
    sums = lax.psum_scatter(sums_local, "pts", scatter_dimension=0, tiled=True)
    mass = lax.psum_scatter(mass_local, "pts", scatter_dimension=0, tiled=True)
    return (sums[None], mass[None])


def exchange(a, axes, partner):
    count = math.prod(lax.axis_size(axis) for axis in axes)
    return lax.ppermute(a, axes, [(partner(at), at) for at in range(count)])


def in_vmem(n):
    return [pl.BlockSpec(memory_space=pltpu.VMEM)] * n


def cells_kernel(centroids, counters, cells, inverse, counters_here, arrived):
    rows = cells.shape[0]
    lines = rows // 128
    chip = lax.axis_index("y") * 2 + lax.axis_index("x")
    copies = [
        pltpu.make_async_copy(counters, counters_here, arrived.at[0]),
        pltpu.make_async_copy(centroids.at[pl.ds(pl.multiple_of(chip * rows, rows), rows), :], cells, arrived.at[1]),
    ]
    for copy in copies:
        copy.start()
    copies[0].wait()
    for line in range(lines):
        row = counters_here[pl.ds(chip * lines + line, 1), :]
        row = lax.rsqrt(row.astype(jnp.float32) + 1.0)
        inverse[line * 128 : (line + 1) * 128, :] = jnp.broadcast_to(row, (128, 128)).T
    copies[1].wait()


def cells_call(centroids, counters, rows):
    counters = counters.reshape(-1, 128)
    return pl.pallas_call(
        cells_kernel,
        in_specs=[pl.BlockSpec(memory_space=pltpu.HBM)] * 2,
        out_specs=in_vmem(2),
        out_shape=[
            jax.ShapeDtypeStruct((rows, centroids.shape[1]), jnp.bfloat16),
            jax.ShapeDtypeStruct((rows, 128), jnp.float32),
        ],
        scratch_shapes=[pltpu.VMEM(counters.shape, counters.dtype), pltpu.SemaphoreType.DMA((2,))],
        compiler_params=pltpu.CompilerParams(vmem_limit_bytes=VMEM_BYTES),
    )(centroids, counters)


def hold(a, after):
    def kernel(a, after, out):
        out[...] = a[...]

    return pl.pallas_call(
        kernel,
        in_specs=in_vmem(2),
        out_specs=in_vmem(1)[0],
        out_shape=jax.ShapeDtypeStruct(a.shape, a.dtype),
        compiler_params=pltpu.CompilerParams(vmem_limit_bytes=VMEM_BYTES),
    )(a, after)


def expo_kernel(rate, block, *refs):
    pieces, (cells, inverse, expo, tops, stats, points) = refs[:4], refs[4:]
    rows = pieces[0].shape[0]
    chip = lax.axis_index("y") * 2 + lax.axis_index("x")
    lo = lax.axis_index("lo")
    for away, piece in zip((0, 1 + lo, 2 - lo, 3), pieces):
        points[pl.ds(pl.multiple_of((chip ^ away) * rows, rows), rows), :] = piece[...]
    every = points[...]
    highest = total = novel = None
    for at in range(cells.shape[0] // block):
        here = slice(at * block, (at + 1) * block)
        logits = lax.dot_general(
            cells[here, :], every, (((1,), (1,)), ((), ())), preferred_element_type=jnp.float32
        )
        top = jnp.max(logits, axis=0, keepdims=True)
        value = jnp.exp2((logits - top) * rate)
        expo[here, :] = value.astype(jnp.bfloat16)
        tops[at : at + 1, :] = top
        part = jnp.sum(value, axis=0, keepdims=True)
        weighed = jnp.concatenate(
            [
                jnp.sum(value[:, i : i + 128] * inverse[here, :], axis=0, keepdims=True)
                for i in range(0, value.shape[1], 128)
            ],
            axis=1,
        )
        if at:
            higher = jnp.maximum(highest, top)
            old, new = jnp.exp2((highest - higher) * rate), jnp.exp2((top - higher) * rate)
            highest, total, novel = higher, total * old + part * new, novel * old + weighed * new
        else:
            highest, total, novel = top, part, weighed
    stats[...] = jnp.concatenate([highest, total, novel], axis=0)


def expo_call(rate, block, pieces, cells, inverse):
    count, width = cells.shape
    n_points = sum(piece.shape[0] for piece in pieces)
    return pl.pallas_call(
        functools.partial(expo_kernel, rate, block),
        in_specs=in_vmem(6),
        out_specs=in_vmem(4),
        out_shape=[
            jax.ShapeDtypeStruct((count, n_points), jnp.bfloat16),
            jax.ShapeDtypeStruct((count // block, n_points), jnp.float32),
            jax.ShapeDtypeStruct((3, n_points), jnp.float32),
            jax.ShapeDtypeStruct((n_points, width), jnp.bfloat16),
        ],
        compiler_params=pltpu.CompilerParams(vmem_limit_bytes=VMEM_BYTES),
        cost_estimate=pl.CostEstimate(
            flops=2 * count * n_points * width,
            bytes_accessed=2 * (count * width + n_points * width + count * n_points),
            transcendentals=count * n_points,
        ),
    )(*pieces, cells, inverse)


def weighed_sums(at, count, expos, points, factor):
    total = weight = None
    here = pl.ds(pl.multiple_of(at * count, count), count)
    for expo, chunk, scales in zip(expos, points, factor):
        share = (expo[here, :].astype(jnp.float32) * scales[pl.ds(at, 1), :]).astype(jnp.bfloat16)
        part = jnp.dot(share, chunk[...], preferred_element_type=jnp.float32)
        wide = share.astype(jnp.float32)
        lanes = sum(wide[:, i : i + 128] for i in range(0, wide.shape[1], 128))
        total = part if total is None else total + part
        weight = lanes if weight is None else weight + lanes
    return total, jnp.sum(weight.T, axis=0, keepdims=True)


def first_block(side, blocks):
    return (lax.axis_index("lo") ^ side) * blocks


def sums_kernel(n, block, first, *refs):
    expos, points, factor, (sums, mass) = refs[:n], refs[n : 2 * n], refs[2 * n], refs[2 * n + 1 :]
    factor = [factor.at[at] for at in range(n)]

    @pl.loop(0, sums.shape[0] // block)
    def _(at):
        here = pl.ds(pl.multiple_of(at * block, block), block)
        total, weight = weighed_sums(first() + at, block, expos, points, factor)
        sums[here, :] = total.astype(sums.dtype)
        mass[:, here] = weight


def last_kernel(n, block, first, *refs):
    expos, points, factor = refs[:n], refs[n : 2 * n], refs[2 * n]
    early, early_mass, there, there_mass, sums, mass, out, left = refs[2 * n + 1 :]
    factor = [factor.at[at] for at in range(n)]
    rows, skip = there.shape[0], early.shape[0]

    def copy(at):
        here = pl.ds(at * block, block)
        return pltpu.make_async_copy(out.at[at % 2], sums.at[here, :], left.at[at % 2])

    mass[:, :skip] = early_mass[...] + there_mass[:, :skip]
    for at in range(rows // block):
        here = slice(at * block, (at + 1) * block)
        if at >= 2:
            copy(at - 2).wait()
        if at * block < skip:
            total = early[here, :]
        else:
            total, weight = weighed_sums(first() + at, block, expos, points, factor)
            mass[:, here] = weight + there_mass[:, here]
        out[at % 2] = total + there[here, :].astype(jnp.float32)
        copy(at).start()
    for at in range(max(rows // block - 2, 0), rows // block):
        copy(at).wait()


def sums_call(kernel, block, side, rows, dtype, expos, points, factor, *more):
    n, last = len(expos), kernel is last_kernel
    n_points, width = points[0].shape
    work = rows - more[0].shape[0] if last else rows
    return pl.pallas_call(
        functools.partial(kernel, n, block, functools.partial(first_block, side, expos[0].shape[0] // 2 // block)),
        in_specs=in_vmem(2 * n + 1 + len(more)),
        out_specs=[pl.BlockSpec(memory_space=pltpu.HBM if last else pltpu.VMEM)] + in_vmem(1),
        out_shape=[jax.ShapeDtypeStruct((rows, width), dtype), jax.ShapeDtypeStruct((1, rows), jnp.float32)],
        scratch_shapes=[pltpu.VMEM((2, block, width), dtype), pltpu.SemaphoreType.DMA((2,))] if last else [],
        compiler_params=pltpu.CompilerParams(vmem_limit_bytes=SUMS_VMEM_BYTES),
        cost_estimate=pl.CostEstimate(
            flops=2 * work * n * n_points * width,
            bytes_accessed=2 * n * n_points * (work + width) + 4 * rows * width,
            transcendentals=0,
        ),
    )(*expos, *points, factor, *more)


def merge(rate, stats):
    top = functools.reduce(jnp.maximum, [s[0] for s in stats])
    scales = [jnp.exp2((s[0] - top) * rate) for s in stats]
    total = sum(s[1] * scale for s, scale in zip(stats, scales))
    novel = sum(s[2] * scale for s, scale in zip(stats, scales))
    return jnp.stack([top, total, novel])


def split_cells(codes, exponents, centroids, counters):
    own = to_points(codes, exponents)
    rate = 4.0 / math.sqrt(own.shape[1]) * math.log2(math.e)
    plane = ("y", "x", "lo")

    turn = lambda a: exchange(a, plane, lambda at: at ^ (4 if at % 2 else 2))
    turn_back = lambda a: exchange(a, plane, lambda at: at ^ (2 if at % 2 else 4))
    along_z = lambda a, by: exchange(a, ("cells",), lambda at: at ^ by)

    per_device = centroids.shape[0] // 8
    block = per_device // 3

    cells, inverse = cells_call(centroids, counters, 2 * per_device)
    nears = [own] + [along_z(own, by) for by in (1, 2, 3)]
    expos, tops, stats, points = [], [], [], []
    for step, near in enumerate(nears):
        first, second = turn(near), turn_back(near)
        across = turn_back(hold(first, stats[step // 2]) if step % 2 else first)
        expo, top, stat, chunk = expo_call(rate, block, (near, first, second, across), cells, inverse)
        expos.append(expo), tops.append(top), stats.append(stat), points.append(chunk)

    stat = jnp.stack(stats, axis=1)
    stat = merge(rate, [stat] + [exchange(stat, ("y", "x"), lambda at: at ^ by) for by in (1, 2, 3)])
    every = [stat]
    for by in (1, 2, 3):
        theirs = along_z(stat, by)
        every.append(jnp.stack([theirs[:, step ^ by] for step in range(4)], axis=1))
    stat = merge(rate, every)
    factor = jnp.exp2((jnp.stack(tops) - stat[0][:, None]) * rate) * (stat[2] / stat[1] / stat[1])[:, None]

    parts = (expos, points, factor)
    there, there_mass = sums_call(sums_kernel, block, 1, per_device, jnp.bfloat16, *parts)
    there, there_mass = (exchange(a, ("lo",), lambda at: at ^ 1) for a in (there, there_mass))
    early, early_mass = sums_call(sums_kernel, block, 0, 2 * block, jnp.float32, *parts)
    out, mass = sums_call(
        last_kernel, block, 0, per_device, jnp.float32, *parts, early, early_mass, there, there_mass
    )
    return (out[None], mass)


def solution(mesh):
    pts, cells = (mesh.shape[name] for name in ("pts", "cells"))
    square = (pts, cells) == (8, 4)
    shape, names = ((2, 2, 2, cells), ("y", "x", "lo", "cells")) if square else ((pts, cells), ("pts", "cells"))
    fine = Mesh(mesh.devices.reshape(shape), names)
    spread = names[:-1]
    in_specs = (P(names, None), P(names), P("cells", None), P("cells"))
    out_specs = (P("cells", spread, None), P("cells", spread))

    def run(codes, exponents, centroids, counters):
        small = codes.size * 2 <= GATHER_BYTES
        body = split_cells if square and small else split_points
        mapped = jax.shard_map(body, mesh=fine, in_specs=in_specs, out_specs=out_specs, check_vma=False)
        return mapped(codes, exponents, centroids, counters)

    return run
```

```python
import functools
import math

import jax
import jax.numpy as jnp
from jax import lax
from jax.experimental import pallas as pl
from jax.experimental.pallas import tpu as pltpu
from jax.sharding import Mesh, PartitionSpec as P

GATHER_BYTES = 8 << 20
VMEM_BYTES = 16 << 20
FETCH_VMEM_BYTES = 43 << 20


def to_points(codes, exponents):
    scale = lax.shift_left(jnp.ones_like(exponents), 16 - exponents).astype(jnp.float32) * 2.0**-16
    return (codes.astype(jnp.float32) * scale[:, None]).astype(jnp.bfloat16)


def split_points(codes, exponents, centroids, counters):
    local_rows = to_points(codes, exponents)
    points = lax.all_gather(local_rows, "cells", axis=0, tiled=True)
    beta = 4.0 / math.sqrt(points.shape[1])
    logits = (
        lax.dot_general(
            points, centroids, (((1,), (1,)), ((), ())), preferred_element_type=jnp.float32
        )
        * beta
    )
    inverse = lax.rsqrt(counters.astype(jnp.float32) + 1.0)
    top = lax.pmax(jnp.max(logits, axis=1), "cells")
    expo = jnp.exp(logits - top[:, None])
    total, novel = lax.psum(
        (jnp.sum(expo, axis=1), jnp.dot(expo, inverse, preferred_element_type=jnp.float32)), "cells"
    )
    weight = novel / total
    share = (expo * (weight / total)[:, None]).astype(jnp.bfloat16)
    mass_local = jnp.sum(share.astype(jnp.float32), axis=0)
    sums_local = lax.dot_general(
        share, points, (((0,), (0,)), ((), ())), preferred_element_type=jnp.float32
    )
    sums = lax.psum_scatter(sums_local, "pts", scatter_dimension=0, tiled=True)
    mass = lax.psum_scatter(mass_local, "pts", scatter_dimension=0, tiled=True)
    return (sums[None], mass[None])


def exchange(a, axes, partner):
    count = math.prod(lax.axis_size(axis) for axis in axes)
    return lax.ppermute(a, axes, [(partner(at), at) for at in range(count)])


def in_vmem(n):
    return [pl.BlockSpec(memory_space=pltpu.VMEM)] * n


def join(above, below, after):
    def kernel(above, below, after, out):
        out[: above.shape[0], :] = above[...]
        out[above.shape[0] :, :] = below[...]

    return pl.pallas_call(
        kernel,
        in_specs=in_vmem(3),
        out_specs=in_vmem(1)[0],
        out_shape=jax.ShapeDtypeStruct((above.shape[0] + below.shape[0], above.shape[1]), above.dtype),
        compiler_params=pltpu.CompilerParams(vmem_limit_bytes=VMEM_BYTES),
    )(above, below, after)


def scores(cells, points):
    return lax.dot_general(cells, points, (((1,), (1,)), ((), ())), preferred_element_type=jnp.float32)


def chip_index():
    return lax.axis_index("y") * 2 + lax.axis_index("x")


def totals_kernel(rate, block, fetch, points, cells_from, inverse_from, *refs):
    every = points[...]
    if fetch:
        cells, inverse, stats, counters, arrived = refs
    else:
        cells, inverse, (stats,) = cells_from, inverse_from, refs
    count = cells.shape[0] // block

    def copy(at):
        if at == count:
            return pltpu.make_async_copy(inverse_from, counters, arrived.at[at])
        here = pl.ds(at * block, block)
        return pltpu.make_async_copy(cells_from.at[here, :], cells.at[here, :], arrived.at[at])

    if fetch:
        for at in (count, *range(count)):
            copy(at).start()
        copy(count).wait()
    highest = total = novel = None
    for at in range(count):
        here = slice(at * block, (at + 1) * block)
        if fetch:
            for line in range(at * block // 128, (at + 1) * block // 128):
                row = lax.rsqrt(counters[line : line + 1, :].astype(jnp.float32) + 1.0)
                inverse[line * 128 : (line + 1) * 128, :] = jnp.broadcast_to(row, (128, 128)).T
            copy(at).wait()
        logits = scores(cells[here, :], every)
        top = jnp.max(logits, axis=0, keepdims=True)
        value = jnp.exp2((logits - top) * rate)
        part = jnp.sum(value, axis=0, keepdims=True)
        scale = inverse[here, :]
        weighed = jnp.concatenate(
            [
                jnp.sum(value[:, i : i + 128] * scale, axis=0, keepdims=True)
                for i in range(0, value.shape[1], 128)
            ],
            axis=1,
        )
        if at:
            higher = jnp.maximum(highest, top)
            old, new = jnp.exp2((highest - higher) * rate), jnp.exp2((top - higher) * rate)
            highest, total, novel = higher, total * old + part * new, novel * old + weighed * new
        else:
            highest, total, novel = top, part, weighed
    stats[...] = jnp.concatenate([highest, total, novel], axis=0)


def totals_call(rate, block, points, cells, inverse=None, counters=None):
    fetch = inverse is None
    n_points, width = points.shape
    n_cells = cells.shape[0]
    out_shape = [jax.ShapeDtypeStruct((3, n_points), jnp.float32)]
    scratch = []
    if fetch:
        inverse = counters.reshape(-1, 128)
        out_shape = [
            jax.ShapeDtypeStruct(cells.shape, cells.dtype),
            jax.ShapeDtypeStruct((n_cells, 128), jnp.float32),
        ] + out_shape
        scratch = [pltpu.VMEM(inverse.shape, inverse.dtype), pltpu.SemaphoreType.DMA((n_cells // block + 1,))]
    return pl.pallas_call(
        functools.partial(totals_kernel, rate, block, fetch),
        in_specs=in_vmem(1) + [pl.BlockSpec(memory_space=pltpu.HBM if fetch else pltpu.VMEM)] * 2,
        out_specs=in_vmem(len(out_shape)),
        out_shape=out_shape,
        scratch_shapes=scratch,
        compiler_params=pltpu.CompilerParams(vmem_limit_bytes=FETCH_VMEM_BYTES if fetch else VMEM_BYTES),
        cost_estimate=pl.CostEstimate(
            flops=2 * n_cells * n_points * width,
            bytes_accessed=2 * n_cells * width,
            transcendentals=n_cells * n_points,
        ),
    )(points, cells, inverse)


def goal_kernel(rate, *refs):
    *stats, goal = refs
    for at in range(4):
        here = [stat[:, (at ^ by) * 128 : ((at ^ by) + 1) * 128] for by, stat in enumerate(stats)]
        top = functools.reduce(jnp.maximum, [s[:1] for s in here])
        scales = [jnp.exp2((s[:1] - top) * rate) for s in here]
        total = sum(s[1:2] * scale for s, scale in zip(here, scales))
        novel = sum(s[2:] * scale for s, scale in zip(here, scales))
        goal[:, at * 128 : (at + 1) * 128] = jnp.concatenate([top, novel / total / total], axis=0)


def goal_call(rate, *stats):
    return pl.pallas_call(
        functools.partial(goal_kernel, rate),
        in_specs=in_vmem(len(stats)),
        out_specs=in_vmem(1)[0],
        out_shape=jax.ShapeDtypeStruct((2, stats[0].shape[1]), jnp.float32),
        compiler_params=pltpu.CompilerParams(vmem_limit_bytes=VMEM_BYTES),
    )(*stats)


def factor_kernel(rate, *refs):
    goals, tops, (factor, top, weight) = refs[:4], refs[4:6], refs[6:]
    chip = chip_index()
    for by, goal in enumerate(goals):
        for at in range(4):
            spot = pl.ds(pl.multiple_of((at % 2 * 4 + (chip ^ by)) * 128, 128), 128)
            piece = goal[:, at * 128 : (at + 1) * 128]
            top[at // 2, :, spot] = piece[:1]
            weight[at // 2, :, spot] = piece[1:]
    for group in range(2):
        factor[group] = jnp.exp2((tops[group][...] - top[group]) * rate) * weight[group]


def factor_call(rate, goals, tops):
    blocks, n_points = tops[0].shape
    return pl.pallas_call(
        functools.partial(factor_kernel, rate),
        in_specs=in_vmem(6),
        out_specs=in_vmem(1)[0],
        out_shape=jax.ShapeDtypeStruct((2, blocks, n_points), jnp.float32),
        scratch_shapes=[pltpu.VMEM((2, 1, n_points), jnp.float32)] * 2,
        compiler_params=pltpu.CompilerParams(vmem_limit_bytes=VMEM_BYTES),
    )(*goals, *tops)


def expo_kernel(rate, block, *refs):
    pieces, (cells, expo, tops, points) = refs[:4], refs[4:]
    rows = pieces[0].shape[0] // 2
    chip, lo = chip_index(), lax.axis_index("lo")
    for away, piece in zip((0, 1 + lo, 2 - lo, 3), pieces):
        for at in range(2):
            spot = pl.ds(pl.multiple_of((at * 4 + (chip ^ away)) * rows, rows), rows)
            points[spot, :] = piece[at * rows : (at + 1) * rows, :]
    count = expo.shape[0] // block
    for part in range(2):
        some = slice(part * 4 * rows, (part + 1) * 4 * rows)
        for at in range(count):
            mine = pl.ds(pl.multiple_of((chip * count + at) * block, block), block)
            logits = scores(cells[mine, :], points[some, :])
            top = jnp.max(logits, axis=0, keepdims=True)
            expo[at * block : (at + 1) * block, some] = jnp.exp2((logits - top) * rate).astype(jnp.bfloat16)
            tops[at : at + 1, some] = top


def expo_call(rate, block, count, pieces, cells):
    width = cells.shape[1]
    n_points = sum(piece.shape[0] for piece in pieces)
    return pl.pallas_call(
        functools.partial(expo_kernel, rate, block),
        in_specs=in_vmem(5),
        out_specs=in_vmem(3),
        out_shape=[
            jax.ShapeDtypeStruct((count, n_points), jnp.bfloat16),
            jax.ShapeDtypeStruct((count // block, n_points), jnp.float32),
            jax.ShapeDtypeStruct((n_points, width), jnp.bfloat16),
        ],
        compiler_params=pltpu.CompilerParams(vmem_limit_bytes=VMEM_BYTES),
        cost_estimate=pl.CostEstimate(
            flops=2 * count * n_points * width,
            bytes_accessed=2 * (count * width + n_points * width + count * n_points),
            transcendentals=count * n_points,
        ),
    )(*pieces, cells)


def weighed_sums(at, count, expos, points, factor):
    total = weight = None
    here = pl.ds(pl.multiple_of(at * count, count), count)
    for expo, chunk, scales in zip(expos, points, factor):
        share = (expo[here, :].astype(jnp.float32) * scales[pl.ds(at, 1), :]).astype(jnp.bfloat16)
        part = jnp.dot(share, chunk[...], preferred_element_type=jnp.float32)
        wide = share.astype(jnp.float32)
        lanes = sum(wide[:, i : i + 128] for i in range(0, wide.shape[1], 128))
        total = part if total is None else total + part
        weight = lanes if weight is None else weight + lanes
    return total, jnp.sum(weight.T, axis=0, keepdims=True)


def sums_kernel(n, block, side, *refs):
    expos, points, factor, (sums, mass) = refs[:n], refs[n : 2 * n], refs[2 * n], refs[2 * n + 1 :]
    factor = [factor.at[at] for at in range(n)]
    count = sums.shape[0] // block
    first = (lax.axis_index("lo") ^ side) * count
    for at in range(count):
        here = slice(at * block, (at + 1) * block)
        total, weight = weighed_sums(first + at, block, expos, points, factor)
        sums[here, :] = total.astype(sums.dtype)
        mass[:, here] = weight


def sums_call(block, side, rows, dtype, expos, points, factor):
    n = len(expos)
    n_points, width = points[0].shape
    return pl.pallas_call(
        functools.partial(sums_kernel, n, block, side),
        in_specs=in_vmem(2 * n + 1),
        out_specs=in_vmem(2),
        out_shape=[jax.ShapeDtypeStruct((rows, width), dtype), jax.ShapeDtypeStruct((1, rows), jnp.float32)],
        compiler_params=pltpu.CompilerParams(vmem_limit_bytes=VMEM_BYTES),
        cost_estimate=pl.CostEstimate(
            flops=2 * rows * n * n_points * width,
            bytes_accessed=2 * n * n_points * (rows + width) + 4 * rows * width,
            transcendentals=0,
        ),
    )(*expos, *points, factor)


def add_kernel(block, here, here_mass, there, there_mass, sums, mass, out, left):
    def copy(at):
        rows = pl.ds(at * block, block)
        return pltpu.make_async_copy(out.at[rows, :], sums.at[rows, :], left.at[at])

    count = here.shape[0] // block
    for at in range(count):
        rows = slice(at * block, (at + 1) * block)
        out[rows, :] = here[rows, :] + there[rows, :].astype(jnp.float32)
        copy(at).start()
    mass[...] = here_mass[...] + there_mass[...]
    for at in range(count):
        copy(at).wait()


def add_call(block, here, here_mass, there, there_mass):
    return pl.pallas_call(
        functools.partial(add_kernel, block),
        in_specs=in_vmem(4),
        out_specs=[pl.BlockSpec(memory_space=pltpu.HBM)] + in_vmem(1),
        out_shape=[
            jax.ShapeDtypeStruct(here.shape, jnp.float32),
            jax.ShapeDtypeStruct(here_mass.shape, jnp.float32),
        ],
        scratch_shapes=[
            pltpu.VMEM(here.shape, jnp.float32),
            pltpu.SemaphoreType.DMA((here.shape[0] // block,)),
        ],
        compiler_params=pltpu.CompilerParams(vmem_limit_bytes=VMEM_BYTES),
    )(here, here_mass, there, there_mass)


def split_cells(codes, exponents, centroids, counters):
    own = to_points(codes, exponents)
    rate = 4.0 / math.sqrt(own.shape[1]) * math.log2(math.e)
    plane = ("y", "x", "lo")

    turn = lambda a: exchange(a, plane, lambda at: at ^ (4 if at % 2 else 2))
    turn_back = lambda a: exchange(a, plane, lambda at: at ^ (2 if at % 2 else 4))
    along_z = lambda a, by: exchange(a, ("cells",), lambda at: at ^ by)
    around = lambda a, by: exchange(a, ("y", "x"), lambda at: at ^ by)

    per_device = centroids.shape[0] // 8
    block = per_device // 3

    near_1, near_2, near_3 = (along_z(own, by) for by in (1, 2, 3))
    near = jnp.concatenate([own, near_1])
    cells, inverse, stat = totals_call(rate, 2 * block, near, centroids, counters=counters)
    nears, stats = [near], [stat]
    near = join(near_2, near_3, stat)
    nears.append(near)
    stats += totals_call(rate, 2 * block, near, cells, inverse)

    stat = jnp.concatenate(stats, axis=1)
    goal = goal_call(rate, stat, *(along_z(stat, by) for by in (1, 2, 3)))
    goals = [goal] + [around(goal, by) for by in (1, 2, 3)]

    expos, tops, points = [], [], []
    for near in nears:
        first, second = turn(near), turn_back(near)
        pieces = (near, first, second, turn_back(first))
        expo, top, chunks = expo_call(rate, block, 2 * per_device, pieces, cells)
        expos.append(expo), tops.append(top), points.append(chunks)
    factor = factor_call(rate, goals, tops)

    there = sums_call(block, 1, per_device, jnp.bfloat16, expos, points, factor)
    there = [exchange(a, ("lo",), lambda at: at ^ 1) for a in there]
    here = sums_call(block, 0, per_device, jnp.float32, expos, points, factor)
    out, mass = add_call(block, *here, *there)
    return (out[None], mass)


def solution(mesh):
    pts, cells = (mesh.shape[name] for name in ("pts", "cells"))
    square = (pts, cells) == (8, 4)
    shape, names = ((2, 2, 2, cells), ("y", "x", "lo", "cells")) if square else ((pts, cells), ("pts", "cells"))
    fine = Mesh(mesh.devices.reshape(shape), names)
    spread = names[:-1]
    in_specs = (P(names, None), P(names), P("cells", None), P("cells"))
    out_specs = (P("cells", spread, None), P("cells", spread))

    def run(codes, exponents, centroids, counters):
        small = codes.size * 2 <= GATHER_BYTES and codes.shape[0] == 128 * pts * cells
        body = split_cells if square and small else split_points
        mapped = jax.shard_map(body, mesh=fine, in_specs=in_specs, out_specs=out_specs, check_vma=False)
        return mapped(codes, exponents, centroids, counters)

    return run
```

```python
import functools
import math

import jax
import jax.numpy as jnp
from jax import lax
from jax.experimental import pallas as pl
from jax.experimental.pallas import tpu as pltpu
from jax.sharding import Mesh, PartitionSpec as P

GATHER_BYTES = 8 << 20
VMEM_BYTES = 16 << 20
FETCH_VMEM_BYTES = 43 << 20


def to_points(codes, exponents):
    scale = lax.shift_left(jnp.ones_like(exponents), 16 - exponents).astype(jnp.float32) * 2.0**-16
    return (codes.astype(jnp.float32) * scale[:, None]).astype(jnp.bfloat16)


def split_points(codes, exponents, centroids, counters):
    local_rows = to_points(codes, exponents)
    points = lax.all_gather(local_rows, "cells", axis=0, tiled=True)
    beta = 4.0 / math.sqrt(points.shape[1])
    logits = (
        lax.dot_general(
            points, centroids, (((1,), (1,)), ((), ())), preferred_element_type=jnp.float32
        )
        * beta
    )
    inverse = lax.rsqrt(counters.astype(jnp.float32) + 1.0)
    top = lax.pmax(jnp.max(logits, axis=1), "cells")
    expo = jnp.exp(logits - top[:, None])
    total, novel = lax.psum(
        (jnp.sum(expo, axis=1), jnp.dot(expo, inverse, preferred_element_type=jnp.float32)), "cells"
    )
    weight = novel / total
    share = (expo * (weight / total)[:, None]).astype(jnp.bfloat16)
    mass_local = jnp.sum(share.astype(jnp.float32), axis=0)
    sums_local = lax.dot_general(
        share, points, (((0,), (0,)), ((), ())), preferred_element_type=jnp.float32
    )
    sums = lax.psum_scatter(sums_local, "pts", scatter_dimension=0, tiled=True)
    mass = lax.psum_scatter(mass_local, "pts", scatter_dimension=0, tiled=True)
    return (sums[None], mass[None])


def exchange(a, axes, partner):
    count = math.prod(lax.axis_size(axis) for axis in axes)
    return lax.ppermute(a, axes, [(partner(at), at) for at in range(count)])


def in_vmem(n):
    return [pl.BlockSpec(memory_space=pltpu.VMEM)] * n


def join(above, below, *after):
    def kernel(above, below, *refs):
        out = refs[-1]
        out[: above.shape[0], :] = above[...]
        out[above.shape[0] :, :] = below[...]

    return pl.pallas_call(
        kernel,
        in_specs=in_vmem(2 + len(after)),
        out_specs=in_vmem(1)[0],
        out_shape=jax.ShapeDtypeStruct((above.shape[0] + below.shape[0], above.shape[1]), above.dtype),
        compiler_params=pltpu.CompilerParams(vmem_limit_bytes=VMEM_BYTES),
    )(above, below, *after)


def scores(cells, points):
    return lax.dot_general(cells, points, (((1,), (1,)), ((), ())), preferred_element_type=jnp.float32)


def chip_index():
    return lax.axis_index("y") * 2 + lax.axis_index("x")


def totals_kernel(rate, block, fetch, tokens, points, cells_from, inverse_from, *refs):
    every = points[...]
    refs = refs[tokens:]
    if fetch:
        cells, inverse, stats, counters, arrived = refs
    else:
        cells, inverse, (stats,) = cells_from, inverse_from, refs
    count = cells.shape[0] // block

    def copy(at):
        if at == count:
            return pltpu.make_async_copy(inverse_from, counters, arrived.at[at])
        here = pl.ds(at * block, block)
        return pltpu.make_async_copy(cells_from.at[here, :], cells.at[here, :], arrived.at[at])

    if fetch:
        for at in (count, *range(count)):
            copy(at).start(priority=at % 2)
        copy(count).wait()
    highest = total = novel = None
    for at in range(count):
        here = slice(at * block, (at + 1) * block)
        if fetch:
            for line in range(at * block // 128, (at + 1) * block // 128):
                row = lax.rsqrt(counters[line : line + 1, :].astype(jnp.float32) + 1.0)
                inverse[line * 128 : (line + 1) * 128, :] = jnp.broadcast_to(row, (128, 128)).T
            copy(at).wait()
        logits = scores(cells[here, :], every)
        top = jnp.max(logits, axis=0, keepdims=True)
        value = jnp.exp2((logits - top) * rate)
        part = jnp.sum(value, axis=0, keepdims=True)
        scale = inverse[here, :]
        weighed = jnp.concatenate(
            [
                jnp.sum(value[:, i : i + 128] * scale, axis=0, keepdims=True)
                for i in range(0, value.shape[1], 128)
            ],
            axis=1,
        )
        if at:
            higher = jnp.maximum(highest, top)
            old, new = jnp.exp2((highest - higher) * rate), jnp.exp2((top - higher) * rate)
            highest, total, novel = higher, total * old + part * new, novel * old + weighed * new
        else:
            highest, total, novel = top, part, weighed
    stats[...] = jnp.concatenate([highest, total, novel], axis=0)


def totals_call(rate, block, points, cells, inverse=None, counters=None, after=()):
    fetch = inverse is None
    n_points, width = points.shape
    n_cells = cells.shape[0]
    out_shape = [jax.ShapeDtypeStruct((3, n_points), jnp.float32)]
    scratch = []
    if fetch:
        inverse = counters.reshape(-1, 128)
        out_shape = [
            jax.ShapeDtypeStruct(cells.shape, cells.dtype),
            jax.ShapeDtypeStruct((n_cells, 128), jnp.float32),
        ] + out_shape
        scratch = [pltpu.VMEM(inverse.shape, inverse.dtype), pltpu.SemaphoreType.DMA((n_cells // block + 1,))]
    return pl.pallas_call(
        functools.partial(totals_kernel, rate, block, fetch, len(after)),
        in_specs=in_vmem(1) + [pl.BlockSpec(memory_space=pltpu.HBM if fetch else pltpu.VMEM)] * 2 + in_vmem(len(after)),
        out_specs=in_vmem(len(out_shape)),
        out_shape=out_shape,
        scratch_shapes=scratch,
        compiler_params=pltpu.CompilerParams(vmem_limit_bytes=FETCH_VMEM_BYTES if fetch else VMEM_BYTES),
        cost_estimate=pl.CostEstimate(
            flops=2 * n_cells * n_points * width,
            bytes_accessed=2 * n_cells * width,
            transcendentals=n_cells * n_points,
        ),
    )(points, cells, inverse, *after)


def goal_kernel(rate, *refs):
    stats, goal = refs[:4], refs[-1]
    for at in range(4):
        here = [stat[:, (at ^ by) * 128 : ((at ^ by) + 1) * 128] for by, stat in enumerate(stats)]
        top = functools.reduce(jnp.maximum, [s[:1] for s in here])
        scales = [jnp.exp2((s[:1] - top) * rate) for s in here]
        total = sum(s[1:2] * scale for s, scale in zip(here, scales))
        novel = sum(s[2:] * scale for s, scale in zip(here, scales))
        goal[:, at * 128 : (at + 1) * 128] = jnp.concatenate([top, novel / total / total], axis=0)


def goal_call(rate, *stats):
    return pl.pallas_call(
        functools.partial(goal_kernel, rate),
        in_specs=in_vmem(len(stats)),
        out_specs=in_vmem(1)[0],
        out_shape=jax.ShapeDtypeStruct((2, stats[0].shape[1]), jnp.float32),
        compiler_params=pltpu.CompilerParams(vmem_limit_bytes=VMEM_BYTES),
    )(*stats)


def factor_kernel(rate, *refs):
    goals, tops, (factor,) = refs[:4], refs[4:6], refs[6:]
    rows = goals[0].shape[1] // 2
    for group in range(2):
        mine = slice(group * rows, (group + 1) * rows)
        for at, goal in enumerate(goals):
            here = slice(at * rows, (at + 1) * rows)
            factor[group, :, here] = jnp.exp2((tops[group][:, here] - goal[:1, mine]) * rate) * goal[1:, mine]


def factor_call(rate, goals, tops):
    blocks, n_points = tops[0].shape
    return pl.pallas_call(
        functools.partial(factor_kernel, rate),
        in_specs=in_vmem(6),
        out_specs=in_vmem(1)[0],
        out_shape=jax.ShapeDtypeStruct((2, blocks, n_points), jnp.float32),
        compiler_params=pltpu.CompilerParams(vmem_limit_bytes=VMEM_BYTES),
    )(*goals, *tops)


def expo_kernel(rate, block, *refs):
    pieces, (cells, expo, tops, points) = refs[:4], refs[4:]
    rows = pieces[0].shape[0]
    for at, piece in enumerate(pieces):
        points[at * rows : (at + 1) * rows, :] = piece[...]
    count = expo.shape[0] // block
    chip = chip_index()
    for part in range(2):
        some = slice(part * 2 * rows, (part + 1) * 2 * rows)
        for at in range(count):
            mine = pl.ds(pl.multiple_of((chip * count + at) * block, block), block)
            logits = scores(cells[mine, :], points[some, :])
            top = jnp.max(logits, axis=0, keepdims=True)
            expo[at * block : (at + 1) * block, some] = jnp.exp2((logits - top) * rate).astype(jnp.bfloat16)
            tops[at : at + 1, some] = top


def expo_call(rate, block, count, pieces, cells):
    width = cells.shape[1]
    n_points = sum(piece.shape[0] for piece in pieces)
    return pl.pallas_call(
        functools.partial(expo_kernel, rate, block),
        in_specs=in_vmem(5),
        out_specs=in_vmem(3),
        out_shape=[
            jax.ShapeDtypeStruct((count, n_points), jnp.bfloat16),
            jax.ShapeDtypeStruct((count // block, n_points), jnp.float32),
            jax.ShapeDtypeStruct((n_points, width), jnp.bfloat16),
        ],
        compiler_params=pltpu.CompilerParams(vmem_limit_bytes=VMEM_BYTES),
        cost_estimate=pl.CostEstimate(
            flops=2 * count * n_points * width,
            bytes_accessed=2 * (count * width + n_points * width + count * n_points),
            transcendentals=count * n_points,
        ),
    )(*pieces, cells)


def weighed_sums(at, count, expos, points, factor):
    total = weight = None
    here = pl.ds(pl.multiple_of(at * count, count), count)
    for expo, chunk, scales in zip(expos, points, factor):
        share = (expo[here, :].astype(jnp.float32) * scales[pl.ds(at, 1), :]).astype(jnp.bfloat16)
        part = jnp.dot(share, chunk[...], preferred_element_type=jnp.float32)
        wide = share.astype(jnp.float32)
        lanes = sum(wide[:, i : i + 128] for i in range(0, wide.shape[1], 128))
        total = part if total is None else total + part
        weight = lanes if weight is None else weight + lanes
    return total, jnp.sum(weight.T, axis=0, keepdims=True)


def sums_kernel(n, block, side, *refs):
    expos, points, factor, (sums, mass) = refs[:n], refs[n : 2 * n], refs[2 * n], refs[2 * n + 1 :]
    factor = [factor.at[at] for at in range(n)]
    count = sums.shape[0] // block
    first = (lax.axis_index("lo") ^ side) * count
    for at in range(count):
        here = slice(at * block, (at + 1) * block)
        total, weight = weighed_sums(first + at, block, expos, points, factor)
        sums[here, :] = total.astype(sums.dtype)
        mass[:, here] = weight


def sums_call(block, side, rows, dtype, expos, points, factor):
    n = len(expos)
    n_points, width = points[0].shape
    return pl.pallas_call(
        functools.partial(sums_kernel, n, block, side),
        in_specs=in_vmem(2 * n + 1),
        out_specs=in_vmem(2),
        out_shape=[jax.ShapeDtypeStruct((rows, width), dtype), jax.ShapeDtypeStruct((1, rows), jnp.float32)],
        compiler_params=pltpu.CompilerParams(vmem_limit_bytes=VMEM_BYTES),
        cost_estimate=pl.CostEstimate(
            flops=2 * rows * n * n_points * width,
            bytes_accessed=2 * n * n_points * (rows + width) + 4 * rows * width,
            transcendentals=0,
        ),
    )(*expos, *points, factor)


def add_kernel(block, here, here_mass, there, there_mass, sums, mass, out, left):
    def copy(at):
        rows = pl.ds(at * block, block)
        return pltpu.make_async_copy(out.at[rows, :], sums.at[rows, :], left.at[at])

    count = here.shape[0] // block
    for at in range(count):
        rows = slice(at * block, (at + 1) * block)
        out[rows, :] = here[rows, :] + there[rows, :].astype(jnp.float32)
        copy(at).start(priority=at % 2)
    mass[...] = here_mass[...] + there_mass[...]
    for at in range(count):
        copy(at).wait()


def add_call(block, here, here_mass, there, there_mass):
    return pl.pallas_call(
        functools.partial(add_kernel, block),
        in_specs=in_vmem(4),
        out_specs=[pl.BlockSpec(memory_space=pltpu.HBM)] + in_vmem(1),
        out_shape=[
            jax.ShapeDtypeStruct(here.shape, jnp.float32),
            jax.ShapeDtypeStruct(here_mass.shape, jnp.float32),
        ],
        scratch_shapes=[
            pltpu.VMEM(here.shape, jnp.float32),
            pltpu.SemaphoreType.DMA((here.shape[0] // block,)),
        ],
        compiler_params=pltpu.CompilerParams(vmem_limit_bytes=VMEM_BYTES),
    )(here, here_mass, there, there_mass)


def split_cells(codes, exponents, centroids, counters):
    own = to_points(codes, exponents)
    rate = 4.0 / math.sqrt(own.shape[1]) * math.log2(math.e)
    plane = ("y", "x", "lo")

    turn = lambda a: exchange(a, plane, lambda at: at ^ (4 if at % 2 else 2))
    turn_back = lambda a: exchange(a, plane, lambda at: at ^ (2 if at % 2 else 4))
    along_z = lambda a, by: exchange(a, ("cells",), lambda at: at ^ by)
    around = lambda a, by: exchange(a, ("y", "x"), lambda at: at ^ by)

    per_device = centroids.shape[0] // 8
    block = per_device // 3

    near_1, near_2, near_3 = (along_z(own, by) for by in (1, 2, 3))
    cells, inverse, stat_0 = totals_call(rate, 2 * block, own, centroids, counters=counters)
    (stat_1,) = totals_call(rate, 2 * block, near_1, cells, inverse)

    nears = [join(own, near_1, stat_0), join(near_2, near_3, stat_1)]
    firsts, seconds = [turn(near) for near in nears], [turn_back(near) for near in nears]
    acrosses = [turn_back(first) for first in firsts]

    (stat_2,) = totals_call(rate, 2 * block, nears[1], cells, inverse, after=(firsts[0], seconds[0]))
    stat = jnp.concatenate([stat_0, stat_1, stat_2], axis=1)
    goal = goal_call(rate, stat, *(along_z(stat, by) for by in (1, 2, 3)), acrosses[0])
    goals = [goal, turn(goal), turn_back(goal), around(goal, 3)]

    expos, tops, points = [], [], []
    for pieces in zip(nears, firsts, seconds, acrosses):
        expo, top, chunks = expo_call(rate, block, 2 * per_device, pieces, cells)
        expos.append(expo), tops.append(top), points.append(chunks)
    factor = factor_call(rate, goals, tops)

    there = sums_call(block, 1, per_device, jnp.bfloat16, expos, points, factor)
    there = [exchange(a, ("lo",), lambda at: at ^ 1) for a in there]
    here = sums_call(block, 0, per_device, jnp.float32, expos, points, factor)
    out, mass = add_call(block // 2, *here, *there)
    return (out[None], mass)


def solution(mesh):
    pts, cells = (mesh.shape[name] for name in ("pts", "cells"))
    square = (pts, cells) == (8, 4)
    shape, names = ((2, 2, 2, cells), ("y", "x", "lo", "cells")) if square else ((pts, cells), ("pts", "cells"))
    fine = Mesh(mesh.devices.reshape(shape), names)
    spread = names[:-1]
    in_specs = (P(names, None), P(names), P("cells", None), P("cells"))
    out_specs = (P("cells", spread, None), P("cells", spread))

    def run(codes, exponents, centroids, counters):
        small = codes.size * 2 <= GATHER_BYTES and codes.shape[0] == 128 * pts * cells
        body = split_cells if square and small else split_points
        mapped = jax.shard_map(body, mesh=fine, in_specs=in_specs, out_specs=out_specs, check_vma=False)
        return mapped(codes, exponents, centroids, counters)

    return run
```

```python
import functools
import math

import jax
import jax.numpy as jnp
from jax import lax
from jax.experimental import pallas as pl
from jax.experimental.pallas import tpu as pltpu
from jax.sharding import Mesh, PartitionSpec as P

GATHER_BYTES = 8 << 20
VMEM_BYTES = 16 << 20


def to_points(codes, exponents):
    scale = lax.shift_left(jnp.ones_like(exponents), 16 - exponents).astype(jnp.float32) * 2.0**-16
    return (codes.astype(jnp.float32) * scale[:, None]).astype(jnp.bfloat16)


def split_points(codes, exponents, centroids, counters):
    local_rows = to_points(codes, exponents)
    points = lax.all_gather(local_rows, "cells", axis=0, tiled=True)
    beta = 4.0 / math.sqrt(points.shape[1])
    logits = (
        lax.dot_general(
            points, centroids, (((1,), (1,)), ((), ())), preferred_element_type=jnp.float32
        )
        * beta
    )
    inverse = lax.rsqrt(counters.astype(jnp.float32) + 1.0)
    top = lax.pmax(jnp.max(logits, axis=1), "cells")
    expo = jnp.exp(logits - top[:, None])
    total, novel = lax.psum(
        (jnp.sum(expo, axis=1), jnp.dot(expo, inverse, preferred_element_type=jnp.float32)), "cells"
    )
    weight = novel / total
    share = (expo * (weight / total)[:, None]).astype(jnp.bfloat16)
    mass_local = jnp.sum(share.astype(jnp.float32), axis=0)
    sums_local = lax.dot_general(
        share, points, (((0,), (0,)), ((), ())), preferred_element_type=jnp.float32
    )
    sums = lax.psum_scatter(sums_local, "pts", scatter_dimension=0, tiled=True)
    mass = lax.psum_scatter(mass_local, "pts", scatter_dimension=0, tiled=True)
    return (sums[None], mass[None])


def exchange(a, axes, partner):
    count = math.prod(lax.axis_size(axis) for axis in axes)
    return lax.ppermute(a, axes, [(partner(at), at) for at in range(count)])


def in_vmem(n):
    return [pl.BlockSpec(memory_space=pltpu.VMEM)] * n


def join(above, below, *after):
    def kernel(above, below, *refs):
        out = refs[-1]
        out[: above.shape[0], :] = above[...]
        out[above.shape[0] :, :] = below[...]

    return pl.pallas_call(
        kernel,
        in_specs=in_vmem(2 + len(after)),
        out_specs=in_vmem(1)[0],
        out_shape=jax.ShapeDtypeStruct((above.shape[0] + below.shape[0], above.shape[1]), above.dtype),
        compiler_params=pltpu.CompilerParams(vmem_limit_bytes=VMEM_BYTES),
    )(above, below, *after)


def hold(a, after):
    def kernel(a, after, out):
        out[...] = a[...]

    return pl.pallas_call(
        kernel,
        in_specs=in_vmem(2),
        out_specs=in_vmem(1)[0],
        out_shape=jax.ShapeDtypeStruct(a.shape, a.dtype),
        compiler_params=pltpu.CompilerParams(vmem_limit_bytes=VMEM_BYTES),
    )(a, after)


def scores(cells, points):
    return lax.dot_general(cells, points, (((1,), (1,)), ((), ())), preferred_element_type=jnp.float32)


def chip_index():
    return lax.axis_index("y") * 2 + lax.axis_index("x")


def inverse_kernel(counters, inverse):
    for line in range(counters.shape[0]):
        row = lax.rsqrt(counters[line : line + 1, :].astype(jnp.float32) + 1.0)
        inverse[line * 128 : (line + 1) * 128, :] = jnp.broadcast_to(row, (128, 128)).T


def inverse_call(counters):
    return pl.pallas_call(
        inverse_kernel,
        in_specs=in_vmem(1),
        out_specs=in_vmem(1)[0],
        out_shape=jax.ShapeDtypeStruct((counters.shape[0], 128), jnp.float32),
        compiler_params=pltpu.CompilerParams(vmem_limit_bytes=VMEM_BYTES),
    )(counters.reshape(-1, 128))


def totals_kernel(rate, block, points, low, high, inverse, *refs):
    stats = refs[-1]
    every = points[...]
    half, count = low.shape[0], inverse.shape[0]
    parts = []
    for at in range(0, count, block):
        here = slice(at, at + block)
        cells = low[here, :] if at < half else high[at - half : at - half + block, :]
        logits = scores(cells, every)
        top = jnp.max(logits, axis=0, keepdims=True)
        value = jnp.exp2((logits - top) * rate)
        scale = inverse[here, :]
        weighed = [
            jnp.sum(value[:, i : i + 128] * scale, axis=0, keepdims=True) for i in range(0, value.shape[1], 128)
        ]
        parts.append((top, jnp.sum(value, axis=0, keepdims=True), jnp.concatenate(weighed, axis=1)))
        while len(parts) > 1 and (at + block == count or len(parts) == 4):
            parts = [join_stats(rate, parts)]
    stats[...] = jnp.concatenate(parts[0], axis=0)


def join_stats(rate, parts):
    top = functools.reduce(jnp.maximum, [part[0] for part in parts])
    scales = [jnp.exp2((part[0] - top) * rate) for part in parts]
    return (top, *(sum(part[at] * scale for part, scale in zip(parts, scales)) for at in (1, 2)))


def totals_call(rate, block, points, halves, inverse, after=()):
    n_points, width = points.shape
    n_cells = inverse.shape[0]
    return pl.pallas_call(
        functools.partial(totals_kernel, rate, block),
        in_specs=in_vmem(4 + len(after)),
        out_specs=in_vmem(1)[0],
        out_shape=jax.ShapeDtypeStruct((3, n_points), jnp.float32),
        compiler_params=pltpu.CompilerParams(vmem_limit_bytes=VMEM_BYTES),
        cost_estimate=pl.CostEstimate(
            flops=2 * n_cells * n_points * width,
            bytes_accessed=2 * n_cells * width,
            transcendentals=n_cells * n_points,
        ),
    )(points, *halves, inverse, *after)


def goal_kernel(rate, *refs):
    stats, goal = refs[:4], refs[-1]
    for at in range(4):
        here = [stat[:, (at ^ by) * 128 : ((at ^ by) + 1) * 128] for by, stat in enumerate(stats)]
        top, total, novel = join_stats(rate, [(s[:1], s[1:2], s[2:]) for s in here])
        goal[:, at * 128 : (at + 1) * 128] = jnp.concatenate([top, novel / total / total], axis=0)


def goal_call(rate, *stats):
    return pl.pallas_call(
        functools.partial(goal_kernel, rate),
        in_specs=in_vmem(len(stats)),
        out_specs=in_vmem(1)[0],
        out_shape=jax.ShapeDtypeStruct((2, stats[0].shape[1]), jnp.float32),
        compiler_params=pltpu.CompilerParams(vmem_limit_bytes=VMEM_BYTES),
    )(*stats)


def factor_kernel(rate, *refs):
    goals, tops, factors = refs[:4], refs[4:6], refs[6:]
    rows = goals[0].shape[1] // 2
    for group in range(2):
        mine = slice(group * rows, (group + 1) * rows)
        for at, goal in enumerate(goals):
            here = slice(at * rows, (at + 1) * rows)
            factors[group][:, here] = jnp.exp2((tops[group][:, here] - goal[:1, mine]) * rate) * goal[1:, mine]


def factor_call(rate, goals, tops):
    return pl.pallas_call(
        functools.partial(factor_kernel, rate),
        in_specs=in_vmem(6),
        out_specs=in_vmem(2),
        out_shape=[jax.ShapeDtypeStruct(top.shape, jnp.float32) for top in tops],
        compiler_params=pltpu.CompilerParams(vmem_limit_bytes=VMEM_BYTES),
    )(*goals, *tops)


def expo_kernel(rate, block, *refs):
    pieces, (cells, expo, tops, points) = refs[:-4], refs[-4:]
    start = 0
    for piece in pieces:
        points[start : start + piece.shape[0], :] = piece[...]
        start += piece.shape[0]
    count = expo.shape[0] // block
    chip = chip_index()
    for at in range(count):
        mine = pl.ds(pl.multiple_of((chip * count + at) * block, block), block)
        for part in range(0, points.shape[0], 256):
            some = slice(part, part + 256)
            logits = scores(cells[mine, :], points[some, :])
            top = jnp.max(logits, axis=0, keepdims=True)
            expo[at * block : (at + 1) * block, some] = jnp.exp2((logits - top) * rate).astype(jnp.bfloat16)
            tops[at : at + 1, some] = top


def expo_call(rate, block, count, pieces, cells):
    width = cells.shape[1]
    n_points = sum(piece.shape[0] for piece in pieces)
    return pl.pallas_call(
        functools.partial(expo_kernel, rate, block),
        in_specs=in_vmem(len(pieces) + 1),
        out_specs=in_vmem(3),
        out_shape=[
            jax.ShapeDtypeStruct((count, n_points), jnp.bfloat16),
            jax.ShapeDtypeStruct((count // block, n_points), jnp.float32),
            jax.ShapeDtypeStruct((n_points, width), jnp.bfloat16),
        ],
        compiler_params=pltpu.CompilerParams(vmem_limit_bytes=VMEM_BYTES),
        cost_estimate=pl.CostEstimate(
            flops=2 * count * n_points * width,
            bytes_accessed=2 * (count * width + n_points * width + count * n_points),
            transcendentals=count * n_points,
        ),
    )(*pieces, cells)


def weighed_sums(start, count, expos, points, factors):
    total = weight = None
    for expo, chunk, factor in zip(expos, points, factors):
        block = expo.shape[0] // factor.shape[0]
        shares = []
        for at in range(0, count, block):
            here = pl.ds(pl.multiple_of(start + at, block), block)
            scale = factor[pl.ds((start + at) // block, 1), :]
            shares.append((expo[here, :].astype(jnp.float32) * scale).astype(jnp.bfloat16))
        share = jnp.concatenate(shares, axis=0)
        part = jnp.dot(share, chunk[...], preferred_element_type=jnp.float32)
        wide = share.astype(jnp.float32)
        lanes = sum(wide[:, i : i + 128] for i in range(0, wide.shape[1], 128))
        total = part if total is None else total + part
        weight = lanes if weight is None else weight + lanes
    return total, jnp.sum(weight.T, axis=0, keepdims=True)


def sums_kernel(n, block, side, *refs):
    expos, points, factors, (sums, mass) = refs[:n], refs[n : 2 * n], refs[2 * n : 3 * n], refs[3 * n :]
    rows = sums.shape[0]
    first = (lax.axis_index("lo") ^ side) * rows
    for at in range(0, rows, block):
        here = slice(at, at + block)
        total, weight = weighed_sums(first + at, block, expos, points, factors)
        sums[here, :] = total.astype(sums.dtype)
        mass[:, here] = weight


def sums_call(block, side, rows, dtype, expos, points, factors):
    n = len(expos)
    n_points, width = points[0].shape
    return pl.pallas_call(
        functools.partial(sums_kernel, n, block, side),
        in_specs=in_vmem(3 * n),
        out_specs=in_vmem(2),
        out_shape=[jax.ShapeDtypeStruct((rows, width), dtype), jax.ShapeDtypeStruct((1, rows), jnp.float32)],
        compiler_params=pltpu.CompilerParams(vmem_limit_bytes=VMEM_BYTES),
        cost_estimate=pl.CostEstimate(
            flops=2 * rows * n * n_points * width,
            bytes_accessed=2 * n * n_points * (rows + width) + 4 * rows * width,
            transcendentals=0,
        ),
    )(*expos, *points, *factors)


def add_kernel(block, here, here_mass, there, there_mass, sums, mass, out, left):
    def copy(at):
        rows = pl.ds(at * block, block)
        return pltpu.make_async_copy(out.at[rows, :], sums.at[rows, :], left.at[at])

    count = here.shape[0] // block
    for at in range(count):
        rows = slice(at * block, (at + 1) * block)
        out[rows, :] = here[rows, :] + there[rows, :].astype(jnp.float32)
        copy(at).start(priority=at % 2)
    mass[...] = here_mass[...] + there_mass[...]
    for at in range(count):
        copy(at).wait()


def add_call(block, here, here_mass, there, there_mass):
    return pl.pallas_call(
        functools.partial(add_kernel, block),
        in_specs=in_vmem(4),
        out_specs=[pl.BlockSpec(memory_space=pltpu.HBM)] + in_vmem(1),
        out_shape=[
            jax.ShapeDtypeStruct(here.shape, jnp.float32),
            jax.ShapeDtypeStruct(here_mass.shape, jnp.float32),
        ],
        scratch_shapes=[
            pltpu.VMEM(here.shape, jnp.float32),
            pltpu.SemaphoreType.DMA((here.shape[0] // block,)),
        ],
        compiler_params=pltpu.CompilerParams(vmem_limit_bytes=VMEM_BYTES),
    )(here, here_mass, there, there_mass)


def split_cells(codes, exponents, centroids, counters):
    own = to_points(codes, exponents)
    rate = 4.0 / math.sqrt(own.shape[1]) * math.log2(math.e)
    plane = ("y", "x", "lo")

    turn = lambda a: exchange(a, plane, lambda at: at ^ (4 if at % 2 else 2))
    turn_back = lambda a: exchange(a, plane, lambda at: at ^ (2 if at % 2 else 4))
    along_z = lambda a, by: exchange(a, ("cells",), lambda at: at ^ by)
    around = lambda a, by: exchange(a, ("y", "x"), lambda at: at ^ by)

    per_device = centroids.shape[0] // 8
    block = per_device // 3

    near_1, near_2, near_3 = (along_z(own, by) for by in (1, 2, 3))
    inverse = inverse_call(counters)
    halves = jnp.split(centroids, 2)
    near = join(own, near_1)
    stats = [totals_call(rate, 128, near, halves, inverse)]
    nears = [near, join(near_2, near_3, *stats)]
    firsts = [turn(near) for near in nears]
    stats.append(totals_call(rate, 256, nears[1], halves, inverse, after=firsts[:1]))
    seconds = [[turn_back(join(nears[0], firsts[0]))], [turn_back(nears[1]), turn_back(hold(firsts[1], stats[1]))]]

    stat = jnp.concatenate(stats, axis=1)
    goal = goal_call(rate, stat, *(along_z(stat, by) for by in (1, 2, 3)))
    goals = [goal, turn(goal), turn_back(goal), around(goal, 3)]

    expos, tops, points = [], [], []
    for cells, near, first, second in zip((128, 256), nears, firsts, seconds):
        expo, top, chunks = expo_call(rate, cells, 2 * per_device, (near, first, *second), centroids)
        expos.append(expo), tops.append(top), points.append(chunks)
    factors = factor_call(rate, goals, tops)

    there = sums_call(block, 1, per_device, jnp.bfloat16, expos, points, factors)
    there = [exchange(a, ("lo",), lambda at: at ^ 1) for a in there]
    here = sums_call(block, 0, per_device, jnp.float32, expos, points, factors)
    out, mass = add_call(block // 2, *here, *there)
    return (out[None], mass)


def solution(mesh):
    pts, cells = (mesh.shape[name] for name in ("pts", "cells"))
    square = (pts, cells) == (8, 4)
    shape, names = ((2, 2, 2, cells), ("y", "x", "lo", "cells")) if square else ((pts, cells), ("pts", "cells"))
    fine = Mesh(mesh.devices.reshape(shape), names)
    spread = names[:-1]
    in_specs = (P(names, None), P(names), P("cells", None), P("cells"))
    out_specs = (P("cells", spread, None), P("cells", spread))

    def run(codes, exponents, centroids, counters):
        small = codes.size * 2 <= GATHER_BYTES and codes.shape[0] == 128 * pts * cells
        body = split_cells if square and small else split_points
        mapped = jax.shard_map(body, mesh=fine, in_specs=in_specs, out_specs=out_specs, check_vma=False)
        return mapped(codes, exponents, centroids, counters)

    return run
```

```python
import functools
import math

import jax
import jax.numpy as jnp
from jax import lax
from jax.experimental import pallas as pl
from jax.experimental.pallas import tpu as pltpu
from jax.sharding import Mesh, PartitionSpec as P

GATHER_BYTES = 8 << 20
VMEM_BYTES = 16 << 20


def to_points(codes, exponents):
    scale = lax.shift_left(jnp.ones_like(exponents), 16 - exponents).astype(jnp.float32) * 2.0**-16
    return (codes.astype(jnp.float32) * scale[:, None]).astype(jnp.bfloat16)


def split_points(codes, exponents, centroids, counters):
    local_rows = to_points(codes, exponents)
    points = lax.all_gather(local_rows, "cells", axis=0, tiled=True)
    beta = 4.0 / math.sqrt(points.shape[1])
    logits = (
        lax.dot_general(
            points, centroids, (((1,), (1,)), ((), ())), preferred_element_type=jnp.float32
        )
        * beta
    )
    inverse = lax.rsqrt(counters.astype(jnp.float32) + 1.0)
    top = lax.pmax(jnp.max(logits, axis=1), "cells")
    expo = jnp.exp(logits - top[:, None])
    total, novel = lax.psum(
        (jnp.sum(expo, axis=1), jnp.dot(expo, inverse, preferred_element_type=jnp.float32)), "cells"
    )
    weight = novel / total
    share = (expo * (weight / total)[:, None]).astype(jnp.bfloat16)
    mass_local = jnp.sum(share.astype(jnp.float32), axis=0)
    sums_local = lax.dot_general(
        share, points, (((0,), (0,)), ((), ())), preferred_element_type=jnp.float32
    )
    sums = lax.psum_scatter(sums_local, "pts", scatter_dimension=0, tiled=True)
    mass = lax.psum_scatter(mass_local, "pts", scatter_dimension=0, tiled=True)
    return (sums[None], mass[None])


def exchange(a, axes, partner):
    count = math.prod(lax.axis_size(axis) for axis in axes)
    return lax.ppermute(a, axes, [(partner(at), at) for at in range(count)])


def in_vmem(n):
    return [pl.BlockSpec(memory_space=pltpu.VMEM)] * n


def join(above, below, *after):
    def kernel(above, below, *refs):
        out = refs[-1]
        out[: above.shape[0], :] = above[...]
        out[above.shape[0] :, :] = below[...]

    return pl.pallas_call(
        kernel,
        in_specs=in_vmem(2 + len(after)),
        out_specs=in_vmem(1)[0],
        out_shape=jax.ShapeDtypeStruct((above.shape[0] + below.shape[0], above.shape[1]), above.dtype),
        compiler_params=pltpu.CompilerParams(vmem_limit_bytes=VMEM_BYTES),
    )(above, below, *after)


def hold(a, *after):
    def kernel(a, *refs):
        refs[-1][...] = a[...]

    return pl.pallas_call(
        kernel,
        in_specs=in_vmem(1 + len(after)),
        out_specs=in_vmem(1)[0],
        out_shape=jax.ShapeDtypeStruct(a.shape, a.dtype),
        compiler_params=pltpu.CompilerParams(vmem_limit_bytes=VMEM_BYTES),
    )(a, *after)


def scores(cells, points):
    return lax.dot_general(cells, points, (((1,), (1,)), ((), ())), preferred_element_type=jnp.float32)


def chip_index():
    return lax.axis_index("y") * 2 + lax.axis_index("x")


def inverse_kernel(counters, inverse):
    for line in range(counters.shape[0]):
        row = lax.rsqrt(counters[line : line + 1, :].astype(jnp.float32) + 1.0)
        inverse[line * 128 : (line + 1) * 128, :] = jnp.broadcast_to(row, (128, 128)).T


def inverse_call(counters):
    return pl.pallas_call(
        inverse_kernel,
        in_specs=in_vmem(1),
        out_specs=in_vmem(1)[0],
        out_shape=jax.ShapeDtypeStruct((counters.shape[0], 128), jnp.float32),
        compiler_params=pltpu.CompilerParams(vmem_limit_bytes=VMEM_BYTES),
    )(counters.reshape(-1, 128))


def totals_kernel(rate, block, n, *refs):
    pieces, (low, high, inverse), stats = refs[:n], refs[n : n + 3], refs[-1]
    every = jnp.concatenate([piece[...] for piece in pieces], axis=0)
    half, count = low.shape[0], inverse.shape[0]
    parts = []
    for at in range(0, count, block):
        here = slice(at, at + block)
        cells = low[here, :] if at < half else high[at - half : at - half + block, :]
        logits = scores(cells, every)
        top = jnp.max(logits, axis=0, keepdims=True)
        value = jnp.exp2((logits - top) * rate)
        scale = inverse[here, :]
        weighed = [
            jnp.sum(value[:, i : i + 128] * scale, axis=0, keepdims=True) for i in range(0, value.shape[1], 128)
        ]
        parts.append((top, jnp.sum(value, axis=0, keepdims=True), jnp.concatenate(weighed, axis=1)))
        while len(parts) > 1 and (at + block == count or len(parts) == 4):
            parts = [join_stats(rate, parts)]
    stats[...] = jnp.concatenate(parts[0], axis=0)


def join_stats(rate, parts):
    top = functools.reduce(jnp.maximum, [part[0] for part in parts])
    scales = [jnp.exp2((part[0] - top) * rate) for part in parts]
    return (top, *(sum(part[at] * scale for part, scale in zip(parts, scales)) for at in (1, 2)))


def totals_call(rate, block, pieces, halves, inverse, after=()):
    n_points, width = sum(piece.shape[0] for piece in pieces), pieces[0].shape[1]
    n_cells = inverse.shape[0]
    args = (*pieces, *halves, inverse, *after)
    return pl.pallas_call(
        functools.partial(totals_kernel, rate, block, len(pieces)),
        in_specs=in_vmem(len(args)),
        out_specs=in_vmem(1)[0],
        out_shape=jax.ShapeDtypeStruct((3, n_points), jnp.float32),
        compiler_params=pltpu.CompilerParams(vmem_limit_bytes=VMEM_BYTES),
        cost_estimate=pl.CostEstimate(
            flops=2 * n_cells * n_points * width,
            bytes_accessed=2 * n_cells * width,
            transcendentals=n_cells * n_points,
        ),
    )(*args)


def goal_kernel(rate, *refs):
    stats, goal = refs[:4], refs[-1]
    for at in range(4):
        here = [stat[:, (at ^ by) * 128 : ((at ^ by) + 1) * 128] for by, stat in enumerate(stats)]
        top, total, novel = join_stats(rate, [(s[:1], s[1:2], s[2:]) for s in here])
        goal[:, at * 128 : (at + 1) * 128] = jnp.concatenate([top, novel / total / total], axis=0)


def goal_call(rate, *stats):
    return pl.pallas_call(
        functools.partial(goal_kernel, rate),
        in_specs=in_vmem(len(stats)),
        out_specs=in_vmem(1)[0],
        out_shape=jax.ShapeDtypeStruct((2, stats[0].shape[1]), jnp.float32),
        compiler_params=pltpu.CompilerParams(vmem_limit_bytes=VMEM_BYTES),
    )(*stats)


def factor_kernel(rate, *refs):
    goals, tops, factors = refs[:4], refs[4:6], refs[6:]
    rows = goals[0].shape[1] // 2
    for group in range(2):
        mine = slice(group * rows, (group + 1) * rows)
        for at, goal in enumerate(goals):
            here = slice(at * rows, (at + 1) * rows)
            factors[group][:, here] = jnp.exp2((tops[group][:, here] - goal[:1, mine]) * rate) * goal[1:, mine]


def factor_call(rate, goals, tops):
    return pl.pallas_call(
        functools.partial(factor_kernel, rate),
        in_specs=in_vmem(6),
        out_specs=in_vmem(2),
        out_shape=[jax.ShapeDtypeStruct(top.shape, jnp.float32) for top in tops],
        compiler_params=pltpu.CompilerParams(vmem_limit_bytes=VMEM_BYTES),
    )(*goals, *tops)


def expo_kernel(rate, block, *refs):
    pieces, (cells, expo, tops, points) = refs[:-4], refs[-4:]
    start = 0
    for piece in pieces:
        points[start : start + piece.shape[0], :] = piece[...]
        start += piece.shape[0]
    count = expo.shape[0] // block
    chip = chip_index()
    for at in range(count):
        mine = pl.ds(pl.multiple_of((chip * count + at) * block, block), block)
        for part in range(0, points.shape[0], 256):
            some = slice(part, part + 256)
            logits = scores(cells[mine, :], points[some, :])
            top = jnp.max(logits, axis=0, keepdims=True)
            expo[at * block : (at + 1) * block, some] = jnp.exp2((logits - top) * rate).astype(jnp.bfloat16)
            tops[at : at + 1, some] = top


def expo_call(rate, block, count, pieces, cells):
    width = cells.shape[1]
    n_points = sum(piece.shape[0] for piece in pieces)
    return pl.pallas_call(
        functools.partial(expo_kernel, rate, block),
        in_specs=in_vmem(len(pieces) + 1),
        out_specs=in_vmem(3),
        out_shape=[
            jax.ShapeDtypeStruct((count, n_points), jnp.bfloat16),
            jax.ShapeDtypeStruct((count // block, n_points), jnp.float32),
            jax.ShapeDtypeStruct((n_points, width), jnp.bfloat16),
        ],
        compiler_params=pltpu.CompilerParams(vmem_limit_bytes=VMEM_BYTES),
        cost_estimate=pl.CostEstimate(
            flops=2 * count * n_points * width,
            bytes_accessed=2 * (count * width + n_points * width + count * n_points),
            transcendentals=count * n_points,
        ),
    )(*pieces, cells)


def weighed_sums(start, count, expos, points, factors):
    total = weight = None
    for expo, chunk, factor in zip(expos, points, factors):
        block = expo.shape[0] // factor.shape[0]
        shares = []
        for at in range(0, count, block):
            here = pl.ds(pl.multiple_of(start + at, block), block)
            scale = factor[pl.ds((start + at) // block, 1), :]
            shares.append((expo[here, :].astype(jnp.float32) * scale).astype(jnp.bfloat16))
        share = jnp.concatenate(shares, axis=0)
        part = jnp.dot(share, chunk[...], preferred_element_type=jnp.float32)
        wide = share.astype(jnp.float32)
        lanes = sum(wide[:, i : i + 128] for i in range(0, wide.shape[1], 128))
        total = part if total is None else total + part
        weight = lanes if weight is None else weight + lanes
    return total, jnp.sum(weight.T, axis=0, keepdims=True)


def sums_kernel(n, block, side, *refs):
    expos, points, factors, (sums, mass) = refs[:n], refs[n : 2 * n], refs[2 * n : 3 * n], refs[3 * n :]
    rows = sums.shape[0]
    first = (lax.axis_index("lo") ^ side) * rows
    for at in range(0, rows, block):
        here = slice(at, at + block)
        total, weight = weighed_sums(first + at, block, expos, points, factors)
        sums[here, :] = total.astype(sums.dtype)
        mass[:, here] = weight


def sums_call(block, side, rows, dtype, expos, points, factors):
    n = len(expos)
    n_points, width = points[0].shape
    return pl.pallas_call(
        functools.partial(sums_kernel, n, block, side),
        in_specs=in_vmem(3 * n),
        out_specs=in_vmem(2),
        out_shape=[jax.ShapeDtypeStruct((rows, width), dtype), jax.ShapeDtypeStruct((1, rows), jnp.float32)],
        compiler_params=pltpu.CompilerParams(vmem_limit_bytes=VMEM_BYTES),
        cost_estimate=pl.CostEstimate(
            flops=2 * rows * n * n_points * width,
            bytes_accessed=2 * n * n_points * (rows + width) + 4 * rows * width,
            transcendentals=0,
        ),
    )(*expos, *points, *factors)


def add_kernel(block, here, here_mass, there, there_mass, sums, mass, out, left):
    def copy(at):
        rows = pl.ds(at * block, block)
        return pltpu.make_async_copy(out.at[rows, :], sums.at[rows, :], left.at[at])

    count = here.shape[0] // block
    for at in range(count):
        rows = slice(at * block, (at + 1) * block)
        out[rows, :] = here[rows, :] + there[rows, :].astype(jnp.float32)
        copy(at).start(priority=at % 2)
    mass[...] = here_mass[...] + there_mass[...]
    for at in range(count):
        copy(at).wait()


def add_call(block, here, here_mass, there, there_mass):
    return pl.pallas_call(
        functools.partial(add_kernel, block),
        in_specs=in_vmem(4),
        out_specs=[pl.BlockSpec(memory_space=pltpu.HBM)] + in_vmem(1),
        out_shape=[
            jax.ShapeDtypeStruct(here.shape, jnp.float32),
            jax.ShapeDtypeStruct(here_mass.shape, jnp.float32),
        ],
        scratch_shapes=[
            pltpu.VMEM(here.shape, jnp.float32),
            pltpu.SemaphoreType.DMA((here.shape[0] // block,)),
        ],
        compiler_params=pltpu.CompilerParams(vmem_limit_bytes=VMEM_BYTES),
    )(here, here_mass, there, there_mass)


def split_cells(codes, exponents, centroids, counters):
    own = to_points(codes, exponents)
    rate = 4.0 / math.sqrt(own.shape[1]) * math.log2(math.e)
    plane = ("y", "x", "lo")

    turn = lambda a: exchange(a, plane, lambda at: at ^ (4 if at % 2 else 2))
    turn_back = lambda a: exchange(a, plane, lambda at: at ^ (2 if at % 2 else 4))
    along_z = lambda a, by: exchange(a, ("cells",), lambda at: at ^ by)
    around = lambda a, by: exchange(a, ("y", "x"), lambda at: at ^ by)

    per_device = centroids.shape[0] // 8
    block = per_device // 3

    near_1, near_2, near_3 = (along_z(own, by) for by in (1, 2, 3))
    inverse = inverse_call(counters)
    halves = jnp.split(centroids, 2)
    expand = lambda near: (near, turn(near), turn_back(near))
    own, first_0, second_0 = expand(own)
    near_1, first_1, second_1 = expand(near_1)
    across_0, across_1 = turn_back(first_0), turn_back(first_1)
    stats = [totals_call(rate, block, (own, near_1), halves, inverse, after=(first_0, second_0))]
    near_23, first_23, second_23 = expand(join(near_2, near_3, *stats))
    stats.append(totals_call(rate, block, (near_23,), halves, inverse, after=(first_1, second_1, across_0)))
    across_23 = turn_back(hold(first_23, stats[1], across_1))

    groups = [
        (own, near_1, first_0, first_1, second_0, second_1, across_0, across_1),
        (near_23, first_23, second_23, across_23),
    ]
    expos, tops, points = zip(*(expo_call(rate, block, 2 * per_device, group, centroids) for group in groups))
    stat = jnp.concatenate(stats, axis=1)
    goal = goal_call(rate, stat, *(along_z(stat, by) for by in (1, 2, 3)), tops[0])
    goals = [goal, turn(goal), turn_back(goal), around(goal, 3)]
    factors = factor_call(rate, goals, tops)

    there = sums_call(block, 1, per_device, jnp.bfloat16, expos, points, factors)
    there = [exchange(a, ("lo",), lambda at: at ^ 1) for a in there]
    here = sums_call(block, 0, per_device, jnp.float32, expos, points, factors)
    out, mass = add_call(block // 2, *here, *there)
    return (out[None], mass)


def solution(mesh):
    pts, cells = (mesh.shape[name] for name in ("pts", "cells"))
    square = (pts, cells) == (8, 4)
    shape, names = ((2, 2, 2, cells), ("y", "x", "lo", "cells")) if square else ((pts, cells), ("pts", "cells"))
    fine = Mesh(mesh.devices.reshape(shape), names)
    spread = names[:-1]
    in_specs = (P(names, None), P(names), P("cells", None), P("cells"))
    out_specs = (P("cells", spread, None), P("cells", spread))

    def run(codes, exponents, centroids, counters):
        small = codes.size * 2 <= GATHER_BYTES and codes.shape[0] == 128 * pts * cells
        body = split_cells if square and small else split_points
        mapped = jax.shard_map(body, mesh=fine, in_specs=in_specs, out_specs=out_specs, check_vma=False)
        return mapped(codes, exponents, centroids, counters)

    return run
```

```python
import functools
import math

import jax
import jax.numpy as jnp
from jax import lax
from jax.experimental import pallas as pl
from jax.experimental.pallas import tpu as pltpu
from jax.sharding import Mesh, PartitionSpec as P

GATHER_BYTES = 8 << 20
VMEM_BYTES = 16 << 20


def to_points(codes, exponents):
    scale = lax.shift_left(jnp.ones_like(exponents), 16 - exponents).astype(jnp.float32) * 2.0**-16
    return (codes.astype(jnp.float32) * scale[:, None]).astype(jnp.bfloat16)


def split_points(codes, exponents, centroids, counters):
    local_rows = to_points(codes, exponents)
    points = lax.all_gather(local_rows, "cells", axis=0, tiled=True)
    beta = 4.0 / math.sqrt(points.shape[1])
    logits = (
        lax.dot_general(
            points, centroids, (((1,), (1,)), ((), ())), preferred_element_type=jnp.float32
        )
        * beta
    )
    inverse = lax.rsqrt(counters.astype(jnp.float32) + 1.0)
    top = lax.pmax(jnp.max(logits, axis=1), "cells")
    expo = jnp.exp(logits - top[:, None])
    total, novel = lax.psum(
        (jnp.sum(expo, axis=1), jnp.dot(expo, inverse, preferred_element_type=jnp.float32)), "cells"
    )
    weight = novel / total
    share = (expo * (weight / total)[:, None]).astype(jnp.bfloat16)
    mass_local = jnp.sum(share.astype(jnp.float32), axis=0)
    sums_local = lax.dot_general(
        share, points, (((0,), (0,)), ((), ())), preferred_element_type=jnp.float32
    )
    sums = lax.psum_scatter(sums_local, "pts", scatter_dimension=0, tiled=True)
    mass = lax.psum_scatter(mass_local, "pts", scatter_dimension=0, tiled=True)
    return (sums[None], mass[None])


def exchange(a, axes, partner):
    count = math.prod(lax.axis_size(axis) for axis in axes)
    return lax.ppermute(a, axes, [(partner(at), at) for at in range(count)])


def in_vmem(n):
    return [pl.BlockSpec(memory_space=pltpu.VMEM)] * n


def join(above, below, *after):
    def kernel(above, below, *refs):
        out = refs[-1]
        out[: above.shape[0], :] = above[...]
        out[above.shape[0] :, :] = below[...]

    return pl.pallas_call(
        kernel,
        in_specs=in_vmem(2 + len(after)),
        out_specs=in_vmem(1)[0],
        out_shape=jax.ShapeDtypeStruct((above.shape[0] + below.shape[0], above.shape[1]), above.dtype),
        compiler_params=pltpu.CompilerParams(vmem_limit_bytes=VMEM_BYTES),
    )(above, below, *after)


def beside(left, right, *after):
    def kernel(left, right, *refs):
        refs[-1][...] = jnp.concatenate([left[...], right[...]], axis=1)

    return pl.pallas_call(
        kernel,
        in_specs=in_vmem(2 + len(after)),
        out_specs=in_vmem(1)[0],
        out_shape=jax.ShapeDtypeStruct((left.shape[0], left.shape[1] + right.shape[1]), left.dtype),
        compiler_params=pltpu.CompilerParams(vmem_limit_bytes=VMEM_BYTES),
    )(left, right, *after)


def hold(a, *after):
    def kernel(a, *refs):
        refs[-1][...] = a[...]

    return pl.pallas_call(
        kernel,
        in_specs=in_vmem(1 + len(after)),
        out_specs=in_vmem(1)[0],
        out_shape=jax.ShapeDtypeStruct(a.shape, a.dtype),
        compiler_params=pltpu.CompilerParams(vmem_limit_bytes=VMEM_BYTES),
    )(a, *after)


def scores(cells, points):
    return lax.dot_general(cells, points, (((1,), (1,)), ((), ())), preferred_element_type=jnp.float32)


def chip_index():
    return lax.axis_index("y") * 2 + lax.axis_index("x")


def inverse_kernel(counters, *refs):
    inverse = refs[-1]
    for line in range(counters.shape[0]):
        row = lax.rsqrt(counters[line : line + 1, :].astype(jnp.float32) + 1.0)
        inverse[line * 128 : (line + 1) * 128, :] = jnp.broadcast_to(row, (128, 128)).T


def inverse_call(counters, *after):
    return pl.pallas_call(
        inverse_kernel,
        in_specs=in_vmem(1 + len(after)),
        out_specs=in_vmem(1)[0],
        out_shape=jax.ShapeDtypeStruct((counters.shape[0], 128), jnp.float32),
        compiler_params=pltpu.CompilerParams(vmem_limit_bytes=VMEM_BYTES),
        cost_estimate=pl.CostEstimate(flops=4 * 10**9, bytes_accessed=0, transcendentals=0),
    )(counters.reshape(-1, 128), *after)


def totals_kernel(rate, block, n, *refs):
    pieces, (cells, inverse), stats = refs[:n], refs[n : n + 2], refs[-1]
    every = jnp.concatenate([piece[...] for piece in pieces], axis=0)
    count = cells.shape[0]
    parts = []
    for at in range(0, count, block):
        here = slice(at, at + block)
        logits = scores(cells[here, :], every)
        top = jnp.max(logits, axis=0, keepdims=True)
        value = jnp.exp2((logits - top) * rate)
        scale = inverse[here, :]
        weighed = [
            jnp.sum(value[:, i : i + 128] * scale, axis=0, keepdims=True) for i in range(0, value.shape[1], 128)
        ]
        parts.append((top, jnp.sum(value, axis=0, keepdims=True), jnp.concatenate(weighed, axis=1)))
        while len(parts) > 1 and (at + block == count or len(parts) == 4):
            parts = [join_stats(rate, parts)]
    stats[...] = jnp.concatenate(parts[0], axis=0)


def join_stats(rate, parts):
    top = functools.reduce(jnp.maximum, [part[0] for part in parts])
    scales = [jnp.exp2((part[0] - top) * rate) for part in parts]
    return (top, *(sum(part[at] * scale for part, scale in zip(parts, scales)) for at in (1, 2)))


def totals_call(rate, block, pieces, cells, inverse, after=()):
    n_points, width = sum(piece.shape[0] for piece in pieces), pieces[0].shape[1]
    n_cells = inverse.shape[0]
    args = (*pieces, cells, inverse, *after)
    return pl.pallas_call(
        functools.partial(totals_kernel, rate, block, len(pieces)),
        in_specs=in_vmem(len(args)),
        out_specs=in_vmem(1)[0],
        out_shape=jax.ShapeDtypeStruct((3, n_points), jnp.float32),
        compiler_params=pltpu.CompilerParams(vmem_limit_bytes=VMEM_BYTES),
        cost_estimate=pl.CostEstimate(
            flops=2 * n_cells * n_points * width,
            bytes_accessed=2 * n_cells * width,
            transcendentals=n_cells * n_points,
        ),
    )(*args)


def goal_kernel(rate, *refs):
    stats, goal = refs[:4], refs[-1]
    for at in range(4):
        here = [stat[:, (at ^ by) * 128 : ((at ^ by) + 1) * 128] for by, stat in enumerate(stats)]
        top, total, novel = join_stats(rate, [(s[:1], s[1:2], s[2:]) for s in here])
        goal[:, at * 128 : (at + 1) * 128] = jnp.concatenate([top, novel / total / total], axis=0)


def goal_call(rate, *stats):
    return pl.pallas_call(
        functools.partial(goal_kernel, rate),
        in_specs=in_vmem(len(stats)),
        out_specs=in_vmem(1)[0],
        out_shape=jax.ShapeDtypeStruct((2, stats[0].shape[1]), jnp.float32),
        compiler_params=pltpu.CompilerParams(vmem_limit_bytes=VMEM_BYTES),
    )(*stats)


def factor_kernel(rate, *refs):
    goals, tops, factors = refs[:4], refs[4:6], refs[6:]
    rows = goals[0].shape[1] // 2
    for group in range(2):
        mine = slice(group * rows, (group + 1) * rows)
        for at, goal in enumerate(goals):
            here = slice(at * rows, (at + 1) * rows)
            factors[group][:, here] = jnp.exp2((tops[group][:, here] - goal[:1, mine]) * rate) * goal[1:, mine]


def factor_call(rate, goals, tops):
    return pl.pallas_call(
        functools.partial(factor_kernel, rate),
        in_specs=in_vmem(6),
        out_specs=in_vmem(2),
        out_shape=[jax.ShapeDtypeStruct(top.shape, jnp.float32) for top in tops],
        compiler_params=pltpu.CompilerParams(vmem_limit_bytes=VMEM_BYTES),
    )(*goals, *tops)


def expo_kernel(rate, block, n, *refs):
    pieces, cells, (expo, tops, points) = refs[:n], refs[n], refs[-3:]
    start = 0
    for piece in pieces:
        points[start : start + piece.shape[0], :] = piece[...]
        start += piece.shape[0]
    count = expo.shape[0] // block
    chip = chip_index()
    for at in range(count):
        mine = pl.ds(pl.multiple_of((chip * count + at) * block, block), block)
        for part in range(0, points.shape[0], 256):
            some = slice(part, part + 256)
            logits = scores(cells[mine, :], points[some, :])
            top = jnp.max(logits, axis=0, keepdims=True)
            expo[at * block : (at + 1) * block, some] = jnp.exp2((logits - top) * rate).astype(jnp.bfloat16)
            tops[at : at + 1, some] = top


def expo_call(rate, block, count, pieces, cells, *after):
    width = cells.shape[1]
    n_points = sum(piece.shape[0] for piece in pieces)
    return pl.pallas_call(
        functools.partial(expo_kernel, rate, block, len(pieces)),
        in_specs=in_vmem(len(pieces) + 1 + len(after)),
        out_specs=in_vmem(3),
        out_shape=[
            jax.ShapeDtypeStruct((count, n_points), jnp.bfloat16),
            jax.ShapeDtypeStruct((count // block, n_points), jnp.float32),
            jax.ShapeDtypeStruct((n_points, width), jnp.bfloat16),
        ],
        compiler_params=pltpu.CompilerParams(vmem_limit_bytes=VMEM_BYTES),
        cost_estimate=pl.CostEstimate(
            flops=2 * count * n_points * width,
            bytes_accessed=2 * (count * width + n_points * width + count * n_points),
            transcendentals=count * n_points,
        ),
    )(*pieces, cells, *after)


def weighed_sums(start, count, expos, points, factors):
    total = weight = None
    for expo, chunk, factor in zip(expos, points, factors):
        block = expo.shape[0] // factor.shape[0]
        shares = []
        for at in range(0, count, block):
            here = pl.ds(pl.multiple_of(start + at, block), block)
            scale = factor[pl.ds((start + at) // block, 1), :]
            shares.append((expo[here, :].astype(jnp.float32) * scale).astype(jnp.bfloat16))
        share = jnp.concatenate(shares, axis=0)
        part = jnp.dot(share, chunk[...], preferred_element_type=jnp.float32)
        wide = share.astype(jnp.float32)
        lanes = sum(wide[:, i : i + 128] for i in range(0, wide.shape[1], 128))
        total = part if total is None else total + part
        weight = lanes if weight is None else weight + lanes
    return total, jnp.sum(weight.T, axis=0, keepdims=True)


def sums_kernel(n, block, side, *refs):
    expos, points, factors, (sums, mass) = refs[:n], refs[n : 2 * n], refs[2 * n : 3 * n], refs[3 * n :]
    rows = sums.shape[0]
    first = (lax.axis_index("lo") ^ side) * rows
    for at in range(0, rows, block):
        here = slice(at, at + block)
        total, weight = weighed_sums(first + at, block, expos, points, factors)
        sums[here, :] = total.astype(sums.dtype)
        mass[:, here] = weight


def sums_call(block, side, rows, dtype, expos, points, factors):
    n = len(expos)
    n_points, width = points[0].shape
    return pl.pallas_call(
        functools.partial(sums_kernel, n, block, side),
        in_specs=in_vmem(3 * n),
        out_specs=in_vmem(2),
        out_shape=[jax.ShapeDtypeStruct((rows, width), dtype), jax.ShapeDtypeStruct((1, rows), jnp.float32)],
        compiler_params=pltpu.CompilerParams(vmem_limit_bytes=VMEM_BYTES),
        cost_estimate=pl.CostEstimate(
            flops=2 * rows * n * n_points * width,
            bytes_accessed=2 * n * n_points * (rows + width) + 4 * rows * width,
            transcendentals=0,
        ),
    )(*expos, *points, *factors)


def add_kernel(block, here, here_mass, there, there_mass, sums, mass, out, left):
    def copy(at):
        rows = pl.ds(at * block, block)
        return pltpu.make_async_copy(out.at[rows, :], sums.at[rows, :], left.at[at])

    count = here.shape[0] // block
    for at in range(count):
        rows = slice(at * block, (at + 1) * block)
        out[rows, :] = here[rows, :] + there[rows, :].astype(jnp.float32)
        copy(at).start(priority=at % 2)
    mass[...] = here_mass[...] + there_mass[...]
    for at in range(count):
        copy(at).wait()


def add_call(block, here, here_mass, there, there_mass):
    return pl.pallas_call(
        functools.partial(add_kernel, block),
        in_specs=in_vmem(4),
        out_specs=[pl.BlockSpec(memory_space=pltpu.HBM)] + in_vmem(1),
        out_shape=[
            jax.ShapeDtypeStruct(here.shape, jnp.float32),
            jax.ShapeDtypeStruct(here_mass.shape, jnp.float32),
        ],
        scratch_shapes=[
            pltpu.VMEM(here.shape, jnp.float32),
            pltpu.SemaphoreType.DMA((here.shape[0] // block,)),
        ],
        compiler_params=pltpu.CompilerParams(vmem_limit_bytes=VMEM_BYTES),
    )(here, here_mass, there, there_mass)


def split_cells(codes, exponents, centroids, counters):
    own = to_points(codes, exponents)
    rate = 4.0 / math.sqrt(own.shape[1]) * math.log2(math.e)
    plane = ("y", "x", "lo")

    turn = lambda a: exchange(a, plane, lambda at: at ^ (4 if at % 2 else 2))
    turn_back = lambda a: exchange(a, plane, lambda at: at ^ (2 if at % 2 else 4))
    along_z = lambda a, by: exchange(a, ("cells",), lambda at: at ^ by)
    around = lambda a, by: exchange(a, ("y", "x"), lambda at: at ^ by)

    per_device = centroids.shape[0] // 8
    block = per_device // 3

    near_1, near_2, near_3 = (along_z(own, by) for by in (1, 2, 3))
    expand = lambda near: (near, turn(near), turn_back(near))
    own, first_0, second_0 = expand(own)
    near_1, first_1, second_1 = expand(near_1)
    across_0, across_1 = turn_back(first_0), turn_back(first_1)
    inverse = inverse_call(counters, first_0, near_1)
    stats = [totals_call(rate, block, (own, near_1), centroids, inverse, after=(second_0,))]
    near_23, first_23, second_23 = expand(join(near_2, near_3, *stats))
    stats.append(totals_call(rate, block, (near_23,), centroids, inverse, after=(first_1, second_1, across_0)))

    expand = functools.partial(expo_call, rate, block, 2 * per_device)
    groups = [expand((own, near_1, first_0, first_1, second_0, second_1, across_0, across_1), centroids, stats[1])]
    tops = groups[0][1]
    stat = beside(*stats, across_1)
    theirs = [along_z(stat, by) for by in (1, 2, 3)]
    goal = goal_call(rate, stat, *theirs, tops, second_23)
    across_23 = turn_back(hold(first_23, goal))
    groups.append(expand((near_23, first_23, second_23, across_23), centroids))
    expos, tops, points = zip(*groups)
    goals = [goal, turn(goal), turn_back(goal), around(goal, 3)]
    factors = factor_call(rate, goals, tops)

    there = sums_call(block, 1, per_device, jnp.bfloat16, expos, points, factors)
    there = [exchange(a, ("lo",), lambda at: at ^ 1) for a in there]
    here = sums_call(block, 0, per_device, jnp.float32, expos, points, factors)
    out, mass = add_call(block // 2, *here, *there)
    return (out[None], mass)


def solution(mesh):
    pts, cells = (mesh.shape[name] for name in ("pts", "cells"))
    square = (pts, cells) == (8, 4)
    shape, names = ((2, 2, 2, cells), ("y", "x", "lo", "cells")) if square else ((pts, cells), ("pts", "cells"))
    fine = Mesh(mesh.devices.reshape(shape), names)
    spread = names[:-1]
    in_specs = (P(names, None), P(names), P("cells", None), P("cells"))
    out_specs = (P("cells", spread, None), P("cells", spread))

    def run(codes, exponents, centroids, counters):
        small = codes.size * 2 <= GATHER_BYTES and codes.shape[0] == 128 * pts * cells
        body = split_cells if square and small else split_points
        mapped = jax.shard_map(body, mesh=fine, in_specs=in_specs, out_specs=out_specs, check_vma=False)
        return mapped(codes, exponents, centroids, counters)

    return run
```

```python
import functools
import math

import jax
import jax.numpy as jnp
from jax import lax
from jax.experimental import pallas as pl
from jax.experimental.pallas import tpu as pltpu
from jax.sharding import Mesh, PartitionSpec as P

GATHER_BYTES = 8 << 20
VMEM_BYTES = 16 << 20


def to_points(codes, exponents):
    scale = lax.shift_left(jnp.ones_like(exponents), 16 - exponents).astype(jnp.float32) * 2.0**-16
    return (codes.astype(jnp.float32) * scale[:, None]).astype(jnp.bfloat16)


def split_points(codes, exponents, centroids, counters):
    local_rows = to_points(codes, exponents)
    points = lax.all_gather(local_rows, "cells", axis=0, tiled=True)
    beta = 4.0 / math.sqrt(points.shape[1])
    logits = (
        lax.dot_general(
            points, centroids, (((1,), (1,)), ((), ())), preferred_element_type=jnp.float32
        )
        * beta
    )
    inverse = lax.rsqrt(counters.astype(jnp.float32) + 1.0)
    top = lax.pmax(jnp.max(logits, axis=1), "cells")
    expo = jnp.exp(logits - top[:, None])
    total, novel = lax.psum(
        (jnp.sum(expo, axis=1), jnp.dot(expo, inverse, preferred_element_type=jnp.float32)), "cells"
    )
    weight = novel / total
    share = (expo * (weight / total)[:, None]).astype(jnp.bfloat16)
    mass_local = jnp.sum(share.astype(jnp.float32), axis=0)
    sums_local = lax.dot_general(
        share, points, (((0,), (0,)), ((), ())), preferred_element_type=jnp.float32
    )
    sums = lax.psum_scatter(sums_local, "pts", scatter_dimension=0, tiled=True)
    mass = lax.psum_scatter(mass_local, "pts", scatter_dimension=0, tiled=True)
    return (sums[None], mass[None])


def exchange(a, axes, partner):
    count = math.prod(lax.axis_size(axis) for axis in axes)
    return lax.ppermute(a, axes, [(partner(at), at) for at in range(count)])


def in_vmem(n):
    return [pl.BlockSpec(memory_space=pltpu.VMEM)] * n


def join(above, below, *after):
    def kernel(above, below, *refs):
        out = refs[-1]
        out[: above.shape[0], :] = above[...]
        out[above.shape[0] :, :] = below[...]

    return pl.pallas_call(
        kernel,
        in_specs=in_vmem(2 + len(after)),
        out_specs=in_vmem(1)[0],
        out_shape=jax.ShapeDtypeStruct((above.shape[0] + below.shape[0], above.shape[1]), above.dtype),
        compiler_params=pltpu.CompilerParams(vmem_limit_bytes=VMEM_BYTES),
    )(above, below, *after)


def beside(left, right, *after):
    def kernel(left, right, *refs):
        refs[-1][...] = jnp.concatenate([left[...], right[...]], axis=1)

    return pl.pallas_call(
        kernel,
        in_specs=in_vmem(2 + len(after)),
        out_specs=in_vmem(1)[0],
        out_shape=jax.ShapeDtypeStruct((left.shape[0], left.shape[1] + right.shape[1]), left.dtype),
        compiler_params=pltpu.CompilerParams(vmem_limit_bytes=VMEM_BYTES),
    )(left, right, *after)


def hold(a, *after):
    def kernel(a, *refs):
        refs[-1][...] = a[...]

    return pl.pallas_call(
        kernel,
        in_specs=in_vmem(1 + len(after)),
        out_specs=in_vmem(1)[0],
        out_shape=jax.ShapeDtypeStruct(a.shape, a.dtype),
        compiler_params=pltpu.CompilerParams(vmem_limit_bytes=VMEM_BYTES),
    )(a, *after)


def scores(cells, points):
    return lax.dot_general(cells, points, (((1,), (1,)), ((), ())), preferred_element_type=jnp.float32)


def chip_index():
    return lax.axis_index("y") * 2 + lax.axis_index("x")


def inverse_kernel(counters, *refs):
    inverse = refs[-1]
    for line in range(counters.shape[0]):
        row = lax.rsqrt(counters[line : line + 1, :].astype(jnp.float32) + 1.0)
        inverse[line * 128 : (line + 1) * 128, :] = jnp.broadcast_to(row, (128, 128)).T


def inverse_call(counters, *after):
    return pl.pallas_call(
        inverse_kernel,
        in_specs=in_vmem(1 + len(after)),
        out_specs=in_vmem(1)[0],
        out_shape=jax.ShapeDtypeStruct((counters.shape[0], 128), jnp.float32),
        compiler_params=pltpu.CompilerParams(vmem_limit_bytes=VMEM_BYTES),
        cost_estimate=pl.CostEstimate(flops=4 * 10**9, bytes_accessed=0, transcendentals=0),
    )(counters.reshape(-1, 128), *after)


def totals_kernel(rate, block, n, *refs):
    pieces, (cells, inverse), stats = refs[:n], refs[n : n + 2], refs[-1]
    every = jnp.concatenate([piece[...] for piece in pieces], axis=0)
    count = cells.shape[0]
    parts = []
    for at in range(0, count, block):
        here = slice(at, at + block)
        logits = scores(cells[here, :], every)
        top = jnp.max(logits, axis=0, keepdims=True)
        value = jnp.exp2((logits - top) * rate)
        scale = inverse[here, :]
        weighed = [
            jnp.sum(value[:, i : i + 128] * scale, axis=0, keepdims=True) for i in range(0, value.shape[1], 128)
        ]
        parts.append((top, jnp.sum(value, axis=0, keepdims=True), jnp.concatenate(weighed, axis=1)))
        while len(parts) > 1 and (at + block == count or len(parts) == 4):
            parts = [join_stats(rate, parts)]
    stats[...] = jnp.concatenate(parts[0], axis=0)


def join_stats(rate, parts):
    top = functools.reduce(jnp.maximum, [part[0] for part in parts])
    scales = [jnp.exp2((part[0] - top) * rate) for part in parts]
    return (top, *(sum(part[at] * scale for part, scale in zip(parts, scales)) for at in (1, 2)))


def totals_call(rate, block, pieces, cells, inverse, after=()):
    n_points, width = sum(piece.shape[0] for piece in pieces), pieces[0].shape[1]
    n_cells = inverse.shape[0]
    args = (*pieces, cells, inverse, *after)
    return pl.pallas_call(
        functools.partial(totals_kernel, rate, block, len(pieces)),
        in_specs=in_vmem(len(args)),
        out_specs=in_vmem(1)[0],
        out_shape=jax.ShapeDtypeStruct((3, n_points), jnp.float32),
        compiler_params=pltpu.CompilerParams(vmem_limit_bytes=VMEM_BYTES),
        cost_estimate=pl.CostEstimate(
            flops=2 * n_cells * n_points * width,
            bytes_accessed=2 * n_cells * width,
            transcendentals=n_cells * n_points,
        ),
    )(*args)


def goal_kernel(rate, *refs):
    stats, goal = refs[:4], refs[-1]
    for at in range(4):
        here = [stat[:, (at ^ by) * 128 : ((at ^ by) + 1) * 128] for by, stat in enumerate(stats)]
        top, total, novel = join_stats(rate, [(s[:1], s[1:2], s[2:]) for s in here])
        goal[:, at * 128 : (at + 1) * 128] = jnp.concatenate([top, novel / total / total], axis=0)


def goal_call(rate, *stats):
    return pl.pallas_call(
        functools.partial(goal_kernel, rate),
        in_specs=in_vmem(len(stats)),
        out_specs=in_vmem(1)[0],
        out_shape=jax.ShapeDtypeStruct((2, stats[0].shape[1]), jnp.float32),
        compiler_params=pltpu.CompilerParams(vmem_limit_bytes=VMEM_BYTES),
    )(*stats)


def factor_kernel(rate, *refs):
    goals, tops, factors = refs[:4], refs[4:6], refs[6:]
    rows = goals[0].shape[1] // 2
    for group in range(2):
        mine = slice(group * rows, (group + 1) * rows)
        for at, goal in enumerate(goals):
            here = slice(at * rows, (at + 1) * rows)
            factors[group][:, here] = jnp.exp2((tops[group][:, here] - goal[:1, mine]) * rate) * goal[1:, mine]


def factor_call(rate, goals, tops):
    return pl.pallas_call(
        functools.partial(factor_kernel, rate),
        in_specs=in_vmem(6),
        out_specs=in_vmem(2),
        out_shape=[jax.ShapeDtypeStruct(top.shape, jnp.float32) for top in tops],
        compiler_params=pltpu.CompilerParams(vmem_limit_bytes=VMEM_BYTES),
    )(*goals, *tops)


def expo_kernel(rate, block, n, *refs):
    pieces, cells, (expo, tops, points) = refs[:n], refs[n], refs[-3:]
    start = 0
    for piece in pieces:
        points[start : start + piece.shape[0], :] = piece[...]
        start += piece.shape[0]
    count = expo.shape[0] // block
    chip = chip_index()
    for at in range(count):
        mine = pl.ds(pl.multiple_of((chip * count + at) * block, block), block)
        for part in range(0, points.shape[0], 256):
            some = slice(part, part + 256)
            logits = scores(cells[mine, :], points[some, :])
            top = jnp.max(logits, axis=0, keepdims=True)
            expo[at * block : (at + 1) * block, some] = jnp.exp2((logits - top) * rate).astype(jnp.bfloat16)
            tops[at : at + 1, some] = top


def expo_call(rate, block, count, pieces, cells, *after):
    width = cells.shape[1]
    n_points = sum(piece.shape[0] for piece in pieces)
    return pl.pallas_call(
        functools.partial(expo_kernel, rate, block, len(pieces)),
        in_specs=in_vmem(len(pieces) + 1 + len(after)),
        out_specs=in_vmem(3),
        out_shape=[
            jax.ShapeDtypeStruct((count, n_points), jnp.bfloat16),
            jax.ShapeDtypeStruct((count // block, n_points), jnp.float32),
            jax.ShapeDtypeStruct((n_points, width), jnp.bfloat16),
        ],
        compiler_params=pltpu.CompilerParams(vmem_limit_bytes=VMEM_BYTES),
        cost_estimate=pl.CostEstimate(
            flops=2 * count * n_points * width,
            bytes_accessed=2 * (count * width + n_points * width + count * n_points),
            transcendentals=count * n_points,
        ),
    )(*pieces, cells, *after)


def weighed_sums(start, count, expos, points, factors):
    total = weight = None
    for expo, chunk, factor in zip(expos, points, factors):
        block = expo.shape[0] // factor.shape[0]
        shares = []
        for at in range(0, count, block):
            here = pl.ds(pl.multiple_of(start + at, block), block)
            scale = factor[pl.ds((start + at) // block, 1), :]
            shares.append((expo[here, :].astype(jnp.float32) * scale).astype(jnp.bfloat16))
        share = jnp.concatenate(shares, axis=0)
        part = jnp.dot(share, chunk[...], preferred_element_type=jnp.float32)
        wide = share.astype(jnp.float32)
        lanes = sum(wide[:, i : i + 128] for i in range(0, wide.shape[1], 128))
        total = part if total is None else total + part
        weight = lanes if weight is None else weight + lanes
    return total, jnp.sum(weight.T, axis=0, keepdims=True)


def sums_kernel(n, block, side, *refs):
    expos, points, factors, (sums, mass) = refs[:n], refs[n : 2 * n], refs[2 * n : 3 * n], refs[3 * n :]
    rows = sums.shape[0]
    first = (lax.axis_index("lo") ^ side) * rows
    for at in range(0, rows, block):
        here = slice(at, at + block)
        total, weight = weighed_sums(first + at, block, expos, points, factors)
        sums[here, :] = total.astype(sums.dtype)
        mass[:, here] = weight


def sums_call(block, side, rows, dtype, expos, points, factors):
    n = len(expos)
    n_points, width = points[0].shape
    return pl.pallas_call(
        functools.partial(sums_kernel, n, block, side),
        in_specs=in_vmem(3 * n),
        out_specs=in_vmem(2),
        out_shape=[jax.ShapeDtypeStruct((rows, width), dtype), jax.ShapeDtypeStruct((1, rows), jnp.float32)],
        compiler_params=pltpu.CompilerParams(vmem_limit_bytes=VMEM_BYTES),
        cost_estimate=pl.CostEstimate(
            flops=2 * rows * n * n_points * width,
            bytes_accessed=2 * n * n_points * (rows + width) + 4 * rows * width,
            transcendentals=0,
        ),
    )(*expos, *points, *factors)


def add_kernel(block, here, here_mass, there, there_mass, sums, mass, out, left):
    def copy(at):
        rows = pl.ds(at * block, block)
        return pltpu.make_async_copy(out.at[rows, :], sums.at[rows, :], left.at[at])

    count = here.shape[0] // block
    for at in range(count):
        rows = slice(at * block, (at + 1) * block)
        out[rows, :] = here[rows, :] + there[rows, :].astype(jnp.float32)
        copy(at).start(priority=at % 2)
    mass[...] = here_mass[...] + there_mass[...]
    for at in range(count):
        copy(at).wait()


def add_call(block, here, here_mass, there, there_mass):
    return pl.pallas_call(
        functools.partial(add_kernel, block),
        in_specs=in_vmem(4),
        out_specs=[pl.BlockSpec(memory_space=pltpu.HBM)] + in_vmem(1),
        out_shape=[
            jax.ShapeDtypeStruct(here.shape, jnp.float32),
            jax.ShapeDtypeStruct(here_mass.shape, jnp.float32),
        ],
        scratch_shapes=[
            pltpu.VMEM(here.shape, jnp.float32),
            pltpu.SemaphoreType.DMA((here.shape[0] // block,)),
        ],
        compiler_params=pltpu.CompilerParams(vmem_limit_bytes=VMEM_BYTES),
    )(here, here_mass, there, there_mass)


def split_cells(codes, exponents, centroids, counters):
    own = to_points(codes, exponents)
    rate = 4.0 / math.sqrt(own.shape[1]) * math.log2(math.e)
    plane = ("y", "x", "lo")

    turn = lambda a: exchange(a, plane, lambda at: at ^ (4 if at % 2 else 2))
    turn_back = lambda a: exchange(a, plane, lambda at: at ^ (2 if at % 2 else 4))
    along_z = lambda a, by: exchange(a, ("cells",), lambda at: at ^ by)
    around = lambda a, by: exchange(a, ("y", "x"), lambda at: at ^ by)

    per_device = centroids.shape[0] // 8
    block = per_device // 3

    near_1, near_2, near_3 = (along_z(own, by) for by in (1, 2, 3))
    expand = lambda near: (near, turn(near), turn_back(near))
    own, first_0, second_0 = expand(own)
    near_1, first_1, second_1 = expand(near_1)
    across_0, across_1 = turn_back(first_0), turn_back(first_1)
    inverse = inverse_call(counters, first_0, near_1)
    stats = [totals_call(rate, block, (own, near_1), centroids, inverse, after=(second_0,))]
    near_23 = join(near_2, near_3, *stats)
    first_23 = turn(near_23)
    after = (first_1, second_1, across_0, across_1)
    stats.append(totals_call(rate, block, (near_23,), centroids, inverse, after=after))
    second_23, across_23 = turn_back(hold(near_23, stats[1])), turn_back(hold(first_23, stats[1]))

    expand = functools.partial(expo_call, rate, block, 2 * per_device)
    groups = [expand((own, near_1, first_0, first_1, second_0, second_1, across_0, across_1), centroids, stats[1])]
    tops = groups[0][1]
    stat = beside(*stats)
    theirs = [along_z(stat, by) for by in (1, 2, 3)]
    goal = goal_call(rate, stat, *theirs, tops, second_23)
    groups.append(expand((near_23, first_23, second_23, across_23), centroids))
    expos, tops, points = zip(*groups)
    goals = [goal, turn(goal), turn_back(goal), around(goal, 3)]
    factors = factor_call(rate, goals, tops)

    there = sums_call(block, 1, per_device, jnp.bfloat16, expos, points, factors)
    there = [exchange(a, ("lo",), lambda at: at ^ 1) for a in there]
    here = sums_call(block, 0, per_device, jnp.float32, expos, points, factors)
    out, mass = add_call(block // 2, *here, *there)
    return (out[None], mass)


def solution(mesh):
    pts, cells = (mesh.shape[name] for name in ("pts", "cells"))
    square = (pts, cells) == (8, 4)
    shape, names = ((2, 2, 2, cells), ("y", "x", "lo", "cells")) if square else ((pts, cells), ("pts", "cells"))
    fine = Mesh(mesh.devices.reshape(shape), names)
    spread = names[:-1]
    in_specs = (P(names, None), P(names), P("cells", None), P("cells"))
    out_specs = (P("cells", spread, None), P("cells", spread))

    def run(codes, exponents, centroids, counters):
        small = codes.size * 2 <= GATHER_BYTES and codes.shape[0] == 128 * pts * cells
        body = split_cells if square and small else split_points
        mapped = jax.shard_map(body, mesh=fine, in_specs=in_specs, out_specs=out_specs, check_vma=False)
        return mapped(codes, exponents, centroids, counters)

    return run
```

```python
import functools
import math

import jax
import jax.numpy as jnp
from jax import lax
from jax.experimental import pallas as pl
from jax.experimental.pallas import tpu as pltpu
from jax.sharding import Mesh, PartitionSpec as P

GATHER_BYTES = 8 << 20
VMEM_BYTES = 16 << 20


def to_points(codes, exponents):
    scale = lax.shift_left(jnp.ones_like(exponents), 16 - exponents).astype(jnp.float32) * 2.0**-16
    return (codes.astype(jnp.float32) * scale[:, None]).astype(jnp.bfloat16)


def split_points(codes, exponents, centroids, counters):
    local_rows = to_points(codes, exponents)
    points = lax.all_gather(local_rows, "cells", axis=0, tiled=True)
    beta = 4.0 / math.sqrt(points.shape[1])
    logits = (
        lax.dot_general(
            points, centroids, (((1,), (1,)), ((), ())), preferred_element_type=jnp.float32
        )
        * beta
    )
    inverse = lax.rsqrt(counters.astype(jnp.float32) + 1.0)
    top = lax.pmax(jnp.max(logits, axis=1), "cells")
    expo = jnp.exp(logits - top[:, None])
    total, novel = lax.psum(
        (jnp.sum(expo, axis=1), jnp.dot(expo, inverse, preferred_element_type=jnp.float32)), "cells"
    )
    weight = novel / total
    share = (expo * (weight / total)[:, None]).astype(jnp.bfloat16)
    mass_local = jnp.sum(share.astype(jnp.float32), axis=0)
    sums_local = lax.dot_general(
        share, points, (((0,), (0,)), ((), ())), preferred_element_type=jnp.float32
    )
    sums = lax.psum_scatter(sums_local, "pts", scatter_dimension=0, tiled=True)
    mass = lax.psum_scatter(mass_local, "pts", scatter_dimension=0, tiled=True)
    return (sums[None], mass[None])


def exchange(a, axes, partner):
    count = math.prod(lax.axis_size(axis) for axis in axes)
    return lax.ppermute(a, axes, [(partner(at), at) for at in range(count)])


def in_vmem(n):
    return [pl.BlockSpec(memory_space=pltpu.VMEM)] * n


def join(above, below, *after):
    def kernel(above, below, *refs):
        out = refs[-1]
        out[: above.shape[0], :] = above[...]
        out[above.shape[0] :, :] = below[...]

    return pl.pallas_call(
        kernel,
        in_specs=in_vmem(2 + len(after)),
        out_specs=in_vmem(1)[0],
        out_shape=jax.ShapeDtypeStruct((above.shape[0] + below.shape[0], above.shape[1]), above.dtype),
        compiler_params=pltpu.CompilerParams(vmem_limit_bytes=VMEM_BYTES),
    )(above, below, *after)


def beside(left, right, *after):
    def kernel(left, right, *refs):
        refs[-1][...] = jnp.concatenate([left[...], right[...]], axis=1)

    return pl.pallas_call(
        kernel,
        in_specs=in_vmem(2 + len(after)),
        out_specs=in_vmem(1)[0],
        out_shape=jax.ShapeDtypeStruct((left.shape[0], left.shape[1] + right.shape[1]), left.dtype),
        compiler_params=pltpu.CompilerParams(vmem_limit_bytes=VMEM_BYTES),
    )(left, right, *after)


def hold(a, *after):
    def kernel(a, *refs):
        refs[-1][...] = a[...]

    return pl.pallas_call(
        kernel,
        in_specs=in_vmem(1 + len(after)),
        out_specs=in_vmem(1)[0],
        out_shape=jax.ShapeDtypeStruct(a.shape, a.dtype),
        compiler_params=pltpu.CompilerParams(vmem_limit_bytes=VMEM_BYTES),
    )(a, *after)


def scores(cells, points):
    return lax.dot_general(cells, points, (((1,), (1,)), ((), ())), preferred_element_type=jnp.float32)


def chip_index():
    return lax.axis_index("y") * 2 + lax.axis_index("x")


def inverse_kernel(counters, *refs):
    inverse = refs[-1]
    for line in range(counters.shape[0]):
        row = lax.rsqrt(counters[line : line + 1, :].astype(jnp.float32) + 1.0)
        inverse[line * 128 : (line + 1) * 128, :] = jnp.broadcast_to(row, (128, 128)).T


def inverse_call(counters, *after):
    return pl.pallas_call(
        inverse_kernel,
        in_specs=in_vmem(1 + len(after)),
        out_specs=in_vmem(1)[0],
        out_shape=jax.ShapeDtypeStruct((counters.shape[0], 128), jnp.float32),
        compiler_params=pltpu.CompilerParams(vmem_limit_bytes=VMEM_BYTES),
        cost_estimate=pl.CostEstimate(flops=4 * 10**9, bytes_accessed=0, transcendentals=0),
    )(counters.reshape(-1, 128), *after)


def totals_kernel(rate, block, n, *refs):
    pieces, (cells, inverse), stats = refs[:n], refs[n : n + 2], refs[-1]
    every = jnp.concatenate([piece[...] for piece in pieces], axis=0)
    count = cells.shape[0]
    parts = []
    for at in range(0, count, block):
        here = slice(at, at + block)
        logits = scores(cells[here, :], every)
        top = jnp.max(logits, axis=0, keepdims=True)
        value = jnp.exp2((logits - top) * rate)
        scale = inverse[here, :]
        weighed = [
            jnp.sum(value[:, i : i + 128] * scale, axis=0, keepdims=True) for i in range(0, value.shape[1], 128)
        ]
        parts.append((top, jnp.sum(value, axis=0, keepdims=True), jnp.concatenate(weighed, axis=1)))
        while len(parts) > 1 and (at + block == count or len(parts) == 4):
            parts = [join_stats(rate, parts)]
    stats[...] = jnp.concatenate(parts[0], axis=0)


def join_stats(rate, parts):
    top = functools.reduce(jnp.maximum, [part[0] for part in parts])
    scales = [jnp.exp2((part[0] - top) * rate) for part in parts]
    return (top, *(sum(part[at] * scale for part, scale in zip(parts, scales)) for at in (1, 2)))


def totals_call(rate, block, pieces, cells, inverse, after=(), declared=1.0):
    n_points, width = sum(piece.shape[0] for piece in pieces), pieces[0].shape[1]
    n_cells = inverse.shape[0]
    args = (*pieces, cells, inverse, *after)
    return pl.pallas_call(
        functools.partial(totals_kernel, rate, block, len(pieces)),
        in_specs=in_vmem(len(args)),
        out_specs=in_vmem(1)[0],
        out_shape=jax.ShapeDtypeStruct((3, n_points), jnp.float32),
        compiler_params=pltpu.CompilerParams(vmem_limit_bytes=VMEM_BYTES),
        cost_estimate=pl.CostEstimate(
            flops=int(declared * 2 * n_cells * n_points * width),
            bytes_accessed=int(declared * 2 * n_cells * width),
            transcendentals=int(declared * n_cells * n_points),
        ),
    )(*args)


def merge_kernel(rate, by, goal, mine, theirs, *refs):
    for at in range(4):
        ours = mine[:, at * 128 : (at + 1) * 128]
        other = theirs[:, (at ^ by) * 128 : ((at ^ by) + 1) * 128]
        top, total, novel = join_stats(rate, [(s[:1], s[1:2], s[2:]) for s in (ours, other)])
        rows = (top, novel / total / total) if goal else (top, total, novel)
        refs[-1][:, at * 128 : (at + 1) * 128] = jnp.concatenate(rows, axis=0)


def merge_call(rate, by, goal, mine, theirs, *after):
    return pl.pallas_call(
        functools.partial(merge_kernel, rate, by, goal),
        in_specs=in_vmem(2 + len(after)),
        out_specs=in_vmem(1)[0],
        out_shape=jax.ShapeDtypeStruct((2 if goal else 3, mine.shape[1]), jnp.float32),
        compiler_params=pltpu.CompilerParams(vmem_limit_bytes=VMEM_BYTES),
    )(mine, theirs, *after)


def factor_kernel(rate, n, *refs):
    goals, tops, factors = refs[:4], refs[4 : 4 + n], refs[4 + n :]
    rows = goals[0].shape[1] // 2
    spots = [(0, 0, 0), (0, 1, rows), (0, 2, 2 * rows), (0, 3, 3 * rows)]
    spots += [(1, 0, 0), (1, 1, rows), (1, 2, 2 * rows), (2, 3, 0)]
    for at, (bundle, goal, start) in enumerate(spots):
        group = at // 4
        mine, here = slice(group * rows, (group + 1) * rows), slice(start, start + rows)
        scale = jnp.exp2((tops[bundle][:, here] - goals[goal][:1, mine]) * rate)
        factors[bundle][:, here] = scale * goals[goal][1:, mine]


def factor_call(rate, goals, tops):
    return pl.pallas_call(
        functools.partial(factor_kernel, rate, len(tops)),
        in_specs=in_vmem(4 + len(tops)),
        out_specs=in_vmem(len(tops)),
        out_shape=[jax.ShapeDtypeStruct(top.shape, jnp.float32) for top in tops],
        compiler_params=pltpu.CompilerParams(vmem_limit_bytes=VMEM_BYTES),
    )(*goals, *tops)


def expo_kernel(rate, block, n, *refs):
    pieces, cells, (expo, tops, points) = refs[:n], refs[n], refs[-3:]
    start = 0
    for piece in pieces:
        points[start : start + piece.shape[0], :] = piece[...]
        start += piece.shape[0]
    count = expo.shape[0] // block
    chip = chip_index()
    for at in range(count):
        mine = pl.ds(pl.multiple_of((chip * count + at) * block, block), block)
        for part in range(0, points.shape[0], 256):
            some = slice(part, part + 256)
            logits = scores(cells[mine, :], points[some, :])
            top = jnp.max(logits, axis=0, keepdims=True)
            expo[at * block : (at + 1) * block, some] = jnp.exp2((logits - top) * rate).astype(jnp.bfloat16)
            tops[at : at + 1, some] = top


def expo_call(rate, block, count, pieces, cells, *after):
    width = cells.shape[1]
    n_points = sum(piece.shape[0] for piece in pieces)
    return pl.pallas_call(
        functools.partial(expo_kernel, rate, block, len(pieces)),
        in_specs=in_vmem(len(pieces) + 1 + len(after)),
        out_specs=in_vmem(3),
        out_shape=[
            jax.ShapeDtypeStruct((count, n_points), jnp.bfloat16),
            jax.ShapeDtypeStruct((count // block, n_points), jnp.float32),
            jax.ShapeDtypeStruct((n_points, width), jnp.bfloat16),
        ],
        compiler_params=pltpu.CompilerParams(vmem_limit_bytes=VMEM_BYTES),
        cost_estimate=pl.CostEstimate(
            flops=2 * count * n_points * width,
            bytes_accessed=2 * (count * width + n_points * width + count * n_points),
            transcendentals=count * n_points,
        ),
    )(*pieces, cells, *after)


def weighed_sums(start, count, expos, points, factors):
    total = weight = None
    for expo, chunk, factor in zip(expos, points, factors):
        block = expo.shape[0] // factor.shape[0]
        shares = []
        for at in range(0, count, block):
            here = pl.ds(pl.multiple_of(start + at, block), block)
            scale = factor[pl.ds((start + at) // block, 1), :]
            shares.append((expo[here, :].astype(jnp.float32) * scale).astype(jnp.bfloat16))
        share = jnp.concatenate(shares, axis=0)
        part = jnp.dot(share, chunk[...], preferred_element_type=jnp.float32)
        wide = share.astype(jnp.float32)
        lanes = sum(wide[:, i : i + 128] for i in range(0, wide.shape[1], 128))
        total = part if total is None else total + part
        weight = lanes if weight is None else weight + lanes
    return total, jnp.sum(weight.T, axis=0, keepdims=True)


def sums_kernel(n, block, side, *refs):
    expos, points, factors, (sums, mass) = refs[:n], refs[n : 2 * n], refs[2 * n : 3 * n], refs[3 * n :]
    rows = sums.shape[0]
    first = (lax.axis_index("lo") ^ side) * rows
    for at in range(0, rows, block):
        here = slice(at, at + block)
        total, weight = weighed_sums(first + at, block, expos, points, factors)
        sums[here, :] = total.astype(sums.dtype)
        mass[:, here] = weight


def sums_call(block, side, rows, dtype, expos, points, factors):
    n = len(expos)
    n_points, width = points[0].shape
    return pl.pallas_call(
        functools.partial(sums_kernel, n, block, side),
        in_specs=in_vmem(3 * n),
        out_specs=in_vmem(2),
        out_shape=[jax.ShapeDtypeStruct((rows, width), dtype), jax.ShapeDtypeStruct((1, rows), jnp.float32)],
        compiler_params=pltpu.CompilerParams(vmem_limit_bytes=VMEM_BYTES),
        cost_estimate=pl.CostEstimate(
            flops=2 * rows * n * n_points * width,
            bytes_accessed=2 * n * n_points * (rows + width) + 4 * rows * width,
            transcendentals=0,
        ),
    )(*expos, *points, *factors)


def add_kernel(block, here, here_mass, there, there_mass, sums, mass, out, left):
    def copy(at):
        rows = pl.ds(at * block, block)
        return pltpu.make_async_copy(out.at[rows, :], sums.at[rows, :], left.at[at])

    count = here.shape[0] // block
    for at in range(count):
        rows = slice(at * block, (at + 1) * block)
        out[rows, :] = here[rows, :] + there[rows, :].astype(jnp.float32)
        copy(at).start(priority=at % 2)
    mass[...] = here_mass[...] + there_mass[...]
    for at in range(count):
        copy(at).wait()


def add_call(block, here, here_mass, there, there_mass):
    return pl.pallas_call(
        functools.partial(add_kernel, block),
        in_specs=in_vmem(4),
        out_specs=[pl.BlockSpec(memory_space=pltpu.HBM)] + in_vmem(1),
        out_shape=[
            jax.ShapeDtypeStruct(here.shape, jnp.float32),
            jax.ShapeDtypeStruct(here_mass.shape, jnp.float32),
        ],
        scratch_shapes=[
            pltpu.VMEM(here.shape, jnp.float32),
            pltpu.SemaphoreType.DMA((here.shape[0] // block,)),
        ],
        compiler_params=pltpu.CompilerParams(vmem_limit_bytes=VMEM_BYTES),
    )(here, here_mass, there, there_mass)


def split_cells(codes, exponents, centroids, counters):
    own = to_points(codes, exponents)
    rate = 4.0 / math.sqrt(own.shape[1]) * math.log2(math.e)
    plane = ("y", "x", "lo")

    turn = lambda a: exchange(a, plane, lambda at: at ^ (4 if at % 2 else 2))
    turn_back = lambda a: exchange(a, plane, lambda at: at ^ (2 if at % 2 else 4))
    along_z = lambda a, by: exchange(a, ("cells",), lambda at: at ^ by)
    around = lambda a, by: exchange(a, ("y", "x"), lambda at: at ^ by)

    per_device = centroids.shape[0] // 8
    block = per_device // 3

    near_1, near_2, near_3 = (along_z(own, by) for by in (1, 2, 3))
    inverse = inverse_call(counters)
    near_01 = join(own, near_1)
    first_01, second_01 = turn(near_01), turn_back(near_01)
    stats = [totals_call(rate, block, (near_01,), centroids, inverse)]
    near_23 = join(near_2, near_3, *stats)
    across_01 = turn_back(hold(first_01, near_23))
    first_23 = turn(near_23)
    stats.append(totals_call(rate, block, (near_23,), centroids, inverse, after=(first_01, second_01)))
    second_23 = turn_back(hold(near_23, stats[1]))

    expand = functools.partial(expo_call, rate, block, 2 * per_device)
    stat = beside(*stats)
    bundles = [expand((near_01, first_01, second_01, across_01), centroids, stat)]
    stat = merge_call(rate, 1, False, stat, along_z(stat, 1), bundles[0][1])
    across_23 = turn_back(hold(first_23, stat))
    bundles.append(expand((near_23, first_23, second_23), centroids, stat))
    goal = merge_call(rate, 2, True, stat, along_z(stat, 2), bundles[1][1])
    bundles.append(expand((across_23,), centroids))
    expos, tops, points = zip(*bundles)
    goals = [goal, turn(goal), turn_back(goal), around(goal, 3)]
    factors = factor_call(rate, goals, tops)

    there = sums_call(block, 1, per_device, jnp.bfloat16, expos, points, factors)
    there = [exchange(a, ("lo",), lambda at: at ^ 1) for a in there]
    here = sums_call(block, 0, per_device, jnp.float32, expos, points, factors)
    out, mass = add_call(block // 2, *here, *there)
    return (out[None], mass)


def solution(mesh):
    pts, cells = (mesh.shape[name] for name in ("pts", "cells"))
    square = (pts, cells) == (8, 4)
    shape, names = ((2, 2, 2, cells), ("y", "x", "lo", "cells")) if square else ((pts, cells), ("pts", "cells"))
    fine = Mesh(mesh.devices.reshape(shape), names)
    spread = names[:-1]
    in_specs = (P(names, None), P(names), P("cells", None), P("cells"))
    out_specs = (P("cells", spread, None), P("cells", spread))

    def run(codes, exponents, centroids, counters):
        small = codes.size * 2 <= GATHER_BYTES and codes.shape[0] == 128 * pts * cells
        body = split_cells if square and small else split_points
        mapped = jax.shard_map(body, mesh=fine, in_specs=in_specs, out_specs=out_specs, check_vma=False)
        return mapped(codes, exponents, centroids, counters)

    return run
```

```python
import functools
import math

import jax
import jax.numpy as jnp
from jax import lax
from jax.experimental import pallas as pl
from jax.experimental.pallas import tpu as pltpu
from jax.sharding import Mesh, PartitionSpec as P

GATHER_BYTES = 8 << 20
VMEM_BYTES = 16 << 20


def to_points(codes, exponents):
    scale = lax.shift_left(jnp.ones_like(exponents), 16 - exponents).astype(jnp.float32) * 2.0**-16
    return (codes.astype(jnp.float32) * scale[:, None]).astype(jnp.bfloat16)


def split_points(codes, exponents, centroids, counters):
    local_rows = to_points(codes, exponents)
    points = lax.all_gather(local_rows, "cells", axis=0, tiled=True)
    beta = 4.0 / math.sqrt(points.shape[1])
    logits = (
        lax.dot_general(
            points, centroids, (((1,), (1,)), ((), ())), preferred_element_type=jnp.float32
        )
        * beta
    )
    inverse = lax.rsqrt(counters.astype(jnp.float32) + 1.0)
    top = lax.pmax(jnp.max(logits, axis=1), "cells")
    expo = jnp.exp(logits - top[:, None])
    total, novel = lax.psum(
        (jnp.sum(expo, axis=1), jnp.dot(expo, inverse, preferred_element_type=jnp.float32)), "cells"
    )
    weight = novel / total
    share = (expo * (weight / total)[:, None]).astype(jnp.bfloat16)
    mass_local = jnp.sum(share.astype(jnp.float32), axis=0)
    sums_local = lax.dot_general(
        share, points, (((0,), (0,)), ((), ())), preferred_element_type=jnp.float32
    )
    sums = lax.psum_scatter(sums_local, "pts", scatter_dimension=0, tiled=True)
    mass = lax.psum_scatter(mass_local, "pts", scatter_dimension=0, tiled=True)
    return (sums[None], mass[None])


def exchange(a, axes, partner):
    count = math.prod(lax.axis_size(axis) for axis in axes)
    return lax.ppermute(a, axes, [(partner(at), at) for at in range(count)])


def in_vmem(n):
    return [pl.BlockSpec(memory_space=pltpu.VMEM)] * n


def join(above, below, *after):
    def kernel(above, below, *refs):
        out = refs[-1]
        out[: above.shape[0], :] = above[...]
        out[above.shape[0] :, :] = below[...]

    return pl.pallas_call(
        kernel,
        in_specs=in_vmem(2 + len(after)),
        out_specs=in_vmem(1)[0],
        out_shape=jax.ShapeDtypeStruct((above.shape[0] + below.shape[0], above.shape[1]), above.dtype),
        compiler_params=pltpu.CompilerParams(vmem_limit_bytes=VMEM_BYTES),
    )(above, below, *after)


def beside(left, right, *after):
    def kernel(left, right, *refs):
        refs[-1][...] = jnp.concatenate([left[...], right[...]], axis=1)

    return pl.pallas_call(
        kernel,
        in_specs=in_vmem(2 + len(after)),
        out_specs=in_vmem(1)[0],
        out_shape=jax.ShapeDtypeStruct((left.shape[0], left.shape[1] + right.shape[1]), left.dtype),
        compiler_params=pltpu.CompilerParams(vmem_limit_bytes=VMEM_BYTES),
    )(left, right, *after)


def hold(a, *after, declared=0):
    def kernel(a, *refs):
        refs[-1][...] = a[...]

    return pl.pallas_call(
        kernel,
        in_specs=in_vmem(1 + len(after)),
        out_specs=in_vmem(1)[0],
        out_shape=jax.ShapeDtypeStruct(a.shape, a.dtype),
        compiler_params=pltpu.CompilerParams(vmem_limit_bytes=VMEM_BYTES),
        cost_estimate=pl.CostEstimate(flops=declared, bytes_accessed=0, transcendentals=0),
    )(a, *after)


def scores(cells, points):
    return lax.dot_general(cells, points, (((1,), (1,)), ((), ())), preferred_element_type=jnp.float32)


def chip_index():
    return lax.axis_index("y") * 2 + lax.axis_index("x")


def inverse_kernel(counters, *refs):
    inverse = refs[-1]
    for line in range(counters.shape[0]):
        row = lax.rsqrt(counters[line : line + 1, :].astype(jnp.float32) + 1.0)
        inverse[line * 128 : (line + 1) * 128, :] = jnp.broadcast_to(row, (128, 128)).T


def inverse_call(counters, *after):
    return pl.pallas_call(
        inverse_kernel,
        in_specs=in_vmem(1 + len(after)),
        out_specs=in_vmem(1)[0],
        out_shape=jax.ShapeDtypeStruct((counters.shape[0], 128), jnp.float32),
        compiler_params=pltpu.CompilerParams(vmem_limit_bytes=VMEM_BYTES),
    )(counters.reshape(-1, 128), *after)


def totals_kernel(rate, block, n, *refs):
    pieces, (cells, inverse), stats = refs[:n], refs[n : n + 2], refs[-1]
    every = jnp.concatenate([piece[...] for piece in pieces], axis=0)
    count = cells.shape[0]
    parts = []
    for at in range(0, count, block):
        here = slice(at, at + block)
        logits = scores(cells[here, :], every)
        top = jnp.max(logits, axis=0, keepdims=True)
        value = jnp.exp2((logits - top) * rate)
        scale = inverse[here, :]
        weighed = [
            jnp.sum(value[:, i : i + 128] * scale, axis=0, keepdims=True) for i in range(0, value.shape[1], 128)
        ]
        parts.append((top, jnp.sum(value, axis=0, keepdims=True), jnp.concatenate(weighed, axis=1)))
        while len(parts) > 1 and (at + block == count or len(parts) == 4):
            parts = [join_stats(rate, parts)]
    stats[...] = jnp.concatenate(parts[0], axis=0)


def join_stats(rate, parts):
    top = functools.reduce(jnp.maximum, [part[0] for part in parts])
    scales = [jnp.exp2((part[0] - top) * rate) for part in parts]
    return (top, *(sum(part[at] * scale for part, scale in zip(parts, scales)) for at in (1, 2)))


def totals_call(rate, block, pieces, cells, inverse, after=(), declared=1.0):
    n_points, width = sum(piece.shape[0] for piece in pieces), pieces[0].shape[1]
    n_cells = inverse.shape[0]
    args = (*pieces, cells, inverse, *after)
    return pl.pallas_call(
        functools.partial(totals_kernel, rate, block, len(pieces)),
        in_specs=in_vmem(len(args)),
        out_specs=in_vmem(1)[0],
        out_shape=jax.ShapeDtypeStruct((3, n_points), jnp.float32),
        compiler_params=pltpu.CompilerParams(vmem_limit_bytes=VMEM_BYTES),
        cost_estimate=pl.CostEstimate(
            flops=int(declared * 2 * n_cells * n_points * width),
            bytes_accessed=int(declared * 2 * n_cells * width),
            transcendentals=int(declared * n_cells * n_points),
        ),
    )(*args)


def merge_kernel(rate, by, goal, mine, theirs, *refs):
    for at in range(4):
        ours = mine[:, at * 128 : (at + 1) * 128]
        other = theirs[:, (at ^ by) * 128 : ((at ^ by) + 1) * 128]
        top, total, novel = join_stats(rate, [(s[:1], s[1:2], s[2:]) for s in (ours, other)])
        rows = (top, novel / total / total) if goal else (top, total, novel)
        refs[-1][:, at * 128 : (at + 1) * 128] = jnp.concatenate(rows, axis=0)


def merge_call(rate, by, goal, mine, theirs, *after):
    return pl.pallas_call(
        functools.partial(merge_kernel, rate, by, goal),
        in_specs=in_vmem(2 + len(after)),
        out_specs=in_vmem(1)[0],
        out_shape=jax.ShapeDtypeStruct((2 if goal else 3, mine.shape[1]), jnp.float32),
        compiler_params=pltpu.CompilerParams(vmem_limit_bytes=VMEM_BYTES),
    )(mine, theirs, *after)


def factor_kernel(rate, n, *refs):
    goals, tops, factors = refs[:4], refs[4 : 4 + n], refs[4 + n :]
    rows = goals[0].shape[1] // 2
    spots = [(0, 0, 0), (0, 1, rows), (0, 2, 2 * rows), (0, 3, 3 * rows)]
    spots += [(1, 0, 0), (1, 1, rows), (1, 2, 2 * rows), (2, 3, 0)]
    for at, (bundle, goal, start) in enumerate(spots):
        group = at // 4
        mine, here = slice(group * rows, (group + 1) * rows), slice(start, start + rows)
        scale = jnp.exp2((tops[bundle][:, here] - goals[goal][:1, mine]) * rate)
        factors[bundle][:, here] = scale * goals[goal][1:, mine]


def factor_call(rate, goals, tops):
    return pl.pallas_call(
        functools.partial(factor_kernel, rate, len(tops)),
        in_specs=in_vmem(4 + len(tops)),
        out_specs=in_vmem(len(tops)),
        out_shape=[jax.ShapeDtypeStruct(top.shape, jnp.float32) for top in tops],
        compiler_params=pltpu.CompilerParams(vmem_limit_bytes=VMEM_BYTES),
    )(*goals, *tops)


def expo_kernel(rate, block, n, *refs):
    pieces, cells, (expo, tops, points) = refs[:n], refs[n], refs[-3:]
    start = 0
    for piece in pieces:
        points[start : start + piece.shape[0], :] = piece[...]
        start += piece.shape[0]
    count = expo.shape[0] // block
    chip = chip_index()
    for at in range(count):
        mine = pl.ds(pl.multiple_of((chip * count + at) * block, block), block)
        for part in range(0, points.shape[0], 256):
            some = slice(part, part + 256)
            logits = scores(cells[mine, :], points[some, :])
            top = jnp.max(logits, axis=0, keepdims=True)
            expo[at * block : (at + 1) * block, some] = jnp.exp2((logits - top) * rate).astype(jnp.bfloat16)
            tops[at : at + 1, some] = top


def expo_call(rate, block, count, pieces, cells, *after, declared=1.0):
    width = cells.shape[1]
    n_points = sum(piece.shape[0] for piece in pieces)
    return pl.pallas_call(
        functools.partial(expo_kernel, rate, block, len(pieces)),
        in_specs=in_vmem(len(pieces) + 1 + len(after)),
        out_specs=in_vmem(3),
        out_shape=[
            jax.ShapeDtypeStruct((count, n_points), jnp.bfloat16),
            jax.ShapeDtypeStruct((count // block, n_points), jnp.float32),
            jax.ShapeDtypeStruct((n_points, width), jnp.bfloat16),
        ],
        compiler_params=pltpu.CompilerParams(vmem_limit_bytes=VMEM_BYTES),
        cost_estimate=pl.CostEstimate(
            flops=int(declared * 2 * count * n_points * width),
            bytes_accessed=int(declared * 2 * (count * width + n_points * width + count * n_points)),
            transcendentals=int(declared * count * n_points),
        ),
    )(*pieces, cells, *after)


def weighed_sums(start, count, expos, points, factors):
    total = weight = None
    for expo, chunk, factor in zip(expos, points, factors):
        block = expo.shape[0] // factor.shape[0]
        shares = []
        step = min(block, count)
        for at in range(0, count, step):
            here = pl.ds(pl.multiple_of(start + at, step), step)
            scale = factor[pl.ds((start + at) // block, 1), :]
            shares.append((expo[here, :].astype(jnp.float32) * scale).astype(jnp.bfloat16))
        share = jnp.concatenate(shares, axis=0)
        part = jnp.dot(share, chunk[...], preferred_element_type=jnp.float32)
        wide = share.astype(jnp.float32)
        lanes = sum(wide[:, i : i + 128] for i in range(0, wide.shape[1], 128))
        total = part if total is None else total + part
        weight = lanes if weight is None else weight + lanes
    return total, jnp.sum(weight.T, axis=0, keepdims=True)


def sums_kernel(n, block, side, *refs):
    expos, points, factors, (sums, mass) = refs[:n], refs[n : 2 * n], refs[2 * n : 3 * n], refs[3 * n :]
    half = expos[0].shape[0] // 2
    first = (lax.axis_index("lo") ^ side) * half
    for at in range(0, sums.shape[0], block):
        here = slice(at, at + block)
        total, weight = weighed_sums(first + at, block, expos, points, factors)
        sums[here, :] = total.astype(sums.dtype)
        mass[:, here] = weight


def last_kernel(n, block, *refs):
    expos, points, factors = refs[:n], refs[n : 2 * n], refs[2 * n : 3 * n]
    early, early_mass, there, there_mass, sums, mass, out, left = refs[3 * n :]
    done, half = early.shape[0], there.shape[0]
    first = lax.axis_index("lo") * half
    copies = []

    def store(start, stop, total):
        out[start:stop, :] = total + there[start:stop, :].astype(jnp.float32)
        here = pl.ds(start, stop - start)
        copies.append(pltpu.make_async_copy(out.at[here, :], sums.at[here, :], left.at[len(copies)]))
        copies[-1].start()

    store(0, done, early[...])
    mass[:, :done] = early_mass[...] + there_mass[:, :done]
    for at in range(done, half, block):
        here = slice(at, at + block)
        total, weight = weighed_sums(first + at, block, expos, points, factors)
        store(at, at + block, total)
        mass[:, here] = weight + there_mass[:, here]
    for copy in copies:
        copy.wait()


def sums_call(block, side, rows, dtype, expos, points, factors, *last):
    n = len(expos)
    width = points[0].shape[1]
    kernel = functools.partial(sums_kernel, n, block, side)
    done, scratch = 0, []
    if last:
        kernel, done = functools.partial(last_kernel, n, block), last[0].shape[0]
        scratch = [pltpu.VMEM((rows, width), dtype), pltpu.SemaphoreType.DMA((1 + (rows - done) // block,))]
    n_points = sum(chunk.shape[0] for chunk in points)
    return pl.pallas_call(
        kernel,
        in_specs=in_vmem(3 * n + len(last)),
        out_specs=[pl.BlockSpec(memory_space=pltpu.HBM if last else pltpu.VMEM)] + in_vmem(1),
        out_shape=[jax.ShapeDtypeStruct((rows, width), dtype), jax.ShapeDtypeStruct((1, rows), jnp.float32)],
        scratch_shapes=scratch,
        compiler_params=pltpu.CompilerParams(vmem_limit_bytes=VMEM_BYTES),
        cost_estimate=pl.CostEstimate(
            flops=2 * (rows - done) * n_points * width,
            bytes_accessed=2 * n_points * (rows + width) + 4 * rows * width,
            transcendentals=0,
        ),
    )(*expos, *points, *factors, *last)


def split_cells(codes, exponents, centroids, counters):
    own = to_points(codes, exponents)
    rate = 4.0 / math.sqrt(own.shape[1]) * math.log2(math.e)
    plane = ("y", "x", "lo")

    turn = lambda a: exchange(a, plane, lambda at: at ^ (4 if at % 2 else 2))
    turn_back = lambda a: exchange(a, plane, lambda at: at ^ (2 if at % 2 else 4))
    along_z = lambda a, by: exchange(a, ("cells",), lambda at: at ^ by)
    around = lambda a, by: exchange(a, ("y", "x"), lambda at: at ^ by)

    per_device = centroids.shape[0] // 8
    block = per_device // 3

    near_1, near_2, near_3 = (along_z(own, by) for by in (1, 2, 3))
    inverse = inverse_call(counters)
    near_01 = join(own, near_1, inverse)
    held_01 = hold(near_01, declared=4 * 10**9)
    first_01, second_01 = turn(near_01), turn_back(near_01)
    stats = [totals_call(rate, block, (held_01,), centroids, inverse)]
    across_01 = turn_back(hold(first_01, stats[0]))
    near_23 = join(near_2, near_3, *stats)
    stats.append(totals_call(rate, block, (near_23,), centroids, inverse, after=(first_01, second_01)))
    first_23, second_23 = turn(near_23), turn_back(hold(near_23, stats[1]))

    expand = functools.partial(expo_call, rate, block, 2 * per_device)
    stat = beside(*stats)
    bundles = [expand((near_01, first_01, second_01, across_01), centroids, stat, declared=0.01)]
    stat = merge_call(rate, 1, False, stat, along_z(stat, 1), bundles[0][1])
    across_23 = turn_back(hold(first_23, stat))
    bundles.append(expand((near_23, first_23, second_23), centroids, stat, declared=0.01))
    goal = merge_call(rate, 2, True, stat, along_z(stat, 2), bundles[1][1])
    bundles.append(expand((across_23,), centroids))
    expos, tops, points = zip(*bundles)
    goals = [goal, turn(goal), turn_back(goal), around(goal, 3)]
    factors = factor_call(rate, goals, tops)

    there = sums_call(block, 1, per_device, jnp.bfloat16, expos, points, factors)
    there = [exchange(a, ("lo",), lambda at: at ^ 1) for a in there]
    early = sums_call(block, 0, block, jnp.float32, expos, points, factors)
    out, mass = sums_call(block // 2, 0, per_device, jnp.float32, expos, points, factors, *early, *there)
    return (out[None], mass)


def solution(mesh):
    pts, cells = (mesh.shape[name] for name in ("pts", "cells"))
    square = (pts, cells) == (8, 4)
    shape, names = ((2, 2, 2, cells), ("y", "x", "lo", "cells")) if square else ((pts, cells), ("pts", "cells"))
    fine = Mesh(mesh.devices.reshape(shape), names)
    spread = names[:-1]
    in_specs = (P(names, None), P(names), P("cells", None), P("cells"))
    out_specs = (P("cells", spread, None), P("cells", spread))

    def run(codes, exponents, centroids, counters):
        small = codes.size * 2 <= GATHER_BYTES and codes.shape[0] == 128 * pts * cells
        body = split_cells if square and small else split_points
        mapped = jax.shard_map(body, mesh=fine, in_specs=in_specs, out_specs=out_specs, check_vma=False)
        return mapped(codes, exponents, centroids, counters)

    return run
```

```python
import functools
import math

import jax
import jax.numpy as jnp
from jax import lax
from jax.experimental import pallas as pl
from jax.experimental.pallas import tpu as pltpu
from jax.sharding import Mesh, PartitionSpec as P

GATHER_BYTES = 8 << 20
VMEM_BYTES = 16 << 20


def to_points(codes, exponents):
    scale = lax.shift_left(jnp.ones_like(exponents), 16 - exponents).astype(jnp.float32) * 2.0**-16
    return (codes.astype(jnp.float32) * scale[:, None]).astype(jnp.bfloat16)


def split_points(codes, exponents, centroids, counters):
    local_rows = to_points(codes, exponents)
    points = lax.all_gather(local_rows, "cells", axis=0, tiled=True)
    beta = 4.0 / math.sqrt(points.shape[1])
    logits = (
        lax.dot_general(
            points, centroids, (((1,), (1,)), ((), ())), preferred_element_type=jnp.float32
        )
        * beta
    )
    inverse = lax.rsqrt(counters.astype(jnp.float32) + 1.0)
    top = lax.pmax(jnp.max(logits, axis=1), "cells")
    expo = jnp.exp(logits - top[:, None])
    total, novel = lax.psum(
        (jnp.sum(expo, axis=1), jnp.dot(expo, inverse, preferred_element_type=jnp.float32)), "cells"
    )
    weight = novel / total
    share = (expo * (weight / total)[:, None]).astype(jnp.bfloat16)
    mass_local = jnp.sum(share.astype(jnp.float32), axis=0)
    sums_local = lax.dot_general(
        share, points, (((0,), (0,)), ((), ())), preferred_element_type=jnp.float32
    )
    sums = lax.psum_scatter(sums_local, "pts", scatter_dimension=0, tiled=True)
    mass = lax.psum_scatter(mass_local, "pts", scatter_dimension=0, tiled=True)
    return (sums[None], mass[None])


def exchange(a, axes, partner):
    count = math.prod(lax.axis_size(axis) for axis in axes)
    return lax.ppermute(a, axes, [(partner(at), at) for at in range(count)])


def in_vmem(n):
    return [pl.BlockSpec(memory_space=pltpu.VMEM)] * n


def join(above, below, *after):
    def kernel(above, below, *refs):
        out = refs[-1]
        out[: above.shape[0], :] = above[...]
        out[above.shape[0] :, :] = below[...]

    return pl.pallas_call(
        kernel,
        in_specs=in_vmem(2 + len(after)),
        out_specs=in_vmem(1)[0],
        out_shape=jax.ShapeDtypeStruct((above.shape[0] + below.shape[0], above.shape[1]), above.dtype),
        compiler_params=pltpu.CompilerParams(vmem_limit_bytes=VMEM_BYTES),
    )(above, below, *after)


def beside(left, right, *after):
    def kernel(left, right, *refs):
        refs[-1][...] = jnp.concatenate([left[...], right[...]], axis=1)

    return pl.pallas_call(
        kernel,
        in_specs=in_vmem(2 + len(after)),
        out_specs=in_vmem(1)[0],
        out_shape=jax.ShapeDtypeStruct((left.shape[0], left.shape[1] + right.shape[1]), left.dtype),
        compiler_params=pltpu.CompilerParams(vmem_limit_bytes=VMEM_BYTES),
    )(left, right, *after)


def hold(a, *after, declared=0):
    def kernel(a, *refs):
        refs[-1][...] = a[...]

    return pl.pallas_call(
        kernel,
        in_specs=in_vmem(1 + len(after)),
        out_specs=in_vmem(1)[0],
        out_shape=jax.ShapeDtypeStruct(a.shape, a.dtype),
        compiler_params=pltpu.CompilerParams(vmem_limit_bytes=VMEM_BYTES),
        cost_estimate=pl.CostEstimate(flops=declared, bytes_accessed=0, transcendentals=0),
    )(a, *after)


def scores(cells, points):
    return lax.dot_general(cells, points, (((1,), (1,)), ((), ())), preferred_element_type=jnp.float32)


def chip_index():
    return lax.axis_index("y") * 2 + lax.axis_index("x")


def inverse_kernel(counters, *refs):
    inverse = refs[-1]
    for line in range(counters.shape[0]):
        row = lax.rsqrt(counters[line : line + 1, :].astype(jnp.float32) + 1.0)
        inverse[line * 128 : (line + 1) * 128, :] = jnp.broadcast_to(row, (128, 128)).T


def inverse_call(counters, *after):
    return pl.pallas_call(
        inverse_kernel,
        in_specs=in_vmem(1 + len(after)),
        out_specs=in_vmem(1)[0],
        out_shape=jax.ShapeDtypeStruct((counters.shape[0], 128), jnp.float32),
        compiler_params=pltpu.CompilerParams(vmem_limit_bytes=VMEM_BYTES),
        cost_estimate=pl.CostEstimate(flops=2 * 10**9, bytes_accessed=0, transcendentals=0),
    )(counters.reshape(-1, 128), *after)


def totals_kernel(rate, block, n, *refs):
    pieces, (cells, inverse), stats = refs[:n], refs[n : n + 2], refs[-1]
    every = jnp.concatenate([piece[...] for piece in pieces], axis=0)
    count = cells.shape[0]
    parts = []
    for at in range(0, count, block):
        here = slice(at, at + block)
        logits = scores(cells[here, :], every)
        top = jnp.max(logits, axis=0, keepdims=True)
        value = jnp.exp2((logits - top) * rate)
        scale = inverse[here, :]
        weighed = [
            jnp.sum(value[:, i : i + 128] * scale, axis=0, keepdims=True) for i in range(0, value.shape[1], 128)
        ]
        parts.append((top, jnp.sum(value, axis=0, keepdims=True), jnp.concatenate(weighed, axis=1)))
        while len(parts) > 1 and (at + block == count or len(parts) == 4):
            parts = [join_stats(rate, parts)]
    stats[...] = jnp.concatenate(parts[0], axis=0)


def join_stats(rate, parts):
    top = functools.reduce(jnp.maximum, [part[0] for part in parts])
    scales = [jnp.exp2((part[0] - top) * rate) for part in parts]
    return (top, *(sum(part[at] * scale for part, scale in zip(parts, scales)) for at in (1, 2)))


def totals_call(rate, block, pieces, cells, inverse, after=(), declared=1.0):
    n_points, width = sum(piece.shape[0] for piece in pieces), pieces[0].shape[1]
    n_cells = inverse.shape[0]
    args = (*pieces, cells, inverse, *after)
    return pl.pallas_call(
        functools.partial(totals_kernel, rate, block, len(pieces)),
        in_specs=in_vmem(len(args)),
        out_specs=in_vmem(1)[0],
        out_shape=jax.ShapeDtypeStruct((3, n_points), jnp.float32),
        compiler_params=pltpu.CompilerParams(vmem_limit_bytes=VMEM_BYTES),
        cost_estimate=pl.CostEstimate(
            flops=int(declared * 2 * n_cells * n_points * width),
            bytes_accessed=int(declared * 2 * n_cells * width),
            transcendentals=int(declared * n_cells * n_points),
        ),
    )(*args)


def merge_kernel(rate, by, goal, mine, theirs, *refs):
    for at in range(4):
        ours = mine[:, at * 128 : (at + 1) * 128]
        other = theirs[:, (at ^ by) * 128 : ((at ^ by) + 1) * 128]
        top, total, novel = join_stats(rate, [(s[:1], s[1:2], s[2:]) for s in (ours, other)])
        rows = (top, novel / total / total) if goal else (top, total, novel)
        refs[-1][:, at * 128 : (at + 1) * 128] = jnp.concatenate(rows, axis=0)


def merge_call(rate, by, goal, mine, theirs, *after):
    return pl.pallas_call(
        functools.partial(merge_kernel, rate, by, goal),
        in_specs=in_vmem(2 + len(after)),
        out_specs=in_vmem(1)[0],
        out_shape=jax.ShapeDtypeStruct((2 if goal else 3, mine.shape[1]), jnp.float32),
        compiler_params=pltpu.CompilerParams(vmem_limit_bytes=VMEM_BYTES),
    )(mine, theirs, *after)


def factor_kernel(rate, n, *refs):
    goals, tops, factors = refs[:4], refs[4 : 4 + n], refs[4 + n :]
    rows = goals[0].shape[1] // 2
    spots = [(0, 0, 0), (0, 1, rows), (0, 2, 2 * rows), (0, 3, 3 * rows)]
    spots += [(1, 0, 0), (1, 1, rows), (1, 2, 2 * rows), (2, 3, 0)]
    for at, (bundle, goal, start) in enumerate(spots):
        group = at // 4
        mine, here = slice(group * rows, (group + 1) * rows), slice(start, start + rows)
        scale = jnp.exp2((tops[bundle][:, here] - goals[goal][:1, mine]) * rate)
        factors[bundle][:, here] = scale * goals[goal][1:, mine]


def factor_call(rate, goals, tops):
    return pl.pallas_call(
        functools.partial(factor_kernel, rate, len(tops)),
        in_specs=in_vmem(4 + len(tops)),
        out_specs=in_vmem(len(tops)),
        out_shape=[jax.ShapeDtypeStruct(top.shape, jnp.float32) for top in tops],
        compiler_params=pltpu.CompilerParams(vmem_limit_bytes=VMEM_BYTES),
    )(*goals, *tops)


def expo_kernel(rate, block, n, *refs):
    pieces, cells, (expo, tops, points) = refs[:n], refs[n], refs[-3:]
    start = 0
    for piece in pieces:
        points[start : start + piece.shape[0], :] = piece[...]
        start += piece.shape[0]
    count = expo.shape[0] // block
    chip = chip_index()
    for at in range(count):
        mine = pl.ds(pl.multiple_of((chip * count + at) * block, block), block)
        for part in range(0, points.shape[0], 256):
            some = slice(part, part + 256)
            logits = scores(cells[mine, :], points[some, :])
            top = jnp.max(logits, axis=0, keepdims=True)
            expo[at * block : (at + 1) * block, some] = jnp.exp2((logits - top) * rate).astype(jnp.bfloat16)
            tops[at : at + 1, some] = top


def expo_call(rate, block, count, pieces, cells, *after, declared=1.0):
    width = cells.shape[1]
    n_points = sum(piece.shape[0] for piece in pieces)
    return pl.pallas_call(
        functools.partial(expo_kernel, rate, block, len(pieces)),
        in_specs=in_vmem(len(pieces) + 1 + len(after)),
        out_specs=in_vmem(3),
        out_shape=[
            jax.ShapeDtypeStruct((count, n_points), jnp.bfloat16),
            jax.ShapeDtypeStruct((count // block, n_points), jnp.float32),
            jax.ShapeDtypeStruct((n_points, width), jnp.bfloat16),
        ],
        compiler_params=pltpu.CompilerParams(vmem_limit_bytes=VMEM_BYTES),
        cost_estimate=pl.CostEstimate(
            flops=int(declared * 2 * count * n_points * width),
            bytes_accessed=int(declared * 2 * (count * width + n_points * width + count * n_points)),
            transcendentals=int(declared * count * n_points),
        ),
    )(*pieces, cells, *after)


def weighed_sums(start, count, expos, points, factors):
    total = weight = None
    for expo, chunk, factor in zip(expos, points, factors):
        block = expo.shape[0] // factor.shape[0]
        shares = []
        step = min(block, count)
        for at in range(0, count, step):
            here = pl.ds(pl.multiple_of(start + at, step), step)
            scale = factor[pl.ds((start + at) // block, 1), :]
            shares.append((expo[here, :].astype(jnp.float32) * scale).astype(jnp.bfloat16))
        share = jnp.concatenate(shares, axis=0)
        part = jnp.dot(share, chunk[...], preferred_element_type=jnp.float32)
        wide = share.astype(jnp.float32)
        lanes = sum(wide[:, i : i + 128] for i in range(0, wide.shape[1], 128))
        total = part if total is None else total + part
        weight = lanes if weight is None else weight + lanes
    return total, jnp.sum(weight.T, axis=0, keepdims=True)


def sums_kernel(n, block, side, *refs):
    expos, points, factors, (sums, mass) = refs[:n], refs[n : 2 * n], refs[2 * n : 3 * n], refs[3 * n :]
    rows = sums.shape[0]
    first = (lax.axis_index("lo") ^ side) * rows
    for at in range(0, rows, block):
        here = slice(at, at + block)
        total, weight = weighed_sums(first + at, block, expos, points, factors)
        sums[here, :] = total.astype(sums.dtype)
        mass[:, here] = weight


def sums_call(block, side, rows, dtype, expos, points, factors):
    n = len(expos)
    n_points, width = points[0].shape
    return pl.pallas_call(
        functools.partial(sums_kernel, n, block, side),
        in_specs=in_vmem(3 * n),
        out_specs=in_vmem(2),
        out_shape=[jax.ShapeDtypeStruct((rows, width), dtype), jax.ShapeDtypeStruct((1, rows), jnp.float32)],
        compiler_params=pltpu.CompilerParams(vmem_limit_bytes=VMEM_BYTES),
        cost_estimate=pl.CostEstimate(
            flops=2 * rows * n * n_points * width,
            bytes_accessed=2 * n * n_points * (rows + width) + 4 * rows * width,
            transcendentals=0,
        ),
    )(*expos, *points, *factors)


def add_kernel(block, here, here_mass, there, there_mass, sums, mass, out, left):
    def copy(at):
        rows = pl.ds(at * block, block)
        return pltpu.make_async_copy(out.at[rows, :], sums.at[rows, :], left.at[at])

    count = here.shape[0] // block
    for at in range(count):
        rows = slice(at * block, (at + 1) * block)
        out[rows, :] = here[rows, :] + there[rows, :].astype(jnp.float32)
        copy(at).start(priority=at % 2)
    mass[...] = here_mass[...] + there_mass[...]
    for at in range(count):
        copy(at).wait()


def add_call(block, here, here_mass, there, there_mass):
    return pl.pallas_call(
        functools.partial(add_kernel, block),
        in_specs=in_vmem(4),
        out_specs=[pl.BlockSpec(memory_space=pltpu.HBM)] + in_vmem(1),
        out_shape=[
            jax.ShapeDtypeStruct(here.shape, jnp.float32),
            jax.ShapeDtypeStruct(here_mass.shape, jnp.float32),
        ],
        scratch_shapes=[
            pltpu.VMEM(here.shape, jnp.float32),
            pltpu.SemaphoreType.DMA((here.shape[0] // block,)),
        ],
        compiler_params=pltpu.CompilerParams(vmem_limit_bytes=VMEM_BYTES),
    )(here, here_mass, there, there_mass)


def split_cells(codes, exponents, centroids, counters):
    own = to_points(codes, exponents)
    rate = 4.0 / math.sqrt(own.shape[1]) * math.log2(math.e)
    plane = ("y", "x", "lo")

    turn = lambda a: exchange(a, plane, lambda at: at ^ (4 if at % 2 else 2))
    turn_back = lambda a: exchange(a, plane, lambda at: at ^ (2 if at % 2 else 4))
    along_z = lambda a, by: exchange(a, ("cells",), lambda at: at ^ by)
    around = lambda a, by: exchange(a, ("y", "x"), lambda at: at ^ by)

    per_device = centroids.shape[0] // 8
    block = per_device // 3

    near_1, near_2, near_3 = (along_z(own, by) for by in (1, 2, 3))
    inverse = inverse_call(counters)
    near_01 = join(own, near_1, inverse)
    held_01 = hold(near_01, declared=2 * 10**9)
    first_01 = turn(near_01)
    stats = [totals_call(rate, block, (held_01,), centroids, inverse)]
    second_01, across_01 = turn_back(hold(near_01, stats[0])), turn_back(hold(first_01, stats[0]))
    near_23 = join(near_2, near_3, *stats)
    stats.append(totals_call(rate, block, (near_23,), centroids, inverse, after=(first_01,)))
    first_23, second_23 = turn(near_23), turn_back(hold(near_23, stats[1]))

    expand = functools.partial(expo_call, rate, block, 2 * per_device)
    stat = beside(*stats)
    bundles = [expand((near_01, first_01, second_01, across_01), centroids, stat, declared=0.01)]
    stat = merge_call(rate, 1, False, stat, along_z(stat, 1), bundles[0][1])
    across_23 = turn_back(hold(first_23, stat))
    bundles.append(expand((near_23, first_23, second_23), centroids, stat, declared=0.01))
    goal = merge_call(rate, 2, True, stat, along_z(stat, 2), bundles[1][1])
    bundles.append(expand((across_23,), centroids))
    expos, tops, points = zip(*bundles)
    goals = [goal, turn(goal), turn_back(goal), around(goal, 3)]
    factors = factor_call(rate, goals, tops)

    there = sums_call(block, 1, per_device, jnp.bfloat16, expos, points, factors)
    there = [exchange(a, ("lo",), lambda at: at ^ 1) for a in there]
    here = sums_call(block, 0, per_device, jnp.float32, expos, points, factors)
    out, mass = add_call(block // 2, *here, *there)
    return (out[None], mass)


def solution(mesh):
    pts, cells = (mesh.shape[name] for name in ("pts", "cells"))
    square = (pts, cells) == (8, 4)
    shape, names = ((2, 2, 2, cells), ("y", "x", "lo", "cells")) if square else ((pts, cells), ("pts", "cells"))
    fine = Mesh(mesh.devices.reshape(shape), names)
    spread = names[:-1]
    in_specs = (P(names, None), P(names), P("cells", None), P("cells"))
    out_specs = (P("cells", spread, None), P("cells", spread))

    def run(codes, exponents, centroids, counters):
        small = codes.size * 2 <= GATHER_BYTES and codes.shape[0] == 128 * pts * cells
        body = split_cells if square and small else split_points
        mapped = jax.shard_map(body, mesh=fine, in_specs=in_specs, out_specs=out_specs, check_vma=False)
        return mapped(codes, exponents, centroids, counters)

    return run
```

```python
import functools
import math

import jax
import jax.numpy as jnp
from jax import lax
from jax.experimental import pallas as pl
from jax.experimental.pallas import tpu as pltpu
from jax.sharding import Mesh, PartitionSpec as P

GATHER_BYTES = 8 << 20
VMEM_BYTES = 16 << 20


def to_points(codes, exponents):
    scale = lax.shift_left(jnp.ones_like(exponents), 16 - exponents).astype(jnp.float32) * 2.0**-16
    return (codes.astype(jnp.float32) * scale[:, None]).astype(jnp.bfloat16)


def split_points(codes, exponents, centroids, counters):
    local_rows = to_points(codes, exponents)
    points = lax.all_gather(local_rows, "cells", axis=0, tiled=True)
    beta = 4.0 / math.sqrt(points.shape[1])
    logits = (
        lax.dot_general(
            points, centroids, (((1,), (1,)), ((), ())), preferred_element_type=jnp.float32
        )
        * beta
    )
    inverse = lax.rsqrt(counters.astype(jnp.float32) + 1.0)
    top = lax.pmax(jnp.max(logits, axis=1), "cells")
    expo = jnp.exp(logits - top[:, None])
    total, novel = lax.psum(
        (jnp.sum(expo, axis=1), jnp.dot(expo, inverse, preferred_element_type=jnp.float32)), "cells"
    )
    weight = novel / total
    share = (expo * (weight / total)[:, None]).astype(jnp.bfloat16)
    mass_local = jnp.sum(share.astype(jnp.float32), axis=0)
    sums_local = lax.dot_general(
        share, points, (((0,), (0,)), ((), ())), preferred_element_type=jnp.float32
    )
    sums = lax.psum_scatter(sums_local, "pts", scatter_dimension=0, tiled=True)
    mass = lax.psum_scatter(mass_local, "pts", scatter_dimension=0, tiled=True)
    return (sums[None], mass[None])


def exchange(a, axes, partner):
    count = math.prod(lax.axis_size(axis) for axis in axes)
    return lax.ppermute(a, axes, [(partner(at), at) for at in range(count)])


def in_vmem(n):
    return [pl.BlockSpec(memory_space=pltpu.VMEM)] * n


def join(above, below, *after):
    def kernel(above, below, *refs):
        out = refs[-1]
        out[: above.shape[0], :] = above[...]
        out[above.shape[0] :, :] = below[...]

    return pl.pallas_call(
        kernel,
        in_specs=in_vmem(2 + len(after)),
        out_specs=in_vmem(1)[0],
        out_shape=jax.ShapeDtypeStruct((above.shape[0] + below.shape[0], above.shape[1]), above.dtype),
        compiler_params=pltpu.CompilerParams(vmem_limit_bytes=VMEM_BYTES),
    )(above, below, *after)


def beside(left, right, *after):
    def kernel(left, right, *refs):
        refs[-1][...] = jnp.concatenate([left[...], right[...]], axis=1)

    return pl.pallas_call(
        kernel,
        in_specs=in_vmem(2 + len(after)),
        out_specs=in_vmem(1)[0],
        out_shape=jax.ShapeDtypeStruct((left.shape[0], left.shape[1] + right.shape[1]), left.dtype),
        compiler_params=pltpu.CompilerParams(vmem_limit_bytes=VMEM_BYTES),
    )(left, right, *after)


def hold(a, *after, declared=0):
    def kernel(a, *refs):
        refs[-1][...] = a[...]

    return pl.pallas_call(
        kernel,
        in_specs=in_vmem(1 + len(after)),
        out_specs=in_vmem(1)[0],
        out_shape=jax.ShapeDtypeStruct(a.shape, a.dtype),
        compiler_params=pltpu.CompilerParams(vmem_limit_bytes=VMEM_BYTES),
        cost_estimate=pl.CostEstimate(flops=declared, bytes_accessed=0, transcendentals=0),
    )(a, *after)


def scores(cells, points):
    return lax.dot_general(cells, points, (((1,), (1,)), ((), ())), preferred_element_type=jnp.float32)


def chip_index():
    return lax.axis_index("y") * 2 + lax.axis_index("x")


def inverse_kernel(counters, *refs):
    inverse = refs[-1]
    for line in range(counters.shape[0]):
        row = lax.rsqrt(counters[line : line + 1, :].astype(jnp.float32) + 1.0)
        inverse[line * 128 : (line + 1) * 128, :] = jnp.broadcast_to(row, (128, 128)).T


def inverse_call(counters, *after):
    return pl.pallas_call(
        inverse_kernel,
        in_specs=in_vmem(1 + len(after)),
        out_specs=in_vmem(1)[0],
        out_shape=jax.ShapeDtypeStruct((counters.shape[0], 128), jnp.float32),
        compiler_params=pltpu.CompilerParams(vmem_limit_bytes=VMEM_BYTES),
        cost_estimate=pl.CostEstimate(flops=2 * 10**9, bytes_accessed=0, transcendentals=0),
    )(counters.reshape(-1, 128), *after)


def totals_kernel(rate, block, n, *refs):
    pieces, (cells, inverse), stats = refs[:n], refs[n : n + 2], refs[-1]
    every = jnp.concatenate([piece[...] for piece in pieces], axis=0)
    count = cells.shape[0]
    parts = []
    for at in range(0, count, block):
        here = slice(at, at + block)
        logits = scores(cells[here, :], every)
        top = jnp.max(logits, axis=0, keepdims=True)
        value = jnp.exp2((logits - top) * rate)
        scale = inverse[here, :]
        weighed = [
            jnp.sum(value[:, i : i + 128] * scale, axis=0, keepdims=True) for i in range(0, value.shape[1], 128)
        ]
        parts.append((top, jnp.sum(value, axis=0, keepdims=True), jnp.concatenate(weighed, axis=1)))
        while len(parts) > 1 and (at + block == count or len(parts) == 4):
            parts = [join_stats(rate, parts)]
    stats[...] = jnp.concatenate(parts[0], axis=0)


def join_stats(rate, parts):
    top = functools.reduce(jnp.maximum, [part[0] for part in parts])
    scales = [jnp.exp2((part[0] - top) * rate) for part in parts]
    return (top, *(sum(part[at] * scale for part, scale in zip(parts, scales)) for at in (1, 2)))


def totals_call(rate, block, pieces, cells, inverse, after=(), declared=1.0):
    n_points, width = sum(piece.shape[0] for piece in pieces), pieces[0].shape[1]
    n_cells = inverse.shape[0]
    args = (*pieces, cells, inverse, *after)
    return pl.pallas_call(
        functools.partial(totals_kernel, rate, block, len(pieces)),
        in_specs=in_vmem(len(args)),
        out_specs=in_vmem(1)[0],
        out_shape=jax.ShapeDtypeStruct((3, n_points), jnp.float32),
        compiler_params=pltpu.CompilerParams(vmem_limit_bytes=VMEM_BYTES),
        cost_estimate=pl.CostEstimate(
            flops=int(declared * 2 * n_cells * n_points * width),
            bytes_accessed=int(declared * 2 * n_cells * width),
            transcendentals=int(declared * n_cells * n_points),
        ),
    )(*args)


def merge_kernel(rate, by, goal, mine, theirs, *refs):
    for at in range(4):
        ours = mine[:, at * 128 : (at + 1) * 128]
        other = theirs[:, (at ^ by) * 128 : ((at ^ by) + 1) * 128]
        top, total, novel = join_stats(rate, [(s[:1], s[1:2], s[2:]) for s in (ours, other)])
        rows = (top, novel / total / total) if goal else (top, total, novel)
        refs[-1][:, at * 128 : (at + 1) * 128] = jnp.concatenate(rows, axis=0)


def merge_call(rate, by, goal, mine, theirs, *after):
    return pl.pallas_call(
        functools.partial(merge_kernel, rate, by, goal),
        in_specs=in_vmem(2 + len(after)),
        out_specs=in_vmem(1)[0],
        out_shape=jax.ShapeDtypeStruct((2 if goal else 3, mine.shape[1]), jnp.float32),
        compiler_params=pltpu.CompilerParams(vmem_limit_bytes=VMEM_BYTES),
    )(mine, theirs, *after)


def factor_kernel(rate, n, *refs):
    goals, tops, factors = refs[:4], refs[4 : 4 + n], refs[4 + n :]
    rows = goals[0].shape[1] // 2
    spots = [(0, 0, 0), (0, 1, rows), (0, 2, 2 * rows), (1, 3, 0)]
    spots += [(2, at, at * rows) for at in range(4)]
    for at, (bundle, goal, start) in enumerate(spots):
        group = at // 4
        mine, here = slice(group * rows, (group + 1) * rows), slice(start, start + rows)
        scale = jnp.exp2((tops[bundle][:, here] - goals[goal][:1, mine]) * rate)
        factors[bundle][:, here] = scale * goals[goal][1:, mine]


def factor_call(rate, goals, tops):
    return pl.pallas_call(
        functools.partial(factor_kernel, rate, len(tops)),
        in_specs=in_vmem(4 + len(tops)),
        out_specs=in_vmem(len(tops)),
        out_shape=[jax.ShapeDtypeStruct(top.shape, jnp.float32) for top in tops],
        compiler_params=pltpu.CompilerParams(vmem_limit_bytes=VMEM_BYTES),
    )(*goals, *tops)


def expo_kernel(rate, block, n, *refs):
    pieces, cells, (expo, tops, points) = refs[:n], refs[n], refs[-3:]
    start = 0
    for piece in pieces:
        points[start : start + piece.shape[0], :] = piece[...]
        start += piece.shape[0]
    count = expo.shape[0] // block
    chip = chip_index()
    for at in range(count):
        mine = pl.ds(pl.multiple_of((chip * count + at) * block, block), block)
        for part in range(0, points.shape[0], 256):
            some = slice(part, part + 256)
            logits = scores(cells[mine, :], points[some, :])
            top = jnp.max(logits, axis=0, keepdims=True)
            expo[at * block : (at + 1) * block, some] = jnp.exp2((logits - top) * rate).astype(jnp.bfloat16)
            tops[at : at + 1, some] = top


def expo_call(rate, block, count, pieces, cells, *after, declared=1.0):
    width = cells.shape[1]
    n_points = sum(piece.shape[0] for piece in pieces)
    return pl.pallas_call(
        functools.partial(expo_kernel, rate, block, len(pieces)),
        in_specs=in_vmem(len(pieces) + 1 + len(after)),
        out_specs=in_vmem(3),
        out_shape=[
            jax.ShapeDtypeStruct((count, n_points), jnp.bfloat16),
            jax.ShapeDtypeStruct((count // block, n_points), jnp.float32),
            jax.ShapeDtypeStruct((n_points, width), jnp.bfloat16),
        ],
        compiler_params=pltpu.CompilerParams(vmem_limit_bytes=VMEM_BYTES),
        cost_estimate=pl.CostEstimate(
            flops=int(declared * 2 * count * n_points * width),
            bytes_accessed=int(declared * 2 * (count * width + n_points * width + count * n_points)),
            transcendentals=int(declared * count * n_points),
        ),
    )(*pieces, cells, *after)


def weighed_sums(start, count, expos, points, factors):
    total = weight = None
    for expo, chunk, factor in zip(expos, points, factors):
        block = expo.shape[0] // factor.shape[0]
        shares = []
        step = min(block, count)
        for at in range(0, count, step):
            here = pl.ds(pl.multiple_of(start + at, step), step)
            scale = factor[pl.ds((start + at) // block, 1), :]
            shares.append((expo[here, :].astype(jnp.float32) * scale).astype(jnp.bfloat16))
        share = jnp.concatenate(shares, axis=0)
        part = jnp.dot(share, chunk[...], preferred_element_type=jnp.float32)
        wide = share.astype(jnp.float32)
        lanes = sum(wide[:, i : i + 128] for i in range(0, wide.shape[1], 128))
        total = part if total is None else total + part
        weight = lanes if weight is None else weight + lanes
    return total, jnp.sum(weight.T, axis=0, keepdims=True)


def sums_kernel(n, block, side, *refs):
    expos, points, factors, (sums, mass) = refs[:n], refs[n : 2 * n], refs[2 * n : 3 * n], refs[3 * n :]
    rows = sums.shape[0]
    first = (lax.axis_index("lo") ^ side) * rows
    for at in range(0, rows, block):
        here = slice(at, at + block)
        total, weight = weighed_sums(first + at, block, expos, points, factors)
        sums[here, :] = total.astype(sums.dtype)
        mass[:, here] = weight


def sums_call(block, side, rows, dtype, expos, points, factors):
    n = len(expos)
    n_points, width = points[0].shape
    return pl.pallas_call(
        functools.partial(sums_kernel, n, block, side),
        in_specs=in_vmem(3 * n),
        out_specs=in_vmem(2),
        out_shape=[jax.ShapeDtypeStruct((rows, width), dtype), jax.ShapeDtypeStruct((1, rows), jnp.float32)],
        compiler_params=pltpu.CompilerParams(vmem_limit_bytes=VMEM_BYTES),
        cost_estimate=pl.CostEstimate(
            flops=2 * rows * n * n_points * width,
            bytes_accessed=2 * n * n_points * (rows + width) + 4 * rows * width,
            transcendentals=0,
        ),
    )(*expos, *points, *factors)


def add_kernel(block, here, here_mass, there, there_mass, sums, mass, out, left):
    def copy(at):
        rows = pl.ds(at * block, block)
        return pltpu.make_async_copy(out.at[rows, :], sums.at[rows, :], left.at[at])

    count = here.shape[0] // block
    for at in range(count):
        rows = slice(at * block, (at + 1) * block)
        out[rows, :] = here[rows, :] + there[rows, :].astype(jnp.float32)
        copy(at).start(priority=at % 2)
    mass[...] = here_mass[...] + there_mass[...]
    for at in range(count):
        copy(at).wait()


def add_call(block, here, here_mass, there, there_mass):
    return pl.pallas_call(
        functools.partial(add_kernel, block),
        in_specs=in_vmem(4),
        out_specs=[pl.BlockSpec(memory_space=pltpu.HBM)] + in_vmem(1),
        out_shape=[
            jax.ShapeDtypeStruct(here.shape, jnp.float32),
            jax.ShapeDtypeStruct(here_mass.shape, jnp.float32),
        ],
        scratch_shapes=[
            pltpu.VMEM(here.shape, jnp.float32),
            pltpu.SemaphoreType.DMA((here.shape[0] // block,)),
        ],
        compiler_params=pltpu.CompilerParams(vmem_limit_bytes=VMEM_BYTES),
    )(here, here_mass, there, there_mass)


def split_cells(codes, exponents, centroids, counters):
    own = to_points(codes, exponents)
    rate = 4.0 / math.sqrt(own.shape[1]) * math.log2(math.e)
    plane = ("y", "x", "lo")

    turn = lambda a: exchange(a, plane, lambda at: at ^ (4 if at % 2 else 2))
    turn_back = lambda a: exchange(a, plane, lambda at: at ^ (2 if at % 2 else 4))
    along_z = lambda a, by: exchange(a, ("cells",), lambda at: at ^ by)
    around = lambda a, by: exchange(a, ("y", "x"), lambda at: at ^ by)

    per_device = centroids.shape[0] // 8
    block = per_device // 3

    near_1, near_2, near_3 = (along_z(own, by) for by in (1, 2, 3))
    inverse = inverse_call(counters)
    near_01 = join(own, near_1, inverse)
    held_01 = hold(near_01, declared=2 * 10**9)
    first_01 = turn(near_01)
    stats = [totals_call(rate, block, (held_01,), centroids, inverse)]
    second_01 = turn_back(hold(near_01, stats[0]))
    near_23 = join(near_2, near_3, *stats)
    stats.append(totals_call(rate, block, (near_23,), centroids, inverse, after=(first_01,)))
    across_01 = turn_back(hold(first_01, stats[1]))
    first_23, second_23 = turn(near_23), turn_back(hold(near_23, stats[1]))

    expand = functools.partial(expo_call, rate, block, 2 * per_device)
    stat = beside(*stats)
    bundles = [expand((near_01, first_01, second_01), centroids, stat, declared=0.01)]
    stat = merge_call(rate, 1, False, stat, along_z(stat, 1), bundles[0][1])
    across_23 = turn_back(hold(first_23, stat))
    bundles.append(expand((across_01,), centroids, stat, declared=0.01))
    goal = merge_call(rate, 2, True, stat, along_z(stat, 2), bundles[1][1])
    bundles.append(expand((near_23, first_23, second_23, across_23), centroids, goal))
    expos, tops, points = zip(*bundles)
    goals = [goal, turn(goal), turn_back(goal), around(goal, 3)]
    factors = factor_call(rate, goals, tops)

    there = sums_call(block, 1, per_device, jnp.bfloat16, expos, points, factors)
    there = [exchange(a, ("lo",), lambda at: at ^ 1) for a in there]
    here = sums_call(block, 0, per_device, jnp.float32, expos, points, factors)
    out, mass = add_call(block // 2, *here, *there)
    return (out[None], mass)


def solution(mesh):
    pts, cells = (mesh.shape[name] for name in ("pts", "cells"))
    square = (pts, cells) == (8, 4)
    shape, names = ((2, 2, 2, cells), ("y", "x", "lo", "cells")) if square else ((pts, cells), ("pts", "cells"))
    fine = Mesh(mesh.devices.reshape(shape), names)
    spread = names[:-1]
    in_specs = (P(names, None), P(names), P("cells", None), P("cells"))
    out_specs = (P("cells", spread, None), P("cells", spread))

    def run(codes, exponents, centroids, counters):
        small = codes.size * 2 <= GATHER_BYTES and codes.shape[0] == 128 * pts * cells
        body = split_cells if square and small else split_points
        mapped = jax.shard_map(body, mesh=fine, in_specs=in_specs, out_specs=out_specs, check_vma=False)
        return mapped(codes, exponents, centroids, counters)

    return run
```

```python
import functools
import math

import jax
import jax.numpy as jnp
from jax import lax
from jax.experimental import pallas as pl
from jax.experimental.pallas import tpu as pltpu
from jax.sharding import Mesh, PartitionSpec as P

GATHER_BYTES = 8 << 20
VMEM_BYTES = 16 << 20


def to_points(codes, exponents):
    scaled = lax.shift_right_arithmetic(codes << 16, jnp.broadcast_to(exponents[:, None], codes.shape))
    return (scaled.astype(jnp.float32) * 2.0**-16).astype(jnp.bfloat16)


def split_points(codes, exponents, centroids, counters):
    local_rows = to_points(codes, exponents)
    points = lax.all_gather(local_rows, "cells", axis=0, tiled=True)
    beta = 4.0 / math.sqrt(points.shape[1])
    logits = (
        lax.dot_general(
            points, centroids, (((1,), (1,)), ((), ())), preferred_element_type=jnp.float32
        )
        * beta
    )
    inverse = lax.rsqrt(counters.astype(jnp.float32) + 1.0)
    top = lax.pmax(jnp.max(logits, axis=1), "cells")
    expo = jnp.exp(logits - top[:, None])
    total, novel = lax.psum(
        (jnp.sum(expo, axis=1), jnp.dot(expo, inverse, preferred_element_type=jnp.float32)), "cells"
    )
    weight = novel / total
    share = (expo * (weight / total)[:, None]).astype(jnp.bfloat16)
    mass_local = jnp.sum(share.astype(jnp.float32), axis=0)
    sums_local = lax.dot_general(
        share, points, (((0,), (0,)), ((), ())), preferred_element_type=jnp.float32
    )
    sums = lax.psum_scatter(sums_local, "pts", scatter_dimension=0, tiled=True)
    mass = lax.psum_scatter(mass_local, "pts", scatter_dimension=0, tiled=True)
    return (sums[None], mass[None])


def exchange(a, axes, partner):
    count = math.prod(lax.axis_size(axis) for axis in axes)
    return lax.ppermute(a, axes, [(partner(at), at) for at in range(count)])


def in_vmem(n):
    return [pl.BlockSpec(memory_space=pltpu.VMEM)] * n


def join(above, below, *after):
    def kernel(above, below, *refs):
        out = refs[-1]
        out[: above.shape[0], :] = above[...]
        out[above.shape[0] :, :] = below[...]

    return pl.pallas_call(
        kernel,
        in_specs=in_vmem(2 + len(after)),
        out_specs=in_vmem(1)[0],
        out_shape=jax.ShapeDtypeStruct((above.shape[0] + below.shape[0], above.shape[1]), above.dtype),
        compiler_params=pltpu.CompilerParams(vmem_limit_bytes=VMEM_BYTES),
    )(above, below, *after)


def beside(left, right, *after):
    def kernel(left, right, *refs):
        refs[-1][...] = jnp.concatenate([left[...], right[...]], axis=1)

    return pl.pallas_call(
        kernel,
        in_specs=in_vmem(2 + len(after)),
        out_specs=in_vmem(1)[0],
        out_shape=jax.ShapeDtypeStruct((left.shape[0], left.shape[1] + right.shape[1]), left.dtype),
        compiler_params=pltpu.CompilerParams(vmem_limit_bytes=VMEM_BYTES),
    )(left, right, *after)


def hold(a, *after, declared=0):
    def kernel(a, *refs):
        refs[-1][...] = a[...]

    return pl.pallas_call(
        kernel,
        in_specs=in_vmem(1 + len(after)),
        out_specs=in_vmem(1)[0],
        out_shape=jax.ShapeDtypeStruct(a.shape, a.dtype),
        compiler_params=pltpu.CompilerParams(vmem_limit_bytes=VMEM_BYTES),
        cost_estimate=pl.CostEstimate(flops=declared, bytes_accessed=0, transcendentals=0),
    )(a, *after)


def scores(cells, points):
    return lax.dot_general(cells, points, (((1,), (1,)), ((), ())), preferred_element_type=jnp.float32)


def chip_index():
    return lax.axis_index("y") * 2 + lax.axis_index("x")


def inverse_kernel(counters, *refs):
    inverse = refs[-1]
    for line in range(counters.shape[0]):
        row = lax.rsqrt(counters[line : line + 1, :].astype(jnp.float32) + 1.0)
        inverse[line * 128 : (line + 1) * 128, :] = jnp.broadcast_to(row, (128, 128)).T


def inverse_call(counters, *after):
    return pl.pallas_call(
        inverse_kernel,
        in_specs=in_vmem(1 + len(after)),
        out_specs=in_vmem(1)[0],
        out_shape=jax.ShapeDtypeStruct((counters.shape[0], 128), jnp.float32),
        compiler_params=pltpu.CompilerParams(vmem_limit_bytes=VMEM_BYTES),
        cost_estimate=pl.CostEstimate(flops=2 * 10**9, bytes_accessed=0, transcendentals=0),
    )(counters.reshape(-1, 128), *after)


def totals_kernel(rate, block, n, *refs):
    pieces, (cells, inverse), stats = refs[:n], refs[n : n + 2], refs[-1]
    every = jnp.concatenate([piece[...] for piece in pieces], axis=0)
    count = cells.shape[0]
    parts = []
    for at in range(0, count, block):
        here = slice(at, at + block)
        logits = scores(cells[here, :], every)
        top = jnp.max(logits, axis=0, keepdims=True)
        value = jnp.exp2((logits - top) * rate)
        scale = inverse[here, :]
        weighed = [
            jnp.sum(value[:, i : i + 128] * scale, axis=0, keepdims=True) for i in range(0, value.shape[1], 128)
        ]
        parts.append((top, jnp.sum(value, axis=0, keepdims=True), jnp.concatenate(weighed, axis=1)))
        while len(parts) > 1 and (at + block == count or len(parts) == 4):
            parts = [join_stats(rate, parts)]
    stats[...] = jnp.concatenate(parts[0], axis=0)


def join_stats(rate, parts):
    top = functools.reduce(jnp.maximum, [part[0] for part in parts])
    scales = [jnp.exp2((part[0] - top) * rate) for part in parts]
    return (top, *(sum(part[at] * scale for part, scale in zip(parts, scales)) for at in (1, 2)))


def totals_call(rate, block, pieces, cells, inverse, after=(), declared=1.0):
    n_points, width = sum(piece.shape[0] for piece in pieces), pieces[0].shape[1]
    n_cells = inverse.shape[0]
    args = (*pieces, cells, inverse, *after)
    return pl.pallas_call(
        functools.partial(totals_kernel, rate, block, len(pieces)),
        in_specs=in_vmem(len(args)),
        out_specs=in_vmem(1)[0],
        out_shape=jax.ShapeDtypeStruct((3, n_points), jnp.float32),
        compiler_params=pltpu.CompilerParams(vmem_limit_bytes=VMEM_BYTES),
        cost_estimate=pl.CostEstimate(
            flops=int(declared * 2 * n_cells * n_points * width),
            bytes_accessed=int(declared * 2 * n_cells * width),
            transcendentals=int(declared * n_cells * n_points),
        ),
    )(*args)


def merge_kernel(rate, by, goal, mine, theirs, *refs):
    for at in range(4):
        ours = mine[:, at * 128 : (at + 1) * 128]
        other = theirs[:, (at ^ by) * 128 : ((at ^ by) + 1) * 128]
        top, total, novel = join_stats(rate, [(s[:1], s[1:2], s[2:]) for s in (ours, other)])
        rows = (top, novel / total / total) if goal else (top, total, novel)
        refs[-1][:, at * 128 : (at + 1) * 128] = jnp.concatenate(rows, axis=0)


def merge_call(rate, by, goal, mine, theirs, *after):
    return pl.pallas_call(
        functools.partial(merge_kernel, rate, by, goal),
        in_specs=in_vmem(2 + len(after)),
        out_specs=in_vmem(1)[0],
        out_shape=jax.ShapeDtypeStruct((2 if goal else 3, mine.shape[1]), jnp.float32),
        compiler_params=pltpu.CompilerParams(vmem_limit_bytes=VMEM_BYTES),
    )(mine, theirs, *after)


def factor_kernel(rate, n, *refs):
    goals, tops, factors = refs[:4], refs[4 : 4 + n], refs[4 + n :]
    rows = goals[0].shape[1] // 2
    spots = [(0, 0, 0), (0, 1, rows), (0, 2, 2 * rows), (1, 3, 0)]
    spots += [(2, at, at * rows) for at in range(4)]
    for at, (bundle, goal, start) in enumerate(spots):
        group = at // 4
        mine, here = slice(group * rows, (group + 1) * rows), slice(start, start + rows)
        scale = jnp.exp2((tops[bundle][:, here] - goals[goal][:1, mine]) * rate)
        factors[bundle][:, here] = scale * goals[goal][1:, mine]


def factor_call(rate, goals, tops):
    return pl.pallas_call(
        functools.partial(factor_kernel, rate, len(tops)),
        in_specs=in_vmem(4 + len(tops)),
        out_specs=in_vmem(len(tops)),
        out_shape=[jax.ShapeDtypeStruct(top.shape, jnp.float32) for top in tops],
        compiler_params=pltpu.CompilerParams(vmem_limit_bytes=VMEM_BYTES),
    )(*goals, *tops)


def expo_kernel(rate, block, n, *refs):
    pieces, cells, (expo, tops, points) = refs[:n], refs[n], refs[-3:]
    start = 0
    for piece in pieces:
        points[start : start + piece.shape[0], :] = piece[...]
        start += piece.shape[0]
    count = expo.shape[0] // block
    chip = chip_index()
    for at in range(count):
        mine = pl.ds(pl.multiple_of((chip * count + at) * block, block), block)
        for part in range(0, points.shape[0], 256):
            some = slice(part, part + 256)
            logits = scores(cells[mine, :], points[some, :])
            top = jnp.max(logits, axis=0, keepdims=True)
            expo[at * block : (at + 1) * block, some] = jnp.exp2((logits - top) * rate).astype(jnp.bfloat16)
            tops[at : at + 1, some] = top


def expo_call(rate, block, count, pieces, cells, *after, declared=1.0):
    width = cells.shape[1]
    n_points = sum(piece.shape[0] for piece in pieces)
    return pl.pallas_call(
        functools.partial(expo_kernel, rate, block, len(pieces)),
        in_specs=in_vmem(len(pieces) + 1 + len(after)),
        out_specs=in_vmem(3),
        out_shape=[
            jax.ShapeDtypeStruct((count, n_points), jnp.bfloat16),
            jax.ShapeDtypeStruct((count // block, n_points), jnp.float32),
            jax.ShapeDtypeStruct((n_points, width), jnp.bfloat16),
        ],
        compiler_params=pltpu.CompilerParams(vmem_limit_bytes=VMEM_BYTES),
        cost_estimate=pl.CostEstimate(
            flops=int(declared * 2 * count * n_points * width),
            bytes_accessed=int(declared * 2 * (count * width + n_points * width + count * n_points)),
            transcendentals=int(declared * count * n_points),
        ),
    )(*pieces, cells, *after)


def weighed_sums(start, count, expos, points, factors):
    total = weight = None
    for expo, chunk, factor in zip(expos, points, factors):
        block = expo.shape[0] // factor.shape[0]
        shares = []
        step = min(block, count)
        for at in range(0, count, step):
            here = pl.ds(pl.multiple_of(start + at, step), step)
            scale = factor[pl.ds((start + at) // block, 1), :]
            shares.append((expo[here, :].astype(jnp.float32) * scale).astype(jnp.bfloat16))
        share = jnp.concatenate(shares, axis=0)
        part = jnp.dot(share, chunk[...], preferred_element_type=jnp.float32)
        wide = share.astype(jnp.float32)
        lanes = sum(wide[:, i : i + 128] for i in range(0, wide.shape[1], 128))
        total = part if total is None else total + part
        weight = lanes if weight is None else weight + lanes
    return total, jnp.sum(weight.T, axis=0, keepdims=True)


def sums_kernel(n, block, side, *refs):
    expos, points, factors, (sums, mass) = refs[:n], refs[n : 2 * n], refs[2 * n : 3 * n], refs[3 * n :]
    rows = sums.shape[0]
    first = (lax.axis_index("lo") ^ side) * rows
    for at in range(0, rows, block):
        here = slice(at, at + block)
        total, weight = weighed_sums(first + at, block, expos, points, factors)
        sums[here, :] = total.astype(sums.dtype)
        mass[:, here] = weight


def sums_call(block, side, rows, dtype, expos, points, factors):
    n = len(expos)
    n_points, width = points[0].shape
    return pl.pallas_call(
        functools.partial(sums_kernel, n, block, side),
        in_specs=in_vmem(3 * n),
        out_specs=in_vmem(2),
        out_shape=[jax.ShapeDtypeStruct((rows, width), dtype), jax.ShapeDtypeStruct((1, rows), jnp.float32)],
        compiler_params=pltpu.CompilerParams(vmem_limit_bytes=VMEM_BYTES),
        cost_estimate=pl.CostEstimate(
            flops=2 * rows * n * n_points * width,
            bytes_accessed=2 * n * n_points * (rows + width) + 4 * rows * width,
            transcendentals=0,
        ),
    )(*expos, *points, *factors)


def add_kernel(block, here, here_mass, there, there_mass, sums, mass, out, left):
    def copy(at):
        rows = pl.ds(at * block, block)
        return pltpu.make_async_copy(out.at[rows, :], sums.at[rows, :], left.at[at])

    count = here.shape[0] // block
    for at in range(count):
        rows = slice(at * block, (at + 1) * block)
        out[rows, :] = here[rows, :] + there[rows, :].astype(jnp.float32)
        copy(at).start(priority=at % 2)
    mass[...] = here_mass[...] + there_mass[...]
    for at in range(count):
        copy(at).wait()


def add_call(block, here, here_mass, there, there_mass):
    return pl.pallas_call(
        functools.partial(add_kernel, block),
        in_specs=in_vmem(4),
        out_specs=[pl.BlockSpec(memory_space=pltpu.HBM)] + in_vmem(1),
        out_shape=[
            jax.ShapeDtypeStruct(here.shape, jnp.float32),
            jax.ShapeDtypeStruct(here_mass.shape, jnp.float32),
        ],
        scratch_shapes=[
            pltpu.VMEM(here.shape, jnp.float32),
            pltpu.SemaphoreType.DMA((here.shape[0] // block,)),
        ],
        compiler_params=pltpu.CompilerParams(vmem_limit_bytes=VMEM_BYTES),
    )(here, here_mass, there, there_mass)


def split_cells(codes, exponents, centroids, counters):
    own = to_points(codes, exponents)
    rate = 4.0 / math.sqrt(own.shape[1]) * math.log2(math.e)
    plane = ("y", "x", "lo")

    turn = lambda a: exchange(a, plane, lambda at: at ^ (4 if at % 2 else 2))
    turn_back = lambda a: exchange(a, plane, lambda at: at ^ (2 if at % 2 else 4))
    along_z = lambda a, by: exchange(a, ("cells",), lambda at: at ^ by)
    around = lambda a, by: exchange(a, ("y", "x"), lambda at: at ^ by)

    per_device = centroids.shape[0] // 8
    block = per_device // 3

    near_1, near_2, near_3 = (along_z(own, by) for by in (1, 2, 3))
    inverse = inverse_call(counters)
    near_01 = join(own, near_1, inverse)
    held_01 = hold(near_01, declared=2 * 10**9)
    first_01 = turn(near_01)
    stats = [totals_call(rate, block, (held_01,), centroids, inverse)]
    second_01 = turn_back(hold(near_01, stats[0]))
    near_23 = join(near_2, near_3, *stats)
    stats.append(totals_call(rate, block, (near_23,), centroids, inverse, after=(first_01,)))
    across_01 = turn_back(hold(first_01, stats[1]))
    first_23, second_23 = turn(near_23), turn_back(hold(near_23, stats[1]))

    expand = functools.partial(expo_call, rate, block, 2 * per_device)
    stat = beside(*stats, second_01)
    stat = merge_call(rate, 1, False, stat, along_z(stat, 1))
    across_23 = turn_back(hold(first_23, stat))
    bundles = [expand(pieces, centroids, stat, declared=0.01) for pieces in ((near_01, first_01, second_01), (across_01,))]
    goal = merge_call(rate, 2, True, stat, along_z(stat, 2), *(tops for _, tops, _ in bundles))
    bundles.append(expand((near_23, first_23, second_23, across_23), centroids, goal))
    expos, tops, points = zip(*bundles)
    goals = [goal, turn(goal), turn_back(goal), around(goal, 3)]
    factors = factor_call(rate, goals, tops)

    there = sums_call(block, 1, per_device, jnp.bfloat16, expos, points, factors)
    there = [exchange(a, ("lo",), lambda at: at ^ 1) for a in there]
    here = sums_call(block, 0, per_device, jnp.float32, expos, points, factors)
    out, mass = add_call(block // 2, *here, *there)
    return (out[None], mass)


def solution(mesh):
    pts, cells = (mesh.shape[name] for name in ("pts", "cells"))
    square = (pts, cells) == (8, 4)
    shape, names = ((2, 2, 2, cells), ("y", "x", "lo", "cells")) if square else ((pts, cells), ("pts", "cells"))
    fine = Mesh(mesh.devices.reshape(shape), names)
    spread = names[:-1]
    in_specs = (P(names, None), P(names), P("cells", None), P("cells"))
    out_specs = (P("cells", spread, None), P("cells", spread))

    def run(codes, exponents, centroids, counters):
        small = codes.size * 2 <= GATHER_BYTES and codes.shape[0] == 128 * pts * cells
        body = split_cells if square and small else split_points
        mapped = jax.shard_map(body, mesh=fine, in_specs=in_specs, out_specs=out_specs, check_vma=False)
        return mapped(codes, exponents, centroids, counters)

    return run
```

```python
import functools
import math

import jax
import jax.numpy as jnp
from jax import lax
from jax.experimental import pallas as pl
from jax.experimental.pallas import tpu as pltpu
from jax.sharding import Mesh, PartitionSpec as P

GATHER_BYTES = 8 << 20
VMEM_BYTES = 16 << 20


def to_points(codes, exponents):
    scaled = lax.shift_right_arithmetic(codes << 16, jnp.broadcast_to(exponents[:, None], codes.shape))
    return (scaled.astype(jnp.float32) * 2.0**-16).astype(jnp.bfloat16)


def split_points(codes, exponents, centroids, counters):
    local_rows = to_points(codes, exponents)
    points = lax.all_gather(local_rows, "cells", axis=0, tiled=True)
    beta = 4.0 / math.sqrt(points.shape[1])
    logits = (
        lax.dot_general(
            points, centroids, (((1,), (1,)), ((), ())), preferred_element_type=jnp.float32
        )
        * beta
    )
    inverse = lax.rsqrt(counters.astype(jnp.float32) + 1.0)
    top = lax.pmax(jnp.max(logits, axis=1), "cells")
    expo = jnp.exp(logits - top[:, None])
    total, novel = lax.psum(
        (jnp.sum(expo, axis=1), jnp.dot(expo, inverse, preferred_element_type=jnp.float32)), "cells"
    )
    weight = novel / total
    share = (expo * (weight / total)[:, None]).astype(jnp.bfloat16)
    mass_local = jnp.sum(share.astype(jnp.float32), axis=0)
    sums_local = lax.dot_general(
        share, points, (((0,), (0,)), ((), ())), preferred_element_type=jnp.float32
    )
    sums = lax.psum_scatter(sums_local, "pts", scatter_dimension=0, tiled=True)
    mass = lax.psum_scatter(mass_local, "pts", scatter_dimension=0, tiled=True)
    return (sums[None], mass[None])


def exchange(a, axes, partner):
    count = math.prod(lax.axis_size(axis) for axis in axes)
    return lax.ppermute(a, axes, [(partner(at), at) for at in range(count)])


def in_vmem(n):
    return [pl.BlockSpec(memory_space=pltpu.VMEM)] * n


def join(above, below, *after):
    def kernel(above, below, *refs):
        out = refs[-1]
        out[: above.shape[0], :] = above[...]
        out[above.shape[0] :, :] = below[...]

    return pl.pallas_call(
        kernel,
        in_specs=in_vmem(2 + len(after)),
        out_specs=in_vmem(1)[0],
        out_shape=jax.ShapeDtypeStruct((above.shape[0] + below.shape[0], above.shape[1]), above.dtype),
        compiler_params=pltpu.CompilerParams(vmem_limit_bytes=VMEM_BYTES),
    )(above, below, *after)


def beside(left, right, *after):
    def kernel(left, right, *refs):
        refs[-1][...] = jnp.concatenate([left[...], right[...]], axis=1)

    return pl.pallas_call(
        kernel,
        in_specs=in_vmem(2 + len(after)),
        out_specs=in_vmem(1)[0],
        out_shape=jax.ShapeDtypeStruct((left.shape[0], left.shape[1] + right.shape[1]), left.dtype),
        compiler_params=pltpu.CompilerParams(vmem_limit_bytes=VMEM_BYTES),
    )(left, right, *after)


def hold(a, *after, declared=0):
    def kernel(a, *refs):
        refs[-1][...] = a[...]

    return pl.pallas_call(
        kernel,
        in_specs=in_vmem(1 + len(after)),
        out_specs=in_vmem(1)[0],
        out_shape=jax.ShapeDtypeStruct(a.shape, a.dtype),
        compiler_params=pltpu.CompilerParams(vmem_limit_bytes=VMEM_BYTES),
        cost_estimate=pl.CostEstimate(flops=declared, bytes_accessed=0, transcendentals=0),
    )(a, *after)


def scores(cells, points):
    return lax.dot_general(cells, points, (((1,), (1,)), ((), ())), preferred_element_type=jnp.float32)


def chip_index():
    return lax.axis_index("y") * 2 + lax.axis_index("x")


def inverse_kernel(counters, *refs):
    inverse = refs[-1]
    for line in range(counters.shape[0]):
        row = lax.rsqrt(counters[line : line + 1, :].astype(jnp.float32) + 1.0)
        inverse[line * 128 : (line + 1) * 128, :] = jnp.broadcast_to(row, (128, 128)).T


def inverse_call(counters, *after):
    return pl.pallas_call(
        inverse_kernel,
        in_specs=in_vmem(1 + len(after)),
        out_specs=in_vmem(1)[0],
        out_shape=jax.ShapeDtypeStruct((counters.shape[0], 128), jnp.float32),
        compiler_params=pltpu.CompilerParams(vmem_limit_bytes=VMEM_BYTES),
        cost_estimate=pl.CostEstimate(flops=2 * 10**9, bytes_accessed=0, transcendentals=0),
    )(counters.reshape(-1, 128), *after)


def totals_kernel(rate, block, n, *refs):
    pieces, (cells, inverse), stats = refs[:n], refs[n : n + 2], refs[-1]
    every = jnp.concatenate([piece[...] for piece in pieces], axis=0)
    count = cells.shape[0]
    parts = []
    for at in range(0, count, block):
        here = slice(at, at + block)
        logits = scores(cells[here, :], every)
        top = jnp.max(logits, axis=0, keepdims=True)
        value = jnp.exp2((logits - top) * rate)
        scale = inverse[here, :]
        weighed = [
            jnp.sum(value[:, i : i + 128] * scale, axis=0, keepdims=True) for i in range(0, value.shape[1], 128)
        ]
        parts.append((top, jnp.sum(value, axis=0, keepdims=True), jnp.concatenate(weighed, axis=1)))
        while len(parts) > 1 and (at + block == count or len(parts) == 4):
            parts = [join_stats(rate, parts)]
    stats[...] = jnp.concatenate(parts[0], axis=0)


def join_stats(rate, parts):
    top = functools.reduce(jnp.maximum, [part[0] for part in parts])
    scales = [jnp.exp2((part[0] - top) * rate) for part in parts]
    return (top, *(sum(part[at] * scale for part, scale in zip(parts, scales)) for at in (1, 2)))


def totals_call(rate, block, pieces, cells, inverse, after=(), declared=1.0):
    n_points, width = sum(piece.shape[0] for piece in pieces), pieces[0].shape[1]
    n_cells = inverse.shape[0]
    args = (*pieces, cells, inverse, *after)
    return pl.pallas_call(
        functools.partial(totals_kernel, rate, block, len(pieces)),
        in_specs=in_vmem(len(args)),
        out_specs=in_vmem(1)[0],
        out_shape=jax.ShapeDtypeStruct((3, n_points), jnp.float32),
        compiler_params=pltpu.CompilerParams(vmem_limit_bytes=VMEM_BYTES),
        cost_estimate=pl.CostEstimate(
            flops=int(declared * 2 * n_cells * n_points * width),
            bytes_accessed=int(declared * 2 * n_cells * width),
            transcendentals=int(declared * n_cells * n_points),
        ),
    )(*args)


def goal_kernel(rate, *refs):
    stats, goal = refs[:4], refs[-1]
    for at in range(4):
        here = [stat[:, (at ^ by) * 128 : ((at ^ by) + 1) * 128] for by, stat in enumerate(stats)]
        top, total, novel = join_stats(rate, [(s[:1], s[1:2], s[2:]) for s in here])
        goal[:, at * 128 : (at + 1) * 128] = jnp.concatenate([top, novel / total / total], axis=0)


def goal_call(rate, *stats):
    return pl.pallas_call(
        functools.partial(goal_kernel, rate),
        in_specs=in_vmem(len(stats)),
        out_specs=in_vmem(1)[0],
        out_shape=jax.ShapeDtypeStruct((2, stats[0].shape[1]), jnp.float32),
        compiler_params=pltpu.CompilerParams(vmem_limit_bytes=VMEM_BYTES),
    )(*stats)


def factor_kernel(rate, n, *refs):
    goals, tops, factors = refs[:4], refs[4 : 4 + n], refs[4 + n :]
    rows = goals[0].shape[1] // 2
    spots = [(0, 0, 0), (0, 0, 1), (0, 0, 2), (1, 0, 3), (1, 1, 0), (1, 1, 1), (1, 1, 2), (2, 1, 3)]
    for at, (bundle, group, goal) in enumerate(spots):
        start = (at - (0, 3, 7)[bundle]) * rows
        mine, here = slice(group * rows, (group + 1) * rows), slice(start, start + rows)
        scale = jnp.exp2((tops[bundle][:, here] - goals[goal][:1, mine]) * rate)
        factors[bundle][:, here] = scale * goals[goal][1:, mine]


def factor_call(rate, goals, tops):
    return pl.pallas_call(
        functools.partial(factor_kernel, rate, len(tops)),
        in_specs=in_vmem(4 + len(tops)),
        out_specs=in_vmem(len(tops)),
        out_shape=[jax.ShapeDtypeStruct(top.shape, jnp.float32) for top in tops],
        compiler_params=pltpu.CompilerParams(vmem_limit_bytes=VMEM_BYTES),
    )(*goals, *tops)


def expo_kernel(rate, block, spots, *refs):
    pieces, cells, (expo, tops, points) = refs[: len(spots)], refs[len(spots)], refs[-3:]
    start = 0
    for piece, (first, rows) in zip(pieces, spots):
        points[start : start + rows, :] = piece[first : first + rows, :]
        start += rows
    count = expo.shape[0] // block
    chip = chip_index()
    for at in range(count):
        mine = pl.ds(pl.multiple_of((chip * count + at) * block, block), block)
        for part in range(0, points.shape[0], 256):
            some = slice(part, part + 256)
            logits = scores(cells[mine, :], points[some, :])
            top = jnp.max(logits, axis=0, keepdims=True)
            expo[at * block : (at + 1) * block, some] = jnp.exp2((logits - top) * rate).astype(jnp.bfloat16)
            tops[at : at + 1, some] = top


def expo_call(rate, block, count, pieces, cells, *after, declared=1.0):
    width = cells.shape[1]
    pieces, spots = zip(*((piece[0], piece[1:]) if isinstance(piece, tuple) else (piece, (0, len(piece))) for piece in pieces))
    n_points = sum(rows for _, rows in spots)
    return pl.pallas_call(
        functools.partial(expo_kernel, rate, block, spots),
        in_specs=in_vmem(len(pieces) + 1 + len(after)),
        out_specs=in_vmem(3),
        out_shape=[
            jax.ShapeDtypeStruct((count, n_points), jnp.bfloat16),
            jax.ShapeDtypeStruct((count // block, n_points), jnp.float32),
            jax.ShapeDtypeStruct((n_points, width), jnp.bfloat16),
        ],
        compiler_params=pltpu.CompilerParams(vmem_limit_bytes=VMEM_BYTES),
        cost_estimate=pl.CostEstimate(
            flops=int(declared * 2 * count * n_points * width),
            bytes_accessed=int(declared * 2 * (count * width + n_points * width + count * n_points)),
            transcendentals=int(declared * count * n_points),
        ),
    )(*pieces, cells, *after)


def weighed_sums(start, count, expos, points, factors):
    total = weight = None
    for expo, chunk, factor in zip(expos, points, factors):
        block = expo.shape[0] // factor.shape[0]
        shares = []
        step = min(block, count)
        for at in range(0, count, step):
            here = pl.ds(pl.multiple_of(start + at, step), step)
            scale = factor[pl.ds((start + at) // block, 1), :]
            shares.append((expo[here, :].astype(jnp.float32) * scale).astype(jnp.bfloat16))
        share = jnp.concatenate(shares, axis=0)
        part = jnp.dot(share, chunk[...], preferred_element_type=jnp.float32)
        wide = share.astype(jnp.float32)
        lanes = sum(wide[:, i : i + 128] for i in range(0, wide.shape[1], 128))
        total = part if total is None else total + part
        weight = lanes if weight is None else weight + lanes
    return total, jnp.sum(weight.T, axis=0, keepdims=True)


def sums_kernel(n, block, side, *refs):
    expos, points, factors, (sums, mass) = refs[:n], refs[n : 2 * n], refs[2 * n : 3 * n], refs[3 * n :]
    rows = sums.shape[0]
    first = (lax.axis_index("lo") ^ side) * rows
    for at in range(0, rows, block):
        here = slice(at, at + block)
        total, weight = weighed_sums(first + at, block, expos, points, factors)
        sums[here, :] = total.astype(sums.dtype)
        mass[:, here] = weight


def sums_call(block, side, rows, dtype, expos, points, factors):
    n = len(expos)
    n_points, width = points[0].shape
    return pl.pallas_call(
        functools.partial(sums_kernel, n, block, side),
        in_specs=in_vmem(3 * n),
        out_specs=in_vmem(2),
        out_shape=[jax.ShapeDtypeStruct((rows, width), dtype), jax.ShapeDtypeStruct((1, rows), jnp.float32)],
        compiler_params=pltpu.CompilerParams(vmem_limit_bytes=VMEM_BYTES),
        cost_estimate=pl.CostEstimate(
            flops=2 * rows * n * n_points * width,
            bytes_accessed=2 * n * n_points * (rows + width) + 4 * rows * width,
            transcendentals=0,
        ),
    )(*expos, *points, *factors)


def add_kernel(block, here, here_mass, there, there_mass, sums, mass, out, left):
    def copy(at):
        rows = pl.ds(at * block, block)
        return pltpu.make_async_copy(out.at[rows, :], sums.at[rows, :], left.at[at])

    count = here.shape[0] // block
    for at in range(count):
        rows = slice(at * block, (at + 1) * block)
        out[rows, :] = here[rows, :] + there[rows, :].astype(jnp.float32)
        copy(at).start(priority=at % 2)
    mass[...] = here_mass[...] + there_mass[...]
    for at in range(count):
        copy(at).wait()


def add_call(block, here, here_mass, there, there_mass):
    return pl.pallas_call(
        functools.partial(add_kernel, block),
        in_specs=in_vmem(4),
        out_specs=[pl.BlockSpec(memory_space=pltpu.HBM)] + in_vmem(1),
        out_shape=[
            jax.ShapeDtypeStruct(here.shape, jnp.float32),
            jax.ShapeDtypeStruct(here_mass.shape, jnp.float32),
        ],
        scratch_shapes=[
            pltpu.VMEM(here.shape, jnp.float32),
            pltpu.SemaphoreType.DMA((here.shape[0] // block,)),
        ],
        compiler_params=pltpu.CompilerParams(vmem_limit_bytes=VMEM_BYTES),
    )(here, here_mass, there, there_mass)


def split_cells(codes, exponents, centroids, counters):
    own = to_points(codes, exponents)
    rate = 4.0 / math.sqrt(own.shape[1]) * math.log2(math.e)
    plane = ("y", "x", "lo")

    turn = lambda a: exchange(a, plane, lambda at: at ^ (4 if at % 2 else 2))
    turn_back = lambda a: exchange(a, plane, lambda at: at ^ (2 if at % 2 else 4))
    along_z = lambda a, by: exchange(a, ("cells",), lambda at: at ^ by)
    around = lambda a, by: exchange(a, ("y", "x"), lambda at: at ^ by)

    per_device = centroids.shape[0] // 8
    block = per_device // 3

    near_1, near_2, near_3 = (along_z(own, by) for by in (1, 2, 3))
    inverse = inverse_call(counters)
    near_01 = join(own, near_1, inverse)
    held_01 = hold(near_01, declared=2 * 10**9)
    first_01 = turn(near_01)
    stats = [totals_call(rate, block, (held_01,), centroids, inverse)]
    second_01 = turn_back(hold(near_01, stats[0]))
    near_23 = join(near_2, near_3, *stats)
    stats.append(totals_call(rate, block, (near_23,), centroids, inverse, after=(first_01,)))
    first_23 = turn(near_23)
    rows = near_01.shape[0]
    both = turn_back(join(first_01, near_23, stats[1]))
    across_01, second_23 = (both, 0, rows), (both, rows, rows)
    stat = beside(*stats)
    expand = functools.partial(expo_call, rate, block, 2 * per_device)
    bundles = [expand((near_01, first_01, second_01), centroids, stat, declared=0.01)]
    goal = goal_call(rate, stat, *(along_z(stat, by) for by in (1, 2, 3)), bundles[0][1])
    across_23 = turn_back(hold(first_23, goal))

    bundles.append(expand((across_01, near_23, first_23, second_23), centroids, goal))
    bundles.append(expand((across_23,), centroids, bundles[1][1]))
    expos, tops, points = zip(*bundles)
    goals = [goal, turn(goal), turn_back(goal), around(goal, 3)]
    factors = factor_call(rate, goals, tops)

    there = sums_call(block, 1, per_device, jnp.bfloat16, expos, points, factors)
    there = [exchange(a, ("lo",), lambda at: at ^ 1) for a in there]
    here = sums_call(block, 0, per_device, jnp.float32, expos, points, factors)
    out, mass = add_call(block // 2, *here, *there)
    return (out[None], mass)


def solution(mesh):
    pts, cells = (mesh.shape[name] for name in ("pts", "cells"))
    square = (pts, cells) == (8, 4)
    shape, names = ((2, 2, 2, cells), ("y", "x", "lo", "cells")) if square else ((pts, cells), ("pts", "cells"))
    fine = Mesh(mesh.devices.reshape(shape), names)
    spread = names[:-1]
    in_specs = (P(names, None), P(names), P("cells", None), P("cells"))
    out_specs = (P("cells", spread, None), P("cells", spread))

    def run(codes, exponents, centroids, counters):
        small = codes.size * 2 <= GATHER_BYTES and codes.shape[0] == 128 * pts * cells
        body = split_cells if square and small else split_points
        mapped = jax.shard_map(body, mesh=fine, in_specs=in_specs, out_specs=out_specs, check_vma=False)
        return mapped(codes, exponents, centroids, counters)

    return run
```

```python
import functools
import math

import jax
import jax.numpy as jnp
from jax import lax
from jax.experimental import pallas as pl
from jax.experimental.pallas import tpu as pltpu
from jax.sharding import Mesh, PartitionSpec as P

GATHER_BYTES = 8 << 20
VMEM_BYTES = 16 << 20


def to_points(codes, exponents):
    scaled = lax.shift_right_arithmetic(codes << 16, jnp.broadcast_to(exponents[:, None], codes.shape))
    return (scaled.astype(jnp.float32) * 2.0**-16).astype(jnp.bfloat16)


def split_points(codes, exponents, centroids, counters):
    local_rows = to_points(codes, exponents)
    points = lax.all_gather(local_rows, "cells", axis=0, tiled=True)
    beta = 4.0 / math.sqrt(points.shape[1])
    logits = (
        lax.dot_general(
            points, centroids, (((1,), (1,)), ((), ())), preferred_element_type=jnp.float32
        )
        * beta
    )
    inverse = lax.rsqrt(counters.astype(jnp.float32) + 1.0)
    top = lax.pmax(jnp.max(logits, axis=1), "cells")
    expo = jnp.exp(logits - top[:, None])
    total, novel = lax.psum(
        (jnp.sum(expo, axis=1), jnp.dot(expo, inverse, preferred_element_type=jnp.float32)), "cells"
    )
    weight = novel / total
    share = (expo * (weight / total)[:, None]).astype(jnp.bfloat16)
    mass_local = jnp.sum(share.astype(jnp.float32), axis=0)
    sums_local = lax.dot_general(
        share, points, (((0,), (0,)), ((), ())), preferred_element_type=jnp.float32
    )
    sums = lax.psum_scatter(sums_local, "pts", scatter_dimension=0, tiled=True)
    mass = lax.psum_scatter(mass_local, "pts", scatter_dimension=0, tiled=True)
    return (sums[None], mass[None])


def exchange(a, axes, partner):
    count = math.prod(lax.axis_size(axis) for axis in axes)
    return lax.ppermute(a, axes, [(partner(at), at) for at in range(count)])


def in_vmem(n):
    return [pl.BlockSpec(memory_space=pltpu.VMEM)] * n


def join(above, below, *after):
    def kernel(above, below, *refs):
        out = refs[-1]
        out[: above.shape[0], :] = above[...]
        out[above.shape[0] :, :] = below[...]

    return pl.pallas_call(
        kernel,
        in_specs=in_vmem(2 + len(after)),
        out_specs=in_vmem(1)[0],
        out_shape=jax.ShapeDtypeStruct((above.shape[0] + below.shape[0], above.shape[1]), above.dtype),
        compiler_params=pltpu.CompilerParams(vmem_limit_bytes=VMEM_BYTES),
    )(above, below, *after)


def beside(left, right, *after):
    def kernel(left, right, *refs):
        refs[-1][...] = jnp.concatenate([left[...], right[...]], axis=1)

    return pl.pallas_call(
        kernel,
        in_specs=in_vmem(2 + len(after)),
        out_specs=in_vmem(1)[0],
        out_shape=jax.ShapeDtypeStruct((left.shape[0], left.shape[1] + right.shape[1]), left.dtype),
        compiler_params=pltpu.CompilerParams(vmem_limit_bytes=VMEM_BYTES),
    )(left, right, *after)


def hold(a, *after, declared=0):
    def kernel(a, *refs):
        refs[-1][...] = a[...]

    return pl.pallas_call(
        kernel,
        in_specs=in_vmem(1 + len(after)),
        out_specs=in_vmem(1)[0],
        out_shape=jax.ShapeDtypeStruct(a.shape, a.dtype),
        compiler_params=pltpu.CompilerParams(vmem_limit_bytes=VMEM_BYTES),
        cost_estimate=pl.CostEstimate(flops=declared, bytes_accessed=0, transcendentals=0),
    )(a, *after)


def scores(cells, points):
    return lax.dot_general(cells, points, (((1,), (1,)), ((), ())), preferred_element_type=jnp.float32)


def chip_index():
    return lax.axis_index("y") * 2 + lax.axis_index("x")


def inverse_kernel(counters, *refs):
    inverse = refs[-1]
    for line in range(counters.shape[0]):
        row = lax.rsqrt(counters[line : line + 1, :].astype(jnp.float32) + 1.0)
        inverse[line * 128 : (line + 1) * 128, :] = jnp.broadcast_to(row, (128, 128)).T


def inverse_call(counters, *after):
    return pl.pallas_call(
        inverse_kernel,
        in_specs=in_vmem(1 + len(after)),
        out_specs=in_vmem(1)[0],
        out_shape=jax.ShapeDtypeStruct((counters.shape[0], 128), jnp.float32),
        compiler_params=pltpu.CompilerParams(vmem_limit_bytes=VMEM_BYTES),
        cost_estimate=pl.CostEstimate(flops=2 * 10**9, bytes_accessed=0, transcendentals=0),
    )(counters.reshape(-1, 128), *after)


def totals_kernel(rate, block, n, *refs):
    pieces, (cells, inverse), stats = refs[:n], refs[n : n + 2], refs[-1]
    every = jnp.concatenate([piece[...] for piece in pieces], axis=0)
    count = cells.shape[0]
    parts = []
    for at in range(0, count, block):
        here = slice(at, at + block)
        logits = scores(cells[here, :], every)
        top = jnp.max(logits, axis=0, keepdims=True)
        value = jnp.exp2((logits - top) * rate)
        scale = inverse[here, :]
        weighed = [
            jnp.sum(value[:, i : i + 128] * scale, axis=0, keepdims=True) for i in range(0, value.shape[1], 128)
        ]
        parts.append((top, jnp.sum(value, axis=0, keepdims=True), jnp.concatenate(weighed, axis=1)))
        while len(parts) > 1 and (at + block == count or len(parts) == 4):
            parts = [join_stats(rate, parts)]
    stats[...] = jnp.concatenate(parts[0], axis=0)


def join_stats(rate, parts):
    top = functools.reduce(jnp.maximum, [part[0] for part in parts])
    scales = [jnp.exp2((part[0] - top) * rate) for part in parts]
    return (top, *(sum(part[at] * scale for part, scale in zip(parts, scales)) for at in (1, 2)))


def totals_call(rate, block, pieces, cells, inverse, after=(), declared=1.0):
    n_points, width = sum(piece.shape[0] for piece in pieces), pieces[0].shape[1]
    n_cells = inverse.shape[0]
    args = (*pieces, cells, inverse, *after)
    return pl.pallas_call(
        functools.partial(totals_kernel, rate, block, len(pieces)),
        in_specs=in_vmem(len(args)),
        out_specs=in_vmem(1)[0],
        out_shape=jax.ShapeDtypeStruct((3, n_points), jnp.float32),
        compiler_params=pltpu.CompilerParams(vmem_limit_bytes=VMEM_BYTES),
        cost_estimate=pl.CostEstimate(
            flops=int(declared * 2 * n_cells * n_points * width),
            bytes_accessed=int(declared * 2 * n_cells * width),
            transcendentals=int(declared * n_cells * n_points),
        ),
    )(*args)


def goal_kernel(rate, *refs):
    stats, goal = refs[:4], refs[-1]
    for at in range(4):
        here = [stat[:, (at ^ by) * 128 : ((at ^ by) + 1) * 128] for by, stat in enumerate(stats)]
        top, total, novel = join_stats(rate, [(s[:1], s[1:2], s[2:]) for s in here])
        goal[:, at * 128 : (at + 1) * 128] = jnp.concatenate([top, novel / total / total], axis=0)


def goal_call(rate, *stats):
    return pl.pallas_call(
        functools.partial(goal_kernel, rate),
        in_specs=in_vmem(len(stats)),
        out_specs=in_vmem(1)[0],
        out_shape=jax.ShapeDtypeStruct((2, stats[0].shape[1]), jnp.float32),
        compiler_params=pltpu.CompilerParams(vmem_limit_bytes=VMEM_BYTES),
    )(*stats)


def factor_kernel(rate, n, *refs):
    goals, tops, factors = refs[:4], refs[4 : 4 + n], refs[4 + n :]
    rows = goals[0].shape[1] // 2
    spots = [(0, 0, 0), (0, 0, 1), (0, 0, 2), (1, 0, 3), (1, 1, 0), (1, 1, 1), (1, 1, 2), (2, 1, 3)]
    for at, (bundle, group, goal) in enumerate(spots):
        start = (at - (0, 3, 7)[bundle]) * rows
        mine, here = slice(group * rows, (group + 1) * rows), slice(start, start + rows)
        scale = jnp.exp2((tops[bundle][:, here] - goals[goal][:1, mine]) * rate)
        factors[bundle][:, here] = scale * goals[goal][1:, mine]


def factor_call(rate, goals, tops):
    return pl.pallas_call(
        functools.partial(factor_kernel, rate, len(tops)),
        in_specs=in_vmem(4 + len(tops)),
        out_specs=in_vmem(len(tops)),
        out_shape=[jax.ShapeDtypeStruct(top.shape, jnp.float32) for top in tops],
        compiler_params=pltpu.CompilerParams(vmem_limit_bytes=VMEM_BYTES),
    )(*goals, *tops)


def expo_kernel(rate, block, spots, *refs):
    pieces, cells, (expo, tops, points) = refs[: len(spots)], refs[len(spots)], refs[-3:]
    start = 0
    for piece, (first, rows) in zip(pieces, spots):
        points[start : start + rows, :] = piece[first : first + rows, :]
        start += rows
    count = expo.shape[0] // block
    chip = chip_index()
    for at in range(count):
        mine = pl.ds(pl.multiple_of((chip * count + at) * block, block), block)
        for part in range(0, points.shape[0], 256):
            some = slice(part, part + 256)
            logits = scores(cells[mine, :], points[some, :])
            top = jnp.max(logits, axis=0, keepdims=True)
            expo[at * block : (at + 1) * block, some] = jnp.exp2((logits - top) * rate).astype(jnp.bfloat16)
            tops[at : at + 1, some] = top


def expo_call(rate, block, count, pieces, cells, *after, declared=1.0):
    width = cells.shape[1]
    pieces, spots = zip(*((piece[0], piece[1:]) if isinstance(piece, tuple) else (piece, (0, len(piece))) for piece in pieces))
    n_points = sum(rows for _, rows in spots)
    return pl.pallas_call(
        functools.partial(expo_kernel, rate, block, spots),
        in_specs=in_vmem(len(pieces) + 1 + len(after)),
        out_specs=in_vmem(3),
        out_shape=[
            jax.ShapeDtypeStruct((count, n_points), jnp.bfloat16),
            jax.ShapeDtypeStruct((count // block, n_points), jnp.float32),
            jax.ShapeDtypeStruct((n_points, width), jnp.bfloat16),
        ],
        compiler_params=pltpu.CompilerParams(vmem_limit_bytes=VMEM_BYTES),
        cost_estimate=pl.CostEstimate(
            flops=int(declared * 2 * count * n_points * width),
            bytes_accessed=int(declared * 2 * (count * width + n_points * width + count * n_points)),
            transcendentals=int(declared * count * n_points),
        ),
    )(*pieces, cells, *after)


def weighed_sums(start, count, expos, points, factors):
    total = weight = None
    for expo, chunk, factor in zip(expos, points, factors):
        block = expo.shape[0] // factor.shape[0]
        shares = []
        step = min(block, count)
        for at in range(0, count, step):
            here = pl.ds(pl.multiple_of(start + at, step), step)
            scale = factor[pl.ds((start + at) // block, 1), :]
            shares.append((expo[here, :].astype(jnp.float32) * scale).astype(jnp.bfloat16))
        share = jnp.concatenate(shares, axis=0)
        part = jnp.dot(share, chunk[...], preferred_element_type=jnp.float32)
        wide = share.astype(jnp.float32)
        lanes = sum(wide[:, i : i + 128] for i in range(0, wide.shape[1], 128))
        total = part if total is None else total + part
        weight = lanes if weight is None else weight + lanes
    return total, jnp.sum(weight.T, axis=0, keepdims=True)


def sums_kernel(n, block, side, *refs):
    expos, points, factors, (sums, mass) = refs[:n], refs[n : 2 * n], refs[2 * n : 3 * n], refs[3 * n :]
    rows = sums.shape[0]
    first = (lax.axis_index("lo") ^ side) * rows
    for at in range(0, rows, block):
        here = slice(at, at + block)
        total, weight = weighed_sums(first + at, block, expos, points, factors)
        sums[here, :] = total.astype(sums.dtype)
        mass[:, here] = weight


def sums_call(block, side, rows, dtype, expos, points, factors):
    n = len(expos)
    n_points, width = points[0].shape
    return pl.pallas_call(
        functools.partial(sums_kernel, n, block, side),
        in_specs=in_vmem(3 * n),
        out_specs=in_vmem(2),
        out_shape=[jax.ShapeDtypeStruct((rows, width), dtype), jax.ShapeDtypeStruct((1, rows), jnp.float32)],
        compiler_params=pltpu.CompilerParams(vmem_limit_bytes=VMEM_BYTES),
        cost_estimate=pl.CostEstimate(
            flops=2 * rows * n * n_points * width,
            bytes_accessed=2 * n * n_points * (rows + width) + 4 * rows * width,
            transcendentals=0,
        ),
    )(*expos, *points, *factors)


def add_kernel(block, here, here_mass, there, there_mass, sums, mass, out, left):
    def copy(at):
        rows = pl.ds(at * block, block)
        return pltpu.make_async_copy(out.at[rows, :], sums.at[rows, :], left.at[at])

    count = here.shape[0] // block
    for at in range(count):
        rows = slice(at * block, (at + 1) * block)
        out[rows, :] = here[rows, :] + there[rows, :].astype(jnp.float32)
        copy(at).start(priority=at % 2)
    mass[...] = here_mass[...] + there_mass[...]
    for at in range(count):
        copy(at).wait()


def add_call(block, here, here_mass, there, there_mass):
    return pl.pallas_call(
        functools.partial(add_kernel, block),
        in_specs=in_vmem(4),
        out_specs=[pl.BlockSpec(memory_space=pltpu.HBM)] + in_vmem(1),
        out_shape=[
            jax.ShapeDtypeStruct(here.shape, jnp.float32),
            jax.ShapeDtypeStruct(here_mass.shape, jnp.float32),
        ],
        scratch_shapes=[
            pltpu.VMEM(here.shape, jnp.float32),
            pltpu.SemaphoreType.DMA((here.shape[0] // block,)),
        ],
        compiler_params=pltpu.CompilerParams(vmem_limit_bytes=VMEM_BYTES),
    )(here, here_mass, there, there_mass)


def split_cells(codes, exponents, centroids, counters):
    own = to_points(codes, exponents)
    rate = 4.0 / math.sqrt(own.shape[1]) * math.log2(math.e)
    plane = ("y", "x", "lo")

    turn = lambda a: exchange(a, plane, lambda at: at ^ (4 if at % 2 else 2))
    turn_back = lambda a: exchange(a, plane, lambda at: at ^ (2 if at % 2 else 4))
    along_z = lambda a, by: exchange(a, ("cells",), lambda at: at ^ by)
    around = lambda a, by: exchange(a, ("y", "x"), lambda at: at ^ by)

    per_device = centroids.shape[0] // 8
    block = per_device // 3

    near_1, near_2, near_3 = (along_z(own, by) for by in (1, 2, 3))
    inverse = inverse_call(counters)
    near_01 = join(own, near_1, inverse)
    held_01 = hold(near_01, declared=2 * 10**9)
    first_01 = turn(near_01)
    stats = [totals_call(rate, block, (held_01,), centroids, inverse)]
    second_01 = turn_back(hold(near_01, stats[0]))
    near_23 = join(near_2, near_3, *stats)
    stats.append(totals_call(rate, block, (near_23,), centroids, inverse, after=(first_01,)))
    first_23 = turn(near_23)
    rows = near_01.shape[0]
    both = turn_back(join(first_01, near_23, stats[1]))
    across_01, second_23 = (both, 0, rows), (both, rows, rows)
    stat = beside(*stats)
    expand = functools.partial(expo_call, rate, block, 2 * per_device)
    bundles = [expand((near_01, first_01, second_01), centroids, stat, declared=0.01)]
    goal = goal_call(rate, stat, *(along_z(stat, by) for by in (1, 2, 3)), bundles[0][1])
    across_23 = turn_back(hold(first_23, goal))

    bundles.append(expand((across_01, near_23, first_23, second_23), centroids, goal, declared=0.01))
    bundles.append(expand((across_23,), centroids, bundles[1][1]))
    expos, tops, points = zip(*bundles)
    goals = [goal, turn(goal), turn_back(goal), around(goal, 3)]
    factors = factor_call(rate, goals, tops)

    there = sums_call(block, 1, per_device, jnp.bfloat16, expos, points, factors)
    there = [exchange(a, ("lo",), lambda at: at ^ 1) for a in there]
    here = sums_call(block, 0, per_device, jnp.float32, expos, points, factors)
    out, mass = add_call(block // 2, *here, *there)
    return (out[None], mass)


def solution(mesh):
    pts, cells = (mesh.shape[name] for name in ("pts", "cells"))
    square = (pts, cells) == (8, 4)
    shape, names = ((2, 2, 2, cells), ("y", "x", "lo", "cells")) if square else ((pts, cells), ("pts", "cells"))
    fine = Mesh(mesh.devices.reshape(shape), names)
    spread = names[:-1]
    in_specs = (P(names, None), P(names), P("cells", None), P("cells"))
    out_specs = (P("cells", spread, None), P("cells", spread))

    def run(codes, exponents, centroids, counters):
        small = codes.size * 2 <= GATHER_BYTES and codes.shape[0] == 128 * pts * cells
        body = split_cells if square and small else split_points
        mapped = jax.shard_map(body, mesh=fine, in_specs=in_specs, out_specs=out_specs, check_vma=False)
        return mapped(codes, exponents, centroids, counters)

    return run
```

```python
import functools
import math

import jax
import jax.numpy as jnp
from jax import lax
from jax.experimental import pallas as pl
from jax.experimental.pallas import tpu as pltpu
from jax.sharding import Mesh, PartitionSpec as P

GATHER_BYTES = 8 << 20
VMEM_BYTES = 16 << 20


def to_points(codes, exponents):
    scaled = lax.shift_right_arithmetic(codes << 16, jnp.broadcast_to(exponents[:, None], codes.shape))
    return (scaled.astype(jnp.float32) * 2.0**-16).astype(jnp.bfloat16)


def split_points(codes, exponents, centroids, counters):
    local_rows = to_points(codes, exponents)
    points = lax.all_gather(local_rows, "cells", axis=0, tiled=True)
    beta = 4.0 / math.sqrt(points.shape[1])
    logits = (
        lax.dot_general(
            points, centroids, (((1,), (1,)), ((), ())), preferred_element_type=jnp.float32
        )
        * beta
    )
    inverse = lax.rsqrt(counters.astype(jnp.float32) + 1.0)
    top = lax.pmax(jnp.max(logits, axis=1), "cells")
    expo = jnp.exp(logits - top[:, None])
    total, novel = lax.psum(
        (jnp.sum(expo, axis=1), jnp.dot(expo, inverse, preferred_element_type=jnp.float32)), "cells"
    )
    weight = novel / total
    share = (expo * (weight / total)[:, None]).astype(jnp.bfloat16)
    mass_local = jnp.sum(share.astype(jnp.float32), axis=0)
    sums_local = lax.dot_general(
        share, points, (((0,), (0,)), ((), ())), preferred_element_type=jnp.float32
    )
    sums = lax.psum_scatter(sums_local, "pts", scatter_dimension=0, tiled=True)
    mass = lax.psum_scatter(mass_local, "pts", scatter_dimension=0, tiled=True)
    return (sums[None], mass[None])


def exchange(a, axes, partner):
    count = math.prod(lax.axis_size(axis) for axis in axes)
    return lax.ppermute(a, axes, [(partner(at), at) for at in range(count)])


def in_vmem(n):
    return [pl.BlockSpec(memory_space=pltpu.VMEM)] * n


def join(above, below, *after):
    def kernel(above, below, *refs):
        out = refs[-1]
        out[: above.shape[0], :] = above[...]
        out[above.shape[0] :, :] = below[...]

    return pl.pallas_call(
        kernel,
        in_specs=in_vmem(2 + len(after)),
        out_specs=in_vmem(1)[0],
        out_shape=jax.ShapeDtypeStruct((above.shape[0] + below.shape[0], above.shape[1]), above.dtype),
        compiler_params=pltpu.CompilerParams(vmem_limit_bytes=VMEM_BYTES),
    )(above, below, *after)


def beside(left, right, *after):
    def kernel(left, right, *refs):
        refs[-1][...] = jnp.concatenate([left[...], right[...]], axis=1)

    return pl.pallas_call(
        kernel,
        in_specs=in_vmem(2 + len(after)),
        out_specs=in_vmem(1)[0],
        out_shape=jax.ShapeDtypeStruct((left.shape[0], left.shape[1] + right.shape[1]), left.dtype),
        compiler_params=pltpu.CompilerParams(vmem_limit_bytes=VMEM_BYTES),
    )(left, right, *after)


def hold(a, *after, declared=0):
    def kernel(a, *refs):
        refs[-1][...] = a[...]

    return pl.pallas_call(
        kernel,
        in_specs=in_vmem(1 + len(after)),
        out_specs=in_vmem(1)[0],
        out_shape=jax.ShapeDtypeStruct(a.shape, a.dtype),
        compiler_params=pltpu.CompilerParams(vmem_limit_bytes=VMEM_BYTES),
        cost_estimate=pl.CostEstimate(flops=declared, bytes_accessed=0, transcendentals=0),
    )(a, *after)


def scores(cells, points):
    return lax.dot_general(cells, points, (((1,), (1,)), ((), ())), preferred_element_type=jnp.float32)


def chip_index():
    return lax.axis_index("y") * 2 + lax.axis_index("x")


def inverse_kernel(counters, *refs):
    inverse = refs[-1]
    for line in range(counters.shape[0]):
        row = lax.rsqrt(counters[line : line + 1, :].astype(jnp.float32) + 1.0)
        inverse[line * 128 : (line + 1) * 128, :] = jnp.broadcast_to(row, (128, 128)).T


def inverse_call(counters, *after):
    return pl.pallas_call(
        inverse_kernel,
        in_specs=in_vmem(1 + len(after)),
        out_specs=in_vmem(1)[0],
        out_shape=jax.ShapeDtypeStruct((counters.shape[0], 128), jnp.float32),
        compiler_params=pltpu.CompilerParams(vmem_limit_bytes=VMEM_BYTES),
        cost_estimate=pl.CostEstimate(flops=2 * 10**9, bytes_accessed=0, transcendentals=0),
    )(counters.reshape(-1, 128), *after)


def totals_kernel(rate, block, n, *refs):
    pieces, (cells, inverse), stats = refs[:n], refs[n : n + 2], refs[-1]
    every = jnp.concatenate([piece[...] for piece in pieces], axis=0)
    count = cells.shape[0]
    parts = []
    for at in range(0, count, block):
        here = slice(at, at + block)
        logits = scores(cells[here, :], every)
        top = jnp.max(logits, axis=0, keepdims=True)
        value = jnp.exp2((logits - top) * rate)
        scale = inverse[here, :]
        weighed = [
            jnp.sum(value[:, i : i + 128] * scale, axis=0, keepdims=True) for i in range(0, value.shape[1], 128)
        ]
        parts.append((top, jnp.sum(value, axis=0, keepdims=True), jnp.concatenate(weighed, axis=1)))
        while len(parts) > 1 and (at + block == count or len(parts) == 4):
            parts = [join_stats(rate, parts)]
    stats[...] = jnp.concatenate(parts[0], axis=0)


def join_stats(rate, parts):
    top = functools.reduce(jnp.maximum, [part[0] for part in parts])
    scales = [jnp.exp2((part[0] - top) * rate) for part in parts]
    return (top, *(sum(part[at] * scale for part, scale in zip(parts, scales)) for at in (1, 2)))


def totals_call(rate, block, pieces, cells, inverse, after=(), declared=1.0):
    n_points, width = sum(piece.shape[0] for piece in pieces), pieces[0].shape[1]
    n_cells = inverse.shape[0]
    args = (*pieces, cells, inverse, *after)
    return pl.pallas_call(
        functools.partial(totals_kernel, rate, block, len(pieces)),
        in_specs=in_vmem(len(args)),
        out_specs=in_vmem(1)[0],
        out_shape=jax.ShapeDtypeStruct((3, n_points), jnp.float32),
        compiler_params=pltpu.CompilerParams(vmem_limit_bytes=VMEM_BYTES),
        cost_estimate=pl.CostEstimate(
            flops=int(declared * 2 * n_cells * n_points * width),
            bytes_accessed=int(declared * 2 * n_cells * width),
            transcendentals=int(declared * n_cells * n_points),
        ),
    )(*args)


def goal_kernel(rate, *refs):
    stats, goal = refs[:4], refs[-1]
    for at in range(4):
        here = [stat[:, (at ^ by) * 128 : ((at ^ by) + 1) * 128] for by, stat in enumerate(stats)]
        top, total, novel = join_stats(rate, [(s[:1], s[1:2], s[2:]) for s in here])
        goal[:, at * 128 : (at + 1) * 128] = jnp.concatenate([top, novel / total / total], axis=0)


def goal_call(rate, *stats):
    return pl.pallas_call(
        functools.partial(goal_kernel, rate),
        in_specs=in_vmem(len(stats)),
        out_specs=in_vmem(1)[0],
        out_shape=jax.ShapeDtypeStruct((2, stats[0].shape[1]), jnp.float32),
        compiler_params=pltpu.CompilerParams(vmem_limit_bytes=VMEM_BYTES),
    )(*stats)


def factor_kernel(rate, n, *refs):
    goals, tops, factors = refs[:4], refs[4 : 4 + n], refs[4 + n :]
    rows = goals[0].shape[1] // 2
    spots = [(0, 0, 0), (0, 0, 1), (0, 0, 2), (0, 1, 0), (1, 0, 3), (1, 1, 1), (1, 1, 2), (2, 1, 3)]
    for at, (bundle, group, goal) in enumerate(spots):
        start = (at - (0, 4, 7)[bundle]) * rows
        mine, here = slice(group * rows, (group + 1) * rows), slice(start, start + rows)
        scale = jnp.exp2((tops[bundle][:, here] - goals[goal][:1, mine]) * rate)
        factors[bundle][:, here] = scale * goals[goal][1:, mine]


def factor_call(rate, goals, tops):
    return pl.pallas_call(
        functools.partial(factor_kernel, rate, len(tops)),
        in_specs=in_vmem(4 + len(tops)),
        out_specs=in_vmem(len(tops)),
        out_shape=[jax.ShapeDtypeStruct(top.shape, jnp.float32) for top in tops],
        compiler_params=pltpu.CompilerParams(vmem_limit_bytes=VMEM_BYTES),
    )(*goals, *tops)


def expo_kernel(rate, block, spots, *refs):
    pieces, cells, (expo, tops, points) = refs[: len(spots)], refs[len(spots)], refs[-3:]
    start = 0
    for piece, (first, rows) in zip(pieces, spots):
        points[start : start + rows, :] = piece[first : first + rows, :]
        start += rows
    count = expo.shape[0] // block
    chip = chip_index()
    for at in range(count):
        mine = pl.ds(pl.multiple_of((chip * count + at) * block, block), block)
        for part in range(0, points.shape[0], 256):
            some = slice(part, part + 256)
            logits = scores(cells[mine, :], points[some, :])
            top = jnp.max(logits, axis=0, keepdims=True)
            expo[at * block : (at + 1) * block, some] = jnp.exp2((logits - top) * rate).astype(jnp.bfloat16)
            tops[at : at + 1, some] = top


def expo_call(rate, block, count, pieces, cells, *after, declared=1.0):
    width = cells.shape[1]
    pieces, spots = zip(*((piece[0], piece[1:]) if isinstance(piece, tuple) else (piece, (0, len(piece))) for piece in pieces))
    n_points = sum(rows for _, rows in spots)
    return pl.pallas_call(
        functools.partial(expo_kernel, rate, block, spots),
        in_specs=in_vmem(len(pieces) + 1 + len(after)),
        out_specs=in_vmem(3),
        out_shape=[
            jax.ShapeDtypeStruct((count, n_points), jnp.bfloat16),
            jax.ShapeDtypeStruct((count // block, n_points), jnp.float32),
            jax.ShapeDtypeStruct((n_points, width), jnp.bfloat16),
        ],
        compiler_params=pltpu.CompilerParams(vmem_limit_bytes=VMEM_BYTES),
        cost_estimate=pl.CostEstimate(
            flops=int(declared * 2 * count * n_points * width),
            bytes_accessed=int(declared * 2 * (count * width + n_points * width + count * n_points)),
            transcendentals=int(declared * count * n_points),
        ),
    )(*pieces, cells, *after)


def weighed_sums(start, count, expos, points, factors):
    total = weight = None
    for expo, chunk, factor in zip(expos, points, factors):
        block = expo.shape[0] // factor.shape[0]
        shares, lanes = [], []
        for at in range(0, count, block):
            here = pl.ds(pl.multiple_of(start + at, block), block)
            share = expo[here, :].astype(jnp.float32) * factor[pl.ds((start + at) // block, 1), :]
            shares.append(share.astype(jnp.bfloat16))
            lanes.append(sum(share[:, i : i + 128] for i in range(0, share.shape[1], 128)))
        share, lanes = jnp.concatenate(shares, axis=0), jnp.concatenate(lanes, axis=0)
        part = jnp.dot(share, chunk[...], preferred_element_type=jnp.float32)
        total = part if total is None else total + part
        weight = lanes if weight is None else weight + lanes
    return total, jnp.sum(weight.T, axis=0, keepdims=True)


def sums_kernel(n, block, side, *refs):
    expos, points, factors, (sums, mass) = refs[:n], refs[n : 2 * n], refs[2 * n : 3 * n], refs[3 * n :]
    rows = sums.shape[0]
    first = (lax.axis_index("lo") ^ side) * rows
    for at in range(0, rows, block):
        here = slice(at, at + block)
        total, weight = weighed_sums(first + at, block, expos, points, factors)
        sums[here, :] = total.astype(sums.dtype)
        mass[:, here] = weight


def sums_call(block, side, rows, dtype, expos, points, factors):
    n = len(expos)
    n_points, width = points[0].shape
    return pl.pallas_call(
        functools.partial(sums_kernel, n, block, side),
        in_specs=in_vmem(3 * n),
        out_specs=in_vmem(2),
        out_shape=[jax.ShapeDtypeStruct((rows, width), dtype), jax.ShapeDtypeStruct((1, rows), jnp.float32)],
        compiler_params=pltpu.CompilerParams(vmem_limit_bytes=VMEM_BYTES),
        cost_estimate=pl.CostEstimate(
            flops=2 * rows * n * n_points * width,
            bytes_accessed=2 * n * n_points * (rows + width) + 4 * rows * width,
            transcendentals=0,
        ),
    )(*expos, *points, *factors)


def add_kernel(block, here, here_mass, there, there_mass, sums, mass, out, left):
    def copy(at):
        rows = pl.ds(at * block, block)
        return pltpu.make_async_copy(out.at[rows, :], sums.at[rows, :], left.at[at])

    count = here.shape[0] // block
    for at in range(count):
        rows = slice(at * block, (at + 1) * block)
        out[rows, :] = here[rows, :] + there[rows, :].astype(jnp.float32)
        copy(at).start(priority=at % 2)
    mass[...] = here_mass[...] + there_mass[...]
    for at in range(count):
        copy(at).wait()


def add_call(block, here, here_mass, there, there_mass):
    return pl.pallas_call(
        functools.partial(add_kernel, block),
        in_specs=in_vmem(4),
        out_specs=[pl.BlockSpec(memory_space=pltpu.HBM)] + in_vmem(1),
        out_shape=[
            jax.ShapeDtypeStruct(here.shape, jnp.float32),
            jax.ShapeDtypeStruct(here_mass.shape, jnp.float32),
        ],
        scratch_shapes=[
            pltpu.VMEM(here.shape, jnp.float32),
            pltpu.SemaphoreType.DMA((here.shape[0] // block,)),
        ],
        compiler_params=pltpu.CompilerParams(vmem_limit_bytes=VMEM_BYTES),
    )(here, here_mass, there, there_mass)


def split_cells(codes, exponents, centroids, counters):
    own = to_points(codes, exponents)
    rate = 4.0 / math.sqrt(own.shape[1]) * math.log2(math.e)
    plane = ("y", "x", "lo")

    turn = lambda a: exchange(a, plane, lambda at: at ^ (4 if at % 2 else 2))
    turn_back = lambda a: exchange(a, plane, lambda at: at ^ (2 if at % 2 else 4))
    along_z = lambda a, by: exchange(a, ("cells",), lambda at: at ^ by)
    around = lambda a, by: exchange(a, ("y", "x"), lambda at: at ^ by)

    per_device = centroids.shape[0] // 8
    block = per_device // 3

    near_1, near_2, near_3 = (along_z(own, by) for by in (1, 2, 3))
    inverse = inverse_call(counters)
    near_01 = join(own, near_1, inverse)
    held_01 = hold(near_01, declared=2 * 10**9)
    first_01 = turn(near_01)
    stats = [totals_call(rate, block, (held_01,), centroids, inverse)]
    second_01 = turn_back(hold(near_01, stats[0]))
    near_23 = join(near_2, near_3, *stats)
    stats.append(totals_call(rate, block, (near_23,), centroids, inverse, after=(first_01,)))
    first_23 = turn(near_23)
    rows = near_01.shape[0]
    both = turn_back(join(first_01, near_23, stats[1]))
    across_01, second_23 = (both, 0, rows), (both, rows, rows)
    stat = beside(*stats)
    expand = functools.partial(expo_call, rate, block, 2 * per_device)
    bundles = [expand((near_01, first_01, second_01, near_23), centroids, stat, declared=0.01)]
    goal = goal_call(rate, stat, *(along_z(stat, by) for by in (1, 2, 3)), bundles[0][1])
    across_23 = turn_back(hold(first_23, goal))

    bundles.append(expand((across_01, first_23, second_23), centroids, goal, declared=0.01))
    bundles.append(expand((across_23,), centroids, bundles[1][1]))
    expos, tops, points = zip(*bundles)
    goals = [goal, turn(goal), turn_back(goal), around(goal, 3)]
    factors = factor_call(rate, goals, tops)

    there = sums_call(per_device, 1, per_device, jnp.bfloat16, expos, points, factors)
    there = [exchange(a, ("lo",), lambda at: at ^ 1) for a in there]
    here = sums_call(per_device, 0, per_device, jnp.float32, expos, points, factors)
    out, mass = add_call(block // 2, *here, *there)
    return (out[None], mass)


def solution(mesh):
    pts, cells = (mesh.shape[name] for name in ("pts", "cells"))
    square = (pts, cells) == (8, 4)
    shape, names = ((2, 2, 2, cells), ("y", "x", "lo", "cells")) if square else ((pts, cells), ("pts", "cells"))
    fine = Mesh(mesh.devices.reshape(shape), names)
    spread = names[:-1]
    in_specs = (P(names, None), P(names), P("cells", None), P("cells"))
    out_specs = (P("cells", spread, None), P("cells", spread))

    def run(codes, exponents, centroids, counters):
        small = codes.size * 2 <= GATHER_BYTES and codes.shape[0] == 128 * pts * cells
        body = split_cells if square and small else split_points
        mapped = jax.shard_map(body, mesh=fine, in_specs=in_specs, out_specs=out_specs, check_vma=False)
        return mapped(codes, exponents, centroids, counters)

    return run
```

```python
import functools
import math

import jax
import jax.numpy as jnp
from jax import lax
from jax.experimental import pallas as pl
from jax.experimental.pallas import tpu as pltpu
from jax.sharding import Mesh, PartitionSpec as P

GATHER_BYTES = 8 << 20
VMEM_BYTES = 16 << 20


def to_points(codes, exponents):
    scaled = lax.shift_right_arithmetic(codes << 16, jnp.broadcast_to(exponents[:, None], codes.shape))
    return (scaled.astype(jnp.float32) * 2.0**-16).astype(jnp.bfloat16)


def split_points(codes, exponents, centroids, counters):
    local_rows = to_points(codes, exponents)
    points = lax.all_gather(local_rows, "cells", axis=0, tiled=True)
    beta = 4.0 / math.sqrt(points.shape[1])
    logits = (
        lax.dot_general(
            points, centroids, (((1,), (1,)), ((), ())), preferred_element_type=jnp.float32
        )
        * beta
    )
    inverse = lax.rsqrt(counters.astype(jnp.float32) + 1.0)
    top = lax.pmax(jnp.max(logits, axis=1), "cells")
    expo = jnp.exp(logits - top[:, None])
    total, novel = lax.psum(
        (jnp.sum(expo, axis=1), jnp.dot(expo, inverse, preferred_element_type=jnp.float32)), "cells"
    )
    weight = novel / total
    share = (expo * (weight / total)[:, None]).astype(jnp.bfloat16)
    mass_local = jnp.sum(share.astype(jnp.float32), axis=0)
    sums_local = lax.dot_general(
        share, points, (((0,), (0,)), ((), ())), preferred_element_type=jnp.float32
    )
    sums = lax.psum_scatter(sums_local, "pts", scatter_dimension=0, tiled=True)
    mass = lax.psum_scatter(mass_local, "pts", scatter_dimension=0, tiled=True)
    return (sums[None], mass[None])


def exchange(a, axes, partner):
    count = math.prod(lax.axis_size(axis) for axis in axes)
    return lax.ppermute(a, axes, [(partner(at), at) for at in range(count)])


def in_vmem(n):
    return [pl.BlockSpec(memory_space=pltpu.VMEM)] * n


def join(above, below, *after):
    def kernel(above, below, *refs):
        out = refs[-1]
        out[: above.shape[0], :] = above[...]
        out[above.shape[0] :, :] = below[...]

    return pl.pallas_call(
        kernel,
        in_specs=in_vmem(2 + len(after)),
        out_specs=in_vmem(1)[0],
        out_shape=jax.ShapeDtypeStruct((above.shape[0] + below.shape[0], above.shape[1]), above.dtype),
        compiler_params=pltpu.CompilerParams(vmem_limit_bytes=VMEM_BYTES),
    )(above, below, *after)


def beside(left, right, *after):
    def kernel(left, right, *refs):
        refs[-1][...] = jnp.concatenate([left[...], right[...]], axis=1)

    return pl.pallas_call(
        kernel,
        in_specs=in_vmem(2 + len(after)),
        out_specs=in_vmem(1)[0],
        out_shape=jax.ShapeDtypeStruct((left.shape[0], left.shape[1] + right.shape[1]), left.dtype),
        compiler_params=pltpu.CompilerParams(vmem_limit_bytes=VMEM_BYTES),
    )(left, right, *after)


def hold(a, *after, declared=0):
    def kernel(a, *refs):
        refs[-1][...] = a[...]

    return pl.pallas_call(
        kernel,
        in_specs=in_vmem(1 + len(after)),
        out_specs=in_vmem(1)[0],
        out_shape=jax.ShapeDtypeStruct(a.shape, a.dtype),
        compiler_params=pltpu.CompilerParams(vmem_limit_bytes=VMEM_BYTES),
        cost_estimate=pl.CostEstimate(flops=declared, bytes_accessed=0, transcendentals=0),
    )(a, *after)


def scores(cells, points):
    return lax.dot_general(cells, points, (((1,), (1,)), ((), ())), preferred_element_type=jnp.float32)


def chip_index():
    return lax.axis_index("y") * 2 + lax.axis_index("x")


def inverse_kernel(counters, *refs):
    inverse = refs[-1]
    for line in range(counters.shape[0]):
        row = lax.rsqrt(counters[line : line + 1, :].astype(jnp.float32) + 1.0)
        inverse[line * 128 : (line + 1) * 128, :] = jnp.broadcast_to(row, (128, 128)).T


def inverse_call(counters, *after):
    return pl.pallas_call(
        inverse_kernel,
        in_specs=in_vmem(1 + len(after)),
        out_specs=in_vmem(1)[0],
        out_shape=jax.ShapeDtypeStruct((counters.shape[0], 128), jnp.float32),
        compiler_params=pltpu.CompilerParams(vmem_limit_bytes=VMEM_BYTES),
        cost_estimate=pl.CostEstimate(flops=2 * 10**9, bytes_accessed=0, transcendentals=0),
    )(counters.reshape(-1, 128), *after)


def totals_kernel(rate, block, n, *refs):
    pieces, (cells, inverse), stats = refs[:n], refs[n : n + 2], refs[-1]
    every = jnp.concatenate([piece[...] for piece in pieces], axis=0)
    count = cells.shape[0]
    parts = []
    for at in range(0, count, block):
        here = slice(at, at + block)
        logits = scores(cells[here, :], every)
        top = jnp.max(logits, axis=0, keepdims=True)
        value = jnp.exp2((logits - top) * rate)
        scale = inverse[here, :]
        weighed = [
            jnp.sum(value[:, i : i + 128] * scale, axis=0, keepdims=True) for i in range(0, value.shape[1], 128)
        ]
        parts.append((top, jnp.sum(value, axis=0, keepdims=True), jnp.concatenate(weighed, axis=1)))
        while len(parts) > 1 and (at + block == count or len(parts) == 4):
            parts = [join_stats(rate, parts)]
    stats[...] = jnp.concatenate(parts[0], axis=0)


def join_stats(rate, parts):
    top = functools.reduce(jnp.maximum, [part[0] for part in parts])
    scales = [jnp.exp2((part[0] - top) * rate) for part in parts]
    return (top, *(sum(part[at] * scale for part, scale in zip(parts, scales)) for at in (1, 2)))


def totals_call(rate, block, pieces, cells, inverse, after=(), declared=1.0):
    n_points, width = sum(piece.shape[0] for piece in pieces), pieces[0].shape[1]
    n_cells = inverse.shape[0]
    args = (*pieces, cells, inverse, *after)
    return pl.pallas_call(
        functools.partial(totals_kernel, rate, block, len(pieces)),
        in_specs=in_vmem(len(args)),
        out_specs=in_vmem(1)[0],
        out_shape=jax.ShapeDtypeStruct((3, n_points), jnp.float32),
        compiler_params=pltpu.CompilerParams(vmem_limit_bytes=VMEM_BYTES),
        cost_estimate=pl.CostEstimate(
            flops=int(declared * 2 * n_cells * n_points * width),
            bytes_accessed=int(declared * 2 * n_cells * width),
            transcendentals=int(declared * n_cells * n_points),
        ),
    )(*args)


def goal_kernel(rate, *refs):
    stats, goal = refs[:4], refs[-1]
    for at in range(4):
        here = [stat[:, (at ^ by) * 128 : ((at ^ by) + 1) * 128] for by, stat in enumerate(stats)]
        top, total, novel = join_stats(rate, [(s[:1], s[1:2], s[2:]) for s in here])
        goal[:, at * 128 : (at + 1) * 128] = jnp.concatenate([top, novel / total / total], axis=0)


def goal_call(rate, *stats):
    return pl.pallas_call(
        functools.partial(goal_kernel, rate),
        in_specs=in_vmem(len(stats)),
        out_specs=in_vmem(1)[0],
        out_shape=jax.ShapeDtypeStruct((2, stats[0].shape[1]), jnp.float32),
        compiler_params=pltpu.CompilerParams(vmem_limit_bytes=VMEM_BYTES),
    )(*stats)


def factor_kernel(rate, n, *refs):
    goals, tops, factors = refs[:4], refs[4 : 4 + n], refs[4 + n :]
    rows = goals[0].shape[1] // 2
    spots = [(0, 0, 0), (0, 0, 1), (0, 0, 2), (0, 1, 0), (1, 0, 3), (1, 1, 1), (1, 1, 2), (2, 1, 3)]
    for at, (bundle, group, goal) in enumerate(spots):
        start = (at - (0, 4, 7)[bundle]) * rows
        mine, here = slice(group * rows, (group + 1) * rows), slice(start, start + rows)
        scale = jnp.exp2((tops[bundle][:, here] - goals[goal][:1, mine]) * rate)
        factors[bundle][:, here] = scale * goals[goal][1:, mine]


def factor_call(rate, goals, tops):
    return pl.pallas_call(
        functools.partial(factor_kernel, rate, len(tops)),
        in_specs=in_vmem(4 + len(tops)),
        out_specs=in_vmem(len(tops)),
        out_shape=[jax.ShapeDtypeStruct(top.shape, jnp.float32) for top in tops],
        compiler_params=pltpu.CompilerParams(vmem_limit_bytes=VMEM_BYTES),
    )(*goals, *tops)


def expo_kernel(rate, block, spots, *refs):
    pieces, cells, (expo, tops, points) = refs[: len(spots)], refs[len(spots)], refs[-3:]
    start = 0
    for piece, (first, rows) in zip(pieces, spots):
        points[start : start + rows, :] = piece[first : first + rows, :]
        start += rows
    count = expo.shape[0] // block
    chip = chip_index()
    for at in range(count):
        mine = pl.ds(pl.multiple_of((chip * count + at) * block, block), block)
        for part in range(0, points.shape[0], 256):
            some = slice(part, part + 256)
            logits = scores(cells[mine, :], points[some, :])
            top = jnp.max(logits, axis=0, keepdims=True)
            expo[at * block : (at + 1) * block, some] = jnp.exp2((logits - top) * rate).astype(jnp.bfloat16)
            tops[at : at + 1, some] = top


def expo_call(rate, block, count, pieces, cells, *after, declared=1.0):
    width = cells.shape[1]
    pieces, spots = zip(*((piece[0], piece[1:]) if isinstance(piece, tuple) else (piece, (0, len(piece))) for piece in pieces))
    n_points = sum(rows for _, rows in spots)
    return pl.pallas_call(
        functools.partial(expo_kernel, rate, block, spots),
        in_specs=in_vmem(len(pieces) + 1 + len(after)),
        out_specs=in_vmem(3),
        out_shape=[
            jax.ShapeDtypeStruct((count, n_points), jnp.bfloat16),
            jax.ShapeDtypeStruct((count // block, n_points), jnp.float32),
            jax.ShapeDtypeStruct((n_points, width), jnp.bfloat16),
        ],
        compiler_params=pltpu.CompilerParams(vmem_limit_bytes=VMEM_BYTES),
        cost_estimate=pl.CostEstimate(
            flops=int(declared * 2 * count * n_points * width),
            bytes_accessed=int(declared * 2 * (count * width + n_points * width + count * n_points)),
            transcendentals=int(declared * count * n_points),
        ),
    )(*pieces, cells, *after)


def weighed_sums(start, count, expos, points, factors):
    total = weight = None
    for expo, chunk, factor in zip(expos, points, factors):
        block = expo.shape[0] // factor.shape[0]
        shares, lanes = [], []
        for at in range(0, count, block):
            here = pl.ds(pl.multiple_of(start + at, block), block)
            share = expo[here, :].astype(jnp.float32) * factor[pl.ds((start + at) // block, 1), :]
            shares.append(share.astype(jnp.bfloat16))
            lanes.append(sum(share[:, i : i + 128] for i in range(0, share.shape[1], 128)))
        share, lanes = jnp.concatenate(shares, axis=0), jnp.concatenate(lanes, axis=0)
        part = jnp.dot(share, chunk[...], preferred_element_type=jnp.float32)
        total = part if total is None else total + part
        weight = lanes if weight is None else weight + lanes
    return total, jnp.sum(weight.T, axis=0, keepdims=True)


def sums_kernel(n, block, side, *refs):
    expos, points, factors, (sums, mass) = refs[:n], refs[n : 2 * n], refs[2 * n : 3 * n], refs[3 * n :]
    rows = sums.shape[0]
    first = (lax.axis_index("lo") ^ side) * rows
    for at in range(0, rows, block):
        here = slice(at, at + block)
        total, weight = weighed_sums(first + at, block, expos, points, factors)
        sums[here, :] = total.astype(sums.dtype)
        mass[:, here] = weight


def sums_call(block, side, rows, dtype, expos, points, factors):
    n = len(expos)
    n_points, width = points[0].shape
    return pl.pallas_call(
        functools.partial(sums_kernel, n, block, side),
        in_specs=in_vmem(3 * n),
        out_specs=in_vmem(2),
        out_shape=[jax.ShapeDtypeStruct((rows, width), dtype), jax.ShapeDtypeStruct((1, rows), jnp.float32)],
        compiler_params=pltpu.CompilerParams(vmem_limit_bytes=VMEM_BYTES),
        cost_estimate=pl.CostEstimate(
            flops=2 * rows * n * n_points * width,
            bytes_accessed=2 * n * n_points * (rows + width) + 4 * rows * width,
            transcendentals=0,
        ),
    )(*expos, *points, *factors)


def add_kernel(block, here, here_mass, there, there_mass, sums, mass, out, left):
    def copy(at):
        rows = pl.ds(at * block, block)
        return pltpu.make_async_copy(out.at[rows, :], sums.at[rows, :], left.at[at])

    count = here.shape[0] // block
    for at in range(count):
        rows = slice(at * block, (at + 1) * block)
        out[rows, :] = here[rows, :] + there[rows, :].astype(jnp.float32)
        copy(at).start(priority=at % 2)
    mass[...] = here_mass[...] + there_mass[...]
    for at in range(count):
        copy(at).wait()


def add_call(block, here, here_mass, there, there_mass):
    return pl.pallas_call(
        functools.partial(add_kernel, block),
        in_specs=in_vmem(4),
        out_specs=[pl.BlockSpec(memory_space=pltpu.HBM)] + in_vmem(1),
        out_shape=[
            jax.ShapeDtypeStruct(here.shape, jnp.float32),
            jax.ShapeDtypeStruct(here_mass.shape, jnp.float32),
        ],
        scratch_shapes=[
            pltpu.VMEM(here.shape, jnp.float32),
            pltpu.SemaphoreType.DMA((here.shape[0] // block,)),
        ],
        compiler_params=pltpu.CompilerParams(vmem_limit_bytes=VMEM_BYTES),
    )(here, here_mass, there, there_mass)


def split_cells(codes, exponents, centroids, counters):
    own = to_points(codes, exponents)
    rate = 4.0 / math.sqrt(own.shape[1]) * math.log2(math.e)
    plane = ("y", "x", "lo")

    turn = lambda a: exchange(a, plane, lambda at: at ^ (4 if at % 2 else 2))
    turn_back = lambda a: exchange(a, plane, lambda at: at ^ (2 if at % 2 else 4))
    along_z = lambda a, by: exchange(a, ("cells",), lambda at: at ^ by)
    around = lambda a, by: exchange(a, ("y", "x"), lambda at: at ^ by)

    per_device = centroids.shape[0] // 8
    block = per_device // 3

    near_1, near_2, near_3 = (along_z(own, by) for by in (1, 2, 3))
    inverse = inverse_call(counters)
    near_01 = join(own, near_1, inverse)
    held_01 = hold(near_01, declared=2 * 10**9)
    first_01 = turn(near_01)
    stats = [totals_call(rate, block, (held_01,), centroids, inverse)]
    second_01, across_01 = turn_back(hold(near_01, stats[0])), turn_back(hold(first_01, stats[0]))
    near_23 = join(near_2, near_3, *stats)
    stats.append(totals_call(rate, block, (near_23,), centroids, inverse, after=(first_01,)))
    first_23 = turn(near_23)
    stat = beside(*stats)
    expand = functools.partial(expo_call, rate, block, 2 * per_device)
    bundles = [expand((near_01, first_01, second_01, near_23), centroids, stat, declared=0.01)]
    goal = goal_call(rate, stat, *(along_z(stat, by) for by in (1, 2, 3)), bundles[0][1], across_01)
    across_23 = turn_back(hold(first_23, goal))

    second_23 = turn_back(hold(near_23, bundles[0][1]))
    bundles.append(expand((across_01, first_23, second_23), centroids, goal, declared=0.01))
    bundles.append(expand((across_23,), centroids, bundles[1][1]))
    expos, tops, points = zip(*bundles)
    goals = [goal, turn(goal), turn_back(goal), around(goal, 3)]
    factors = factor_call(rate, goals, tops)

    there = sums_call(per_device, 1, per_device, jnp.bfloat16, expos, points, factors)
    there = [exchange(a, ("lo",), lambda at: at ^ 1) for a in there]
    here = sums_call(per_device, 0, per_device, jnp.float32, expos, points, factors)
    out, mass = add_call(block // 2, *here, *there)
    return (out[None], mass)


def solution(mesh):
    pts, cells = (mesh.shape[name] for name in ("pts", "cells"))
    square = (pts, cells) == (8, 4)
    shape, names = ((2, 2, 2, cells), ("y", "x", "lo", "cells")) if square else ((pts, cells), ("pts", "cells"))
    fine = Mesh(mesh.devices.reshape(shape), names)
    spread = names[:-1]
    in_specs = (P(names, None), P(names), P("cells", None), P("cells"))
    out_specs = (P("cells", spread, None), P("cells", spread))

    def run(codes, exponents, centroids, counters):
        small = codes.size * 2 <= GATHER_BYTES and codes.shape[0] == 128 * pts * cells
        body = split_cells if square and small else split_points
        mapped = jax.shard_map(body, mesh=fine, in_specs=in_specs, out_specs=out_specs, check_vma=False)
        return mapped(codes, exponents, centroids, counters)

    return run
```

```python
import functools
import math

import jax
import jax.numpy as jnp
from jax import lax
from jax.experimental import pallas as pl
from jax.experimental.pallas import tpu as pltpu
from jax.sharding import Mesh, PartitionSpec as P

GATHER_BYTES = 8 << 20
VMEM_BYTES = 16 << 20


def to_points(codes, exponents):
    scaled = lax.shift_right_arithmetic(codes << 16, jnp.broadcast_to(exponents[:, None], codes.shape))
    return (scaled.astype(jnp.float32) * 2.0**-16).astype(jnp.bfloat16)


def split_points(codes, exponents, centroids, counters):
    local_rows = to_points(codes, exponents)
    points = lax.all_gather(local_rows, "cells", axis=0, tiled=True)
    beta = 4.0 / math.sqrt(points.shape[1])
    logits = (
        lax.dot_general(
            points, centroids, (((1,), (1,)), ((), ())), preferred_element_type=jnp.float32
        )
        * beta
    )
    inverse = lax.rsqrt(counters.astype(jnp.float32) + 1.0)
    top = lax.pmax(jnp.max(logits, axis=1), "cells")
    expo = jnp.exp(logits - top[:, None])
    total, novel = lax.psum(
        (jnp.sum(expo, axis=1), jnp.dot(expo, inverse, preferred_element_type=jnp.float32)), "cells"
    )
    weight = novel / total
    share = (expo * (weight / total)[:, None]).astype(jnp.bfloat16)
    mass_local = jnp.sum(share.astype(jnp.float32), axis=0)
    sums_local = lax.dot_general(
        share, points, (((0,), (0,)), ((), ())), preferred_element_type=jnp.float32
    )
    sums = lax.psum_scatter(sums_local, "pts", scatter_dimension=0, tiled=True)
    mass = lax.psum_scatter(mass_local, "pts", scatter_dimension=0, tiled=True)
    return (sums[None], mass[None])


def exchange(a, axes, partner):
    count = math.prod(lax.axis_size(axis) for axis in axes)
    return lax.ppermute(a, axes, [(partner(at), at) for at in range(count)])


def in_vmem(n):
    return [pl.BlockSpec(memory_space=pltpu.VMEM)] * n


def join(above, below, *after):
    def kernel(above, below, *refs):
        out = refs[-1]
        out[: above.shape[0], :] = above[...]
        out[above.shape[0] :, :] = below[...]

    return pl.pallas_call(
        kernel,
        in_specs=in_vmem(2 + len(after)),
        out_specs=in_vmem(1)[0],
        out_shape=jax.ShapeDtypeStruct((above.shape[0] + below.shape[0], above.shape[1]), above.dtype),
        compiler_params=pltpu.CompilerParams(vmem_limit_bytes=VMEM_BYTES),
    )(above, below, *after)


def beside(left, right, *after):
    def kernel(left, right, *refs):
        refs[-1][...] = jnp.concatenate([left[...], right[...]], axis=1)

    return pl.pallas_call(
        kernel,
        in_specs=in_vmem(2 + len(after)),
        out_specs=in_vmem(1)[0],
        out_shape=jax.ShapeDtypeStruct((left.shape[0], left.shape[1] + right.shape[1]), left.dtype),
        compiler_params=pltpu.CompilerParams(vmem_limit_bytes=VMEM_BYTES),
    )(left, right, *after)


def hold(a, *after, declared=0):
    def kernel(a, *refs):
        refs[-1][...] = a[...]

    return pl.pallas_call(
        kernel,
        in_specs=in_vmem(1 + len(after)),
        out_specs=in_vmem(1)[0],
        out_shape=jax.ShapeDtypeStruct(a.shape, a.dtype),
        compiler_params=pltpu.CompilerParams(vmem_limit_bytes=VMEM_BYTES),
        cost_estimate=pl.CostEstimate(flops=declared, bytes_accessed=0, transcendentals=0),
    )(a, *after)


def scores(cells, points):
    return lax.dot_general(cells, points, (((1,), (1,)), ((), ())), preferred_element_type=jnp.float32)


def chip_index():
    return lax.axis_index("y") * 2 + lax.axis_index("x")


def inverse_kernel(counters, *refs):
    inverse = refs[-1]
    for line in range(counters.shape[0]):
        row = lax.rsqrt(counters[line : line + 1, :].astype(jnp.float32) + 1.0)
        inverse[line * 128 : (line + 1) * 128, :] = jnp.broadcast_to(row, (128, 128)).T


def inverse_call(counters, *after):
    return pl.pallas_call(
        inverse_kernel,
        in_specs=in_vmem(1 + len(after)),
        out_specs=in_vmem(1)[0],
        out_shape=jax.ShapeDtypeStruct((counters.shape[0], 128), jnp.float32),
        compiler_params=pltpu.CompilerParams(vmem_limit_bytes=VMEM_BYTES),
        cost_estimate=pl.CostEstimate(flops=2 * 10**9, bytes_accessed=0, transcendentals=0),
    )(counters.reshape(-1, 128), *after)


def totals_kernel(rate, block, n, *refs):
    pieces, (cells, inverse), stats = refs[:n], refs[n : n + 2], refs[-1]
    every = jnp.concatenate([piece[...] for piece in pieces], axis=0)
    count = cells.shape[0]
    parts = []
    for at in range(0, count, block):
        here = slice(at, at + block)
        logits = scores(cells[here, :], every)
        top = jnp.max(logits, axis=0, keepdims=True)
        value = jnp.exp2((logits - top) * rate)
        scale = inverse[here, :]
        weighed = [
            jnp.sum(value[:, i : i + 128] * scale, axis=0, keepdims=True) for i in range(0, value.shape[1], 128)
        ]
        parts.append((top, jnp.sum(value, axis=0, keepdims=True), jnp.concatenate(weighed, axis=1)))
        while len(parts) > 1 and (at + block == count or len(parts) == 4):
            parts = [join_stats(rate, parts)]
    stats[...] = jnp.concatenate(parts[0], axis=0)


def join_stats(rate, parts):
    top = functools.reduce(jnp.maximum, [part[0] for part in parts])
    scales = [jnp.exp2((part[0] - top) * rate) for part in parts]
    return (top, *(sum(part[at] * scale for part, scale in zip(parts, scales)) for at in (1, 2)))


def totals_call(rate, block, pieces, cells, inverse, after=(), declared=1.0):
    n_points, width = sum(piece.shape[0] for piece in pieces), pieces[0].shape[1]
    n_cells = inverse.shape[0]
    args = (*pieces, cells, inverse, *after)
    return pl.pallas_call(
        functools.partial(totals_kernel, rate, block, len(pieces)),
        in_specs=in_vmem(len(args)),
        out_specs=in_vmem(1)[0],
        out_shape=jax.ShapeDtypeStruct((3, n_points), jnp.float32),
        compiler_params=pltpu.CompilerParams(vmem_limit_bytes=VMEM_BYTES),
        cost_estimate=pl.CostEstimate(
            flops=int(declared * 2 * n_cells * n_points * width),
            bytes_accessed=int(declared * 2 * n_cells * width),
            transcendentals=int(declared * n_cells * n_points),
        ),
    )(*args)


def goal_kernel(rate, *refs):
    stats, goal = refs[:4], refs[-1]
    for at in range(4):
        here = [stat[:, (at ^ by) * 128 : ((at ^ by) + 1) * 128] for by, stat in enumerate(stats)]
        top, total, novel = join_stats(rate, [(s[:1], s[1:2], s[2:]) for s in here])
        goal[:, at * 128 : (at + 1) * 128] = jnp.concatenate([top, novel / total / total], axis=0)


def goal_call(rate, *stats):
    return pl.pallas_call(
        functools.partial(goal_kernel, rate),
        in_specs=in_vmem(len(stats)),
        out_specs=in_vmem(1)[0],
        out_shape=jax.ShapeDtypeStruct((2, stats[0].shape[1]), jnp.float32),
        compiler_params=pltpu.CompilerParams(vmem_limit_bytes=VMEM_BYTES),
    )(*stats)


def factor_kernel(rate, n, *refs):
    goals, tops, factors = refs[:4], refs[4 : 4 + n], refs[4 + n :]
    rows = goals[0].shape[1] // 2
    spots = [(0, 0, 0), (0, 0, 1), (0, 0, 2), (0, 1, 0), (1, 0, 3), (1, 1, 1), (1, 1, 3), (2, 1, 2)]
    for at, (bundle, group, goal) in enumerate(spots):
        start = (at - (0, 4, 7)[bundle]) * rows
        mine, here = slice(group * rows, (group + 1) * rows), slice(start, start + rows)
        scale = jnp.exp2((tops[bundle][:, here] - goals[goal][:1, mine]) * rate)
        factors[bundle][:, here] = scale * goals[goal][1:, mine]


def factor_call(rate, goals, tops):
    return pl.pallas_call(
        functools.partial(factor_kernel, rate, len(tops)),
        in_specs=in_vmem(4 + len(tops)),
        out_specs=in_vmem(len(tops)),
        out_shape=[jax.ShapeDtypeStruct(top.shape, jnp.float32) for top in tops],
        compiler_params=pltpu.CompilerParams(vmem_limit_bytes=VMEM_BYTES),
    )(*goals, *tops)


def expo_kernel(rate, block, spots, *refs):
    pieces, cells, (expo, tops, points) = refs[: len(spots)], refs[len(spots)], refs[-3:]
    start = 0
    for piece, (first, rows) in zip(pieces, spots):
        points[start : start + rows, :] = piece[first : first + rows, :]
        start += rows
    count = expo.shape[0] // block
    chip = chip_index()
    for at in range(count):
        mine = pl.ds(pl.multiple_of((chip * count + at) * block, block), block)
        for part in range(0, points.shape[0], 256):
            some = slice(part, part + 256)
            logits = scores(cells[mine, :], points[some, :])
            top = jnp.max(logits, axis=0, keepdims=True)
            expo[at * block : (at + 1) * block, some] = jnp.exp2((logits - top) * rate).astype(jnp.bfloat16)
            tops[at : at + 1, some] = top


def expo_call(rate, block, count, pieces, cells, *after, declared=1.0):
    width = cells.shape[1]
    pieces, spots = zip(*((piece[0], piece[1:]) if isinstance(piece, tuple) else (piece, (0, len(piece))) for piece in pieces))
    n_points = sum(rows for _, rows in spots)
    return pl.pallas_call(
        functools.partial(expo_kernel, rate, block, spots),
        in_specs=in_vmem(len(pieces) + 1 + len(after)),
        out_specs=in_vmem(3),
        out_shape=[
            jax.ShapeDtypeStruct((count, n_points), jnp.bfloat16),
            jax.ShapeDtypeStruct((count // block, n_points), jnp.float32),
            jax.ShapeDtypeStruct((n_points, width), jnp.bfloat16),
        ],
        compiler_params=pltpu.CompilerParams(vmem_limit_bytes=VMEM_BYTES),
        cost_estimate=pl.CostEstimate(
            flops=int(declared * 2 * count * n_points * width),
            bytes_accessed=int(declared * 2 * (count * width + n_points * width + count * n_points)),
            transcendentals=int(declared * count * n_points),
        ),
    )(*pieces, cells, *after)


def weighed_sums(start, count, expos, points, factors):
    total = weight = None
    for expo, chunk, factor in zip(expos, points, factors):
        block = expo.shape[0] // factor.shape[0]
        shares, lanes = [], []
        for at in range(0, count, block):
            here = pl.ds(pl.multiple_of(start + at, block), block)
            share = expo[here, :].astype(jnp.float32) * factor[pl.ds((start + at) // block, 1), :]
            shares.append(share.astype(jnp.bfloat16))
            lanes.append(sum(share[:, i : i + 128] for i in range(0, share.shape[1], 128)))
        share, lanes = jnp.concatenate(shares, axis=0), jnp.concatenate(lanes, axis=0)
        part = jnp.dot(share, chunk[...], preferred_element_type=jnp.float32)
        total = part if total is None else total + part
        weight = lanes if weight is None else weight + lanes
    return total, jnp.sum(weight.T, axis=0, keepdims=True)


def sums_kernel(n, block, side, *refs):
    expos, points, factors, (sums, mass) = refs[:n], refs[n : 2 * n], refs[2 * n : 3 * n], refs[3 * n :]
    rows = sums.shape[0]
    first = (lax.axis_index("lo") ^ side) * rows
    for at in range(0, rows, block):
        here = slice(at, at + block)
        total, weight = weighed_sums(first + at, block, expos, points, factors)
        sums[here, :] = total.astype(sums.dtype)
        mass[:, here] = weight


def sums_call(block, side, rows, dtype, expos, points, factors):
    n = len(expos)
    n_points, width = points[0].shape
    return pl.pallas_call(
        functools.partial(sums_kernel, n, block, side),
        in_specs=in_vmem(3 * n),
        out_specs=in_vmem(2),
        out_shape=[jax.ShapeDtypeStruct((rows, width), dtype), jax.ShapeDtypeStruct((1, rows), jnp.float32)],
        compiler_params=pltpu.CompilerParams(vmem_limit_bytes=VMEM_BYTES),
        cost_estimate=pl.CostEstimate(
            flops=2 * rows * n * n_points * width,
            bytes_accessed=2 * n * n_points * (rows + width) + 4 * rows * width,
            transcendentals=0,
        ),
    )(*expos, *points, *factors)


def add_kernel(block, here, here_mass, there, there_mass, sums, mass, out, left):
    def copy(at):
        rows = pl.ds(at * block, block)
        return pltpu.make_async_copy(out.at[rows, :], sums.at[rows, :], left.at[at])

    count = here.shape[0] // block
    for at in range(count):
        rows = slice(at * block, (at + 1) * block)
        out[rows, :] = here[rows, :] + there[rows, :].astype(jnp.float32)
        copy(at).start(priority=at % 2)
    mass[...] = here_mass[...] + there_mass[...]
    for at in range(count):
        copy(at).wait()


def add_call(block, here, here_mass, there, there_mass):
    return pl.pallas_call(
        functools.partial(add_kernel, block),
        in_specs=in_vmem(4),
        out_specs=[pl.BlockSpec(memory_space=pltpu.HBM)] + in_vmem(1),
        out_shape=[
            jax.ShapeDtypeStruct(here.shape, jnp.float32),
            jax.ShapeDtypeStruct(here_mass.shape, jnp.float32),
        ],
        scratch_shapes=[
            pltpu.VMEM(here.shape, jnp.float32),
            pltpu.SemaphoreType.DMA((here.shape[0] // block,)),
        ],
        compiler_params=pltpu.CompilerParams(vmem_limit_bytes=VMEM_BYTES),
    )(here, here_mass, there, there_mass)


def split_cells(codes, exponents, centroids, counters):
    own = to_points(codes, exponents)
    rate = 4.0 / math.sqrt(own.shape[1]) * math.log2(math.e)
    plane = ("y", "x", "lo")

    turn = lambda a: exchange(a, plane, lambda at: at ^ (4 if at % 2 else 2))
    turn_back = lambda a: exchange(a, plane, lambda at: at ^ (2 if at % 2 else 4))
    along_z = lambda a, by: exchange(a, ("cells",), lambda at: at ^ by)
    around = lambda a, by: exchange(a, ("y", "x"), lambda at: at ^ by)

    per_device = centroids.shape[0] // 8
    block = per_device // 3

    near_1, near_2, near_3 = (along_z(own, by) for by in (1, 2, 3))
    inverse = inverse_call(counters)
    near_01 = join(own, near_1, inverse)
    held_01 = hold(near_01, declared=2 * 10**9)
    first_01 = turn(near_01)
    stats = [totals_call(rate, block, (held_01,), centroids, inverse)]
    second_01, across_01 = turn_back(hold(near_01, stats[0])), turn_back(hold(first_01, stats[0]))
    near_23 = join(near_2, near_3, *stats)
    stats.append(totals_call(rate, block, (near_23,), centroids, inverse, after=(first_01,)))
    first_23 = turn(near_23)
    stat = beside(*stats)
    expand = functools.partial(expo_call, rate, block, 2 * per_device)
    bundles = [expand((near_01, first_01, second_01, near_23), centroids, stat, declared=0.01)]
    goal = goal_call(rate, stat, *(along_z(stat, by) for by in (1, 2, 3)), bundles[0][1], across_01)
    across_23, second_23 = turn_back(hold(first_23, bundles[0][1])), turn_back(hold(near_23, goal))
    bundles.append(expand((across_01, first_23, across_23), centroids, goal, declared=0.01))
    bundles.append(expand((second_23,), centroids, bundles[1][1]))
    expos, tops, points = zip(*bundles)
    goals = [goal, turn(goal), turn_back(goal), around(goal, 3)]
    factors = factor_call(rate, goals, tops)

    there = sums_call(per_device, 1, per_device, jnp.bfloat16, expos, points, factors)
    there = [exchange(a, ("lo",), lambda at: at ^ 1) for a in there]
    here = sums_call(per_device, 0, per_device, jnp.float32, expos, points, factors)
    out, mass = add_call(block // 2, *here, *there)
    return (out[None], mass)


def solution(mesh):
    pts, cells = (mesh.shape[name] for name in ("pts", "cells"))
    square = (pts, cells) == (8, 4)
    shape, names = ((2, 2, 2, cells), ("y", "x", "lo", "cells")) if square else ((pts, cells), ("pts", "cells"))
    fine = Mesh(mesh.devices.reshape(shape), names)
    spread = names[:-1]
    in_specs = (P(names, None), P(names), P("cells", None), P("cells"))
    out_specs = (P("cells", spread, None), P("cells", spread))

    def run(codes, exponents, centroids, counters):
        small = codes.size * 2 <= GATHER_BYTES and codes.shape[0] == 128 * pts * cells
        body = split_cells if square and small else split_points
        mapped = jax.shard_map(body, mesh=fine, in_specs=in_specs, out_specs=out_specs, check_vma=False)
        return mapped(codes, exponents, centroids, counters)

    return run
```

```python
import functools
import math

import jax
import jax.numpy as jnp
from jax import lax
from jax.experimental import pallas as pl
from jax.experimental.pallas import tpu as pltpu
from jax.sharding import Mesh, PartitionSpec as P

GATHER_BYTES = 8 << 20
VMEM_BYTES = 16 << 20


def to_points(codes, exponents):
    scaled = lax.shift_right_arithmetic(codes << 16, jnp.broadcast_to(exponents[:, None], codes.shape))
    return (scaled.astype(jnp.float32) * 2.0**-16).astype(jnp.bfloat16)


def split_points(codes, exponents, centroids, counters):
    local_rows = to_points(codes, exponents)
    points = lax.all_gather(local_rows, "cells", axis=0, tiled=True)
    beta = 4.0 / math.sqrt(points.shape[1])
    logits = (
        lax.dot_general(
            points, centroids, (((1,), (1,)), ((), ())), preferred_element_type=jnp.float32
        )
        * beta
    )
    inverse = lax.rsqrt(counters.astype(jnp.float32) + 1.0)
    top = lax.pmax(jnp.max(logits, axis=1), "cells")
    expo = jnp.exp(logits - top[:, None])
    total, novel = lax.psum(
        (jnp.sum(expo, axis=1), jnp.dot(expo, inverse, preferred_element_type=jnp.float32)), "cells"
    )
    weight = novel / total
    share = (expo * (weight / total)[:, None]).astype(jnp.bfloat16)
    mass_local = jnp.sum(share.astype(jnp.float32), axis=0)
    sums_local = lax.dot_general(
        share, points, (((0,), (0,)), ((), ())), preferred_element_type=jnp.float32
    )
    sums = lax.psum_scatter(sums_local, "pts", scatter_dimension=0, tiled=True)
    mass = lax.psum_scatter(mass_local, "pts", scatter_dimension=0, tiled=True)
    return (sums[None], mass[None])


def exchange(a, axes, partner):
    count = math.prod(lax.axis_size(axis) for axis in axes)
    return lax.ppermute(a, axes, [(partner(at), at) for at in range(count)])


def in_vmem(n):
    return [pl.BlockSpec(memory_space=pltpu.VMEM)] * n


def join(above, below, *after):
    def kernel(above, below, *refs):
        out = refs[-1]
        out[: above.shape[0], :] = above[...]
        out[above.shape[0] :, :] = below[...]

    return pl.pallas_call(
        kernel,
        in_specs=in_vmem(2 + len(after)),
        out_specs=in_vmem(1)[0],
        out_shape=jax.ShapeDtypeStruct((above.shape[0] + below.shape[0], above.shape[1]), above.dtype),
        compiler_params=pltpu.CompilerParams(vmem_limit_bytes=VMEM_BYTES),
    )(above, below, *after)


def beside(left, right, *after):
    def kernel(left, right, *refs):
        refs[-1][...] = jnp.concatenate([left[...], right[...]], axis=1)

    return pl.pallas_call(
        kernel,
        in_specs=in_vmem(2 + len(after)),
        out_specs=in_vmem(1)[0],
        out_shape=jax.ShapeDtypeStruct((left.shape[0], left.shape[1] + right.shape[1]), left.dtype),
        compiler_params=pltpu.CompilerParams(vmem_limit_bytes=VMEM_BYTES),
    )(left, right, *after)


def hold(a, *after, declared=0):
    def kernel(a, *refs):
        refs[-1][...] = a[...]

    return pl.pallas_call(
        kernel,
        in_specs=in_vmem(1 + len(after)),
        out_specs=in_vmem(1)[0],
        out_shape=jax.ShapeDtypeStruct(a.shape, a.dtype),
        compiler_params=pltpu.CompilerParams(vmem_limit_bytes=VMEM_BYTES),
        cost_estimate=pl.CostEstimate(flops=declared, bytes_accessed=0, transcendentals=0),
    )(a, *after)


def scores(cells, points):
    return lax.dot_general(cells, points, (((1,), (1,)), ((), ())), preferred_element_type=jnp.float32)


def chip_index():
    return lax.axis_index("y") * 2 + lax.axis_index("x")


def inverse_kernel(counters, *refs):
    inverse = refs[-1]
    for line in range(counters.shape[0]):
        row = lax.rsqrt(counters[line : line + 1, :].astype(jnp.float32) + 1.0)
        inverse[line * 128 : (line + 1) * 128, :] = jnp.broadcast_to(row, (128, 128)).T


def inverse_call(counters, *after):
    return pl.pallas_call(
        inverse_kernel,
        in_specs=in_vmem(1 + len(after)),
        out_specs=in_vmem(1)[0],
        out_shape=jax.ShapeDtypeStruct((counters.shape[0], 128), jnp.float32),
        compiler_params=pltpu.CompilerParams(vmem_limit_bytes=VMEM_BYTES),
        cost_estimate=pl.CostEstimate(flops=2 * 10**9, bytes_accessed=0, transcendentals=0),
    )(counters.reshape(-1, 128), *after)


def totals_kernel(rate, block, n, *refs):
    pieces, (cells, inverse), stats = refs[:n], refs[n : n + 2], refs[-1]
    every = jnp.concatenate([piece[...] for piece in pieces], axis=0)
    count = cells.shape[0]
    parts = []
    for at in range(0, count, block):
        here = slice(at, at + block)
        logits = scores(cells[here, :], every)
        top = jnp.max(logits, axis=0, keepdims=True)
        value = jnp.exp2((logits - top) * rate)
        scale = inverse[here, :]
        weighed = [
            jnp.sum(value[:, i : i + 128] * scale, axis=0, keepdims=True) for i in range(0, value.shape[1], 128)
        ]
        parts.append((top, jnp.sum(value, axis=0, keepdims=True), jnp.concatenate(weighed, axis=1)))
        while len(parts) > 1 and (at + block == count or len(parts) == 4):
            parts = [join_stats(rate, parts)]
    stats[...] = jnp.concatenate(parts[0], axis=0)


def join_stats(rate, parts):
    top = functools.reduce(jnp.maximum, [part[0] for part in parts])
    scales = [jnp.exp2((part[0] - top) * rate) for part in parts]
    return (top, *(sum(part[at] * scale for part, scale in zip(parts, scales)) for at in (1, 2)))


def totals_call(rate, block, pieces, cells, inverse, after=(), declared=1.0):
    n_points, width = sum(piece.shape[0] for piece in pieces), pieces[0].shape[1]
    n_cells = inverse.shape[0]
    args = (*pieces, cells, inverse, *after)
    return pl.pallas_call(
        functools.partial(totals_kernel, rate, block, len(pieces)),
        in_specs=in_vmem(len(args)),
        out_specs=in_vmem(1)[0],
        out_shape=jax.ShapeDtypeStruct((3, n_points), jnp.float32),
        compiler_params=pltpu.CompilerParams(vmem_limit_bytes=VMEM_BYTES),
        cost_estimate=pl.CostEstimate(
            flops=int(declared * 2 * n_cells * n_points * width),
            bytes_accessed=int(declared * 2 * n_cells * width),
            transcendentals=int(declared * n_cells * n_points),
        ),
    )(*args)


def goal_kernel(rate, *refs):
    stats, goal = refs[:4], refs[-1]
    for at in range(4):
        here = [stat[:, (at ^ by) * 128 : ((at ^ by) + 1) * 128] for by, stat in enumerate(stats)]
        top, total, novel = join_stats(rate, [(s[:1], s[1:2], s[2:]) for s in here])
        goal[:, at * 128 : (at + 1) * 128] = jnp.concatenate([top, novel / total / total], axis=0)


def goal_call(rate, *stats):
    return pl.pallas_call(
        functools.partial(goal_kernel, rate),
        in_specs=in_vmem(len(stats)),
        out_specs=in_vmem(1)[0],
        out_shape=jax.ShapeDtypeStruct((2, stats[0].shape[1]), jnp.float32),
        compiler_params=pltpu.CompilerParams(vmem_limit_bytes=VMEM_BYTES),
    )(*stats)


def factor_kernel(rate, n, *refs):
    goals, tops, factors = refs[:4], refs[4 : 4 + n], refs[4 + n :]
    rows = goals[0].shape[1] // 2
    spots = [(0, 0, 0), (0, 0, 1), (0, 0, 2), (0, 1, 0), (1, 0, 3), (1, 1, 1), (1, 1, 2), (2, 1, 3)]
    for at, (bundle, group, goal) in enumerate(spots):
        start = (at - (0, 4, 7)[bundle]) * rows
        mine, here = slice(group * rows, (group + 1) * rows), slice(start, start + rows)
        scale = jnp.exp2((tops[bundle][:, here] - goals[goal][:1, mine]) * rate)
        factors[bundle][:, here] = scale * goals[goal][1:, mine]


def factor_call(rate, goals, tops):
    return pl.pallas_call(
        functools.partial(factor_kernel, rate, len(tops)),
        in_specs=in_vmem(4 + len(tops)),
        out_specs=in_vmem(len(tops)),
        out_shape=[jax.ShapeDtypeStruct(top.shape, jnp.float32) for top in tops],
        compiler_params=pltpu.CompilerParams(vmem_limit_bytes=VMEM_BYTES),
    )(*goals, *tops)


def expo_kernel(rate, block, spots, *refs):
    pieces, cells, (expo, tops, points) = refs[: len(spots)], refs[len(spots)], refs[-3:]
    start = 0
    for piece, (first, rows) in zip(pieces, spots):
        points[start : start + rows, :] = piece[first : first + rows, :]
        start += rows
    count = expo.shape[0] // block
    chip = chip_index()
    for at in range(count):
        mine = pl.ds(pl.multiple_of((chip * count + at) * block, block), block)
        for part in range(0, points.shape[0], 256):
            some = slice(part, part + 256)
            logits = scores(cells[mine, :], points[some, :])
            top = jnp.max(logits, axis=0, keepdims=True)
            expo[at * block : (at + 1) * block, some] = jnp.exp2((logits - top) * rate).astype(jnp.bfloat16)
            tops[at : at + 1, some] = top


def expo_call(rate, block, count, pieces, cells, *after, declared=1.0):
    width = cells.shape[1]
    pieces, spots = zip(*((piece[0], piece[1:]) if isinstance(piece, tuple) else (piece, (0, len(piece))) for piece in pieces))
    n_points = sum(rows for _, rows in spots)
    return pl.pallas_call(
        functools.partial(expo_kernel, rate, block, spots),
        in_specs=in_vmem(len(pieces) + 1 + len(after)),
        out_specs=in_vmem(3),
        out_shape=[
            jax.ShapeDtypeStruct((count, n_points), jnp.bfloat16),
            jax.ShapeDtypeStruct((count // block, n_points), jnp.float32),
            jax.ShapeDtypeStruct((n_points, width), jnp.bfloat16),
        ],
        compiler_params=pltpu.CompilerParams(vmem_limit_bytes=VMEM_BYTES),
        cost_estimate=pl.CostEstimate(
            flops=int(declared * 2 * count * n_points * width),
            bytes_accessed=int(declared * 2 * (count * width + n_points * width + count * n_points)),
            transcendentals=int(declared * count * n_points),
        ),
    )(*pieces, cells, *after)


def weighed_sums(start, count, expos, points, factors):
    total = weight = None
    for expo, chunk, factor in zip(expos, points, factors):
        block = expo.shape[0] // factor.shape[0]
        shares, lanes = [], []
        for at in range(0, count, block):
            here = pl.ds(pl.multiple_of(start + at, block), block)
            share = expo[here, :].astype(jnp.float32) * factor[pl.ds((start + at) // block, 1), :]
            shares.append(share.astype(jnp.bfloat16))
            lanes.append(sum(share[:, i : i + 128] for i in range(0, share.shape[1], 128)))
        share, lanes = jnp.concatenate(shares, axis=0), jnp.concatenate(lanes, axis=0)
        part = jnp.dot(share, chunk[...], preferred_element_type=jnp.float32)
        total = part if total is None else total + part
        weight = lanes if weight is None else weight + lanes
    return total, jnp.sum(weight.T, axis=0, keepdims=True)


def sums_kernel(n, side, *refs):
    expos, points, factors, outs = refs[:n], refs[n : 2 * n], refs[2 * n : 3 * n], refs[3 * n :]
    rows, width = expos[0].shape[0] // 2, points[0].shape[1]
    first = (lax.axis_index("lo") ^ side) * rows
    total, weight = weighed_sums(first, rows, expos, points, factors)
    outs[0][:rows, :] = total.astype(outs[0].dtype)
    if side:
        high = weight.astype(jnp.bfloat16).astype(jnp.float32)
        empty = jnp.zeros((1, -rows % width), jnp.float32)
        lines = [
            half[:, at : at + width]
            for half in (jnp.concatenate([part, empty], axis=1) for part in (high, weight - high))
            for at in range(0, half.shape[1], width)
        ]
        lines.append(jnp.zeros((16 - len(lines), width), jnp.float32))
        outs[0][rows:, :] = jnp.concatenate(lines, axis=0).astype(jnp.bfloat16)
    else:
        outs[1][...] = weight


def sums_call(side, rows, expos, points, factors):
    n = len(expos)
    width = points[0].shape[1]
    n_points = sum(chunk.shape[0] for chunk in points)
    out_shape = [jax.ShapeDtypeStruct((rows + 16, width), jnp.bfloat16)]
    if not side:
        out_shape = [jax.ShapeDtypeStruct((rows, width), jnp.float32), jax.ShapeDtypeStruct((1, rows), jnp.float32)]
    return pl.pallas_call(
        functools.partial(sums_kernel, n, side),
        in_specs=in_vmem(3 * n),
        out_specs=in_vmem(len(out_shape)),
        out_shape=out_shape,
        compiler_params=pltpu.CompilerParams(vmem_limit_bytes=VMEM_BYTES),
        cost_estimate=pl.CostEstimate(
            flops=2 * rows * n_points * width,
            bytes_accessed=2 * n_points * (rows + width) + 4 * rows * width,
            transcendentals=0,
        ),
    )(*expos, *points, *factors)


def add_kernel(block, here, here_mass, there, sums, mass, out, left):
    def copy(at):
        rows = pl.ds(at * block, block)
        return pltpu.make_async_copy(out.at[rows, :], sums.at[rows, :], left.at[at])

    count, width = here.shape[0] // block, here.shape[1]
    for at in range(count):
        rows = slice(at * block, (at + 1) * block)
        out[rows, :] = here[rows, :] + there[rows, :].astype(jnp.float32)
        copy(at).start(priority=at % 2)
    lines = there[here.shape[0] :, :].astype(jnp.float32)
    n = -(-here.shape[0] // width)
    parts = [jnp.concatenate([lines[at : at + 1, :] for at in range(i * n, i * n + n)], axis=1) for i in range(2)]
    mass[...] = here_mass[...] + (parts[0] + parts[1])[:, : here.shape[0]]
    for at in range(count):
        copy(at).wait()


def add_call(block, here, here_mass, there):
    return pl.pallas_call(
        functools.partial(add_kernel, block),
        in_specs=in_vmem(3),
        out_specs=[pl.BlockSpec(memory_space=pltpu.HBM)] + in_vmem(1),
        out_shape=[
            jax.ShapeDtypeStruct(here.shape, jnp.float32),
            jax.ShapeDtypeStruct(here_mass.shape, jnp.float32),
        ],
        scratch_shapes=[
            pltpu.VMEM(here.shape, jnp.float32),
            pltpu.SemaphoreType.DMA((here.shape[0] // block,)),
        ],
        compiler_params=pltpu.CompilerParams(vmem_limit_bytes=VMEM_BYTES),
    )(here, here_mass, there)


def split_cells(codes, exponents, centroids, counters):
    own = to_points(codes, exponents)
    rate = 4.0 / math.sqrt(own.shape[1]) * math.log2(math.e)
    plane = ("y", "x", "lo")

    turn = lambda a: exchange(a, plane, lambda at: at ^ (4 if at % 2 else 2))
    turn_back = lambda a: exchange(a, plane, lambda at: at ^ (2 if at % 2 else 4))
    along_z = lambda a, by: exchange(a, ("cells",), lambda at: at ^ by)
    around = lambda a, by: exchange(a, ("y", "x"), lambda at: at ^ by)

    per_device = centroids.shape[0] // 8
    block = per_device // 3

    near_1, near_2, near_3 = (along_z(own, by) for by in (1, 2, 3))
    inverse = inverse_call(counters)
    near_01 = join(own, near_1, inverse)
    held_01 = hold(near_01, declared=2 * 10**9)
    first_01 = turn(near_01)
    stats = [totals_call(rate, block, (held_01,), centroids, inverse)]
    second_01, across_01 = turn_back(hold(near_01, stats[0])), turn_back(hold(first_01, stats[0]))
    near_23 = join(near_2, near_3, *stats)
    stats.append(totals_call(rate, block, (near_23,), centroids, inverse, after=(first_01,)))
    first_23 = turn(near_23)
    stat = beside(*stats)
    expand = functools.partial(expo_call, rate, block, 2 * per_device)
    bundles = [expand((near_01, first_01, second_01, near_23), centroids, stat, declared=0.01)]
    goal = goal_call(rate, stat, *(along_z(stat, by) for by in (1, 2, 3)), bundles[0][1], across_01)
    across_23 = turn_back(hold(first_23, goal))

    second_23 = turn_back(hold(near_23, bundles[0][1]))
    bundles.append(expand((across_01, first_23, second_23), centroids, goal, declared=0.01))
    bundles.append(expand((across_23,), centroids, bundles[1][1]))
    expos, tops, points = zip(*bundles)
    goals = [goal, turn(goal), turn_back(goal), around(goal, 3)]
    factors = factor_call(rate, goals, tops)

    (there,) = sums_call(1, per_device, expos, points, factors)
    there = exchange(there, ("lo",), lambda at: at ^ 1)
    here = sums_call(0, per_device, expos, points, factors)
    out, mass = add_call(block // 2, *here, there)
    return (out[None], mass)


def solution(mesh):
    pts, cells = (mesh.shape[name] for name in ("pts", "cells"))
    square = (pts, cells) == (8, 4)
    shape, names = ((2, 2, 2, cells), ("y", "x", "lo", "cells")) if square else ((pts, cells), ("pts", "cells"))
    fine = Mesh(mesh.devices.reshape(shape), names)
    spread = names[:-1]
    in_specs = (P(names, None), P(names), P("cells", None), P("cells"))
    out_specs = (P("cells", spread, None), P("cells", spread))

    def run(codes, exponents, centroids, counters):
        small = codes.size * 2 <= GATHER_BYTES and codes.shape[0] == 128 * pts * cells
        body = split_cells if square and small else split_points
        mapped = jax.shard_map(body, mesh=fine, in_specs=in_specs, out_specs=out_specs, check_vma=False)
        return mapped(codes, exponents, centroids, counters)

    return run
```

```python
import functools
import math

import jax
import jax.numpy as jnp
from jax import lax
from jax.experimental import pallas as pl
from jax.experimental.pallas import tpu as pltpu
from jax.sharding import Mesh, PartitionSpec as P

GATHER_BYTES = 8 << 20
VMEM_BYTES = 16 << 20


def to_points(codes, exponents):
    scaled = lax.shift_right_arithmetic(codes << 16, jnp.broadcast_to(exponents[:, None], codes.shape))
    return (scaled.astype(jnp.float32) * 2.0**-16).astype(jnp.bfloat16)


def split_points(codes, exponents, centroids, counters):
    local_rows = to_points(codes, exponents)
    points = lax.all_gather(local_rows, "cells", axis=0, tiled=True)
    beta = 4.0 / math.sqrt(points.shape[1])
    logits = (
        lax.dot_general(
            points, centroids, (((1,), (1,)), ((), ())), preferred_element_type=jnp.float32
        )
        * beta
    )
    inverse = lax.rsqrt(counters.astype(jnp.float32) + 1.0)
    top = lax.pmax(jnp.max(logits, axis=1), "cells")
    expo = jnp.exp(logits - top[:, None])
    total, novel = lax.psum(
        (jnp.sum(expo, axis=1), jnp.dot(expo, inverse, preferred_element_type=jnp.float32)), "cells"
    )
    weight = novel / total
    share = (expo * (weight / total)[:, None]).astype(jnp.bfloat16)
    mass_local = jnp.sum(share.astype(jnp.float32), axis=0)
    sums_local = lax.dot_general(
        share, points, (((0,), (0,)), ((), ())), preferred_element_type=jnp.float32
    )
    sums = lax.psum_scatter(sums_local, "pts", scatter_dimension=0, tiled=True)
    mass = lax.psum_scatter(mass_local, "pts", scatter_dimension=0, tiled=True)
    return (sums[None], mass[None])


def exchange(a, axes, partner):
    count = math.prod(lax.axis_size(axis) for axis in axes)
    return lax.ppermute(a, axes, [(partner(at), at) for at in range(count)])


def in_vmem(n):
    return [pl.BlockSpec(memory_space=pltpu.VMEM)] * n


def join(above, below, *after):
    def kernel(above, below, *refs):
        out = refs[-1]
        out[: above.shape[0], :] = above[...]
        out[above.shape[0] :, :] = below[...]

    return pl.pallas_call(
        kernel,
        in_specs=in_vmem(2 + len(after)),
        out_specs=in_vmem(1)[0],
        out_shape=jax.ShapeDtypeStruct((above.shape[0] + below.shape[0], above.shape[1]), above.dtype),
        compiler_params=pltpu.CompilerParams(vmem_limit_bytes=VMEM_BYTES),
    )(above, below, *after)


def beside(left, right, *after):
    def kernel(left, right, *refs):
        refs[-1][...] = jnp.concatenate([left[...], right[...]], axis=1)

    return pl.pallas_call(
        kernel,
        in_specs=in_vmem(2 + len(after)),
        out_specs=in_vmem(1)[0],
        out_shape=jax.ShapeDtypeStruct((left.shape[0], left.shape[1] + right.shape[1]), left.dtype),
        compiler_params=pltpu.CompilerParams(vmem_limit_bytes=VMEM_BYTES),
    )(left, right, *after)


def hold(a, *after, declared=0):
    def kernel(a, *refs):
        refs[-1][...] = a[...]

    return pl.pallas_call(
        kernel,
        in_specs=in_vmem(1 + len(after)),
        out_specs=in_vmem(1)[0],
        out_shape=jax.ShapeDtypeStruct(a.shape, a.dtype),
        compiler_params=pltpu.CompilerParams(vmem_limit_bytes=VMEM_BYTES),
        cost_estimate=pl.CostEstimate(flops=declared, bytes_accessed=0, transcendentals=0),
    )(a, *after)


def scores(cells, points):
    return lax.dot_general(cells, points, (((1,), (1,)), ((), ())), preferred_element_type=jnp.float32)


def chip_index():
    return lax.axis_index("y") * 2 + lax.axis_index("x")


def inverse_kernel(counters, *refs):
    inverse = refs[-1]
    for line in range(counters.shape[0]):
        row = lax.rsqrt(counters[line : line + 1, :].astype(jnp.float32) + 1.0)
        inverse[line * 128 : (line + 1) * 128, :] = jnp.broadcast_to(row, (128, 128)).T


def inverse_call(counters, *after):
    return pl.pallas_call(
        inverse_kernel,
        in_specs=in_vmem(1 + len(after)),
        out_specs=in_vmem(1)[0],
        out_shape=jax.ShapeDtypeStruct((counters.shape[0], 128), jnp.float32),
        compiler_params=pltpu.CompilerParams(vmem_limit_bytes=VMEM_BYTES),
        cost_estimate=pl.CostEstimate(flops=2 * 10**9, bytes_accessed=0, transcendentals=0),
    )(counters.reshape(-1, 128), *after)


def totals_kernel(rate, block, n, *refs):
    pieces, (cells, inverse), stats = refs[:n], refs[n : n + 2], refs[-1]
    every = jnp.concatenate([piece[...] for piece in pieces], axis=0)
    count = cells.shape[0]
    parts = []
    for at in range(0, count, block):
        here = slice(at, at + block)
        logits = scores(cells[here, :], every)
        top = jnp.max(logits, axis=0, keepdims=True)
        value = jnp.exp2((logits - top) * rate)
        scale = inverse[here, :]
        weighed = [
            jnp.sum(value[:, i : i + 128] * scale, axis=0, keepdims=True) for i in range(0, value.shape[1], 128)
        ]
        parts.append((top, jnp.sum(value, axis=0, keepdims=True), jnp.concatenate(weighed, axis=1)))
        while len(parts) > 1 and (at + block == count or len(parts) == 4):
            parts = [join_stats(rate, parts)]
    stats[...] = jnp.concatenate(parts[0], axis=0)


def join_stats(rate, parts):
    top = functools.reduce(jnp.maximum, [part[0] for part in parts])
    scales = [jnp.exp2((part[0] - top) * rate) for part in parts]
    return (top, *(sum(part[at] * scale for part, scale in zip(parts, scales)) for at in (1, 2)))


def totals_call(rate, block, pieces, cells, inverse, after=(), declared=1.0):
    n_points, width = sum(piece.shape[0] for piece in pieces), pieces[0].shape[1]
    n_cells = inverse.shape[0]
    args = (*pieces, cells, inverse, *after)
    return pl.pallas_call(
        functools.partial(totals_kernel, rate, block, len(pieces)),
        in_specs=in_vmem(len(args)),
        out_specs=in_vmem(1)[0],
        out_shape=jax.ShapeDtypeStruct((3, n_points), jnp.float32),
        compiler_params=pltpu.CompilerParams(vmem_limit_bytes=VMEM_BYTES),
        cost_estimate=pl.CostEstimate(
            flops=int(declared * 2 * n_cells * n_points * width),
            bytes_accessed=int(declared * 2 * n_cells * width),
            transcendentals=int(declared * n_cells * n_points),
        ),
    )(*args)


def goal_kernel(rate, *refs):
    stats, goal = refs[:4], refs[-1]
    for at in range(4):
        here = [stat[:, (at ^ by) * 128 : ((at ^ by) + 1) * 128] for by, stat in enumerate(stats)]
        top, total, novel = join_stats(rate, [(s[:1], s[1:2], s[2:]) for s in here])
        goal[:, at * 128 : (at + 1) * 128] = jnp.concatenate([top, novel / total / total], axis=0)


def goal_call(rate, *stats):
    return pl.pallas_call(
        functools.partial(goal_kernel, rate),
        in_specs=in_vmem(len(stats)),
        out_specs=in_vmem(1)[0],
        out_shape=jax.ShapeDtypeStruct((2, stats[0].shape[1]), jnp.float32),
        compiler_params=pltpu.CompilerParams(vmem_limit_bytes=VMEM_BYTES),
    )(*stats)


def factor_kernel(rate, n, *refs):
    goals, tops, factors = refs[:4], refs[4 : 4 + n], refs[4 + n :]
    rows = goals[0].shape[1] // 2
    spots = [(0, 0, 0), (0, 0, 1), (0, 0, 2), (0, 1, 0), (1, 0, 3), (1, 1, 1), (1, 1, 2), (2, 1, 3)]
    for at, (bundle, group, goal) in enumerate(spots):
        start = (at - (0, 4, 7)[bundle]) * rows
        mine, here = slice(group * rows, (group + 1) * rows), slice(start, start + rows)
        scale = jnp.exp2((tops[bundle][:, here] - goals[goal][:1, mine]) * rate)
        factors[bundle][:, here] = scale * goals[goal][1:, mine]


def factor_call(rate, goals, tops):
    return pl.pallas_call(
        functools.partial(factor_kernel, rate, len(tops)),
        in_specs=in_vmem(4 + len(tops)),
        out_specs=in_vmem(len(tops)),
        out_shape=[jax.ShapeDtypeStruct(top.shape, jnp.float32) for top in tops],
        compiler_params=pltpu.CompilerParams(vmem_limit_bytes=VMEM_BYTES),
    )(*goals, *tops)


def expo_kernel(rate, block, spots, *refs):
    pieces, cells, (expo, tops, points) = refs[: len(spots)], refs[len(spots)], refs[-3:]
    start = 0
    for piece, (first, rows) in zip(pieces, spots):
        points[start : start + rows, :] = piece[first : first + rows, :]
        start += rows
    count = expo.shape[0] // block
    chip = chip_index()
    for at in range(count):
        mine = pl.ds(pl.multiple_of((chip * count + at) * block, block), block)
        for part in range(0, points.shape[0], 256):
            some = slice(part, part + 256)
            logits = scores(cells[mine, :], points[some, :])
            top = jnp.max(logits, axis=0, keepdims=True)
            expo[at * block : (at + 1) * block, some] = jnp.exp2((logits - top) * rate).astype(jnp.bfloat16)
            tops[at : at + 1, some] = top


def expo_call(rate, block, count, pieces, cells, *after, declared=1.0):
    width = cells.shape[1]
    pieces, spots = zip(*((piece[0], piece[1:]) if isinstance(piece, tuple) else (piece, (0, len(piece))) for piece in pieces))
    n_points = sum(rows for _, rows in spots)
    return pl.pallas_call(
        functools.partial(expo_kernel, rate, block, spots),
        in_specs=in_vmem(len(pieces) + 1 + len(after)),
        out_specs=in_vmem(3),
        out_shape=[
            jax.ShapeDtypeStruct((count, n_points), jnp.bfloat16),
            jax.ShapeDtypeStruct((count // block, n_points), jnp.float32),
            jax.ShapeDtypeStruct((n_points, width), jnp.bfloat16),
        ],
        compiler_params=pltpu.CompilerParams(vmem_limit_bytes=VMEM_BYTES),
        cost_estimate=pl.CostEstimate(
            flops=int(declared * 2 * count * n_points * width),
            bytes_accessed=int(declared * 2 * (count * width + n_points * width + count * n_points)),
            transcendentals=int(declared * count * n_points),
        ),
    )(*pieces, cells, *after)


def weighed_sums(start, count, expos, points, factors):
    total = weight = None
    for expo, chunk, factor in zip(expos, points, factors):
        block = expo.shape[0] // factor.shape[0]
        shares, lanes = [], []
        for at in range(0, count, block):
            here = pl.ds(pl.multiple_of(start + at, block), block)
            share = expo[here, :].astype(jnp.float32) * factor[pl.ds((start + at) // block, 1), :]
            shares.append(share.astype(jnp.bfloat16))
            lanes.append(sum(share[:, i : i + 128] for i in range(0, share.shape[1], 128)))
        share, lanes = jnp.concatenate(shares, axis=0), jnp.concatenate(lanes, axis=0)
        part = jnp.dot(share, chunk[...], preferred_element_type=jnp.float32)
        total = part if total is None else total + part
        weight = lanes if weight is None else weight + lanes
    return total, jnp.sum(weight.T, axis=0, keepdims=True)


def sums_kernel(n, block, side, *refs):
    expos, points, factors, (sums, mass) = refs[:n], refs[n : 2 * n], refs[2 * n : 3 * n], refs[3 * n :]
    rows = sums.shape[0]
    first = (lax.axis_index("lo") ^ side) * rows
    for at in range(0, rows, block):
        here = slice(at, at + block)
        total, weight = weighed_sums(first + at, block, expos, points, factors)
        sums[here, :] = total.astype(sums.dtype)
        mass[:, here] = weight


def sums_call(block, side, rows, dtype, expos, points, factors):
    n = len(expos)
    n_points, width = points[0].shape
    return pl.pallas_call(
        functools.partial(sums_kernel, n, block, side),
        in_specs=in_vmem(3 * n),
        out_specs=in_vmem(2),
        out_shape=[jax.ShapeDtypeStruct((rows, width), dtype), jax.ShapeDtypeStruct((1, rows), jnp.float32)],
        compiler_params=pltpu.CompilerParams(vmem_limit_bytes=VMEM_BYTES),
        cost_estimate=pl.CostEstimate(
            flops=2 * rows * n * n_points * width,
            bytes_accessed=2 * n * n_points * (rows + width) + 4 * rows * width,
            transcendentals=0,
        ),
    )(*expos, *points, *factors)


def add_kernel(block, here, here_mass, there, there_mass, sums, mass, out, left):
    def copy(at):
        rows = pl.ds(at * block, block)
        return pltpu.make_async_copy(out.at[rows, :], sums.at[rows, :], left.at[at])

    count = here.shape[0] // block
    for at in range(count):
        rows = slice(at * block, (at + 1) * block)
        out[rows, :] = here[rows, :] + there[rows, :].astype(jnp.float32)
        copy(at).start(priority=at % 2)
    mass[...] = here_mass[...] + there_mass[...]
    for at in range(count):
        copy(at).wait()


def add_call(block, here, here_mass, there, there_mass):
    return pl.pallas_call(
        functools.partial(add_kernel, block),
        in_specs=in_vmem(4),
        out_specs=[pl.BlockSpec(memory_space=pltpu.HBM)] + in_vmem(1),
        out_shape=[
            jax.ShapeDtypeStruct(here.shape, jnp.float32),
            jax.ShapeDtypeStruct(here_mass.shape, jnp.float32),
        ],
        scratch_shapes=[
            pltpu.VMEM(here.shape, jnp.float32),
            pltpu.SemaphoreType.DMA((here.shape[0] // block,)),
        ],
        compiler_params=pltpu.CompilerParams(vmem_limit_bytes=VMEM_BYTES),
    )(here, here_mass, there, there_mass)


def split_cells(codes, exponents, centroids, counters):
    own = to_points(codes, exponents)
    rate = 4.0 / math.sqrt(own.shape[1]) * math.log2(math.e)
    plane = ("y", "x", "lo")

    turn = lambda a: exchange(a, plane, lambda at: at ^ (4 if at % 2 else 2))
    turn_back = lambda a: exchange(a, plane, lambda at: at ^ (2 if at % 2 else 4))
    along_z = lambda a, by: exchange(a, ("cells",), lambda at: at ^ by)
    around = lambda a, by: exchange(a, ("y", "x"), lambda at: at ^ by)

    per_device = centroids.shape[0] // 8
    block = per_device // 3

    near_1, near_2, near_3 = (along_z(own, by) for by in (1, 2, 3))
    inverse = inverse_call(counters)
    near_01 = join(own, near_1, inverse)
    held_01 = hold(near_01, declared=2 * 10**9)
    first_01 = turn(near_01)
    stats = [totals_call(rate, block, (held_01,), centroids, inverse)]
    second_01 = turn_back(hold(near_01, stats[0]))
    near_23 = join(near_2, near_3, *stats)
    stats.append(totals_call(rate, block, (near_23,), centroids, inverse, after=(first_01,)))
    first_23 = turn(near_23)
    second_23 = turn_back(near_23)
    stat = beside(*stats)
    expand = functools.partial(expo_call, rate, block, 2 * per_device)
    bundles = [expand((near_01, first_01, second_01, near_23), centroids, stat, declared=0.01)]
    goal = goal_call(rate, stat, *(along_z(stat, by) for by in (1, 2, 3)), bundles[0][1])
    across_01, across_23 = turn(hold(second_01, bundles[0][1])), turn_back(hold(first_23, goal))
    bundles.append(expand((across_01, first_23, second_23), centroids, goal, declared=0.01))
    bundles.append(expand((across_23,), centroids, bundles[1][1]))
    expos, tops, points = zip(*bundles)
    goals = [goal, turn(goal), turn_back(goal), around(goal, 3)]
    factors = factor_call(rate, goals, tops)

    there = sums_call(per_device, 1, per_device, jnp.bfloat16, expos, points, factors)
    there = [exchange(a, ("lo",), lambda at: at ^ 1) for a in there]
    here = sums_call(per_device, 0, per_device, jnp.float32, expos, points, factors)
    out, mass = add_call(block // 2, *here, *there)
    return (out[None], mass)


def solution(mesh):
    pts, cells = (mesh.shape[name] for name in ("pts", "cells"))
    square = (pts, cells) == (8, 4)
    shape, names = ((2, 2, 2, cells), ("y", "x", "lo", "cells")) if square else ((pts, cells), ("pts", "cells"))
    fine = Mesh(mesh.devices.reshape(shape), names)
    spread = names[:-1]
    in_specs = (P(names, None), P(names), P("cells", None), P("cells"))
    out_specs = (P("cells", spread, None), P("cells", spread))

    def run(codes, exponents, centroids, counters):
        small = codes.size * 2 <= GATHER_BYTES and codes.shape[0] == 128 * pts * cells
        body = split_cells if square and small else split_points
        mapped = jax.shard_map(body, mesh=fine, in_specs=in_specs, out_specs=out_specs, check_vma=False)
        return mapped(codes, exponents, centroids, counters)

    return run
```

```python
import functools
import math

import jax
import jax.numpy as jnp
from jax import lax
from jax.experimental import pallas as pl
from jax.experimental.pallas import tpu as pltpu
from jax.sharding import Mesh, PartitionSpec as P

GATHER_BYTES = 8 << 20
VMEM_BYTES = 16 << 20


def to_points(codes, exponents):
    scaled = lax.shift_right_arithmetic(codes << 16, jnp.broadcast_to(exponents[:, None], codes.shape))
    return (scaled.astype(jnp.float32) * 2.0**-16).astype(jnp.bfloat16)


def split_points(codes, exponents, centroids, counters):
    local_rows = to_points(codes, exponents)
    points = lax.all_gather(local_rows, "cells", axis=0, tiled=True)
    beta = 4.0 / math.sqrt(points.shape[1])
    logits = (
        lax.dot_general(
            points, centroids, (((1,), (1,)), ((), ())), preferred_element_type=jnp.float32
        )
        * beta
    )
    inverse = lax.rsqrt(counters.astype(jnp.float32) + 1.0)
    top = lax.pmax(jnp.max(logits, axis=1), "cells")
    expo = jnp.exp(logits - top[:, None])
    total, novel = lax.psum(
        (jnp.sum(expo, axis=1), jnp.dot(expo, inverse, preferred_element_type=jnp.float32)), "cells"
    )
    weight = novel / total
    share = (expo * (weight / total)[:, None]).astype(jnp.bfloat16)
    mass_local = jnp.sum(share.astype(jnp.float32), axis=0)
    sums_local = lax.dot_general(
        share, points, (((0,), (0,)), ((), ())), preferred_element_type=jnp.float32
    )
    sums = lax.psum_scatter(sums_local, "pts", scatter_dimension=0, tiled=True)
    mass = lax.psum_scatter(mass_local, "pts", scatter_dimension=0, tiled=True)
    return (sums[None], mass[None])


def exchange(a, axes, partner):
    count = math.prod(lax.axis_size(axis) for axis in axes)
    return lax.ppermute(a, axes, [(partner(at), at) for at in range(count)])


def in_vmem(n):
    return [pl.BlockSpec(memory_space=pltpu.VMEM)] * n


def join(above, below, *after):
    def kernel(above, below, *refs):
        out = refs[-1]
        out[: above.shape[0], :] = above[...]
        out[above.shape[0] :, :] = below[...]

    return pl.pallas_call(
        kernel,
        in_specs=in_vmem(2 + len(after)),
        out_specs=in_vmem(1)[0],
        out_shape=jax.ShapeDtypeStruct((above.shape[0] + below.shape[0], above.shape[1]), above.dtype),
        compiler_params=pltpu.CompilerParams(vmem_limit_bytes=VMEM_BYTES),
    )(above, below, *after)


def beside(left, right, *after):
    def kernel(left, right, *refs):
        refs[-1][...] = jnp.concatenate([left[...], right[...]], axis=1)

    return pl.pallas_call(
        kernel,
        in_specs=in_vmem(2 + len(after)),
        out_specs=in_vmem(1)[0],
        out_shape=jax.ShapeDtypeStruct((left.shape[0], left.shape[1] + right.shape[1]), left.dtype),
        compiler_params=pltpu.CompilerParams(vmem_limit_bytes=VMEM_BYTES),
    )(left, right, *after)


def hold(a, *after, declared=0):
    def kernel(a, *refs):
        refs[-1][...] = a[...]

    return pl.pallas_call(
        kernel,
        in_specs=in_vmem(1 + len(after)),
        out_specs=in_vmem(1)[0],
        out_shape=jax.ShapeDtypeStruct(a.shape, a.dtype),
        compiler_params=pltpu.CompilerParams(vmem_limit_bytes=VMEM_BYTES),
        cost_estimate=pl.CostEstimate(flops=declared, bytes_accessed=0, transcendentals=0),
    )(a, *after)


def scores(cells, points):
    return lax.dot_general(cells, points, (((1,), (1,)), ((), ())), preferred_element_type=jnp.float32)


def chip_index():
    return lax.axis_index("y") * 2 + lax.axis_index("x")


def inverse_kernel(counters, *refs):
    inverse = refs[-1]
    for line in range(counters.shape[0]):
        row = lax.rsqrt(counters[line : line + 1, :].astype(jnp.float32) + 1.0)
        inverse[line * 128 : (line + 1) * 128, :] = jnp.broadcast_to(row, (128, 128)).T


def inverse_call(counters, *after):
    return pl.pallas_call(
        inverse_kernel,
        in_specs=in_vmem(1 + len(after)),
        out_specs=in_vmem(1)[0],
        out_shape=jax.ShapeDtypeStruct((counters.shape[0], 128), jnp.float32),
        compiler_params=pltpu.CompilerParams(vmem_limit_bytes=VMEM_BYTES),
        cost_estimate=pl.CostEstimate(flops=2 * 10**9, bytes_accessed=0, transcendentals=0),
    )(counters.reshape(-1, 128), *after)


def totals_kernel(rate, block, n, *refs):
    pieces, (cells, inverse), stats = refs[:n], refs[n : n + 2], refs[-1]
    every = jnp.concatenate([piece[...] for piece in pieces], axis=0)
    count = cells.shape[0]
    parts = []
    for at in range(0, count, block):
        here = slice(at, at + block)
        logits = scores(cells[here, :], every)
        top = jnp.max(logits, axis=0, keepdims=True)
        value = jnp.exp2((logits - top) * rate)
        scale = inverse[here, :]
        weighed = [
            jnp.sum(value[:, i : i + 128] * scale, axis=0, keepdims=True) for i in range(0, value.shape[1], 128)
        ]
        parts.append((top, jnp.sum(value, axis=0, keepdims=True), jnp.concatenate(weighed, axis=1)))
        while len(parts) > 1 and (at + block == count or len(parts) == 4):
            parts = [join_stats(rate, parts)]
    stats[...] = jnp.concatenate(parts[0], axis=0)


def join_stats(rate, parts):
    top = functools.reduce(jnp.maximum, [part[0] for part in parts])
    scales = [jnp.exp2((part[0] - top) * rate) for part in parts]
    return (top, *(sum(part[at] * scale for part, scale in zip(parts, scales)) for at in (1, 2)))


def totals_call(rate, block, pieces, cells, inverse, after=(), declared=1.0):
    n_points, width = sum(piece.shape[0] for piece in pieces), pieces[0].shape[1]
    n_cells = inverse.shape[0]
    args = (*pieces, cells, inverse, *after)
    return pl.pallas_call(
        functools.partial(totals_kernel, rate, block, len(pieces)),
        in_specs=in_vmem(len(args)),
        out_specs=in_vmem(1)[0],
        out_shape=jax.ShapeDtypeStruct((3, n_points), jnp.float32),
        compiler_params=pltpu.CompilerParams(vmem_limit_bytes=VMEM_BYTES),
        cost_estimate=pl.CostEstimate(
            flops=int(declared * 2 * n_cells * n_points * width),
            bytes_accessed=int(declared * 2 * n_cells * width),
            transcendentals=int(declared * n_cells * n_points),
        ),
    )(*args)


def goal_kernel(rate, *refs):
    stats, goal = refs[:4], refs[-1]
    for at in range(4):
        here = [stat[:, (at ^ by) * 128 : ((at ^ by) + 1) * 128] for by, stat in enumerate(stats)]
        top, total, novel = join_stats(rate, [(s[:1], s[1:2], s[2:]) for s in here])
        goal[:, at * 128 : (at + 1) * 128] = jnp.concatenate([top, novel / total / total], axis=0)


def goal_call(rate, *stats):
    return pl.pallas_call(
        functools.partial(goal_kernel, rate),
        in_specs=in_vmem(len(stats)),
        out_specs=in_vmem(1)[0],
        out_shape=jax.ShapeDtypeStruct((2, stats[0].shape[1]), jnp.float32),
        compiler_params=pltpu.CompilerParams(vmem_limit_bytes=VMEM_BYTES),
    )(*stats)


def factor_kernel(rate, n, *refs):
    goals, tops, factors = refs[:4], refs[4 : 4 + n], refs[4 + n :]
    rows = goals[0].shape[1] // 2
    spots = [(0, 0, 0), (0, 0, 1), (0, 0, 2), (0, 1, 0), (1, 0, 3), (1, 1, 1), (1, 1, 2), (2, 1, 3)]
    for at, (bundle, group, goal) in enumerate(spots):
        start = (at - (0, 4, 7)[bundle]) * rows
        mine, here = slice(group * rows, (group + 1) * rows), slice(start, start + rows)
        scale = jnp.exp2((tops[bundle][:, here] - goals[goal][:1, mine]) * rate)
        factors[bundle][:, here] = scale * goals[goal][1:, mine]


def factor_call(rate, goals, tops):
    return pl.pallas_call(
        functools.partial(factor_kernel, rate, len(tops)),
        in_specs=in_vmem(4 + len(tops)),
        out_specs=in_vmem(len(tops)),
        out_shape=[jax.ShapeDtypeStruct(top.shape, jnp.float32) for top in tops],
        compiler_params=pltpu.CompilerParams(vmem_limit_bytes=VMEM_BYTES),
    )(*goals, *tops)


def expo_kernel(rate, block, spots, *refs):
    pieces, cells, (expo, tops, points) = refs[: len(spots)], refs[len(spots)], refs[-3:]
    start = 0
    for piece, (first, rows) in zip(pieces, spots):
        points[start : start + rows, :] = piece[first : first + rows, :]
        start += rows
    count = expo.shape[0] // block
    chip = chip_index()
    for at in range(count):
        mine = pl.ds(pl.multiple_of((chip * count + at) * block, block), block)
        for part in range(0, points.shape[0], 256):
            some = slice(part, part + 256)
            logits = scores(cells[mine, :], points[some, :])
            top = jnp.max(logits, axis=0, keepdims=True)
            expo[at * block : (at + 1) * block, some] = jnp.exp2((logits - top) * rate).astype(jnp.bfloat16)
            tops[at : at + 1, some] = top


def expo_call(rate, block, count, pieces, cells, *after, declared=1.0):
    width = cells.shape[1]
    pieces, spots = zip(*((piece[0], piece[1:]) if isinstance(piece, tuple) else (piece, (0, len(piece))) for piece in pieces))
    n_points = sum(rows for _, rows in spots)
    return pl.pallas_call(
        functools.partial(expo_kernel, rate, block, spots),
        in_specs=in_vmem(len(pieces) + 1 + len(after)),
        out_specs=in_vmem(3),
        out_shape=[
            jax.ShapeDtypeStruct((count, n_points), jnp.bfloat16),
            jax.ShapeDtypeStruct((count // block, n_points), jnp.float32),
            jax.ShapeDtypeStruct((n_points, width), jnp.bfloat16),
        ],
        compiler_params=pltpu.CompilerParams(vmem_limit_bytes=VMEM_BYTES),
        cost_estimate=pl.CostEstimate(
            flops=int(declared * 2 * count * n_points * width),
            bytes_accessed=int(declared * 2 * (count * width + n_points * width + count * n_points)),
            transcendentals=int(declared * count * n_points),
        ),
    )(*pieces, cells, *after)


def weighed_sums(start, count, expos, points, factors):
    total = weight = None
    for expo, chunk, factor in zip(expos, points, factors):
        block = expo.shape[0] // factor.shape[0]
        shares, lanes = [], []
        step = math.gcd(block, count)
        for at in range(0, count, step):
            here = pl.ds(pl.multiple_of(start + at, step), step)
            share = expo[here, :].astype(jnp.float32) * factor[pl.ds((start + at) // block, 1), :]
            shares.append(share.astype(jnp.bfloat16))
            lanes.append(sum(share[:, i : i + 128] for i in range(0, share.shape[1], 128)))
        share, lanes = jnp.concatenate(shares, axis=0), jnp.concatenate(lanes, axis=0)
        part = jnp.dot(share, chunk[...], preferred_element_type=jnp.float32)
        total = part if total is None else total + part
        weight = lanes if weight is None else weight + lanes
    return total, jnp.sum(weight.T, axis=0, keepdims=True)


def sums_kernel(n, side, part, rows, *refs):
    expos, points, factors, outs = refs[:n], refs[n : 2 * n], refs[2 * n : 3 * n], refs[3 * n :]
    width = points[0].shape[1]
    first = (lax.axis_index("lo") ^ side) * (expos[0].shape[0] // 2) + part * rows
    total, weight = weighed_sums(first, rows, expos, points, factors)
    outs[0][:rows, :] = total.astype(outs[0].dtype)
    if side:
        high = weight.astype(jnp.bfloat16).astype(jnp.float32)
        empty = jnp.zeros((1, width - rows), jnp.float32)
        lines = [jnp.concatenate([line, empty], axis=1) for line in (high, weight - high)]
        lines.append(jnp.zeros((14, width), jnp.float32))
        outs[0][rows:, :] = jnp.concatenate(lines, axis=0).astype(jnp.bfloat16)
    else:
        outs[1][...] = weight


def sums_call(side, part, rows, expos, points, factors):
    n = len(expos)
    width = points[0].shape[1]
    out_shape = [jax.ShapeDtypeStruct((rows + 16, width), jnp.bfloat16)]
    if not side:
        out_shape = [jax.ShapeDtypeStruct((rows, width), jnp.float32), jax.ShapeDtypeStruct((1, rows), jnp.float32)]
    return pl.pallas_call(
        functools.partial(sums_kernel, n, side, part, rows),
        in_specs=in_vmem(3 * n),
        out_specs=in_vmem(len(out_shape)),
        out_shape=out_shape,
        compiler_params=pltpu.CompilerParams(vmem_limit_bytes=VMEM_BYTES),
        cost_estimate=pl.CostEstimate(flops=4 * 10**9, bytes_accessed=0, transcendentals=0),
    )(*expos, *points, *factors)


def masses(here_mass, there):
    rows = here_mass.shape[1]
    lines = there[rows:, :].astype(jnp.float32)
    return here_mass[...] + (lines[:1, :rows] + lines[1:2, :rows])


def half_kernel(n, *refs):
    expos, points, factors = refs[:n], refs[n : 2 * n], refs[2 * n : 3 * n]
    here, here_mass, there, sums, mass, later, later_mass, out, left = refs[3 * n :]
    rows = here.shape[0]
    out[...] = here[...] + there[:rows, :].astype(jnp.float32)
    copy = pltpu.make_async_copy(out, sums.at[pl.ds(0, rows), :], left)
    copy.start()
    mass[...] = masses(here_mass, there)
    first = lax.axis_index("lo") * (2 * rows) + rows
    total, weight = weighed_sums(first, rows, expos, points, factors)
    later[...] = total
    later_mass[...] = weight
    copy.wait()


def half_call(expos, points, factors, here, here_mass, there):
    n, (rows, width) = len(expos), here.shape
    part = [jax.ShapeDtypeStruct((1, rows), jnp.float32), jax.ShapeDtypeStruct((rows, width), jnp.float32)]
    return pl.pallas_call(
        functools.partial(half_kernel, n),
        in_specs=in_vmem(3 * n + 3),
        out_specs=[pl.BlockSpec(memory_space=pltpu.HBM)] + in_vmem(3),
        out_shape=[jax.ShapeDtypeStruct((2 * rows, width), jnp.float32), *part, part[0]],
        scratch_shapes=[pltpu.VMEM((rows, width), jnp.float32), pltpu.SemaphoreType.DMA],
        compiler_params=pltpu.CompilerParams(vmem_limit_bytes=VMEM_BYTES),
    )(*expos, *points, *factors, here, here_mass, there)


def end_kernel(so_far, mass_so_far, here, here_mass, there, sums, mass, out, left):
    rows = here.shape[0]
    half = rows // 2
    copies = []
    for at in (0, half):
        here_rows = slice(at, at + half)
        out[here_rows, :] = here[here_rows, :] + there[here_rows, :].astype(jnp.float32)
        copies.append(
            pltpu.make_async_copy(out.at[pl.ds(at, half), :], sums.at[pl.ds(rows + at, half), :], left.at[len(copies)])
        )
        copies[-1].start()
    mass[:, :rows] = mass_so_far[...]
    mass[:, rows:] = masses(here_mass, there)
    for copy in copies:
        copy.wait()


def end_call(so_far, mass_so_far, here, here_mass, there):
    rows, width = here.shape
    hbm = [pl.BlockSpec(memory_space=pltpu.HBM)]
    return pl.pallas_call(
        end_kernel,
        in_specs=hbm + in_vmem(4),
        out_specs=hbm + in_vmem(1),
        out_shape=[
            jax.ShapeDtypeStruct(so_far.shape, jnp.float32),
            jax.ShapeDtypeStruct((1, 2 * rows), jnp.float32),
        ],
        input_output_aliases={0: 0},
        scratch_shapes=[pltpu.VMEM((rows, width), jnp.float32), pltpu.SemaphoreType.DMA((2,))],
        compiler_params=pltpu.CompilerParams(vmem_limit_bytes=VMEM_BYTES),
    )(so_far, mass_so_far, here, here_mass, there)


def split_cells(codes, exponents, centroids, counters):
    own = to_points(codes, exponents)
    rate = 4.0 / math.sqrt(own.shape[1]) * math.log2(math.e)
    plane = ("y", "x", "lo")

    turn = lambda a: exchange(a, plane, lambda at: at ^ (4 if at % 2 else 2))
    turn_back = lambda a: exchange(a, plane, lambda at: at ^ (2 if at % 2 else 4))
    along_z = lambda a, by: exchange(a, ("cells",), lambda at: at ^ by)
    around = lambda a, by: exchange(a, ("y", "x"), lambda at: at ^ by)

    per_device = centroids.shape[0] // 8
    block = per_device // 3

    near_1, near_2, near_3 = (along_z(own, by) for by in (1, 2, 3))
    inverse = inverse_call(counters)
    near_01 = join(own, near_1, inverse)
    held_01 = hold(near_01, declared=2 * 10**9)
    first_01 = turn(near_01)
    stats = [totals_call(rate, block, (held_01,), centroids, inverse)]
    second_01, across_01 = turn_back(hold(near_01, stats[0])), turn_back(hold(first_01, stats[0]))
    near_23 = join(near_2, near_3, *stats)
    stats.append(totals_call(rate, block, (near_23,), centroids, inverse, after=(first_01,)))
    first_23 = turn(near_23)
    stat = beside(*stats)
    expand = functools.partial(expo_call, rate, block, 2 * per_device)
    bundles = [expand((near_01, first_01, second_01, near_23), centroids, stat, declared=0.01)]
    goal = goal_call(rate, stat, *(along_z(stat, by) for by in (1, 2, 3)), bundles[0][1], across_01)
    across_23 = turn_back(hold(first_23, goal))

    second_23 = turn_back(hold(near_23, bundles[0][1]))
    bundles.append(expand((across_01, first_23, second_23), centroids, goal, declared=0.01))
    bundles.append(expand((across_23,), centroids, bundles[1][1]))
    expos, tops, points = zip(*bundles)
    goals = [goal, turn(goal), turn_back(goal), around(goal, 3)]
    factors = factor_call(rate, goals, tops)

    parts, rows = (expos, points, factors), per_device // 2
    there = [exchange(*sums_call(1, part, rows, *parts), ("lo",), lambda at: at ^ 1) for part in range(2)]
    here = sums_call(0, 0, rows, *parts)
    so_far, mass_so_far, later, later_mass = half_call(*parts, *here, there[0])
    out, mass = end_call(so_far, mass_so_far, later, later_mass, there[1])
    return (out[None], mass)


def solution(mesh):
    pts, cells = (mesh.shape[name] for name in ("pts", "cells"))
    square = (pts, cells) == (8, 4)
    shape, names = ((2, 2, 2, cells), ("y", "x", "lo", "cells")) if square else ((pts, cells), ("pts", "cells"))
    fine = Mesh(mesh.devices.reshape(shape), names)
    spread = names[:-1]
    in_specs = (P(names, None), P(names), P("cells", None), P("cells"))
    out_specs = (P("cells", spread, None), P("cells", spread))

    def run(codes, exponents, centroids, counters):
        small = codes.size * 2 <= GATHER_BYTES and codes.shape[0] == 128 * pts * cells
        body = split_cells if square and small else split_points
        mapped = jax.shard_map(body, mesh=fine, in_specs=in_specs, out_specs=out_specs, check_vma=False)
        return mapped(codes, exponents, centroids, counters)

    return run
```

```python
import functools
import math

import jax
import jax.numpy as jnp
from jax import lax
from jax.experimental import pallas as pl
from jax.experimental.pallas import tpu as pltpu
from jax.sharding import Mesh, PartitionSpec as P

GATHER_BYTES = 8 << 20
VMEM_BYTES = 16 << 20


def to_points(codes, exponents):
    scaled = lax.shift_right_arithmetic(codes << 16, jnp.broadcast_to(exponents[:, None], codes.shape))
    return (scaled.astype(jnp.float32) * 2.0**-16).astype(jnp.bfloat16)


def split_points(codes, exponents, centroids, counters):
    local_rows = to_points(codes, exponents)
    points = lax.all_gather(local_rows, "cells", axis=0, tiled=True)
    beta = 4.0 / math.sqrt(points.shape[1])
    logits = (
        lax.dot_general(
            points, centroids, (((1,), (1,)), ((), ())), preferred_element_type=jnp.float32
        )
        * beta
    )
    inverse = lax.rsqrt(counters.astype(jnp.float32) + 1.0)
    top = lax.pmax(jnp.max(logits, axis=1), "cells")
    expo = jnp.exp(logits - top[:, None])
    total, novel = lax.psum(
        (jnp.sum(expo, axis=1), jnp.dot(expo, inverse, preferred_element_type=jnp.float32)), "cells"
    )
    weight = novel / total
    share = (expo * (weight / total)[:, None]).astype(jnp.bfloat16)
    mass_local = jnp.sum(share.astype(jnp.float32), axis=0)
    sums_local = lax.dot_general(
        share, points, (((0,), (0,)), ((), ())), preferred_element_type=jnp.float32
    )
    sums = lax.psum_scatter(sums_local, "pts", scatter_dimension=0, tiled=True)
    mass = lax.psum_scatter(mass_local, "pts", scatter_dimension=0, tiled=True)
    return (sums[None], mass[None])


def exchange(a, axes, partner):
    count = math.prod(lax.axis_size(axis) for axis in axes)
    return lax.ppermute(a, axes, [(partner(at), at) for at in range(count)])


def in_vmem(n):
    return [pl.BlockSpec(memory_space=pltpu.VMEM)] * n


def join(above, below, *after):
    def kernel(above, below, *refs):
        out = refs[-1]
        out[: above.shape[0], :] = above[...]
        out[above.shape[0] :, :] = below[...]

    return pl.pallas_call(
        kernel,
        in_specs=in_vmem(2 + len(after)),
        out_specs=in_vmem(1)[0],
        out_shape=jax.ShapeDtypeStruct((above.shape[0] + below.shape[0], above.shape[1]), above.dtype),
        compiler_params=pltpu.CompilerParams(vmem_limit_bytes=VMEM_BYTES),
    )(above, below, *after)


def beside(left, right, *after):
    def kernel(left, right, *refs):
        refs[-1][...] = jnp.concatenate([left[...], right[...]], axis=1)

    return pl.pallas_call(
        kernel,
        in_specs=in_vmem(2 + len(after)),
        out_specs=in_vmem(1)[0],
        out_shape=jax.ShapeDtypeStruct((left.shape[0], left.shape[1] + right.shape[1]), left.dtype),
        compiler_params=pltpu.CompilerParams(vmem_limit_bytes=VMEM_BYTES),
    )(left, right, *after)


def hold(a, *after, declared=0):
    def kernel(a, *refs):
        refs[-1][...] = a[...]

    return pl.pallas_call(
        kernel,
        in_specs=in_vmem(1 + len(after)),
        out_specs=in_vmem(1)[0],
        out_shape=jax.ShapeDtypeStruct(a.shape, a.dtype),
        compiler_params=pltpu.CompilerParams(vmem_limit_bytes=VMEM_BYTES),
        cost_estimate=pl.CostEstimate(flops=declared, bytes_accessed=0, transcendentals=0),
    )(a, *after)


def scores(cells, points):
    return lax.dot_general(cells, points, (((1,), (1,)), ((), ())), preferred_element_type=jnp.float32)


def chip_index():
    return lax.axis_index("y") * 2 + lax.axis_index("x")


def inverse_kernel(counters, *refs):
    inverse = refs[-1]
    for line in range(counters.shape[0]):
        row = lax.rsqrt(counters[line : line + 1, :].astype(jnp.float32) + 1.0)
        inverse[line * 128 : (line + 1) * 128, :] = jnp.broadcast_to(row, (128, 128)).T


def inverse_call(counters, *after):
    return pl.pallas_call(
        inverse_kernel,
        in_specs=in_vmem(1 + len(after)),
        out_specs=in_vmem(1)[0],
        out_shape=jax.ShapeDtypeStruct((counters.shape[0], 128), jnp.float32),
        compiler_params=pltpu.CompilerParams(vmem_limit_bytes=VMEM_BYTES),
        cost_estimate=pl.CostEstimate(flops=2 * 10**9, bytes_accessed=0, transcendentals=0),
    )(counters.reshape(-1, 128), *after)


def totals_kernel(rate, block, n, *refs):
    pieces, (cells, inverse), stats = refs[:n], refs[n : n + 2], refs[-1]
    every = jnp.concatenate([piece[...] for piece in pieces], axis=0)
    count = cells.shape[0]
    parts = []
    for at in range(0, count, block):
        here = slice(at, at + block)
        logits = scores(cells[here, :], every)
        top = jnp.max(logits, axis=0, keepdims=True)
        value = jnp.exp2((logits - top) * rate)
        scale = inverse[here, :]
        weighed = [
            jnp.sum(value[:, i : i + 128] * scale, axis=0, keepdims=True) for i in range(0, value.shape[1], 128)
        ]
        parts.append((top, jnp.sum(value, axis=0, keepdims=True), jnp.concatenate(weighed, axis=1)))
        while len(parts) > 1 and (at + block == count or len(parts) == 4):
            parts = [join_stats(rate, parts)]
    stats[...] = jnp.concatenate(parts[0], axis=0)


def join_stats(rate, parts):
    top = functools.reduce(jnp.maximum, [part[0] for part in parts])
    scales = [jnp.exp2((part[0] - top) * rate) for part in parts]
    return (top, *(sum(part[at] * scale for part, scale in zip(parts, scales)) for at in (1, 2)))


def totals_call(rate, block, pieces, cells, inverse, after=(), declared=1.0):
    n_points, width = sum(piece.shape[0] for piece in pieces), pieces[0].shape[1]
    n_cells = inverse.shape[0]
    args = (*pieces, cells, inverse, *after)
    return pl.pallas_call(
        functools.partial(totals_kernel, rate, block, len(pieces)),
        in_specs=in_vmem(len(args)),
        out_specs=in_vmem(1)[0],
        out_shape=jax.ShapeDtypeStruct((3, n_points), jnp.float32),
        compiler_params=pltpu.CompilerParams(vmem_limit_bytes=VMEM_BYTES),
        cost_estimate=pl.CostEstimate(
            flops=int(declared * 2 * n_cells * n_points * width),
            bytes_accessed=int(declared * 2 * n_cells * width),
            transcendentals=int(declared * n_cells * n_points),
        ),
    )(*args)


def goal_kernel(rate, *refs):
    stats, goal = refs[:4], refs[-1]
    for at in range(4):
        here = [stat[:, (at ^ by) * 128 : ((at ^ by) + 1) * 128] for by, stat in enumerate(stats)]
        top, total, novel = join_stats(rate, [(s[:1], s[1:2], s[2:]) for s in here])
        goal[:, at * 128 : (at + 1) * 128] = jnp.concatenate([top, novel / total / total], axis=0)


def goal_call(rate, *stats):
    return pl.pallas_call(
        functools.partial(goal_kernel, rate),
        in_specs=in_vmem(len(stats)),
        out_specs=in_vmem(1)[0],
        out_shape=jax.ShapeDtypeStruct((2, stats[0].shape[1]), jnp.float32),
        compiler_params=pltpu.CompilerParams(vmem_limit_bytes=VMEM_BYTES),
    )(*stats)


def factor_kernel(rate, n, *refs):
    goals, tops, factors = refs[:4], refs[4 : 4 + n], refs[4 + n :]
    rows = goals[0].shape[1] // 2
    spots = [(0, 0, 0), (0, 0, 1), (0, 0, 2), (0, 1, 0), (1, 0, 3), (1, 1, 1), (1, 1, 2), (2, 1, 3)]
    for at, (bundle, group, goal) in enumerate(spots):
        start = (at - (0, 4, 7)[bundle]) * rows
        mine, here = slice(group * rows, (group + 1) * rows), slice(start, start + rows)
        scale = jnp.exp2((tops[bundle][:, here] - goals[goal][:1, mine]) * rate)
        factors[bundle][:, here] = scale * goals[goal][1:, mine]


def factor_call(rate, goals, tops):
    return pl.pallas_call(
        functools.partial(factor_kernel, rate, len(tops)),
        in_specs=in_vmem(4 + len(tops)),
        out_specs=in_vmem(len(tops)),
        out_shape=[jax.ShapeDtypeStruct(top.shape, jnp.float32) for top in tops],
        compiler_params=pltpu.CompilerParams(vmem_limit_bytes=VMEM_BYTES),
    )(*goals, *tops)


def expo_kernel(rate, block, spots, *refs):
    pieces, cells, (expo, tops, points) = refs[: len(spots)], refs[len(spots)], refs[-3:]
    start = 0
    for piece, (first, rows) in zip(pieces, spots):
        points[start : start + rows, :] = piece[first : first + rows, :]
        start += rows
    count = expo.shape[0] // block
    chip = chip_index()
    for at in range(count):
        mine = pl.ds(pl.multiple_of((chip * count + at) * block, block), block)
        for part in range(0, points.shape[0], 256):
            some = slice(part, part + 256)
            logits = scores(cells[mine, :], points[some, :])
            top = jnp.max(logits, axis=0, keepdims=True)
            expo[at * block : (at + 1) * block, some] = jnp.exp2((logits - top) * rate).astype(jnp.bfloat16)
            tops[at : at + 1, some] = top


def expo_call(rate, block, count, pieces, cells, *after, declared=1.0):
    width = cells.shape[1]
    pieces, spots = zip(*((piece[0], piece[1:]) if isinstance(piece, tuple) else (piece, (0, len(piece))) for piece in pieces))
    n_points = sum(rows for _, rows in spots)
    return pl.pallas_call(
        functools.partial(expo_kernel, rate, block, spots),
        in_specs=in_vmem(len(pieces) + 1 + len(after)),
        out_specs=in_vmem(3),
        out_shape=[
            jax.ShapeDtypeStruct((count, n_points), jnp.bfloat16),
            jax.ShapeDtypeStruct((count // block, n_points), jnp.float32),
            jax.ShapeDtypeStruct((n_points, width), jnp.bfloat16),
        ],
        compiler_params=pltpu.CompilerParams(vmem_limit_bytes=VMEM_BYTES),
        cost_estimate=pl.CostEstimate(
            flops=int(declared * 2 * count * n_points * width),
            bytes_accessed=int(declared * 2 * (count * width + n_points * width + count * n_points)),
            transcendentals=int(declared * count * n_points),
        ),
    )(*pieces, cells, *after)


def weighed_sums(start, count, expos, points, factors):
    total = weight = None
    for expo, chunk, factor in zip(expos, points, factors):
        block = expo.shape[0] // factor.shape[0]
        shares, lanes = [], []
        for at in range(0, count, block):
            here = pl.ds(pl.multiple_of(start + at, block), block)
            share = expo[here, :].astype(jnp.float32) * factor[pl.ds((start + at) // block, 1), :]
            shares.append(share.astype(jnp.bfloat16))
            lanes.append(sum(share[:, i : i + 128] for i in range(0, share.shape[1], 128)))
        share, lanes = jnp.concatenate(shares, axis=0), jnp.concatenate(lanes, axis=0)
        part = jnp.dot(share, chunk[...], preferred_element_type=jnp.float32)
        total = part if total is None else total + part
        weight = lanes if weight is None else weight + lanes
    return total, jnp.sum(weight.T, axis=0, keepdims=True)


def sums_kernel(n, block, side, *refs):
    expos, points, factors, (sums, mass) = refs[:n], refs[n : 2 * n], refs[2 * n : 3 * n], refs[3 * n :]
    rows = sums.shape[0]
    first = (lax.axis_index("lo") ^ side) * rows
    for at in range(0, rows, block):
        here = slice(at, at + block)
        total, weight = weighed_sums(first + at, block, expos, points, factors)
        sums[here, :] = total.astype(sums.dtype)
        mass[:, here] = weight


def sums_call(block, side, rows, dtype, expos, points, factors):
    n = len(expos)
    n_points, width = points[0].shape
    return pl.pallas_call(
        functools.partial(sums_kernel, n, block, side),
        in_specs=in_vmem(3 * n),
        out_specs=in_vmem(2),
        out_shape=[jax.ShapeDtypeStruct((rows, width), dtype), jax.ShapeDtypeStruct((1, rows), jnp.float32)],
        compiler_params=pltpu.CompilerParams(vmem_limit_bytes=VMEM_BYTES),
        cost_estimate=pl.CostEstimate(
            flops=2 * rows * n * n_points * width,
            bytes_accessed=2 * n * n_points * (rows + width) + 4 * rows * width,
            transcendentals=0,
        ),
    )(*expos, *points, *factors)


def add_kernel(block, here, here_mass, there, there_mass, sums, mass, out, mass_out, left):
    def copy(at):
        rows = pl.ds(at * block, block)
        return pltpu.make_async_copy(out.at[rows, :], sums.at[rows, :], left.at[at])

    count = here.shape[0] // block
    mass_out[...] = here_mass[...] + there_mass[...]
    mass_copy = pltpu.make_async_copy(mass_out, mass, left.at[count])
    mass_copy.start()
    for at in range(count):
        rows = slice(at * block, (at + 1) * block)
        out[rows, :] = here[rows, :] + there[rows, :].astype(jnp.float32)
        copy(at).start(priority=at % 2)
    mass_copy.wait()
    for at in range(count):
        copy(at).wait()


def add_call(block, here, here_mass, there, there_mass):
    return pl.pallas_call(
        functools.partial(add_kernel, block),
        in_specs=in_vmem(4),
        out_specs=[pl.BlockSpec(memory_space=pltpu.HBM)] * 2,
        out_shape=[
            jax.ShapeDtypeStruct(here.shape, jnp.float32),
            jax.ShapeDtypeStruct(here_mass.shape, jnp.float32),
        ],
        scratch_shapes=[
            pltpu.VMEM(here.shape, jnp.float32),
            pltpu.VMEM(here_mass.shape, jnp.float32),
            pltpu.SemaphoreType.DMA((here.shape[0] // block + 1,)),
        ],
        compiler_params=pltpu.CompilerParams(vmem_limit_bytes=VMEM_BYTES),
    )(here, here_mass, there, there_mass)


def split_cells(codes, exponents, centroids, counters):
    own = to_points(codes, exponents)
    rate = 4.0 / math.sqrt(own.shape[1]) * math.log2(math.e)
    plane = ("y", "x", "lo")

    turn = lambda a: exchange(a, plane, lambda at: at ^ (4 if at % 2 else 2))
    turn_back = lambda a: exchange(a, plane, lambda at: at ^ (2 if at % 2 else 4))
    along_z = lambda a, by: exchange(a, ("cells",), lambda at: at ^ by)
    around = lambda a, by: exchange(a, ("y", "x"), lambda at: at ^ by)

    per_device = centroids.shape[0] // 8
    block = per_device // 3

    near_1, near_2, near_3 = (along_z(own, by) for by in (1, 2, 3))
    inverse = inverse_call(counters)
    near_01 = join(own, near_1, inverse)
    held_01 = hold(near_01, declared=2 * 10**9)
    first_01 = turn(near_01)
    stats = [totals_call(rate, block, (held_01,), centroids, inverse)]
    second_01, across_01 = turn_back(hold(near_01, stats[0])), turn_back(hold(first_01, stats[0]))
    near_23 = join(near_2, near_3, *stats)
    stats.append(totals_call(rate, block, (near_23,), centroids, inverse, after=(first_01,)))
    first_23 = turn(near_23)
    stat = beside(*stats)
    expand = functools.partial(expo_call, rate, block, 2 * per_device)
    bundles = [expand((near_01, first_01, second_01, near_23), centroids, stat, declared=0.01)]
    goal = goal_call(rate, stat, *(along_z(stat, by) for by in (1, 2, 3)), bundles[0][1], across_01)
    across_23 = turn_back(hold(first_23, goal))

    second_23 = turn_back(hold(near_23, bundles[0][1]))
    bundles.append(expand((across_01, first_23, second_23), centroids, goal, declared=0.01))
    bundles.append(expand((across_23,), centroids, bundles[1][1]))
    expos, tops, points = zip(*bundles)
    goals = [goal, turn(goal), turn_back(goal), around(goal, 3)]
    factors = factor_call(rate, goals, tops)

    there = sums_call(per_device, 1, per_device, jnp.bfloat16, expos, points, factors)
    there = [exchange(a, ("lo",), lambda at: at ^ 1) for a in there]
    here = sums_call(per_device, 0, per_device, jnp.float32, expos, points, factors)
    out, mass = add_call(block // 2, *here, *there)
    return (out[None], mass)


def solution(mesh):
    pts, cells = (mesh.shape[name] for name in ("pts", "cells"))
    square = (pts, cells) == (8, 4)
    shape, names = ((2, 2, 2, cells), ("y", "x", "lo", "cells")) if square else ((pts, cells), ("pts", "cells"))
    fine = Mesh(mesh.devices.reshape(shape), names)
    spread = names[:-1]
    in_specs = (P(names, None), P(names), P("cells", None), P("cells"))
    out_specs = (P("cells", spread, None), P("cells", spread))

    def run(codes, exponents, centroids, counters):
        small = codes.size * 2 <= GATHER_BYTES and codes.shape[0] == 128 * pts * cells
        body = split_cells if square and small else split_points
        mapped = jax.shard_map(body, mesh=fine, in_specs=in_specs, out_specs=out_specs, check_vma=False)
        return mapped(codes, exponents, centroids, counters)

    return run
```

```python
import functools
import math

import jax
import jax.numpy as jnp
from jax import lax
from jax.experimental import pallas as pl
from jax.experimental.pallas import tpu as pltpu
from jax.sharding import Mesh, PartitionSpec as P

GATHER_BYTES = 8 << 20
VMEM_BYTES = 16 << 20


def to_points(codes, exponents):
    scaled = lax.shift_right_arithmetic(codes << 16, jnp.broadcast_to(exponents[:, None], codes.shape))
    return (scaled.astype(jnp.float32) * 2.0**-16).astype(jnp.bfloat16)


def split_points(codes, exponents, centroids, counters):
    local_rows = to_points(codes, exponents)
    points = lax.all_gather(local_rows, "cells", axis=0, tiled=True)
    beta = 4.0 / math.sqrt(points.shape[1])
    logits = (
        lax.dot_general(
            points, centroids, (((1,), (1,)), ((), ())), preferred_element_type=jnp.float32
        )
        * beta
    )
    inverse = lax.rsqrt(counters.astype(jnp.float32) + 1.0)
    top = lax.pmax(jnp.max(logits, axis=1), "cells")
    expo = jnp.exp(logits - top[:, None])
    total, novel = lax.psum(
        (jnp.sum(expo, axis=1), jnp.dot(expo, inverse, preferred_element_type=jnp.float32)), "cells"
    )
    weight = novel / total
    share = (expo * (weight / total)[:, None]).astype(jnp.bfloat16)
    mass_local = jnp.sum(share.astype(jnp.float32), axis=0)
    sums_local = lax.dot_general(
        share, points, (((0,), (0,)), ((), ())), preferred_element_type=jnp.float32
    )
    sums = lax.psum_scatter(sums_local, "pts", scatter_dimension=0, tiled=True)
    mass = lax.psum_scatter(mass_local, "pts", scatter_dimension=0, tiled=True)
    return (sums[None], mass[None])


def exchange(a, axes, partner):
    count = math.prod(lax.axis_size(axis) for axis in axes)
    return lax.ppermute(a, axes, [(partner(at), at) for at in range(count)])


def in_vmem(n):
    return [pl.BlockSpec(memory_space=pltpu.VMEM)] * n


def join(above, below, *after):
    def kernel(above, below, *refs):
        out = refs[-1]
        out[: above.shape[0], :] = above[...]
        out[above.shape[0] :, :] = below[...]

    return pl.pallas_call(
        kernel,
        in_specs=in_vmem(2 + len(after)),
        out_specs=in_vmem(1)[0],
        out_shape=jax.ShapeDtypeStruct((above.shape[0] + below.shape[0], above.shape[1]), above.dtype),
        compiler_params=pltpu.CompilerParams(vmem_limit_bytes=VMEM_BYTES),
    )(above, below, *after)


def beside(left, right, *after):
    def kernel(left, right, *refs):
        refs[-1][...] = jnp.concatenate([left[...], right[...]], axis=1)

    return pl.pallas_call(
        kernel,
        in_specs=in_vmem(2 + len(after)),
        out_specs=in_vmem(1)[0],
        out_shape=jax.ShapeDtypeStruct((left.shape[0], left.shape[1] + right.shape[1]), left.dtype),
        compiler_params=pltpu.CompilerParams(vmem_limit_bytes=VMEM_BYTES),
    )(left, right, *after)


def hold(a, *after, declared=0):
    def kernel(a, *refs):
        refs[-1][...] = a[...]

    return pl.pallas_call(
        kernel,
        in_specs=in_vmem(1 + len(after)),
        out_specs=in_vmem(1)[0],
        out_shape=jax.ShapeDtypeStruct(a.shape, a.dtype),
        compiler_params=pltpu.CompilerParams(vmem_limit_bytes=VMEM_BYTES),
        cost_estimate=pl.CostEstimate(flops=declared, bytes_accessed=0, transcendentals=0),
    )(a, *after)


def scores(cells, points):
    return lax.dot_general(cells, points, (((1,), (1,)), ((), ())), preferred_element_type=jnp.float32)


def chip_index():
    return lax.axis_index("y") * 2 + lax.axis_index("x")


def inverse_kernel(counters, *refs):
    inverse = refs[-1]
    for line in range(counters.shape[0]):
        row = lax.rsqrt(counters[line : line + 1, :].astype(jnp.float32) + 1.0)
        inverse[line * 128 : (line + 1) * 128, :] = jnp.broadcast_to(row, (128, 128)).T


def inverse_call(counters, *after):
    return pl.pallas_call(
        inverse_kernel,
        in_specs=in_vmem(1 + len(after)),
        out_specs=in_vmem(1)[0],
        out_shape=jax.ShapeDtypeStruct((counters.shape[0], 128), jnp.float32),
        compiler_params=pltpu.CompilerParams(vmem_limit_bytes=VMEM_BYTES),
        cost_estimate=pl.CostEstimate(flops=2 * 10**9, bytes_accessed=0, transcendentals=0),
    )(counters.reshape(-1, 128), *after)


def totals_kernel(rate, block, n, *refs):
    pieces, (cells, inverse), stats = refs[:n], refs[n : n + 2], refs[-1]
    every = jnp.concatenate([piece[...] for piece in pieces], axis=0)
    count = cells.shape[0]
    parts = []
    for at in range(0, count, block):
        here = slice(at, at + block)
        logits = scores(cells[here, :], every)
        top = jnp.max(logits, axis=0, keepdims=True)
        value = jnp.exp2((logits - top) * rate)
        scale = inverse[here, :]
        weighed = [
            jnp.sum(value[:, i : i + 128] * scale, axis=0, keepdims=True) for i in range(0, value.shape[1], 128)
        ]
        parts.append((top, jnp.sum(value, axis=0, keepdims=True), jnp.concatenate(weighed, axis=1)))
        while len(parts) > 1 and (at + block == count or len(parts) == 4):
            parts = [join_stats(rate, parts)]
    stats[...] = jnp.concatenate(parts[0], axis=0)


def join_stats(rate, parts):
    top = functools.reduce(jnp.maximum, [part[0] for part in parts])
    scales = [jnp.exp2((part[0] - top) * rate) for part in parts]
    return (top, *(sum(part[at] * scale for part, scale in zip(parts, scales)) for at in (1, 2)))


def totals_call(rate, block, pieces, cells, inverse, after=(), declared=1.0):
    n_points, width = sum(piece.shape[0] for piece in pieces), pieces[0].shape[1]
    n_cells = inverse.shape[0]
    args = (*pieces, cells, inverse, *after)
    return pl.pallas_call(
        functools.partial(totals_kernel, rate, block, len(pieces)),
        in_specs=in_vmem(len(args)),
        out_specs=in_vmem(1)[0],
        out_shape=jax.ShapeDtypeStruct((3, n_points), jnp.float32),
        compiler_params=pltpu.CompilerParams(vmem_limit_bytes=VMEM_BYTES),
        cost_estimate=pl.CostEstimate(
            flops=int(declared * 2 * n_cells * n_points * width),
            bytes_accessed=int(declared * 2 * n_cells * width),
            transcendentals=int(declared * n_cells * n_points),
        ),
    )(*args)


def goal_kernel(rate, *refs):
    stats, goal = refs[:4], refs[-1]
    for at in range(4):
        here = [stat[:, (at ^ by) * 128 : ((at ^ by) + 1) * 128] for by, stat in enumerate(stats)]
        top, total, novel = join_stats(rate, [(s[:1], s[1:2], s[2:]) for s in here])
        goal[:, at * 128 : (at + 1) * 128] = jnp.concatenate([top, novel / total / total], axis=0)


def goal_call(rate, *stats):
    return pl.pallas_call(
        functools.partial(goal_kernel, rate),
        in_specs=in_vmem(len(stats)),
        out_specs=in_vmem(1)[0],
        out_shape=jax.ShapeDtypeStruct((2, stats[0].shape[1]), jnp.float32),
        compiler_params=pltpu.CompilerParams(vmem_limit_bytes=VMEM_BYTES),
    )(*stats)


def factor_kernel(rate, n, *refs):
    goals, tops, factors = refs[:4], refs[4 : 4 + n], refs[4 + n :]
    rows = goals[0].shape[1] // 2
    spots = [(0, 0, 0), (0, 0, 1), (0, 0, 2), (0, 1, 0), (1, 0, 3), (1, 1, 1), (1, 1, 2), (2, 1, 3)]
    for at, (bundle, group, goal) in enumerate(spots):
        start = (at - (0, 4, 7)[bundle]) * rows
        mine, here = slice(group * rows, (group + 1) * rows), slice(start, start + rows)
        scale = jnp.exp2((tops[bundle][:, here] - goals[goal][:1, mine]) * rate)
        factors[bundle][:, here] = scale * goals[goal][1:, mine]


def factor_call(rate, goals, tops):
    return pl.pallas_call(
        functools.partial(factor_kernel, rate, len(tops)),
        in_specs=in_vmem(4 + len(tops)),
        out_specs=in_vmem(len(tops)),
        out_shape=[jax.ShapeDtypeStruct(top.shape, jnp.float32) for top in tops],
        compiler_params=pltpu.CompilerParams(vmem_limit_bytes=VMEM_BYTES),
    )(*goals, *tops)


def expo_kernel(rate, block, spots, *refs):
    pieces, cells, (expo, tops, points) = refs[: len(spots)], refs[len(spots)], refs[-3:]
    start = 0
    for piece, (first, rows) in zip(pieces, spots):
        points[start : start + rows, :] = piece[first : first + rows, :]
        start += rows
    count = expo.shape[0] // block
    chip = chip_index()
    for at in range(count):
        mine = pl.ds(pl.multiple_of((chip * count + at) * block, block), block)
        for part in range(0, points.shape[0], 256):
            some = slice(part, part + 256)
            logits = scores(cells[mine, :], points[some, :])
            top = jnp.max(logits, axis=0, keepdims=True)
            expo[at * block : (at + 1) * block, some] = jnp.exp2((logits - top) * rate).astype(jnp.bfloat16)
            tops[at : at + 1, some] = top


def expo_call(rate, block, count, pieces, cells, *after, declared=1.0):
    width = cells.shape[1]
    pieces, spots = zip(*((piece[0], piece[1:]) if isinstance(piece, tuple) else (piece, (0, len(piece))) for piece in pieces))
    n_points = sum(rows for _, rows in spots)
    return pl.pallas_call(
        functools.partial(expo_kernel, rate, block, spots),
        in_specs=in_vmem(len(pieces) + 1 + len(after)),
        out_specs=in_vmem(3),
        out_shape=[
            jax.ShapeDtypeStruct((count, n_points), jnp.bfloat16),
            jax.ShapeDtypeStruct((count // block, n_points), jnp.float32),
            jax.ShapeDtypeStruct((n_points, width), jnp.bfloat16),
        ],
        compiler_params=pltpu.CompilerParams(vmem_limit_bytes=VMEM_BYTES),
        cost_estimate=pl.CostEstimate(
            flops=int(declared * 2 * count * n_points * width),
            bytes_accessed=int(declared * 2 * (count * width + n_points * width + count * n_points)),
            transcendentals=int(declared * count * n_points),
        ),
    )(*pieces, cells, *after)


def weighed_sums(start, count, expos, points, factors):
    total = weight = None
    for expo, chunk, factor in zip(expos, points, factors):
        block = expo.shape[0] // factor.shape[0]
        shares, lanes = [], []
        for at in range(0, count, block):
            here = pl.ds(pl.multiple_of(start + at, block), block)
            share = expo[here, :].astype(jnp.float32) * factor[pl.ds((start + at) // block, 1), :]
            shares.append(share.astype(jnp.bfloat16))
            lanes.append(sum(share[:, i : i + 128] for i in range(0, share.shape[1], 128)))
        share, lanes = jnp.concatenate(shares, axis=0), jnp.concatenate(lanes, axis=0)
        part = jnp.dot(share, chunk[...], preferred_element_type=jnp.float32)
        total = part if total is None else total + part
        weight = lanes if weight is None else weight + lanes
    return total, jnp.sum(weight.T, axis=0, keepdims=True)


def sums_kernel(n, block, side, *refs):
    expos, points, factors, (sums, mass) = refs[:n], refs[n : 2 * n], refs[2 * n : 3 * n], refs[3 * n :]
    rows = sums.shape[0]
    first = (lax.axis_index("lo") ^ side) * rows
    for at in range(0, rows, block):
        here = slice(at, at + block)
        total, weight = weighed_sums(first + at, block, expos, points, factors)
        sums[here, :] = total.astype(sums.dtype)
        mass[:, here] = weight


def sums_call(block, side, rows, dtype, expos, points, factors):
    n = len(expos)
    n_points, width = points[0].shape
    return pl.pallas_call(
        functools.partial(sums_kernel, n, block, side),
        in_specs=in_vmem(3 * n),
        out_specs=in_vmem(2),
        out_shape=[jax.ShapeDtypeStruct((rows, width), dtype), jax.ShapeDtypeStruct((1, rows), jnp.float32)],
        compiler_params=pltpu.CompilerParams(vmem_limit_bytes=VMEM_BYTES),
        cost_estimate=pl.CostEstimate(
            flops=2 * rows * n * n_points * width,
            bytes_accessed=2 * n * n_points * (rows + width) + 4 * rows * width,
            transcendentals=0,
        ),
    )(*expos, *points, *factors)


def add_kernel(block, here, here_mass, there, there_mass, sums, mass, out, mass_out, left):
    def copy(at):
        rows = pl.ds(at * block, block)
        return pltpu.make_async_copy(out.at[rows, :], sums.at[rows, :], left.at[at])

    count = here.shape[0] // block
    mass_out[...] = here_mass[...] + there_mass[...]
    mass_copy = pltpu.make_async_copy(mass_out, mass, left.at[count])
    mass_copy.start()
    for at in range(count):
        rows = slice(at * block, (at + 1) * block)
        out[rows, :] = here[rows, :] + there[rows, :].astype(jnp.float32)
        copy(at).start(priority=at % 2)
    mass_copy.wait()
    for at in range(count):
        copy(at).wait()


def add_call(block, here, here_mass, there, there_mass):
    return pl.pallas_call(
        functools.partial(add_kernel, block),
        in_specs=in_vmem(4),
        out_specs=[pl.BlockSpec(memory_space=pltpu.HBM)] * 2,
        out_shape=[
            jax.ShapeDtypeStruct(here.shape, jnp.float32),
            jax.ShapeDtypeStruct(here_mass.shape, jnp.float32),
        ],
        scratch_shapes=[
            pltpu.VMEM(here.shape, jnp.float32),
            pltpu.VMEM(here_mass.shape, jnp.float32),
            pltpu.SemaphoreType.DMA((here.shape[0] // block + 1,)),
        ],
        compiler_params=pltpu.CompilerParams(vmem_limit_bytes=VMEM_BYTES),
    )(here, here_mass, there, there_mass)


def split_cells(codes, exponents, centroids, counters):
    own = to_points(codes, exponents)
    rate = 4.0 / math.sqrt(own.shape[1]) * math.log2(math.e)
    plane = ("y", "x", "lo")

    turn = lambda a: exchange(a, plane, lambda at: at ^ (4 if at % 2 else 2))
    turn_back = lambda a: exchange(a, plane, lambda at: at ^ (2 if at % 2 else 4))
    along_z = lambda a, by: exchange(a, ("cells",), lambda at: at ^ by)
    around = lambda a, by: exchange(a, ("y", "x"), lambda at: at ^ by)

    per_device = centroids.shape[0] // 8
    block = per_device // 3

    near_1, near_2, near_3 = (along_z(own, by) for by in (1, 2, 3))
    inverse = inverse_call(counters)
    near_01 = join(own, near_1, inverse)
    held_01 = hold(near_01, declared=2 * 10**9)
    first_01 = turn(near_01)
    stats = [totals_call(rate, block, (held_01,), centroids, inverse)]
    second_01, across_01 = turn_back(hold(near_01, stats[0])), turn_back(hold(first_01, stats[0]))
    near_23 = join(near_2, near_3, *stats)
    stats.append(totals_call(rate, block, (near_23,), centroids, inverse, after=(first_01,)))
    first_23 = turn(near_23)
    stat = beside(*stats)
    expand = functools.partial(expo_call, rate, block, 2 * per_device)
    bundles = [expand((near_01, first_01, second_01, near_23), centroids, stat, declared=0.01)]
    goal = goal_call(rate, stat, *(along_z(stat, by) for by in (1, 2, 3)), bundles[0][1], across_01)
    across_23 = turn_back(hold(first_23, goal))

    second_23 = turn_back(hold(near_23, bundles[0][1]))
    bundles.append(expand((across_01, first_23, second_23), centroids, goal, declared=0.01))
    bundles.append(expand((across_23,), centroids, bundles[1][1]))
    expos, tops, points = zip(*bundles)
    goals = [goal, turn(goal), turn_back(goal), around(goal, 3)]
    factors = factor_call(rate, goals, tops)

    there = sums_call(per_device, 1, per_device, jnp.bfloat16, expos, points, factors)
    there = [exchange(a, ("lo",), lambda at: at ^ 1) for a in there]
    here = sums_call(per_device, 0, per_device, jnp.float32, expos, points, factors)
    out, mass = add_call(block, *here, *there)
    return (out[None], mass)


def solution(mesh):
    pts, cells = (mesh.shape[name] for name in ("pts", "cells"))
    square = (pts, cells) == (8, 4)
    shape, names = ((2, 2, 2, cells), ("y", "x", "lo", "cells")) if square else ((pts, cells), ("pts", "cells"))
    fine = Mesh(mesh.devices.reshape(shape), names)
    spread = names[:-1]
    in_specs = (P(names, None), P(names), P("cells", None), P("cells"))
    out_specs = (P("cells", spread, None), P("cells", spread))

    def run(codes, exponents, centroids, counters):
        small = codes.size * 2 <= GATHER_BYTES and codes.shape[0] == 128 * pts * cells
        body = split_cells if square and small else split_points
        mapped = jax.shard_map(body, mesh=fine, in_specs=in_specs, out_specs=out_specs, check_vma=False)
        return mapped(codes, exponents, centroids, counters)

    return run
```
